32 devices in a mesh: section: 2 (over core), dp: 4 (over z), tensor: 4 (over y, x).
Axes of the slice: x: 2, y: 2, z: 4, core: 2. Of those that a mesh axis runs over, the one named last changes fastest.
Arguments:
- tokens: bfloat16 [8, 1024, 1024], P('dp', 'tensor'), may hold values from -6 to 6
- cotangent: bfloat16 [8, 1024, 1024], P('dp', 'tensor'), may hold values from -6 to 6
- buckets: int32 [8], P('dp'), may hold values from 0 to 3, as said below
- lengths: int32 [8, 8], P('dp'), may hold values from 0 to 1024, as said below
- norm_gain_pairs: bfloat16 [2, 2, 1024], P('section'), may hold values from 0.25 to 1.75
- norm_bias_pairs: bfloat16 [2, 2, 1024], P('section'), may hold values from -1.796875 to 1.796875
- query_key_value_weight: bfloat16 [2, 1024, 3, 1024], P('section', None, None, 'tensor'), may hold values from -0.1875 to 0.1875
- query_value_bias: bfloat16 [2, 2, 1024], P('section', None, 'tensor'), may hold values from -1.796875 to 1.796875
- output_weight: bfloat16 [2, 1024, 1024], P('section', 'tensor'), may hold values from -0.75 to 0.75
- upward_weight: bfloat16 [2, 1024, 4096], P('section', None, 'tensor'), may hold values from -0.1875 to 0.1875
- upward_bias: bfloat16 [2, 4096], P('section', 'tensor'), may hold values from -1.796875 to 1.796875
- down_weight: bfloat16 [2, 4096, 1024], P('section', 'tensor'), may hold values from -0.09375 to 0.09375
- output_bias: bfloat16 [2, 2, 1024], P('section'), may hold values from -1.796875 to 1.796875
- adapter_down: bfloat16 [2, 2, 4, 1024], P('section'), may hold values from -0.1875 to 0.1875
- adapter_upper: bfloat16 [2, 2, 4, 1024], P('section', None, None, 'tensor'), may hold values from -0.23925781 to 0.23925781
Outputs:
- activations: bfloat16 [2, 8, 1024, 1024], P('section', 'dp', 'tensor')
- input_grad: bfloat16 [2, 8, 1024, 1024], P('section', 'dp', 'tensor')
- grad_lora_a: float32 [2, 2, 4, 1024], P('section')
- grad_lora_b: float32 [2, 2, 4, 1024], P('section', None, None, 'tensor')
The draws below stay inside these ranges and needn't reach their ends.
Inputs may be any that keep to these rules, and one draw needn't show every extreme that they name: `buckets`: A micro-batch with bucket b holds items padded to 1024 / 2**(3 - b) rows; among the 2 micro-batches of each index of dp one at least has bucket 3. `lengths`: entry i of a micro-batch is item i's true length, more than half of its padded length and at most that; one item of each micro-batch fills its padded length; entries of items past the micro-batch's item count are 0.
All inputs are finite; a program needn't handle non-finite values.
Results may differ from the reference program's by a relative error of at most 0.028.
Values may be sent and summed in bfloat16 or wider, within the bound.
A program may use at most 128 MiB of HBM per device.

```python
import jax
import jax.numpy as jnp
from jax import lax

MODEL_DIMENSION = 1024
HEADS = 16
HEAD_DIM = 64
FF = 4096
ADAPTER_RANK = 4
ROWS = 1024
SLOTS = 8
MICRO = 2
NMB = 8


def plan_draw(key):
    base = jax.random.fold_in(key, 11)
    key_bucket, key_pick, key_length, key_full = jax.random.split(base, 4)
    groups = NMB // MICRO
    bucket = jax.random.randint(key_bucket, (NMB,), 0, 4)
    picked = jax.random.randint(key_pick, (groups,), 0, MICRO)
    positions = jnp.arange(NMB, dtype=jnp.int32)
    bucket = jnp.where(positions % MICRO == picked[positions // MICRO], 3, bucket).astype(jnp.int32)
    item_span = jnp.right_shift(jnp.int32(ROWS), (3 - bucket).astype(jnp.int32))
    item_count = ROWS // item_span
    half_span = item_span // 2
    extra = jax.random.randint(key_length, (NMB, SLOTS), 0, ROWS) % half_span[:, None]
    lengths_all = half_span[:, None] + 1 + extra
    full_item = jax.random.randint(key_full, (NMB,), 0, 1 << 20) % item_count
    item_index = jnp.arange(SLOTS, dtype=jnp.int32)[None, :]
    lengths_all = jnp.where(item_index == full_item[:, None], item_span[:, None], lengths_all)
    lengths_all = jnp.where(item_index < item_count[:, None], lengths_all, 0)
    return (bucket, lengths_all.astype(jnp.int32))


def draw_buckets(key, part):
    return plan_draw(key)[0]


def draw_lengths(key, part):
    return plan_draw(key)[1]


def levels(key, dims, shards, low, top_value):
    gain = 1.0
    for dim, parts in shards:
        draws = jax.random.uniform(jax.random.fold_in(jax.random.fold_in(key, 6), dim), (parts,), jnp.float32, low / len(shards), top_value / len(shards))
        gain = gain * jnp.repeat(jnp.exp(draws), dims[dim] // parts).reshape((-1,) + (1,) * (len(dims) - 1 - dim))
    return gain


def scatter_about(stream_key, dims, scale, most, cuts=(), kind=jnp.bfloat16):
    factor_of = levels(stream_key, dims, cuts, -0.22, 0.18) if cuts else 1.0
    array = jax.random.normal(stream_key, dims, jnp.float32) * scale * factor_of
    return jnp.minimum(jnp.maximum(array, -most), most).astype(kind)


def setup_inputs(seed: int = 0) -> dict:
    key_of = jax.random.split(jax.random.key(seed), 16)
    tokens = scatter_about(key_of[0], (NMB, ROWS, MODEL_DIMENSION), 1.0, 6.0, ((0, 4), (1, 4)))
    cotangent = scatter_about(key_of[1], (NMB, ROWS, MODEL_DIMENSION), 1.0, 6.0, ((0, 4), (1, 4)))
    buckets = draw_buckets(jax.random.fold_in(key_of[15], 71), 0)
    lengths = draw_lengths(jax.random.fold_in(key_of[15], 71), 0)
    norm_gain_pairs = jnp.clip(1.0 + 0.15 * jax.random.normal(key_of[4], (2, 2, MODEL_DIMENSION), jnp.float32), 0.25, 1.75).astype(jnp.bfloat16)
    norm_bias_pairs = scatter_about(key_of[5], (2, 2, MODEL_DIMENSION), 0.3, 1.796875, ((0, 2),))
    query_key_value_weight = scatter_about(key_of[6], (2, MODEL_DIMENSION, 3, MODEL_DIMENSION), MODEL_DIMENSION ** -0.5, 0.1875, ((0, 2), (3, 4)))
    query_value_bias = scatter_about(key_of[7], (2, 2, MODEL_DIMENSION), 0.3, 1.796875, ((0, 2), (2, 4)))
    output_weight = scatter_about(key_of[8], (2, MODEL_DIMENSION, MODEL_DIMENSION), (MODEL_DIMENSION // 16) ** -0.5, 0.75, ((0, 2), (1, 4)))
    upward_weight = scatter_about(key_of[9], (2, MODEL_DIMENSION, FF), MODEL_DIMENSION ** -0.5, 0.1875, ((0, 2), (2, 4)))
    upward_bias = scatter_about(key_of[10], (2, FF), 0.3, 1.796875, ((0, 2), (1, 4)))
    down_weight = scatter_about(key_of[11], (2, FF, MODEL_DIMENSION), FF ** -0.5, 0.09375, ((0, 2), (1, 4)))
    output_bias = scatter_about(key_of[12], (2, 2, MODEL_DIMENSION), 0.3, 1.796875, ((0, 2),))
    adapter_down = scatter_about(key_of[13], (2, 2, ADAPTER_RANK, MODEL_DIMENSION), MODEL_DIMENSION ** -0.5, 0.1875, ((0, 2),))
    adapter_upper = scatter_about(key_of[14], (2, 2, ADAPTER_RANK, MODEL_DIMENSION), 0.04, 0.23925781, ((0, 2), (3, 4)))
    return {"tokens": tokens, "cotangent": cotangent, "buckets": buckets, "lengths": lengths, "norm_gain_pairs": norm_gain_pairs, "norm_bias_pairs": norm_bias_pairs, "query_key_value_weight": query_key_value_weight, "query_value_bias": query_value_bias, "output_weight": output_weight, "upward_weight": upward_weight, "upward_bias": upward_bias, "down_weight": down_weight, "output_bias": output_bias, "adapter_down": adapter_down, "adapter_upper": adapter_upper}


@jax.custom_vjp
def low(v):
    return lax.optimization_barrier(v.astype(jnp.bfloat16)).astype(jnp.float32)

@jax.custom_vjp
def low_back(v):
    return v

def low_keep(v):
    return (low(v), None)

def low_pass(kept, grad):
    return (grad,)

def back_keep(v):
    return (v, None)

def back_low(kept, grad):
    return (low(grad),)
low.defvjp(low_keep, low_pass)
low_back.defvjp(back_keep, back_low)
adapter_scale = 8.0
norm_eps = 1e-05
masked_score = -1000000000.0
highest_precision = lax.Precision.HIGHEST

def layer_norm(values, gain_rows, shifts):
    center = lax.optimization_barrier(jnp.mean(values, axis=-1, keepdims=True))
    centered = values - center
    spread = lax.optimization_barrier(jnp.mean(centered * centered, axis=-1, keepdims=True))
    return centered * lax.rsqrt(spread + norm_eps) * gain_rows + shifts

def row_layout(bucket, lengths_row, row_count):
    item_span = jnp.right_shift(jnp.int32(row_count), (3 - bucket).astype(jnp.int32))
    positions = jnp.arange(row_count, dtype=jnp.int32)
    item_index = positions // item_span
    within = positions - item_index * item_span
    chosen = (item_index[:, None] == jnp.arange(lengths_row.shape[0], dtype=jnp.int32)[None, :]).astype(jnp.int32)
    length = lax.optimization_barrier(jnp.sum(chosen * lengths_row[None, :], axis=1))
    return (item_index, within < length)

def allowed_keys(item_index, is_valid):
    positions = jnp.arange(item_index.shape[0], dtype=jnp.int32)
    same_item = item_index[:, None] == item_index[None, :]
    causal = positions[None, :] <= positions[:, None]
    key_seen = is_valid[None, :] | (positions[None, :] == positions[:, None])
    return same_item & causal & key_seen

def one_layer(hidden, allowed, gain_rows, shifts, weight_qkv, bias_query_value, weight_out, weight_up, bias_up, weight_down, biases, down_factor, upper_factor):
    row_count = hidden.shape[0]
    normed = low(layer_norm(hidden, gain_rows[0], shifts[0]))
    reduced_query = low(jnp.dot(normed, down_factor[0].T, precision=highest_precision))
    reduced_value = low(jnp.dot(normed, down_factor[1].T, precision=highest_precision))
    blended_rows = jnp.einsum('rd,dcn->rcn', normed, weight_qkv, precision=highest_precision)
    query_matrix_rows = blended_rows[:, 0] + bias_query_value[0] + adapter_scale * jnp.dot(reduced_query, upper_factor[0], precision=highest_precision)
    value_matrix_rows = blended_rows[:, 2] + bias_query_value[1] + adapter_scale * jnp.dot(reduced_value, upper_factor[1], precision=highest_precision)
    packed = low(low_back(jnp.stack([query_matrix_rows, blended_rows[:, 1], value_matrix_rows], axis=1)))
    head_split = packed.reshape(row_count, 3, HEADS, HEAD_DIM)
    scores = jnp.einsum('qhe,khe->hqk', head_split[:, 0], head_split[:, 1], precision=highest_precision) * HEAD_DIM ** (-0.5)
    scores = low_back(jnp.where(allowed[None], scores, masked_score))
    attn_probs = low(jax.nn.softmax(scores, axis=-1))
    attended = jnp.einsum('hqk,khe->qhe', attn_probs, head_split[:, 2], precision=highest_precision).reshape(row_count, HEADS * HEAD_DIM)
    attended = low(low_back(attended))
    attn_branch = low_back(jnp.dot(attended, weight_out, precision=highest_precision) + biases[0])
    middle = hidden + attn_branch
    normed_two = low(layer_norm(middle, gain_rows[1], shifts[1]))
    hidden_pre = low_back(jnp.dot(normed_two, weight_up, precision=highest_precision) + bias_up)
    activated = low(jax.nn.gelu(hidden_pre, approximate=True))
    branch = low_back(jnp.dot(activated, weight_down, precision=highest_precision) + biases[1])
    return middle + branch

def reference(tokens, cotangent, buckets, lengths, norm_gain_pairs, norm_bias_pairs, query_key_value_weight, query_value_bias, output_weight, upward_weight, upward_bias, down_weight, output_bias, adapter_down, adapter_upper):
    gain_all = norm_gain_pairs.astype(jnp.float32)
    shift_all = norm_bias_pairs.astype(jnp.float32)
    qkv_all = query_key_value_weight.astype(jnp.float32)
    bias_qv_all = query_value_bias.astype(jnp.float32)
    out_all = output_weight.astype(jnp.float32)
    up_all = upward_weight.astype(jnp.float32)
    bias_up_all = upward_bias.astype(jnp.float32)
    down_all = down_weight.astype(jnp.float32)
    bias_all = output_bias.astype(jnp.float32)
    down_factor_stack = adapter_down.astype(jnp.float32)
    upper_factor_stack = adapter_upper.astype(jnp.float32)

    def layer_at(index, hidden, allowed, factors_a, factors_b):
        return one_layer(hidden, allowed, gain_all[index], shift_all[index], qkv_all[index], bias_qv_all[index], out_all[index], up_all[index], bias_up_all[index], down_all[index], bias_all[index], factors_a[index], factors_b[index])

    def per_batch(totals, inputs):
        token_rows, cot_rows, bucket, lengths_row = inputs
        item_index, is_valid = row_layout(bucket, lengths_row, ROWS)
        allowed = allowed_keys(item_index, is_valid)

        def stacked(layer_input, probe, factors_a, factors_b):
            first_out = layer_at(0, low_back(layer_input), allowed, factors_a, factors_b)
            second_out = layer_at(1, low_back(low(first_out) + probe), allowed, factors_a, factors_b)
            return (second_out, first_out)
        probe_zero = jnp.zeros((ROWS, MODEL_DIMENSION), jnp.float32)
        second_out, pull_back, first_out = jax.vjp(stacked, token_rows.astype(jnp.float32), probe_zero, down_factor_stack, upper_factor_stack, has_aux=True)
        seed_grad = cot_rows.astype(jnp.float32) * is_valid[:, None].astype(jnp.float32)
        grad_tokens, grad_probe, grad_a, grad_b = pull_back(seed_grad)
        totals = (totals[0] + grad_a, totals[1] + grad_b)
        return (totals, (first_out.astype(jnp.bfloat16), second_out.astype(jnp.bfloat16), grad_tokens.astype(jnp.bfloat16), grad_probe.astype(jnp.bfloat16)))
    start_totals = (jnp.zeros(down_factor_stack.shape, jnp.float32), jnp.zeros(upper_factor_stack.shape, jnp.float32))
    totals, results = lax.scan(per_batch, start_totals, (tokens, cotangent, buckets, lengths))
    first_out, second_out, grad_first, grad_second = results
    return (jnp.stack([first_out, second_out]), jnp.stack([grad_first, grad_second]), totals[0], totals[1])
```

```python
from functools import partial

import jax
import jax.numpy as jnp
from jax import lax
from jax.experimental import pallas as pl
from jax.experimental.pallas import tpu as pltpu
from jax.sharding import PartitionSpec as P

HEAD_DIM = 64


adapter_scale = 8.0
norm_eps = 1e-05
masked_score = -1000000000.0
highest_precision = lax.Precision.HIGHEST


def from_behind(block, axis, distance):
    devices = range(lax.axis_size(axis))
    route = [(i - distance, i) for i in devices if i - distance in devices]
    return lax.ppermute(block, axis, route)


def layer_norm(values, gain_rows, shifts):
    center = jnp.mean(values, axis=-1, keepdims=True)
    centered = values - center
    spread = jnp.mean(centered * centered, axis=-1, keepdims=True)
    return centered * lax.rsqrt(spread + norm_eps) * gain_rows + shifts


def row_layout(bucket, lengths_row, row_count):
    item_span = jnp.right_shift(jnp.int32(row_count), 3 - bucket)
    positions = jnp.arange(row_count, dtype=jnp.int32)
    item_index = positions // item_span
    within = positions - item_index * item_span
    chosen = (
        item_index[:, None] == jnp.arange(lengths_row.shape[0], dtype=jnp.int32)[None, :]
    ).astype(jnp.int32)
    length = jnp.sum(chosen * lengths_row[None, :], axis=1)
    return (item_index, within < length)


def allowed_keys(item_index, is_valid):
    positions = jnp.arange(item_index.shape[0], dtype=jnp.int32)
    same_item = item_index[:, None] == item_index[None, :]
    causal = positions[None, :] <= positions[:, None]
    key_seen = is_valid[None, :] | (positions[None, :] == positions[:, None])
    return same_item & causal & key_seen


def take_slot(buffer, slot_index):
    return lax.dynamic_index_in_dim(buffer, slot_index, 0, keepdims=False)


def put_slot(buffer, slot_index, is_live, update):
    previous = take_slot(buffer, slot_index)
    return lax.dynamic_update_index_in_dim(
        buffer, jnp.where(is_live, update, previous), slot_index, 0
    )


def per_device(
    tokens,
    cotangent,
    buckets,
    lengths,
    norm_gain_pairs,
    norm_bias_pairs,
    query_key_value_weight,
    query_value_bias,
    output_weight,
    upward_weight,
    upward_bias,
    down_weight,
    output_bias,
    adapter_down,
    adapter_upper,
):
    section_index = lax.axis_index("section")
    tensor_count = lax.axis_size("tensor")
    micro_count, own_rows, model_width = tokens.shape
    row_count = own_rows * tensor_count
    own_start = lax.axis_index("tensor") * own_rows
    gain_sets = norm_gain_pairs[0].astype(jnp.float32)
    shift_sets = norm_bias_pairs[0].astype(jnp.float32)
    weight_qkv = query_key_value_weight[0]
    bias_query_value = query_value_bias[0].astype(jnp.float32)
    weight_out = output_weight[0]
    weight_up = upward_weight[0]
    bias_up = upward_bias[0].astype(jnp.float32)
    weight_down = down_weight[0]
    biases = output_bias[0].astype(jnp.float32)
    down_factor = adapter_down[0]
    upper_factor = adapter_upper[0]
    factor_wide = down_factor.astype(jnp.float32)
    local_width = weight_qkv.shape[2]
    local_heads = local_width // HEAD_DIM
    score_scale = HEAD_DIM ** (-0.5)

    def widen(values):
        return lax.all_gather(values, "tensor", axis=0, tiled=True)

    def widen_back(values):
        return lax.all_gather(values, "tensor", axis=0, tiled=True)

    def settle(source, weight):

        def row_term(first_row, row_span):
            return jnp.dot(source, weight, preferred_element_type=jnp.float32)

        return lax.psum_scatter(
            row_term(jnp.int32(0), lax.axis_size("tensor") * own_rows).astype(jnp.bfloat16),
            "tensor",
            scatter_dimension=0,
            tiled=True,
        ).astype(jnp.float32)

    def settle_back(row_term):
        return lax.psum_scatter(
            row_term(jnp.int32(0), lax.axis_size("tensor") * own_rows).astype(jnp.bfloat16),
            "tensor",
            scatter_dimension=0,
            tiled=True,
        ).astype(jnp.float32)

    def layout_of(slot_index):
        item_index, is_valid = row_layout(
            take_slot(buckets, slot_index), take_slot(lengths, slot_index), row_count
        )
        own_valid = lax.dynamic_slice_in_dim(is_valid, own_start, own_rows, 0)
        return (allowed_keys(item_index, is_valid), own_valid)

    def attend(normed, allowed):
        reduced_query = jnp.dot(
            normed, down_factor[0].T, preferred_element_type=jnp.float32
        ).astype(jnp.bfloat16)
        reduced_value = jnp.dot(
            normed, down_factor[1].T, preferred_element_type=jnp.float32
        ).astype(jnp.bfloat16)
        blended_rows = jnp.einsum(
            "rd,dcn->rcn", normed, weight_qkv, preferred_element_type=jnp.float32
        )
        query_matrix_rows = (
            blended_rows[:, 0]
            + bias_query_value[0]
            + adapter_scale
            * jnp.dot(reduced_query, upper_factor[0], preferred_element_type=jnp.float32)
        )
        value_matrix_rows = (
            blended_rows[:, 2]
            + bias_query_value[1]
            + adapter_scale
            * jnp.dot(reduced_value, upper_factor[1], preferred_element_type=jnp.float32)
        )
        packed = jnp.stack(
            [query_matrix_rows, blended_rows[:, 1], value_matrix_rows], axis=1
        ).astype(jnp.bfloat16)
        head_split = packed.reshape(row_count, 3, local_heads, HEAD_DIM)
        scores = (
            jnp.einsum(
                "qhe,khe->hqk",
                head_split[:, 0],
                head_split[:, 1],
                preferred_element_type=jnp.float32,
            )
            * score_scale
        )
        scores = jnp.where(allowed[None], scores, masked_score)
        top_score = jnp.max(scores, axis=-1, keepdims=True)
        exponent = jnp.exp(scores - top_score)
        attn_probs = exponent / jnp.sum(exponent, axis=-1, keepdims=True)
        return (reduced_query, reduced_value, head_split, attn_probs)

    def forward(hidden, allowed):
        normed = widen(layer_norm(hidden, gain_sets[0], shift_sets[0]).astype(jnp.bfloat16))
        reduced_query, reduced_value, head_split, attn_probs = attend(normed, allowed)
        probs_low = attn_probs.astype(jnp.bfloat16)
        mixed_heads = jnp.einsum(
            "hqk,khe->qhe", probs_low, head_split[:, 2], preferred_element_type=jnp.float32
        )
        attended = mixed_heads.reshape(row_count, local_width).astype(jnp.bfloat16)
        middle = hidden + (settle(attended, weight_out) + biases[0])
        normed_two = widen(layer_norm(middle, gain_sets[1], shift_sets[1]).astype(jnp.bfloat16))
        hidden_pre = jnp.dot(normed_two, weight_up, preferred_element_type=jnp.float32) + bias_up
        activated = jax.nn.gelu(hidden_pre, approximate=True).astype(jnp.bfloat16)
        output = middle + (settle(activated, weight_down) + biases[1])
        return (output, normed, middle, normed_two)

    def backward(hidden, grad_out, allowed, normed, middle, normed_two):
        reduced_query, reduced_value, head_split, attn_probs = attend(normed, allowed)
        probs_low = attn_probs.astype(jnp.bfloat16)
        hidden_pre = jnp.dot(normed_two, weight_up, preferred_element_type=jnp.float32) + bias_up
        grad_branch = widen_back(grad_out.astype(jnp.bfloat16))
        grad_act = jnp.einsum(
            "rd,fd->rf", grad_branch, weight_down, preferred_element_type=jnp.float32
        )
        gelu_pull = jax.vjp(partial(jax.nn.gelu, approximate=True), hidden_pre)[1]
        grad_pre = gelu_pull(grad_act)[0].astype(jnp.bfloat16)

        def mlp_term(first_row, row_span):
            return jnp.einsum("rf,df->rd", grad_pre, weight_up, preferred_element_type=jnp.float32)

        grad_norm_two = settle_back(mlp_term)
        second_pull = jax.vjp(
            partial(layer_norm, gain_rows=gain_sets[1], shifts=shift_sets[1]), middle
        )[1]
        grad_middle = grad_out + second_pull(grad_norm_two)[0]
        grad_attn = widen_back(grad_middle.astype(jnp.bfloat16))
        grad_heads = jnp.einsum(
            "rd,nd->rn", grad_attn, weight_out, preferred_element_type=jnp.float32
        )
        grad_heads = grad_heads.astype(jnp.bfloat16).reshape(row_count, local_heads, HEAD_DIM)
        grad_probs = jnp.einsum(
            "qhe,khe->hqk", grad_heads, head_split[:, 2], preferred_element_type=jnp.float32
        )
        grad_scores = attn_probs * (
            grad_probs - jnp.sum(attn_probs * grad_probs, axis=-1, keepdims=True)
        )
        grad_scores = grad_scores.astype(jnp.bfloat16)
        grad_query = (
            jnp.einsum(
                "hqk,khe->qhe", grad_scores, head_split[:, 1], preferred_element_type=jnp.float32
            )
            * score_scale
        )
        grad_key = (
            jnp.einsum(
                "hqk,qhe->khe", grad_scores, head_split[:, 0], preferred_element_type=jnp.float32
            )
            * score_scale
        )
        grad_value = jnp.einsum(
            "hqk,qhe->khe", probs_low, grad_heads, preferred_element_type=jnp.float32
        )
        grad_packed = (
            jnp.stack([grad_query, grad_key, grad_value], axis=1)
            .reshape(row_count, 3, local_width)
            .astype(jnp.bfloat16)
        )
        grad_pair = jnp.stack([grad_packed[:, 0], grad_packed[:, 2]])
        gradient_reduced = adapter_scale * jnp.einsum(
            "jrn,jkn->jrk", grad_pair, upper_factor, preferred_element_type=jnp.float32
        )

        def attn_term(first_row, row_span):
            dense_part = jnp.einsum(
                "rcn,dcn->rd", grad_packed, weight_qkv, preferred_element_type=jnp.float32
            )
            return dense_part + jnp.einsum(
                "jrk,jkd->rd", gradient_reduced, factor_wide, precision=highest_precision
            )

        grad_normed = settle_back(attn_term)
        first_pull = jax.vjp(
            partial(layer_norm, gain_rows=gain_sets[0], shifts=shift_sets[0]), hidden
        )[1]
        grad_hidden = grad_middle + first_pull(grad_normed)[0]
        grad_factor_a = jnp.einsum(
            "jrk,rd->jkd", gradient_reduced, normed.astype(jnp.float32), precision=highest_precision
        )
        gradient_upper_factor = adapter_scale * jnp.stack(
            [
                jnp.einsum(
                    "rk,rn->kn",
                    reduced_query,
                    grad_packed[:, 0],
                    preferred_element_type=jnp.float32,
                ),
                jnp.einsum(
                    "rk,rn->kn",
                    reduced_value,
                    grad_packed[:, 2],
                    preferred_element_type=jnp.float32,
                ),
            ]
        )
        return (grad_hidden, grad_factor_a, gradient_upper_factor)

    zero_rows = jnp.zeros((micro_count, own_rows, model_width), jnp.bfloat16)
    saved_start = ()

    def record(buffers, slot_index, is_live, layer_input, results):
        kept_in, outputs, saved = buffers
        output, normed, middle, normed_two = results
        low_output = output.astype(jnp.bfloat16)
        kept_in = put_slot(kept_in, slot_index, is_live, layer_input)
        outputs = put_slot(outputs, slot_index, is_live, low_output)
        return ((kept_in, outputs, saved), low_output)

    buffers = (zero_rows, zero_rows, saved_start)

    def run_phase(buffers, sources, phase_section):

        def phase_turn(slot_index, buffers):
            allowed, own_valid = layout_of(slot_index)
            layer_input = take_slot(sources, slot_index)
            results = forward(layer_input.astype(jnp.float32), allowed)
            return record(
                buffers, slot_index, section_index == phase_section, layer_input, results
            )[0]

        return lax.fori_loop(0, micro_count, phase_turn, buffers)

    buffers = run_phase(buffers, tokens, 0)
    received = from_behind(buffers[1], "section", 1)
    buffers = run_phase(buffers, received, 1)
    kept_in, outputs, saved = buffers

    def back_step(slot_index, grad_out, allowed):
        hidden = take_slot(kept_in, slot_index).astype(jnp.float32)
        output, normed, middle, normed_two = forward(hidden, allowed)
        return backward(hidden, grad_out, allowed, normed, middle, normed_two)

    def top_grad(slot_index, own_valid):
        return take_slot(cotangent, slot_index).astype(jnp.float32) * own_valid[:, None].astype(
            jnp.float32
        )

    zero_a = jnp.zeros(down_factor.shape, jnp.float32)
    zero_b = jnp.zeros(upper_factor.shape, jnp.float32)

    def run_back(loop_state, sources, phase_section):

        def phase_turn(slot_index, loop_state):
            grads_in, sum_a, sum_b = loop_state
            allowed, own_valid = layout_of(slot_index)
            if phase_section == 1:
                grad_out = top_grad(slot_index, own_valid)
            else:
                grad_out = take_slot(sources, slot_index).astype(jnp.float32)
            is_live = section_index == phase_section
            grad_hidden, grad_a, grad_b = back_step(slot_index, grad_out, allowed)
            grads_in = put_slot(grads_in, slot_index, is_live, grad_hidden.astype(jnp.bfloat16))
            sum_a = sum_a + jnp.where(is_live, grad_a, 0.0)
            sum_b = sum_b + jnp.where(is_live, grad_b, 0.0)
            return (grads_in, sum_a, sum_b)

        return lax.fori_loop(0, micro_count, phase_turn, loop_state)

    loop_state = run_back((zero_rows, zero_a, zero_b), zero_rows, 1)
    received_grads = from_behind(loop_state[0], "section", -1)
    grads_in, sum_a, sum_b = run_back(loop_state, received_grads, 0)
    total_a = lax.psum(sum_a, ("dp", "tensor"))
    total_b = lax.psum(sum_b, "dp")
    return (outputs[None], grads_in[None], total_a[None], total_b[None])


R = 256
D = 1024
NEG = -1e30
F32 = jnp.float32
BF16 = jnp.bfloat16
MESH = pl.DeviceIdType.MESH
CHUNK = 32


def nn(a, b):
    return lax.dot_general(a, b, (((1,), (0,)), ((), ())), preferred_element_type=F32)


def nt(a, b):
    return lax.dot_general(a, b, (((1,), (1,)), ((), ())), preferred_element_type=F32)


def tn(a, b):
    return lax.dot_general(a, b, (((0,), (0,)), ((), ())), preferred_element_type=F32)


def normalize(v):
    centered = v - jnp.mean(v, axis=-1, keepdims=True)
    rs = lax.rsqrt(jnp.mean(centered * centered, axis=-1, keepdims=True) + norm_eps)
    return centered * rs, rs


def norm_pull(v, g):
    xhat, rs = normalize(v)
    return rs * (
        g
        - jnp.mean(g, axis=-1, keepdims=True)
        - xhat * jnp.mean(g * xhat, axis=-1, keepdims=True)
    )


def gelu_pair(z):
    c = 0.7978845608028654
    z2 = z * z
    t = jnp.tanh(c * (z + 0.044715 * (z2 * z)))
    half = 0.5 * (1.0 + t)
    slope = half + (0.5 * c) * z * (1.0 - t * t) * (1.0 + (3.0 * 0.044715) * z2)
    return z * half, slope


def fused_kernel(
    tok, cot, buckets, lengths, small_in, wq_in, wo_in, wu_in, wd_in,
    act, ig, ga, gb,
    SP, WQ, WO, WU, WD, H, DY, MID, GP, Q, KV, OT, LSE, SND, RCV, ACC, ST, MSK,
    DKV, DR, DQ, DOT, DO, AB, U, OACC,
    tok_sem, tok_snd, wsem, wloc, wsib, wy, wfwd, kv_rcv, kv_snd, x_rcv, x_snd,
    dr_rcv, dr_snd, out_rcv, out_snd,
):
    s = lax.axis_index("section")
    d = lax.axis_index("dp")
    t = lax.axis_index("tensor")
    x = lax.rem(t, 2)
    y = lax.div(t, 2)
    sib = (1 - s, d, t)
    xp = (s, d, y * 2 + 1 - x)
    yp = (s, d, (1 - y) * 2 + x)
    flip = s + x - 2 * s * x
    own_i = flip

    def blk_of(i):
        return 2 * i + (s + i - 2 * s * i)

    bar = pltpu.get_barrier_semaphore()
    for ds_ in range(2):
        for dx in range(2):
            for dy in range(2):
                if ds_ or dx or dy:
                    s2 = 1 - s if ds_ else s
                    x2 = 1 - x if dx else x
                    y2 = 1 - y if dy else y
                    pl.semaphore_signal(bar, 1, device_id=(s2, d, y2 * 2 + x2), device_id_type=MESH)
    pl.semaphore_wait(bar, 7)

    my_core = x + y - 2 * x * y

    def spread(src, dst, which):
        @pl.when(s == my_core)
        def _():
            for k, (dx, dy) in enumerate(((1, 0), (0, 1), (1, 1))):
                x2 = 1 - x if dx else x
                y2 = 1 - y if dy else y
                pltpu.make_async_remote_copy(
                    src.at[y2], dst.at[y], tok_snd.at[which, k], tok_sem.at[which, y],
                    device_id=(s, d, y2 * 2 + x2), device_id_type=MESH,
                ).start()
            pltpu.make_async_copy(src.at[y], dst.at[y], tok_sem.at[which, y]).start()

    def spread_done(src, dst, which):
        @pl.when(s == my_core)
        def _():
            for k, (dx, dy) in enumerate(((1, 0), (0, 1), (1, 1))):
                x2 = 1 - x if dx else x
                y2 = 1 - y if dy else y
                pltpu.make_async_remote_copy(
                    src.at[y2], dst.at[y], tok_snd.at[which, k], tok_sem.at[which, y],
                    device_id=(s, d, y2 * 2 + x2), device_id_type=MESH,
                ).wait_send()

    pieces = ((small_in, SP), (wq_in, WQ), (wo_in, WO), (wu_in, WU), (wd_in, WD))

    def w_local(p):
        src, dst = pieces[p]
        return pltpu.make_async_copy(src, dst.at[s, y], wsem.at[s, y, p])

    def w_sib(p):
        src, dst = pieces[p]
        return pltpu.make_async_remote_copy(
            src, dst.at[s, y], wsib.at[p], wsem.at[s, y, p], device_id=sib, device_id_type=MESH)

    def w_y(p):
        src, dst = pieces[p]
        return pltpu.make_async_remote_copy(
            src, dst.at[s, y], wy.at[p], wsem.at[s, y, p], device_id=yp, device_id_type=MESH)

    def w_forward(p):
        dst = pieces[p][1]
        return pltpu.make_async_remote_copy(
            dst.at[s, 1 - y], dst.at[s, 1 - y], wfwd.at[p], wsem.at[s, 1 - y, p],
            device_id=sib, device_id_type=MESH)

    def w_wait(l, j, p):
        src, dst = pieces[p]
        pltpu.make_async_copy(src, dst.at[l, j], wsem.at[l, j, p]).wait()

    def w_ready(l, p):
        w_wait(l, 0, p)
        w_wait(l, 1, p)

        @pl.when(l == s)
        def _():
            w_forward(p).start()

    spread(tok, H.at[0], 0)
    for p in range(2):
        w_local(p).start()
        w_sib(p).start()

        @pl.when(s == 0)
        def _():
            w_y(p).start()
    for p in range(2, 5):
        w_local(p).start()
        w_sib(p).start()

        @pl.when(s == 0)
        def _():
            w_y(p).start()

    shift = 7 + buckets[y]
    span_mask = lax.shift_left(jnp.int32(1), shift) - 1

    def length_of(pos):
        item = lax.shift_right_logical(pos, jnp.broadcast_to(shift, pos.shape))
        got = jnp.zeros(pos.shape, jnp.int32)
        for k in range(lengths.shape[1]):
            got = jnp.where(item == k, lengths[y, k], got)
        return item, jnp.bitwise_and(pos, span_mask) < got

    def build_mask(i):
        b = blk_of(i)
        q_row = b * R + lax.broadcasted_iota(jnp.int32, (1, R), 1)
        q_item = lax.shift_right_logical(q_row, jnp.broadcast_to(shift, q_row.shape))

        def rows(r, carry):
            r0 = pl.multiple_of(r * CHUNK, CHUNK)
            k_row = r0 + lax.broadcasted_iota(jnp.int32, (CHUNK, 1), 0)
            k_item, k_ok = length_of(k_row)
            k_tag = jnp.where(k_ok, k_item, -1)
            same = (k_tag == q_item) & (k_row <= q_row)
            allowed = same | (k_row == q_row)
            MSK[i, pl.ds(r0, CHUNK), :] = jnp.where(allowed, 0.0, NEG).astype(BF16)
            return carry

        lax.fori_loop(0, (b + 1) * (R // CHUNK), rows, 0)

    build_mask(0)
    build_mask(1)
    ga[...] = jnp.zeros(ga.shape, F32)
    gb[...] = jnp.zeros(gb.shape, F32)

    def x_copy(slot, i):
        return pltpu.make_async_remote_copy(
            SND.at[slot, i], RCV.at[slot, i], x_snd.at[slot, i], x_rcv.at[slot, i],
            device_id=xp, device_id_type=MESH)

    def by_rows(body, step=CHUNK):
        def turn(r, carry):
            body(pl.ds(pl.multiple_of(r * step, step), step))
            return carry

        lax.fori_loop(0, R // step, turn, 0)

    def swapped(slot, i, rows):
        return SND[slot, i, rows, :].astype(F32) + RCV[slot, i, rows, :].astype(F32)

    def send_result(which, layer, src):
        dst = act if which < 2 else ig
        o = 0 if which < 2 else 1
        here = (s == layer) & (y == own_i)

        @pl.when(here)
        def _():
            pltpu.make_async_copy(src, dst.at[y], out_rcv.at[o, y]).start()

        @pl.when(jnp.logical_not(here))
        def _():
            pltpu.make_async_remote_copy(
                src, dst.at[y], out_snd.at[which], out_rcv.at[o, y],
                device_id=(layer, d, own_i * 2 + x), device_id_type=MESH).start()

    def send_result_done(which, layer, src):
        dst = act if which < 2 else ig
        o = 0 if which < 2 else 1
        here = (s == layer) & (y == own_i)

        @pl.when(jnp.logical_not(here))
        def _():
            pltpu.make_async_remote_copy(
                src, dst.at[y], out_snd.at[which], out_rcv.at[o, y],
                device_id=(layer, d, own_i * 2 + x), device_id_type=MESH).wait_send()

    def vec(l, k):
        return SP[l, 0, k : k + 1, :]

    def head_lanes(pair):
        return pl.ds(pl.multiple_of(pair * 128, 128), 128)

    def split_pair(v, axis):
        which = lax.broadcasted_iota(jnp.int32, v.shape, axis) < HEAD_DIM
        zero = jnp.zeros_like(v)
        return jnp.where(which, v, zero), jnp.where(which, zero, v)

    def kv_copy(l, i):
        rows = pl.ds(pl.multiple_of(blk_of(i) * R, R), R)
        return pltpu.make_async_remote_copy(
            KV.at[l, :, rows, :], KV.at[l, :, rows, :], kv_snd.at[l, i], kv_rcv.at[l, i],
            device_id=sib, device_id_type=MESH)

    def kv_wait(l, i):
        b = 2 * i + (1 - s + i - 2 * (1 - s) * i)
        rows = pl.ds(pl.multiple_of(b * R, R), R)
        pltpu.make_async_remote_copy(
            KV.at[l, :, rows, :], KV.at[l, :, rows, :], kv_snd.at[l, i], kv_rcv.at[l, i],
            device_id=sib, device_id_type=MESH).wait_recv()

    def attend(l, i):
        b = blk_of(i)

        def pair_turn(pair, carry):
            lanes = head_lanes(pair)
            qs = split_pair(Q[l, i, :, lanes], 1)

            def first(j, tops):
                rows = pl.ds(pl.multiple_of(j * R, R), R)
                keys = KV[l, 0, rows, lanes]
                mask = MSK[i, rows, :].astype(F32)
                new = []
                for e in range(2):
                    st = nt(keys, qs[e]) + mask
                    ST[e, rows, :] = st
                    new.append(jnp.maximum(tops[e], jnp.max(st, axis=0, keepdims=True)))
                return tuple(new)

            tops = lax.fori_loop(0, b + 1, first, (jnp.full((1, R), NEG, F32),) * 2)
            OACC[...] = jnp.zeros(OACC.shape, F32)

            def second(j, sums):
                rows = pl.ds(pl.multiple_of(j * R, R), R)
                values = KV[l, 1, rows, lanes]
                new = []
                for e in range(2):
                    p = jnp.exp(ST[e, rows, :] - tops[e])
                    new.append(sums[e] + jnp.sum(p, axis=0, keepdims=True))
                    OACC[e] += tn(values, p.astype(BF16))
                return tuple(new)

            sums = lax.fori_loop(0, b + 1, second, (jnp.zeros((1, R), F32),) * 2)
            for e in range(2):
                OT[l, i, pl.ds(pl.multiple_of(pair * 128 + e * 64, 64), 64), :] = (
                    OACC[e, e * 64 : e * 64 + 64, :] * (1.0 / sums[e])
                ).astype(BF16)
                LSE[l, i, pair * 2 + e] = tops[e] + jnp.log(sums[e])
            return carry

        lax.fori_loop(0, Q.shape[3] // 128, pair_turn, 0)

    def forward_attention(l, i):
        b = blk_of(i)

        @pl.when(i == 0)
        def _():
            w_ready(l, 0)
            w_ready(l, 1)

        @pl.when(l == 0)
        def _():
            pltpu.make_async_copy(tok.at[0], H.at[0, i], tok_sem.at[0, i]).wait()

        @pl.when(l == 1)
        def _():
            x_copy(1, i).wait_recv()

            def rows_in(rows):
                h = MID[0, i, rows, :] + (swapped(1, i, rows) + vec(0, 5))
                H[1, i, rows, :] = h.astype(BF16)

            by_rows(rows_in)

            @pl.when(i == own_i)
            def _():
                send_result(0, 0, H.at[1, i])

        def rows_norm(rows):
            xhat, _ = normalize(H[l, i, rows, :].astype(F32))
            AB[rows, :] = (xhat * vec(l, 0) + vec(l, 1)).astype(BF16)

        by_rows(rows_norm)
        u = nt(AB[...], SP[l, 0, 8:16, :].astype(BF16)).astype(BF16)
        U[l, i] = u
        own_rows = pl.ds(pl.multiple_of(b * R, R), R)
        for j in range(2):
            up = SP[l, j, 24:32, 0:768].astype(BF16)
            qkv = nn(AB[...], WQ[l, j]) + (adapter_scale * nn(u, up) + SP[l, j, 17:18, 0:768])
            cols = slice(j * 256, j * 256 + 256)
            Q[l, i, :, cols] = (qkv[:, 0:256] * HEAD_DIM ** -0.5).astype(BF16)
            KV[l, 0, own_rows, cols] = qkv[:, 256:512].astype(BF16)
            KV[l, 1, own_rows, cols] = qkv[:, 512:768].astype(BF16)

        @pl.when(b != 3)
        def _():
            kv_copy(l, i).start()

        @pl.when((s == 1) & (i == 0))
        def _():
            kv_wait(l, 0)

        @pl.when((s == 0) & (i == 1))
        def _():
            kv_wait(l, 0)
            kv_wait(l, 1)

        attend(l, i)

        @pl.when(i == 0)
        def _():
            w_ready(l, 2)

        @pl.when(l == 1)
        def _():
            x_copy(0, i).wait_send()

        SND[0, i] = (tn(OT[l, i, 0:256, :], WO[l, 0]) + tn(OT[l, i, 256:512, :], WO[l, 1])).astype(BF16)
        x_copy(0, i).start()

    def forward_ff(l, i):
        @pl.when(i == 0)
        def _():
            @pl.when((s == 1) & (l == 0))
            def _():
                for p in range(5):
                    w_y(p).start()

            w_ready(l, 3)
            w_ready(l, 4)

        x_copy(0, i).wait_recv()

        def rows_mid(rows):
            mid = H[l, i, rows, :].astype(F32) + (swapped(0, i, rows) + vec(l, 4))
            MID[l, i, rows, :] = mid
            xhat, _ = normalize(mid)
            AB[rows, :] = (xhat * vec(l, 2) + vec(l, 3)).astype(BF16)

        by_rows(rows_mid)
        for n in range(4):
            j, half = n // 2, n % 2
            cols = slice(half * 512, half * 512 + 512)
            z = nn(AB[...], WU[l, j, :, cols]) + SP[l, j, 16:17, cols]
            g, slope = gelu_pair(z)
            GP[l, i, :, n * 512 : n * 512 + 512] = slope.astype(BF16)
            term = nn(g.astype(BF16), WD[l, j, cols, :])
            if n == 0:
                ACC[...] = term
            else:
                ACC[...] += term
        slot = 1 + l
        SND[slot, i] = ACC[...].astype(BF16)

        @pl.when(l == 0)
        def _():
            x_copy(1, i).start()

        @pl.when((l == 1) & (i != own_i))
        def _():
            x_copy(2, i).start()

    def fwd_layer(l, carry):
        @pl.when(l == 1)
        def _():
            spread(cot, DY, 1)

        def a_turn(i, c):
            forward_attention(l, i)
            return c

        def f_turn(i, c):
            forward_ff(l, i)
            return c

        lax.fori_loop(0, 2, a_turn, 0)
        lax.fori_loop(0, 2, f_turn, 0)
        return carry

    lax.fori_loop(0, 2, fwd_layer, 0)

    def finish_forward():
        x_copy(2, own_i).wait_recv()

        def rows_out(rows):
            out = MID[1, own_i, rows, :] + (swapped(2, own_i, rows) + vec(1, 5))
            SND[2, own_i, rows, :] = out.astype(BF16)

        by_rows(rows_out)
        send_result(1, 1, SND.at[2, own_i])

    def backward_ff(l, i):
        @pl.when(l == 1)
        def _():
            pltpu.make_async_copy(cot.at[0], DY.at[i], tok_sem.at[1, i]).wait()

            def rows_valid(rows):
                pos = blk_of(i) * R + rows.start + lax.broadcasted_iota(jnp.int32, (CHUNK, 1), 0)
                _, ok = length_of(pos)
                DY[i, rows, :] = (DY[i, rows, :].astype(F32) * jnp.where(ok, 1.0, 0.0)).astype(BF16)

            by_rows(rows_valid)

        @pl.when(l == 0)
        def _():
            x_copy(0, i).wait_recv()

            def rows_in(rows):
                g = swapped(0, i, rows) * vec(1, 0)
                DY[i, rows, :] = (MID[1, i, rows, :] + norm_pull(H[1, i, rows, :].astype(F32), g)).astype(BF16)

            by_rows(rows_in)

            @pl.when(i == own_i)
            def _():
                send_result(2, 1, DY.at[i])

        for n in range(4):
            j, half = n // 2, n % 2
            cols = slice(half * 512, half * 512 + 512)
            dg = nt(DY[i], WD[l, j, cols, :])
            dz = (GP[l, i, :, n * 512 : n * 512 + 512].astype(F32) * dg).astype(BF16)
            term = nt(dz, WU[l, j, :, cols])
            if n == 0:
                ACC[...] = term
            else:
                ACC[...] += term

        x_copy(1, i).wait_send()
        SND[1, i] = ACC[...].astype(BF16)
        x_copy(1, i).start()

    def dr_copy(k, b):
        rows = pl.ds(pl.multiple_of(b * R, R), R)
        return pltpu.make_async_remote_copy(
            DKV.at[:, rows, :], DR.at[k], dr_snd.at[k], dr_rcv.at[k], device_id=sib, device_id_type=MESH)

    def attend_back(l, i):
        b = blk_of(i)

        def pair_turn(pair, carry):
            lanes = head_lanes(pair)
            qs = split_pair(Q[l, i, :, lanes], 1)
            dos = split_pair(DO[:, lanes], 1)
            rows_pair = pl.ds(pl.multiple_of(pair * 128, 128), 128)
            dot_pair = DOT[rows_pair, :]
            dots = split_pair(dot_pair, 0)
            prod = dot_pair.astype(F32) * OT[l, i, rows_pair, :].astype(F32)
            deltas = (
                jnp.sum(prod[0:64], axis=0, keepdims=True),
                jnp.sum(prod[64:128], axis=0, keepdims=True),
            )
            lses = (LSE[l, i, pair * 2], LSE[l, i, pair * 2 + 1])
            OACC[...] = jnp.zeros(OACC.shape, F32)

            def turn(j, c):
                rows = pl.ds(pl.multiple_of(j * R, R), R)
                keys = KV[l, 0, rows, lanes]
                values = KV[l, 1, rows, lanes]
                mask = MSK[i, rows, :].astype(F32)
                dk = jnp.zeros((R, 128), F32)
                dv = jnp.zeros((R, 128), F32)
                for e in range(2):
                    p = jnp.exp(nt(keys, qs[e]) + mask - lses[e])
                    dp = nn(values, dots[e])
                    ds = (p * (dp - deltas[e])).astype(BF16)
                    dv += nn(p.astype(BF16), dos[e])
                    dk += nn(ds, qs[e])
                    OACC[e] += tn(keys, ds)
                DKV[0, rows, lanes] += dk
                DKV[1, rows, lanes] += dv
                return c

            lax.fori_loop(0, b + 1, turn, 0)
            upper = lax.broadcasted_iota(jnp.int32, (128, R), 0) < HEAD_DIM
            dq = jnp.where(upper, OACC[0], OACC[1]) * HEAD_DIM ** -0.5
            DQ[pair // 2, :, pl.ds(pl.multiple_of((pair % 2) * 128, 128), 128)] = jnp.transpose(dq).astype(BF16)
            return carry

        lax.fori_loop(0, Q.shape[3] // 128, pair_turn, 0)

    def backward_attention(l, i):
        b = blk_of(i)
        x_copy(1, i).wait_recv()

        def rows_mid(rows):
            g = swapped(1, i, rows) * vec(l, 2)
            dmid = DY[i, rows, :].astype(F32) + norm_pull(MID[l, i, rows, :], g)
            MID[l, i, rows, :] = dmid
            AB[rows, :] = dmid.astype(BF16)

        by_rows(rows_mid)
        for j in range(2):
            DOT[j * 256 : j * 256 + 256, :] = nt(WO[l, j], AB[...]).astype(BF16)
            DO[:, j * 256 : j * 256 + 256] = nt(AB[...], WO[l, j]).astype(BF16)

        @pl.when(i == 1)
        def _():
            @pl.when(l == 0)
            def _():
                @pl.when(s == 0)
                def _():
                    dr_copy(0, 1).wait_send()
                    dr_copy(1, 2).wait_send()

                @pl.when(s == 1)
                def _():
                    dr_copy(0, 0).wait_send()

            def clear(r, c):
                rows = pl.ds(pl.multiple_of(r * CHUNK, CHUNK), CHUNK)
                DKV[:, rows, :] = jnp.zeros((2, CHUNK, DKV.shape[2]), F32)
                return c

            lax.fori_loop(0, 4 * R // CHUNK, clear, 0)

        attend_back(l, i)
        own = pl.ds(pl.multiple_of(b * R, R), R)

        @pl.when((s == 0) & (i == 1))
        def _():
            dr_copy(0, 1).start()
            dr_copy(1, 2).start()

        @pl.when(b != 3)
        def _():
            def add(k):
                dr_copy(k, b).wait_recv()
                DKV[0, own, :] += DR[k, 0]
                DKV[1, own, :] += DR[k, 1]

            @pl.when(s == 1)
            def _():
                add(i)

            @pl.when((s == 1) & (i == 0))
            def _():
                dr_copy(0, 0).start()

            @pl.when(s == 0)
            def _():
                add(0)

        for j in range(2):
            cols = slice(j * 256, j * 256 + 256)
            DQ[j, :, 256:512] = DKV[0, own, cols].astype(BF16)
            DQ[j, :, 512:768] = DKV[1, own, cols].astype(BF16)

        def rows_norm(rows):
            xhat, _ = normalize(H[l, i, rows, :].astype(F32))
            AB[rows, :] = (xhat * vec(l, 0) + vec(l, 1)).astype(BF16)

        by_rows(rows_norm)
        ups = [SP[l, j, 24:32, 0:768].astype(BF16) for j in range(2)]
        du = (adapter_scale * (nt(DQ[0], ups[0]) + nt(DQ[1], ups[1]))).astype(BF16)
        ga[l] += tn(du, AB[...])
        for j in range(2):
            gb[l, j] += adapter_scale * tn(U[l, i], DQ[j])

        x_copy(0, i).wait_send()
        SND[0, i] = (
            nt(DQ[0], WQ[l, 0]) + nt(DQ[1], WQ[l, 1]) + nn(du, SP[l, 0, 8:16, :].astype(BF16))
        ).astype(BF16)

        @pl.when((l == 1) | (i != own_i))
        def _():
            x_copy(0, i).start()

    def bwd_layer(back, carry):
        l = 1 - back

        def f_turn(k, c):
            backward_ff(l, 1 - k)
            return c

        def a_turn(k, c):
            backward_attention(l, 1 - k)
            return c

        lax.fori_loop(0, 2, f_turn, 0)

        @pl.when(l == 1)
        def _():
            finish_forward()

        lax.fori_loop(0, 2, a_turn, 0)
        return carry

    lax.fori_loop(0, 2, bwd_layer, 0)

    x_copy(0, own_i).wait_recv()

    def rows_out(rows):
        g = swapped(0, own_i, rows) * vec(0, 0)
        AB[rows, :] = (MID[0, own_i, rows, :] + norm_pull(H[0, own_i, rows, :].astype(F32), g)).astype(BF16)

    by_rows(rows_out)
    send_result(3, 0, AB)

    x_copy(0, 1 - own_i).wait_send()
    for i in range(2):
        x_copy(1, i).wait_send()
    x_copy(2, 1 - own_i).wait_send()
    for p in range(5):
        w_sib(p).wait_send()
        w_y(p).wait_send()
        w_forward(p).wait_send()
    spread_done(tok, H.at[0], 0)
    spread_done(cot, DY, 1)
    for l in range(2):
        kv_copy(l, 0).wait_send()

        @pl.when(s == 1)
        def _():
            kv_copy(l, 1).wait_send()

    @pl.when(s == 0)
    def _():
        dr_copy(0, 1).wait_send()
        dr_copy(1, 2).wait_send()

    @pl.when(s == 1)
    def _():
        dr_copy(0, 0).wait_send()

    send_result_done(0, 0, H.at[1, 0])
    send_result_done(1, 1, H.at[1, 0])
    send_result_done(2, 1, H.at[1, 0])
    send_result_done(3, 0, H.at[1, 0])
    for o, ref in ((0, act), (1, ig)):
        for m in range(2):
            pltpu.make_async_copy(tok.at[0], ref.at[m], out_rcv.at[o, m]).wait()


def per_pair(
    tokens, cotangent, buckets, lengths, norm_gain_pairs, norm_bias_pairs, query_key_value_weight,
    query_value_bias, output_weight, upward_weight, upward_bias, down_weight, output_bias,
    adapter_down, adapter_upper,
):
    gains, shifts, biases = norm_gain_pairs[0], norm_bias_pairs[0], output_bias[0]
    vectors = jnp.stack([gains[0], shifts[0], gains[1], shifts[1], biases[0], biases[1]])
    bias_qv = query_value_bias[0]
    width = bias_qv.shape[1]
    upper = adapter_upper[0]
    rank = upper.shape[1]
    empty = jnp.zeros((1, width), BF16)
    qkv_bias = jnp.concatenate([bias_qv[0:1], empty, bias_qv[1:2], empty], axis=1)
    none = jnp.zeros((rank, width), BF16)
    upper_rows = jnp.concatenate(
        [
            jnp.concatenate([upper[0], none, none, none], axis=1),
            jnp.concatenate([none, none, upper[1], none], axis=1),
        ]
    )
    down_rows = adapter_down[0].reshape(2 * rank, D)
    small = jnp.concatenate(
        [
            vectors,
            jnp.zeros((2, D), BF16),
            down_rows,
            upward_bias[0][None],
            qkv_bias,
            jnp.zeros((6, D), BF16),
            upper_rows,
        ]
    ).astype(F32)
    weight_qkv = query_key_value_weight[0].reshape(D, 3 * width)
    anywhere = pl.BlockSpec(memory_space=pl.ANY)
    scalars = pl.BlockSpec(memory_space=pltpu.SMEM)
    vmem = pl.BlockSpec(memory_space=pltpu.VMEM)
    dma = pltpu.SemaphoreType.DMA
    act, ig, ga, gb = pl.pallas_call(
        fused_kernel,
        out_shape=(
            jax.ShapeDtypeStruct((2, R, D), BF16),
            jax.ShapeDtypeStruct((2, R, D), BF16),
            jax.ShapeDtypeStruct((2, 8, D), F32),
            jax.ShapeDtypeStruct((2, 2, 8, 768), F32),
        ),
        in_specs=[anywhere, anywhere, scalars, scalars] + [anywhere] * 5,
        out_specs=(anywhere, anywhere, vmem, vmem),
        scratch_shapes=[
            pltpu.VMEM((2, 2, 32, D), F32),
            pltpu.VMEM((2, 2, D, 768), BF16),
            pltpu.VMEM((2, 2, 256, D), BF16),
            pltpu.VMEM((2, 2, D, 1024), BF16),
            pltpu.VMEM((2, 2, 1024, D), BF16),
            pltpu.VMEM((2, 2, R, D), BF16),
            pltpu.VMEM((2, R, D), BF16),
            pltpu.VMEM((2, 2, R, D), F32),
            pltpu.VMEM((2, 2, R, 2048), BF16),
            pltpu.VMEM((2, 2, R, 512), BF16),
            pltpu.VMEM((2, 2, 4 * R, 512), BF16),
            pltpu.VMEM((2, 2, 512, R), BF16),
            pltpu.VMEM((2, 2, 8, 1, R), F32),
            pltpu.VMEM((3, 2, R, D), BF16),
            pltpu.VMEM((3, 2, R, D), BF16),
            pltpu.VMEM((R, D), F32),
            pltpu.VMEM((2, 4 * R, R), F32),
            pltpu.VMEM((2, 4 * R, R), BF16),
            pltpu.VMEM((2, 4 * R, 512), F32),
            pltpu.VMEM((2, 2, R, 512), F32),
            pltpu.VMEM((2, R, 768), BF16),
            pltpu.VMEM((512, R), BF16),
            pltpu.VMEM((R, 512), BF16),
            pltpu.VMEM((R, D), BF16),
            pltpu.VMEM((2, 2, R, 8), BF16),
            pltpu.VMEM((2, 128, R), F32),
            dma((2, 2)),
            dma((2, 3)),
            dma((2, 2, 5)),
            dma((5,)),
            dma((5,)),
            dma((5,)),
            dma((5,)),
            dma((2, 2)),
            dma((2, 2)),
            dma((3, 2)),
            dma((3, 2)),
            dma((2,)),
            dma((2,)),
            dma((2, 2)),
            dma((4,)),
        ],
        compiler_params=pltpu.CompilerParams(
            collective_id=0, has_side_effects=True, vmem_limit_bytes=63 * 2**20
        ),
        name="two_layers",
    )(
        tokens, cotangent, buckets, lengths, small, weight_qkv, output_weight[0],
        upward_weight[0], down_weight[0],
    )
    s = lax.axis_index("section")
    t = lax.axis_index("tensor")
    part = jnp.stack([gb[:, :, 0:rank, 0:width], gb[:, :, rank : 2 * rank, 2 * width : 3 * width]], axis=1)
    x = t % 2
    zero = jnp.zeros_like(part)
    both = jnp.where(x == 0, jnp.stack([part, zero], axis=3), jnp.stack([zero, part], axis=3))
    wide = both.transpose(0, 1, 4, 2, 3, 5).reshape(2, 2, rank, 4 * width)
    sums = lax.psum(jnp.stack([ga.reshape(2, 2, rank, D), wide]), ("section", "dp", "tensor"))
    mine = lax.dynamic_index_in_dim(sums, s, 1, keepdims=False)
    total_b = lax.dynamic_slice_in_dim(mine[1], t * width, width, 2)
    return act[None], ig[None], mine[0][None], total_b[None]


def solution(mesh):
    in_specs = (
        P("dp", "tensor", None),
        P("dp", "tensor", None),
        P("dp"),
        P("dp", None),
        P("section", None, None),
        P("section", None, None),
        P("section", None, None, "tensor"),
        P("section", None, "tensor"),
        P("section", "tensor", None),
        P("section", None, "tensor"),
        P("section", "tensor"),
        P("section", "tensor", None),
        P("section", None, None),
        P("section", None, None, None),
        P("section", None, None, "tensor"),
    )
    out_specs = (
        P("section", "dp", "tensor", None),
        P("section", "dp", "tensor", None),
        P("section", None, None, None),
        P("section", None, None, "tensor"),
    )
    pairs = mesh.shape["section"] == 2 and mesh.shape["tensor"] == 4
    return jax.shard_map(
        per_pair if pairs else per_device, mesh=mesh, in_specs=in_specs, out_specs=out_specs, check_vma=False
    )
```

```python
from functools import partial

import jax
import jax.numpy as jnp
from jax import lax
from jax.experimental import pallas as pl
from jax.experimental.pallas import tpu as pltpu
from jax.sharding import PartitionSpec as P

HEAD_DIM = 64


adapter_scale = 8.0
norm_eps = 1e-05
masked_score = -1000000000.0
highest_precision = lax.Precision.HIGHEST


def from_behind(block, axis, distance):
    devices = range(lax.axis_size(axis))
    route = [(i - distance, i) for i in devices if i - distance in devices]
    return lax.ppermute(block, axis, route)


def layer_norm(values, gain_rows, shifts):
    center = jnp.mean(values, axis=-1, keepdims=True)
    centered = values - center
    spread = jnp.mean(centered * centered, axis=-1, keepdims=True)
    return centered * lax.rsqrt(spread + norm_eps) * gain_rows + shifts


def row_layout(bucket, lengths_row, row_count):
    item_span = jnp.right_shift(jnp.int32(row_count), 3 - bucket)
    positions = jnp.arange(row_count, dtype=jnp.int32)
    item_index = positions // item_span
    within = positions - item_index * item_span
    chosen = (
        item_index[:, None] == jnp.arange(lengths_row.shape[0], dtype=jnp.int32)[None, :]
    ).astype(jnp.int32)
    length = jnp.sum(chosen * lengths_row[None, :], axis=1)
    return (item_index, within < length)


def allowed_keys(item_index, is_valid):
    positions = jnp.arange(item_index.shape[0], dtype=jnp.int32)
    same_item = item_index[:, None] == item_index[None, :]
    causal = positions[None, :] <= positions[:, None]
    key_seen = is_valid[None, :] | (positions[None, :] == positions[:, None])
    return same_item & causal & key_seen


def take_slot(buffer, slot_index):
    return lax.dynamic_index_in_dim(buffer, slot_index, 0, keepdims=False)


def put_slot(buffer, slot_index, is_live, update):
    previous = take_slot(buffer, slot_index)
    return lax.dynamic_update_index_in_dim(
        buffer, jnp.where(is_live, update, previous), slot_index, 0
    )


def per_device(
    tokens,
    cotangent,
    buckets,
    lengths,
    norm_gain_pairs,
    norm_bias_pairs,
    query_key_value_weight,
    query_value_bias,
    output_weight,
    upward_weight,
    upward_bias,
    down_weight,
    output_bias,
    adapter_down,
    adapter_upper,
):
    section_index = lax.axis_index("section")
    tensor_count = lax.axis_size("tensor")
    micro_count, own_rows, model_width = tokens.shape
    row_count = own_rows * tensor_count
    own_start = lax.axis_index("tensor") * own_rows
    gain_sets = norm_gain_pairs[0].astype(jnp.float32)
    shift_sets = norm_bias_pairs[0].astype(jnp.float32)
    weight_qkv = query_key_value_weight[0]
    bias_query_value = query_value_bias[0].astype(jnp.float32)
    weight_out = output_weight[0]
    weight_up = upward_weight[0]
    bias_up = upward_bias[0].astype(jnp.float32)
    weight_down = down_weight[0]
    biases = output_bias[0].astype(jnp.float32)
    down_factor = adapter_down[0]
    upper_factor = adapter_upper[0]
    factor_wide = down_factor.astype(jnp.float32)
    local_width = weight_qkv.shape[2]
    local_heads = local_width // HEAD_DIM
    score_scale = HEAD_DIM ** (-0.5)

    def widen(values):
        return lax.all_gather(values, "tensor", axis=0, tiled=True)

    def widen_back(values):
        return lax.all_gather(values, "tensor", axis=0, tiled=True)

    def settle(source, weight):

        def row_term(first_row, row_span):
            return jnp.dot(source, weight, preferred_element_type=jnp.float32)

        return lax.psum_scatter(
            row_term(jnp.int32(0), lax.axis_size("tensor") * own_rows).astype(jnp.bfloat16),
            "tensor",
            scatter_dimension=0,
            tiled=True,
        ).astype(jnp.float32)

    def settle_back(row_term):
        return lax.psum_scatter(
            row_term(jnp.int32(0), lax.axis_size("tensor") * own_rows).astype(jnp.bfloat16),
            "tensor",
            scatter_dimension=0,
            tiled=True,
        ).astype(jnp.float32)

    def layout_of(slot_index):
        item_index, is_valid = row_layout(
            take_slot(buckets, slot_index), take_slot(lengths, slot_index), row_count
        )
        own_valid = lax.dynamic_slice_in_dim(is_valid, own_start, own_rows, 0)
        return (allowed_keys(item_index, is_valid), own_valid)

    def attend(normed, allowed):
        reduced_query = jnp.dot(
            normed, down_factor[0].T, preferred_element_type=jnp.float32
        ).astype(jnp.bfloat16)
        reduced_value = jnp.dot(
            normed, down_factor[1].T, preferred_element_type=jnp.float32
        ).astype(jnp.bfloat16)
        blended_rows = jnp.einsum(
            "rd,dcn->rcn", normed, weight_qkv, preferred_element_type=jnp.float32
        )
        query_matrix_rows = (
            blended_rows[:, 0]
            + bias_query_value[0]
            + adapter_scale
            * jnp.dot(reduced_query, upper_factor[0], preferred_element_type=jnp.float32)
        )
        value_matrix_rows = (
            blended_rows[:, 2]
            + bias_query_value[1]
            + adapter_scale
            * jnp.dot(reduced_value, upper_factor[1], preferred_element_type=jnp.float32)
        )
        packed = jnp.stack(
            [query_matrix_rows, blended_rows[:, 1], value_matrix_rows], axis=1
        ).astype(jnp.bfloat16)
        head_split = packed.reshape(row_count, 3, local_heads, HEAD_DIM)
        scores = (
            jnp.einsum(
                "qhe,khe->hqk",
                head_split[:, 0],
                head_split[:, 1],
                preferred_element_type=jnp.float32,
            )
            * score_scale
        )
        scores = jnp.where(allowed[None], scores, masked_score)
        top_score = jnp.max(scores, axis=-1, keepdims=True)
        exponent = jnp.exp(scores - top_score)
        attn_probs = exponent / jnp.sum(exponent, axis=-1, keepdims=True)
        return (reduced_query, reduced_value, head_split, attn_probs)

    def forward(hidden, allowed):
        normed = widen(layer_norm(hidden, gain_sets[0], shift_sets[0]).astype(jnp.bfloat16))
        reduced_query, reduced_value, head_split, attn_probs = attend(normed, allowed)
        probs_low = attn_probs.astype(jnp.bfloat16)
        mixed_heads = jnp.einsum(
            "hqk,khe->qhe", probs_low, head_split[:, 2], preferred_element_type=jnp.float32
        )
        attended = mixed_heads.reshape(row_count, local_width).astype(jnp.bfloat16)
        middle = hidden + (settle(attended, weight_out) + biases[0])
        normed_two = widen(layer_norm(middle, gain_sets[1], shift_sets[1]).astype(jnp.bfloat16))
        hidden_pre = jnp.dot(normed_two, weight_up, preferred_element_type=jnp.float32) + bias_up
        activated = jax.nn.gelu(hidden_pre, approximate=True).astype(jnp.bfloat16)
        output = middle + (settle(activated, weight_down) + biases[1])
        return (output, normed, middle, normed_two)

    def backward(hidden, grad_out, allowed, normed, middle, normed_two):
        reduced_query, reduced_value, head_split, attn_probs = attend(normed, allowed)
        probs_low = attn_probs.astype(jnp.bfloat16)
        hidden_pre = jnp.dot(normed_two, weight_up, preferred_element_type=jnp.float32) + bias_up
        grad_branch = widen_back(grad_out.astype(jnp.bfloat16))
        grad_act = jnp.einsum(
            "rd,fd->rf", grad_branch, weight_down, preferred_element_type=jnp.float32
        )
        gelu_pull = jax.vjp(partial(jax.nn.gelu, approximate=True), hidden_pre)[1]
        grad_pre = gelu_pull(grad_act)[0].astype(jnp.bfloat16)

        def mlp_term(first_row, row_span):
            return jnp.einsum("rf,df->rd", grad_pre, weight_up, preferred_element_type=jnp.float32)

        grad_norm_two = settle_back(mlp_term)
        second_pull = jax.vjp(
            partial(layer_norm, gain_rows=gain_sets[1], shifts=shift_sets[1]), middle
        )[1]
        grad_middle = grad_out + second_pull(grad_norm_two)[0]
        grad_attn = widen_back(grad_middle.astype(jnp.bfloat16))
        grad_heads = jnp.einsum(
            "rd,nd->rn", grad_attn, weight_out, preferred_element_type=jnp.float32
        )
        grad_heads = grad_heads.astype(jnp.bfloat16).reshape(row_count, local_heads, HEAD_DIM)
        grad_probs = jnp.einsum(
            "qhe,khe->hqk", grad_heads, head_split[:, 2], preferred_element_type=jnp.float32
        )
        grad_scores = attn_probs * (
            grad_probs - jnp.sum(attn_probs * grad_probs, axis=-1, keepdims=True)
        )
        grad_scores = grad_scores.astype(jnp.bfloat16)
        grad_query = (
            jnp.einsum(
                "hqk,khe->qhe", grad_scores, head_split[:, 1], preferred_element_type=jnp.float32
            )
            * score_scale
        )
        grad_key = (
            jnp.einsum(
                "hqk,qhe->khe", grad_scores, head_split[:, 0], preferred_element_type=jnp.float32
            )
            * score_scale
        )
        grad_value = jnp.einsum(
            "hqk,qhe->khe", probs_low, grad_heads, preferred_element_type=jnp.float32
        )
        grad_packed = (
            jnp.stack([grad_query, grad_key, grad_value], axis=1)
            .reshape(row_count, 3, local_width)
            .astype(jnp.bfloat16)
        )
        grad_pair = jnp.stack([grad_packed[:, 0], grad_packed[:, 2]])
        gradient_reduced = adapter_scale * jnp.einsum(
            "jrn,jkn->jrk", grad_pair, upper_factor, preferred_element_type=jnp.float32
        )

        def attn_term(first_row, row_span):
            dense_part = jnp.einsum(
                "rcn,dcn->rd", grad_packed, weight_qkv, preferred_element_type=jnp.float32
            )
            return dense_part + jnp.einsum(
                "jrk,jkd->rd", gradient_reduced, factor_wide, precision=highest_precision
            )

        grad_normed = settle_back(attn_term)
        first_pull = jax.vjp(
            partial(layer_norm, gain_rows=gain_sets[0], shifts=shift_sets[0]), hidden
        )[1]
        grad_hidden = grad_middle + first_pull(grad_normed)[0]
        grad_factor_a = jnp.einsum(
            "jrk,rd->jkd", gradient_reduced, normed.astype(jnp.float32), precision=highest_precision
        )
        gradient_upper_factor = adapter_scale * jnp.stack(
            [
                jnp.einsum(
                    "rk,rn->kn",
                    reduced_query,
                    grad_packed[:, 0],
                    preferred_element_type=jnp.float32,
                ),
                jnp.einsum(
                    "rk,rn->kn",
                    reduced_value,
                    grad_packed[:, 2],
                    preferred_element_type=jnp.float32,
                ),
            ]
        )
        return (grad_hidden, grad_factor_a, gradient_upper_factor)

    zero_rows = jnp.zeros((micro_count, own_rows, model_width), jnp.bfloat16)
    saved_start = ()

    def record(buffers, slot_index, is_live, layer_input, results):
        kept_in, outputs, saved = buffers
        output, normed, middle, normed_two = results
        low_output = output.astype(jnp.bfloat16)
        kept_in = put_slot(kept_in, slot_index, is_live, layer_input)
        outputs = put_slot(outputs, slot_index, is_live, low_output)
        return ((kept_in, outputs, saved), low_output)

    buffers = (zero_rows, zero_rows, saved_start)

    def run_phase(buffers, sources, phase_section):

        def phase_turn(slot_index, buffers):
            allowed, own_valid = layout_of(slot_index)
            layer_input = take_slot(sources, slot_index)
            results = forward(layer_input.astype(jnp.float32), allowed)
            return record(
                buffers, slot_index, section_index == phase_section, layer_input, results
            )[0]

        return lax.fori_loop(0, micro_count, phase_turn, buffers)

    buffers = run_phase(buffers, tokens, 0)
    received = from_behind(buffers[1], "section", 1)
    buffers = run_phase(buffers, received, 1)
    kept_in, outputs, saved = buffers

    def back_step(slot_index, grad_out, allowed):
        hidden = take_slot(kept_in, slot_index).astype(jnp.float32)
        output, normed, middle, normed_two = forward(hidden, allowed)
        return backward(hidden, grad_out, allowed, normed, middle, normed_two)

    def top_grad(slot_index, own_valid):
        return take_slot(cotangent, slot_index).astype(jnp.float32) * own_valid[:, None].astype(
            jnp.float32
        )

    zero_a = jnp.zeros(down_factor.shape, jnp.float32)
    zero_b = jnp.zeros(upper_factor.shape, jnp.float32)

    def run_back(loop_state, sources, phase_section):

        def phase_turn(slot_index, loop_state):
            grads_in, sum_a, sum_b = loop_state
            allowed, own_valid = layout_of(slot_index)
            if phase_section == 1:
                grad_out = top_grad(slot_index, own_valid)
            else:
                grad_out = take_slot(sources, slot_index).astype(jnp.float32)
            is_live = section_index == phase_section
            grad_hidden, grad_a, grad_b = back_step(slot_index, grad_out, allowed)
            grads_in = put_slot(grads_in, slot_index, is_live, grad_hidden.astype(jnp.bfloat16))
            sum_a = sum_a + jnp.where(is_live, grad_a, 0.0)
            sum_b = sum_b + jnp.where(is_live, grad_b, 0.0)
            return (grads_in, sum_a, sum_b)

        return lax.fori_loop(0, micro_count, phase_turn, loop_state)

    loop_state = run_back((zero_rows, zero_a, zero_b), zero_rows, 1)
    received_grads = from_behind(loop_state[0], "section", -1)
    grads_in, sum_a, sum_b = run_back(loop_state, received_grads, 0)
    total_a = lax.psum(sum_a, ("dp", "tensor"))
    total_b = lax.psum(sum_b, "dp")
    return (outputs[None], grads_in[None], total_a[None], total_b[None])


R = 256
D = 1024
NEG = -1e30
F32 = jnp.float32
BF16 = jnp.bfloat16
MESH = pl.DeviceIdType.MESH
CHUNK = 128


def nn(a, b):
    return lax.dot_general(a, b, (((1,), (0,)), ((), ())), preferred_element_type=F32)


def nt(a, b):
    return lax.dot_general(a, b, (((1,), (1,)), ((), ())), preferred_element_type=F32)


def tn(a, b):
    return lax.dot_general(a, b, (((0,), (0,)), ((), ())), preferred_element_type=F32)


def normalize(v):
    centered = v - jnp.mean(v, axis=-1, keepdims=True)
    rs = lax.rsqrt(jnp.mean(centered * centered, axis=-1, keepdims=True) + norm_eps)
    return centered * rs, rs


def norm_pull(v, g):
    xhat, rs = normalize(v)
    return rs * (
        g
        - jnp.mean(g, axis=-1, keepdims=True)
        - xhat * jnp.mean(g * xhat, axis=-1, keepdims=True)
    )


def gelu_pair(z):
    c = 0.7978845608028654
    z2 = z * z
    t = jnp.tanh(c * (z + 0.044715 * (z2 * z)))
    half = 0.5 * (1.0 + t)
    slope = half + (0.5 * c) * z * (1.0 - t * t) * (1.0 + (3.0 * 0.044715) * z2)
    return z * half, slope


def fused_kernel(
    dp_count,
    tok, cot, buckets, lengths, gain_in, shift_in, wq_in, bqv_in, wo_in, wu_in, bu_in, wd_in, bo_in, ad_in, au_in,
    act, ig, out_a, out_b,
    SP, WQ, WO, WU, WD, H, DY, MID, GP, Q, KV, OT, LSE, SND, RCV, BIG, MSK, DR, DQ, AB, U, OACC, PB,
    GA, GB, GCA, GCB, GXA, GXB, GZA, GZB,
    tok_sem, tok_ys, tok_xs, wl, ws_r, ws_s, wy_r, wy_s, wz_r, wz_s, wa_r, wa_s, wb_r, wb_s,
    kv_rcv, kv_snd, x_rcv, x_snd, dr_rcv, dr_snd, out_rcv, out_snd, gc_r, gc_s, gx_r, gx_s, gz_r, gz_s,
):
    s = lax.axis_index("section")
    d = lax.axis_index("dp")
    t = lax.axis_index("tensor")
    x = lax.rem(t, 2)
    y = lax.div(t, 2)
    sib = (1 - s, d, t)
    xp = (s, d, y * 2 + 1 - x)
    yp = (s, d, (1 - y) * 2 + x)
    z_half = lax.rem(d, 2)
    zp = (s, d + 1 - 2 * z_half, t)
    flip = s + x - 2 * s * x
    own_i = flip

    def blk_of(i):
        return 2 * i + (s + i - 2 * s * i)

    bar = pltpu.get_barrier_semaphore()
    for ds_ in range(2):
        for dx in range(2):
            for dy in range(2):
                if ds_ or dx or dy:
                    s2 = 1 - s if ds_ else s
                    x2 = 1 - x if dx else x
                    y2 = 1 - y if dy else y
                    pl.semaphore_signal(bar, 1, device_id=(s2, d, y2 * 2 + x2), device_id_type=MESH)
    for k in range(1, dp_count):
        pl.semaphore_signal(bar, 1, device_id=(s, lax.rem(d + k, dp_count), t), device_id_type=MESH)
    pl.semaphore_wait(bar, 7 + dp_count - 1)

    def row_copies(src, dst, w):
        def local():
            return pltpu.make_async_copy(src.at[y], dst.at[y], tok_sem.at[w, y])

        def to_y():
            return pltpu.make_async_remote_copy(
                src.at[1 - y], dst.at[y], tok_ys.at[w], tok_sem.at[w, y], device_id=yp, device_id_type=MESH)

        def first_x():
            return pltpu.make_async_remote_copy(
                src.at[y], dst.at[y], tok_xs.at[w], tok_sem.at[w, y], device_id=xp, device_id_type=MESH)

        def then_x():
            return pltpu.make_async_remote_copy(
                dst.at[own_i], dst.at[own_i], tok_xs.at[w], tok_sem.at[w, own_i],
                device_id=xp, device_id_type=MESH)

        return local, to_y, first_x, then_x

    def rows_start(src, dst, w):
        local, to_y, first_x, _ = row_copies(src, dst, w)

        @pl.when(y == own_i)
        def _():
            first_x().start()
            to_y().start()
            local().start()

    def rows_relay(src, dst, w):
        pltpu.make_async_copy(src.at[0], dst.at[own_i], tok_sem.at[w, own_i]).wait()

        @pl.when(y != own_i)
        def _():
            row_copies(src, dst, w)[3]().start()

    def rows_rest(src, dst, w):
        pltpu.make_async_copy(src.at[0], dst.at[1 - own_i], tok_sem.at[w, 1 - own_i]).wait()

    def rows_done(src, dst, w):
        _, to_y, first_x, _ = row_copies(src, dst, w)
        if w == 0:
            first_x().wait_send()

        @pl.when(y == own_i)
        def _():
            to_y().wait_send()

    pieces = (None, (wq_in, WQ, 2), (wo_in, WO, 1), (wu_in, WU, 2), (wd_in, WD, 2))
    base = (7, 0, 2, 3, 5)

    def sources(p, rows):
        src, dst, _ = pieces[p]
        if p == 1:
            return [
                (src.at[c, rows, :], dst.at[s, y, rows, c * 256 : c * 256 + 256]) for c in range(3)
            ]
        return [(src.at[0, rows, :], dst.at[s, y, rows, :])]

    def chunk(p, c, half):
        dst, parts = pieces[p][1], pieces[p][2]
        size = dst.shape[2] // (2 * parts)
        return pl.ds(pl.multiple_of((half * parts + c) * size, size), size)

    def block(p, l, j, rows):
        return pieces[p][1].at[l, j, rows, :]

    def own_start(p):
        everything = pl.ds(0, pieces[p][1].shape[2])
        for src, dst in sources(p, everything):
            pltpu.make_async_copy(src, dst, wl.at[p]).start()
            pltpu.make_async_remote_copy(
                src, dst, ws_s.at[p], ws_r.at[p], device_id=sib, device_id_type=MESH).start()

    def y_start(p):
        if p == 0:
            small_copy(yp, wy_s.at[7], wy_r.at[7]).start()
            return
        for c in range(pieces[p][2]):
            for src, dst in sources(p, chunk(p, c, z_half)):
                k = base[p] + c
                pltpu.make_async_remote_copy(
                    src, dst, wy_s.at[k], wy_r.at[k], device_id=yp, device_id_type=MESH).start()

    def small_copy(to, snd, rcv):
        return pltpu.make_async_remote_copy(
            SP.at[s, y], SP.at[s, y], snd, rcv, device_id=to, device_id_type=MESH)

    def passed(p, c, half, to, snd, rcv):
        ref = SP.at[s, 1 - y] if p == 0 else block(p, s, 1 - y, chunk(p, c, half))
        return pltpu.make_async_remote_copy(ref, ref, snd, rcv, device_id=to, device_id_type=MESH)

    def relay_y(l, p, c=0):
        k = base[p] + c

        @pl.when(l == s)
        def _():
            passed(p, c, z_half, sib, wa_s.at[k], wy_r.at[k]).wait_recv()
            if p:
                passed(p, c, z_half, zp, wz_s.at[k], wz_r.at[k]).start()
            passed(p, c, z_half, sib, wa_s.at[k], wa_r.at[k]).start()

    def relay_z(l, p, c=0):
        k = base[p] + c

        @pl.when(l == s)
        def _():
            passed(p, c, 1 - z_half, zp, wz_s.at[k], wz_r.at[k]).wait_recv()
            passed(p, c, 1 - z_half, sib, wb_s.at[k], wb_r.at[k]).start()

    def own_wait(l, p):
        @pl.when(l == s)
        def _():
            if p:
                ref = pieces[p][1].at[s, y]
                pltpu.make_async_copy(ref, ref, wl.at[p]).wait()

        @pl.when(l != s)
        def _():
            ref = pieces[p][1].at[1 - s, y] if p else SP.at[1 - s, y]
            pltpu.make_async_copy(ref, ref, ws_r.at[p]).wait()

    def other_wait(l, p):
        @pl.when(l != s)
        def _():
            if p == 0:
                ref = SP.at[1 - s, 1 - y]
                pltpu.make_async_copy(ref, ref, wa_r.at[7]).wait()
            else:
                for c in range(pieces[p][2]):
                    k = base[p] + c
                    ref = block(p, 1 - s, 1 - y, chunk(p, c, 0))
                    pltpu.make_async_copy(ref, ref, wa_r.at[k]).wait()
                    pltpu.make_async_copy(ref, ref, wb_r.at[k]).wait()

    @pl.when(s == 0)
    def _():
        y_start(1)

    rows_start(tok, H.at[0], 0)
    SP[s, y] = jnp.zeros(SP.shape[2:], F32)
    for k, (ref, row) in enumerate(
        ((gain_in, 0), (shift_in, 0), (gain_in, 1), (shift_in, 1), (bo_in, 0), (bo_in, 1))
    ):
        SP[s, y, k : k + 1, :] = ref[0, row : row + 1, :].astype(F32)
    SP[s, y, 8:12, :] = ad_in[0, 0].astype(F32)
    SP[s, y, 12:16, :] = ad_in[0, 1].astype(F32)
    SP[s, y, 16:17, :] = bu_in[...].astype(F32)
    SP[s, y, 17:18, 0:256] = bqv_in[0, 0:1, :].astype(F32)
    SP[s, y, 17:18, 512:768] = bqv_in[0, 1:2, :].astype(F32)
    SP[s, y, 24:28, 0:256] = au_in[0, 0].astype(F32)
    SP[s, y, 28:32, 512:768] = au_in[0, 1].astype(F32)
    small_copy(sib, ws_s.at[0], ws_r.at[0]).start()
    for p in range(1, 5):
        own_start(p)

    @pl.when(s == 0)
    def _():
        y_start(0)
        for p in range(2, 5):
            y_start(p)

    rows_start(cot, DY, 1)

    shift = 7 + buckets[y]
    span_mask = lax.shift_left(jnp.int32(1), shift) - 1

    def length_of(pos):
        item = lax.shift_right_logical(pos, jnp.broadcast_to(shift, pos.shape))
        got = jnp.zeros(pos.shape, jnp.int32)
        for k in range(lengths.shape[1]):
            got = jnp.where(item == k, lengths[y, k], got)
        return item, jnp.bitwise_and(pos, span_mask) < got

    def build_mask(i):
        b = blk_of(i)
        q_row = b * R + lax.broadcasted_iota(jnp.int32, (1, R), 1)
        q_item = lax.shift_right_logical(q_row, jnp.broadcast_to(shift, q_row.shape))

        def rows(r, carry):
            r0 = pl.multiple_of(r * CHUNK, CHUNK)
            k_row = r0 + lax.broadcasted_iota(jnp.int32, (CHUNK, 1), 0)
            k_item, k_ok = length_of(k_row)
            k_tag = jnp.where(k_ok, k_item, -1)
            same = (k_tag == q_item) & (k_row <= q_row)
            allowed = same | (k_row == q_row)
            MSK[pl.ds(pl.multiple_of(i * 2 * R + r0, CHUNK), CHUNK), :] = jnp.where(allowed, 0.0, NEG).astype(BF16)
            return carry

        lax.fori_loop(0, (b + 1) * (R // CHUNK), rows, 0)

    build_mask(0)
    build_mask(1)
    GA[...] = jnp.zeros(GA.shape, F32)
    GB[...] = jnp.zeros(GB.shape, F32)

    def x_copy(slot, i):
        return pltpu.make_async_remote_copy(
            SND.at[slot, i], RCV.at[slot * 2 + (i if slot < 2 else 0)], x_snd.at[slot, i], x_rcv.at[slot, i],
            device_id=xp, device_id_type=MESH)

    def by_rows(body):
        body(slice(0, R))

    total_rows = slice(3 * R, 4 * R)

    def gather(n, term):
        for c in range(4):
            part = term[:, c * R : c * R + R]
            BIG[c, total_rows, :] = part if n == 0 else BIG[c, total_rows, :] + part

    def gathered():
        return jnp.concatenate([BIG[c, total_rows, :] for c in range(4)], axis=1).astype(BF16)

    def swapped(slot, i, rows):
        return SND[slot, i, rows, :].astype(F32) + RCV[slot * 2 + (i if slot < 2 else 0), rows, :].astype(F32)

    def send_result(which, layer, src):
        dst = act if which < 2 else ig
        o = 0 if which < 2 else 1
        here = (s == layer) & (y == own_i)

        @pl.when(here)
        def _():
            pltpu.make_async_copy(src, dst.at[y], out_rcv.at[o, y]).start()

        @pl.when(jnp.logical_not(here))
        def _():
            pltpu.make_async_remote_copy(
                src, dst.at[y], out_snd.at[which], out_rcv.at[o, y],
                device_id=(layer, d, own_i * 2 + x), device_id_type=MESH).start()

    def send_result_done(which, layer, src):
        dst = act if which < 2 else ig
        o = 0 if which < 2 else 1
        here = (s == layer) & (y == own_i)

        @pl.when(jnp.logical_not(here))
        def _():
            pltpu.make_async_remote_copy(
                src, dst.at[y], out_snd.at[which], out_rcv.at[o, y],
                device_id=(layer, d, own_i * 2 + x), device_id_type=MESH).wait_send()

    def vec(l, k):
        return SP[l, 0, k : k + 1, :]

    def head_lanes(pair):
        return pl.ds(pl.multiple_of(pair * 128, 128), 128)

    def split_pair(v, axis):
        which = lax.broadcasted_iota(jnp.int32, v.shape, axis) < HEAD_DIM
        zero = jnp.zeros_like(v)
        return jnp.where(which, v, zero), jnp.where(which, zero, v)

    def kv_copy(l, i):
        rows = pl.ds(pl.multiple_of(blk_of(i) * R, R), R)
        return pltpu.make_async_remote_copy(
            KV.at[l, :, rows, :], KV.at[l, :, rows, :], kv_snd.at[l, i], kv_rcv.at[l, i],
            device_id=sib, device_id_type=MESH)

    def kv_wait(l, i):
        b = 2 * i + (1 - s + i - 2 * (1 - s) * i)
        rows = pl.ds(pl.multiple_of(b * R, R), R)
        pltpu.make_async_remote_copy(
            KV.at[l, :, rows, :], KV.at[l, :, rows, :], kv_snd.at[l, i], kv_rcv.at[l, i],
            device_id=sib, device_id_type=MESH).wait_recv()

    GROUP = 4

    def attend(l, i):
        b = blk_of(i)

        def group_turn(g, carry):
            def lanes_of(k):
                return pl.ds(pl.multiple_of(g * (GROUP * HEAD_DIM) + k * 128, 128), 128)

            def first(j, tops):
                rows = pl.ds(pl.multiple_of(j * R, R), R)
                mask = MSK[pl.ds(pl.multiple_of((i * 2 + j) * R, R), R), :].astype(F32)
                new = []
                for k in range(GROUP // 2):
                    qs = split_pair(Q[l, i, :, lanes_of(k)], 1)
                    keys = KV[l, 0, rows, lanes_of(k)]
                    for e in range(2):
                        st = nt(keys, qs[e]) + mask
                        BIG[2 * k + e, rows, :] = st
                        new.append(jnp.maximum(tops[2 * k + e], jnp.max(st, axis=0, keepdims=True)))
                return tuple(new)

            tops = lax.fori_loop(0, b + 1, first, (jnp.full((1, R), NEG, F32),) * GROUP)
            for k in range(GROUP):
                OACC[k] = jnp.zeros(OACC.shape[1:], F32)

            def second(j, sums):
                rows = pl.ds(pl.multiple_of(j * R, R), R)
                new = []
                for k in range(GROUP):
                    p = jnp.exp(BIG[k, rows, :] - tops[k])
                    new.append(sums[k] + jnp.sum(p, axis=0, keepdims=True))
                    PB[k] = p.astype(BF16)
                for k in range(GROUP // 2):
                    values = jnp.transpose(KV[l, 1, rows, lanes_of(k)])
                    for e in range(2):
                        OACC[2 * k + e] += nn(values[e * 64 : e * 64 + 64], PB[2 * k + e])
                return tuple(new)

            sums = lax.fori_loop(0, b + 1, second, (jnp.zeros((1, R), F32),) * GROUP)
            for k in range(GROUP):
                OT[l, i, pl.ds(pl.multiple_of((g * GROUP + k) * 64, 64), 64), :] = (
                    OACC[k] * (1.0 / sums[k])
                ).astype(BF16)
                LSE[l, i, g * GROUP + k] = tops[k] + jnp.log(sums[k])
            return carry

        lax.fori_loop(0, Q.shape[3] // (GROUP * HEAD_DIM), group_turn, 0)

    def forward_attention(l, i):
        b = blk_of(i)

        @pl.when(i == 0)
        def _():
            @pl.when(l == 0)
            def _():
                relay_y(l, 1, 0)
                rows_relay(tok, H.at[0], 0)
                relay_y(l, 0)
                relay_y(l, 1, 1)
                relay_z(l, 1, 0)
                rows_rest(tok, H.at[0], 0)

            own_wait(l, 0)
            other_wait(l, 0)
            own_wait(l, 1)

            @pl.when(l == 1)
            def _():
                relay_z(l, 1, 0)

            relay_y(l, 2)
            relay_z(l, 1, 1)
            other_wait(l, 1)

        @pl.when(i == 1)
        def _():
            relay_y(l, 3, 0)
            relay_y(l, 3, 1)

        @pl.when(l == 1)
        def _():
            x_copy(1, i).wait_recv()

            def rows_in(rows):
                h = MID[0, i, rows, :] + (swapped(1, i, rows) + vec(0, 5))
                H[1, i, rows, :] = h.astype(BF16)

            by_rows(rows_in)

            @pl.when(i == own_i)
            def _():
                send_result(0, 0, H.at[1, i])

        def rows_norm(rows):
            xhat, _ = normalize(H[l, i, rows, :].astype(F32))
            AB[rows, :] = (xhat * vec(l, 0) + vec(l, 1)).astype(BF16)

        by_rows(rows_norm)
        u = nt(AB[...], SP[l, 0, 8:16, :].astype(BF16)).astype(BF16)
        U[l, i] = nt(SP[l, 0, 8:16, :].astype(BF16), AB[...]).astype(BF16)
        own_rows = pl.ds(pl.multiple_of(b * R, R), R)
        for j in range(2):
            up = SP[l, j, 24:32, 0:768].astype(BF16)
            qkv = nn(AB[...], WQ[l, j]) + (adapter_scale * nn(u, up) + SP[l, j, 17:18, 0:768])
            cols = slice(j * 256, j * 256 + 256)
            Q[l, i, :, cols] = (qkv[:, 0:256] * HEAD_DIM ** -0.5).astype(BF16)
            KV[l, 0, own_rows, cols] = qkv[:, 256:512].astype(BF16)
            KV[l, 1, own_rows, cols] = qkv[:, 512:768].astype(BF16)

        @pl.when(b != 3)
        def _():
            kv_copy(l, i).start()

        @pl.when((s == 1) & (i == 0))
        def _():
            kv_wait(l, 0)

        @pl.when((s == 0) & (i == 1))
        def _():
            kv_wait(l, 0)
            kv_wait(l, 1)

        attend(l, i)

        @pl.when(i == 0)
        def _():
            own_wait(l, 2)
            relay_z(l, 2)
            other_wait(l, 2)

        @pl.when(l == 1)
        def _():
            x_copy(0, i).wait_send()

        SND[0, i] = (tn(OT[l, i, 0:256, :], WO[l, 0]) + tn(OT[l, i, 256:512, :], WO[l, 1])).astype(BF16)
        x_copy(0, i).start()

    def forward_ff(l, i):
        @pl.when(i == 0)
        def _():
            @pl.when((s == 1) & (l == 0))
            def _():
                for p in range(5):
                    y_start(p)

            own_wait(l, 3)
            own_wait(l, 4)
            relay_z(l, 3, 0)
            relay_y(l, 4, 0)
            relay_z(l, 3, 1)
            relay_y(l, 4, 1)

        @pl.when((i == 1) & (l == 0))
        def _():
            rows_relay(cot, DY, 1)
            rows_rest(cot, DY, 1)
            relay_y(1, 0)
            relay_y(1, 1, 0)
            relay_y(1, 1, 1)

        x_copy(0, i).wait_recv()

        def rows_mid(rows):
            mid = H[l, i, rows, :].astype(F32) + (swapped(0, i, rows) + vec(l, 4))
            MID[l, i, rows, :] = mid
            xhat, _ = normalize(mid)
            AB[rows, :] = (xhat * vec(l, 2) + vec(l, 3)).astype(BF16)

        by_rows(rows_mid)
        for n in range(4):
            j, half = (y if n < 2 else 1 - y), n % 2
            cols = slice(half * 512, half * 512 + 512)
            if n == 2:

                @pl.when(i == 0)
                def _():
                    relay_z(l, 4, 0)
                    relay_z(l, 4, 1)
                    other_wait(l, 3)
                    other_wait(l, 4)

            z = nn(AB[...], WU[l, j, :, cols]) + SP[l, j, 16:17, cols]
            g, slope = gelu_pair(z)
            GP[l, i, :, n * 512 : n * 512 + 512] = slope.astype(BF16)
            term = nn(g.astype(BF16), WD[l, j, cols, :])
            gather(n, term)
        SND[1 + l, i] = gathered()

        @pl.when(l == 0)
        def _():
            x_copy(1, i).start()

        @pl.when((l == 1) & (i != own_i))
        def _():
            x_copy(2, i).start()

    def fwd_layer(l, carry):
        def a_turn(i, c):
            forward_attention(l, i)
            return c

        def f_turn(i, c):
            forward_ff(l, i)
            return c

        lax.fori_loop(0, 2, a_turn, 0)
        lax.fori_loop(0, 2, f_turn, 0)
        return carry

    lax.fori_loop(0, 2, fwd_layer, 0)

    def finish_forward():
        x_copy(2, own_i).wait_recv()

        def rows_out(rows):
            out = MID[1, own_i, rows, :] + (swapped(2, own_i, rows) + vec(1, 5))
            SND[2, own_i, rows, :] = out.astype(BF16)

        by_rows(rows_out)
        send_result(1, 1, SND.at[2, own_i])

    def backward_ff(l, i):
        @pl.when(l == 1)
        def _():
            @pl.when(i == own_i)
            def _():
                row_copies(cot, DY, 1)[3]().wait_send()

            def rows_valid(rows):
                pos = blk_of(i) * R + lax.broadcasted_iota(jnp.int32, (R, 1), 0)
                _, ok = length_of(pos)
                DY[i, rows, :] = (DY[i, rows, :].astype(F32) * jnp.where(ok, 1.0, 0.0)).astype(BF16)

            by_rows(rows_valid)

        @pl.when(l == 0)
        def _():
            x_copy(0, i).wait_recv()

            def rows_in(rows):
                g = swapped(0, i, rows) * vec(1, 0)
                DY[i, rows, :] = (MID[1, i, rows, :] + norm_pull(H[1, i, rows, :].astype(F32), g)).astype(BF16)

            by_rows(rows_in)

            @pl.when(i == own_i)
            def _():
                send_result(2, 1, DY.at[i])

        for n in range(4):
            j, half = (y if n < 2 else 1 - y), n % 2
            cols = slice(half * 512, half * 512 + 512)
            dg = nt(DY[i], WD[l, j, cols, :])
            dz = (GP[l, i, :, n * 512 : n * 512 + 512].astype(F32) * dg).astype(BF16)
            term = nt(dz, WU[l, j, :, cols])
            gather(n, term)

        x_copy(1, i).wait_send()
        SND[1, i] = gathered()
        x_copy(1, i).start()

    def dr_copy(k, b):
        rows = pl.ds(pl.multiple_of(b * R, R), R)
        return pltpu.make_async_remote_copy(
            BIG.at[:, rows, :], DR.at[k], dr_snd.at[k], dr_rcv.at[k], device_id=sib, device_id_type=MESH)

    def attend_back(l, i):
        b = blk_of(i)
        pairs = Q.shape[3] // 128
        place = RCV.at[2 + i]

        def back_rows(k):
            return place[(k % 2) * 128 : (k % 2) * 128 + 128, 512 + (k // 2) * 256 : 768 + (k // 2) * 256]

        deltas = []
        for k in range(pairs):
            rows = slice(k * 128, k * 128 + 128)
            prod = back_rows(k).astype(F32) * OT[l, i, rows, :].astype(F32)
            deltas.append(jnp.sum(prod[0:64], axis=0, keepdims=True))
            deltas.append(jnp.sum(prod[64:128], axis=0, keepdims=True))
            OACC[2 * k] = jnp.zeros(OACC.shape[1:], F32)
            OACC[2 * k + 1] = jnp.zeros(OACC.shape[1:], F32)

        def turn(j, c):
            rows = pl.ds(pl.multiple_of(j * R, R), R)
            mask = MSK[pl.ds(pl.multiple_of((i * 2 + j) * R, R), R), :].astype(F32)
            for k in range(pairs):
                lanes = slice(k * 128, k * 128 + 128)
                qs = split_pair(Q[l, i, :, lanes], 1)
                dots = split_pair(back_rows(k), 0)
                keys = KV[l, 0, rows, lanes]
                values = KV[l, 1, rows, lanes]
                for e in range(2):
                    h = 2 * k + e
                    p = jnp.exp(nt(keys, qs[e]) + mask - LSE[l, i, h])
                    dp = nn(values, dots[e])
                    PB[h] = (p * (dp - deltas[h])).astype(BF16)
                    PB[2 * pairs + h] = p.astype(BF16)
            for k in range(pairs):
                lanes = slice(k * 128, k * 128 + 128)
                half = slice((k % 2) * 128, (k % 2) * 128 + 128)
                qs = split_pair(Q[l, i, :, lanes], 1)
                dos = split_pair(place[:, lanes], 1)
                h = 2 * k
                BIG[k // 2, rows, half] += nn(PB[h], qs[0]) + nn(PB[h + 1], qs[1])
                BIG[2 + k // 2, rows, half] += nn(PB[2 * pairs + h], dos[0]) + nn(PB[2 * pairs + h + 1], dos[1])
            for k in range(pairs):
                keys = jnp.transpose(KV[l, 0, rows, k * 128 : k * 128 + 128])
                for e in range(2):
                    OACC[2 * k + e] += nn(keys[e * 64 : e * 64 + 64], PB[2 * k + e])
            return c

        lax.fori_loop(0, b + 1, turn, 0)
        for k in range(pairs):
            dq = jnp.concatenate([OACC[2 * k], OACC[2 * k + 1]], axis=0) * HEAD_DIM ** -0.5
            DQ[k // 2, :, (k % 2) * 128 : (k % 2) * 128 + 128] = jnp.transpose(dq).astype(BF16)

    def backward_attention(l, i):
        b = blk_of(i)
        x_copy(1, i).wait_recv()

        def rows_mid(rows):
            g = swapped(1, i, rows) * vec(l, 2)
            dmid = DY[i, rows, :].astype(F32) + norm_pull(MID[l, i, rows, :], g)
            MID[l, i, rows, :] = dmid
            AB[rows, :] = dmid.astype(BF16)

        by_rows(rows_mid)
        for j in range(2):
            RCV[2 + i, :, 512 + j * 256 : 768 + j * 256] = nt(WO[l, j], AB[...]).astype(BF16)
            RCV[2 + i, :, j * 256 : j * 256 + 256] = nt(AB[...], WO[l, j]).astype(BF16)

        @pl.when(i == 1)
        def _():
            @pl.when(l == 0)
            def _():
                @pl.when(s == 0)
                def _():
                    dr_copy(0, 1).wait_send()
                    dr_copy(1, 2).wait_send()

                @pl.when(s == 1)
                def _():
                    dr_copy(0, 0).wait_send()

            def clear(r, c):
                rows = pl.ds(pl.multiple_of(r * R, R), R)
                BIG[:, rows, :] = jnp.zeros((4, R, 256), F32)
                return c

            lax.fori_loop(0, 4, clear, 0)

        attend_back(l, i)
        own = pl.ds(pl.multiple_of(b * R, R), R)

        @pl.when((s == 0) & (i == 1))
        def _():
            dr_copy(0, 1).start()
            dr_copy(1, 2).start()

        @pl.when(b != 3)
        def _():
            def add(k):
                dr_copy(k, b).wait_recv()
                for c in range(4):
                    BIG[c, own, :] += DR[k, c]

            @pl.when(s == 1)
            def _():
                add(i)

            @pl.when((s == 1) & (i == 0))
            def _():
                dr_copy(0, 0).start()

            @pl.when(s == 0)
            def _():
                add(0)

        for j in range(2):
            DQ[j, :, 256:512] = BIG[j, own, :].astype(BF16)
            DQ[j, :, 512:768] = BIG[2 + j, own, :].astype(BF16)

        def rows_norm(rows):
            xhat, _ = normalize(H[l, i, rows, :].astype(F32))
            AB[rows, :] = (xhat * vec(l, 0) + vec(l, 1)).astype(BF16)

        by_rows(rows_norm)
        ups = [SP[l, j, 24:32, 0:768].astype(BF16) for j in range(2)]
        du = (adapter_scale * (nt(ups[0], DQ[0]) + nt(ups[1], DQ[1]))).astype(BF16)
        GA[l] += nn(du, AB[...])
        top = lax.broadcasted_iota(jnp.int32, (8, 256), 0) < 4
        for j in range(2):
            gq = nn(U[l, i], DQ[j, :, 0:256])
            gv = nn(U[l, i], DQ[j, :, 512:768])
            GB[l, j] += adapter_scale * jnp.where(top, gq, gv)

        x_copy(0, i).wait_send()
        SND[0, i] = (
            nt(DQ[0], WQ[l, 0]) + nt(DQ[1], WQ[l, 1]) + tn(du, SP[l, 0, 8:16, :].astype(BF16))
        ).astype(BF16)

        @pl.when((l == 1) | (i != own_i))
        def _():
            x_copy(0, i).start()

    def core_copies(l):
        return (
            pltpu.make_async_remote_copy(
                GA.at[l], GCA, gc_s.at[0], gc_r.at[0], device_id=sib, device_id_type=MESH),
            pltpu.make_async_remote_copy(
                GB.at[l], GCB, gc_s.at[1], gc_r.at[1], device_id=sib, device_id_type=MESH),
        )

    def plane_copies(l):
        out = []
        for k, (dx, dy) in enumerate(((1, 0), (0, 1), (1, 1))):
            x2 = 1 - x if dx else x
            y2 = 1 - y if dy else y
            to = (s, d, y2 * 2 + x2)
            out.append(pltpu.make_async_remote_copy(
                GA.at[l], GXA.at[k], gx_s.at[k], gx_r.at[k], device_id=to, device_id_type=MESH))
        out.append(pltpu.make_async_remote_copy(
            GB.at[l, 1 - y], GXB, gx_s.at[3], gx_r.at[3], device_id=yp, device_id_type=MESH))
        return out

    def line_copies():
        out = []
        for k in range(1, dp_count):
            to = (s, lax.rem(d + k, dp_count), t)
            out.append(pltpu.make_async_remote_copy(
                GZA.at[d], GZA.at[d], gz_s.at[0, k - 1], gz_r.at[0, k - 1], device_id=to, device_id_type=MESH))
            out.append(pltpu.make_async_remote_copy(
                GZB.at[d], GZB.at[d], gz_s.at[1, k - 1], gz_r.at[1, k - 1], device_id=to, device_id_type=MESH))
        return out

    def sum_core(l):
        @pl.when(s != l)
        def _():
            for c in core_copies(l):
                c.start()

    def sum_plane(l):
        @pl.when(s == l)
        def _():
            for c in core_copies(l):
                c.wait_recv()
            GA[l] += GCA[...]
            GB[l] += GCB[...]
            for c in plane_copies(l):
                c.start()

    def sum_line(l):
        @pl.when(s == l)
        def _():
            for c in plane_copies(l):
                c.wait_recv()
            GZA[d] = (GA[l] + GXA[0]) + (GXA[1] + GXA[2])
            GZB[d] = GB[l, y] + GXB[...]
            for c in line_copies():
                c.start()

    def sum_end(l):
        @pl.when(s == l)
        def _():
            for c in line_copies():
                c.wait_recv()
            total_a, total_b = GZA[0], GZB[0]
            for k in range(1, dp_count):
                total_a, total_b = total_a + GZA[k], total_b + GZB[k]
            out_a[0, 0] = total_a[0:4]
            out_a[0, 1] = total_a[4:8]
            out_b[0, 0] = total_b[0:4]
            out_b[0, 1] = total_b[4:8]

    def bwd_layer(back, carry):
        l = 1 - back

        def f_turn(k, c):
            @pl.when((l == 0) & (k == 1))
            def _():
                sum_plane(1)

            backward_ff(l, 1 - k)
            return c

        def a_turn(k, c):
            @pl.when((l == 0) & (k == 0))
            def _():
                sum_line(1)

            @pl.when((l == 0) & (k == 1))
            def _():
                sum_end(1)

            backward_attention(l, 1 - k)
            return c

        lax.fori_loop(0, 2, f_turn, 0)

        @pl.when(l == 1)
        def _():
            finish_forward()

        lax.fori_loop(0, 2, a_turn, 0)
        sum_core(l)
        return carry

    lax.fori_loop(0, 2, bwd_layer, 0)
    sum_plane(0)

    x_copy(0, own_i).wait_recv()

    def rows_out(rows):
        g = swapped(0, own_i, rows) * vec(0, 0)
        AB[rows, :] = (MID[0, own_i, rows, :] + norm_pull(H[0, own_i, rows, :].astype(F32), g)).astype(BF16)

    by_rows(rows_out)
    send_result(3, 0, AB)
    sum_line(0)

    x_copy(0, 1 - own_i).wait_send()
    for i in range(2):
        x_copy(1, i).wait_send()
    x_copy(2, 1 - own_i).wait_send()
    def sent(ref, sem):
        pltpu.make_async_remote_copy(ref, ref, sem, sem, device_id=sib, device_id_type=MESH).wait_send()

    for p in range(5):
        sent(pieces[p][1].at[s, y] if p else SP.at[s, y], ws_s.at[p])
        for c in range(pieces[p][2] if p else 1):
            k = base[p] + c
            ref = block(p, s, y, chunk(p, c, 0)) if p else SP.at[s, y]
            sent(ref, wy_s.at[k])
            sent(ref, wa_s.at[k])
            if p:
                sent(ref, wz_s.at[k])
                sent(ref, wb_s.at[k])
    rows_done(tok, H.at[0], 0)
    rows_done(cot, DY, 1)
    for l in range(2):
        kv_copy(l, 0).wait_send()

        @pl.when(s == 1)
        def _():
            kv_copy(l, 1).wait_send()

    @pl.when(s == 0)
    def _():
        dr_copy(0, 1).wait_send()
        dr_copy(1, 2).wait_send()

    @pl.when(s == 1)
    def _():
        dr_copy(0, 0).wait_send()

    @pl.when(s == 0)
    def _():
        for c in core_copies(1) + tuple(plane_copies(0)) + tuple(line_copies()):
            c.wait_send()

    @pl.when(s == 1)
    def _():
        for c in core_copies(0) + tuple(plane_copies(1)) + tuple(line_copies()):
            c.wait_send()

    send_result_done(0, 0, H.at[1, 0])
    send_result_done(1, 1, H.at[1, 0])
    send_result_done(2, 1, H.at[1, 0])
    send_result_done(3, 0, H.at[1, 0])
    for o, ref in ((0, act), (1, ig)):
        for m in range(2):
            pltpu.make_async_copy(tok.at[0], ref.at[m], out_rcv.at[o, m]).wait()
    sum_end(0)


def per_pair(
    tokens, cotangent, buckets, lengths, norm_gain_pairs, norm_bias_pairs, query_key_value_weight,
    query_value_bias, output_weight, upward_weight, upward_bias, down_weight, output_bias,
    adapter_down, adapter_upper,
):
    weight_qkv = query_key_value_weight[0].transpose(1, 0, 2)
    dp_count = lax.axis_size("dp")
    anywhere = pl.BlockSpec(memory_space=pl.ANY)
    scalars = pl.BlockSpec(memory_space=pltpu.SMEM)
    vmem = pl.BlockSpec(memory_space=pltpu.VMEM)
    dma = pltpu.SemaphoreType.DMA
    act, ig, total_a, total_b = pl.pallas_call(
        partial(fused_kernel, dp_count),
        out_shape=(
            jax.ShapeDtypeStruct((2, R, D), BF16),
            jax.ShapeDtypeStruct((2, R, D), BF16),
            jax.ShapeDtypeStruct((1, 2, 4, D), F32),
            jax.ShapeDtypeStruct((1, 2, 4, 256), F32),
        ),
        in_specs=[anywhere, anywhere, scalars, scalars, vmem, vmem, anywhere, vmem, anywhere, anywhere, vmem,
                  anywhere, vmem, vmem, vmem],
        out_specs=(anywhere, anywhere, vmem, vmem),
        scratch_shapes=[
            pltpu.VMEM((2, 2, 32, D), F32),
            pltpu.VMEM((2, 2, D, 768), BF16),
            pltpu.VMEM((2, 2, 256, D), BF16),
            pltpu.VMEM((2, 2, D, 1024), BF16),
            pltpu.VMEM((2, 2, 1024, D), BF16),
            pltpu.VMEM((2, 2, R, D), BF16),
            pltpu.VMEM((2, R, D), BF16),
            pltpu.VMEM((2, 2, R, D), F32),
            pltpu.VMEM((2, 2, R, 2048), BF16),
            pltpu.VMEM((2, 2, R, 512), BF16),
            pltpu.VMEM((2, 2, 4 * R, 512), BF16),
            pltpu.VMEM((2, 2, 512, R), BF16),
            pltpu.VMEM((2, 2, 8, 1, R), F32),
            pltpu.VMEM((3, 2, R, D), BF16),
            pltpu.VMEM((5, R, D), BF16),
            pltpu.VMEM((4, 4 * R, R), F32),
            pltpu.VMEM((6 * R, R), BF16),
            pltpu.VMEM((2, 4, R, R), F32),
            pltpu.VMEM((2, R, 768), BF16),
            pltpu.VMEM((R, D), BF16),
            pltpu.VMEM((2, 2, 8, R), BF16),
            pltpu.VMEM((8, 64, R), F32),
            pltpu.VMEM((16, R, R), BF16),
            pltpu.VMEM((2, 8, D), F32),
            pltpu.VMEM((2, 2, 8, 256), F32),
            pltpu.VMEM((8, D), F32),
            pltpu.VMEM((2, 8, 256), F32),
            pltpu.VMEM((3, 8, D), F32),
            pltpu.VMEM((8, 256), F32),
            pltpu.VMEM((dp_count, 8, D), F32),
            pltpu.VMEM((dp_count, 8, 256), F32),
            dma((2, 2)),
            dma((2,)),
            dma((2,)),
            dma((5,)),
            dma((5,)),
            dma((5,)),
            dma((8,)),
            dma((8,)),
            dma((7,)),
            dma((7,)),
            dma((8,)),
            dma((8,)),
            dma((7,)),
            dma((7,)),
            dma((2, 2)),
            dma((2, 2)),
            dma((3, 2)),
            dma((3, 2)),
            dma((2,)),
            dma((2,)),
            dma((2, 2)),
            dma((4,)),
            dma((2,)),
            dma((2,)),
            dma((4,)),
            dma((4,)),
            dma((2, dp_count - 1)),
            dma((2, dp_count - 1)),
        ],
        compiler_params=pltpu.CompilerParams(
            collective_id=0, has_side_effects=True, vmem_limit_bytes=127 * 2**19
        ),
        name="two_layers",
    )(
        tokens, cotangent, buckets, lengths, norm_gain_pairs, norm_bias_pairs, weight_qkv, query_value_bias,
        output_weight, upward_weight, upward_bias, down_weight, output_bias, adapter_down, adapter_upper,
    )
    return act[None], ig[None], total_a, total_b


def solution(mesh):
    in_specs = (
        P("dp", "tensor", None),
        P("dp", "tensor", None),
        P("dp"),
        P("dp", None),
        P("section", None, None),
        P("section", None, None),
        P("section", None, None, "tensor"),
        P("section", None, "tensor"),
        P("section", "tensor", None),
        P("section", None, "tensor"),
        P("section", "tensor"),
        P("section", "tensor", None),
        P("section", None, None),
        P("section", None, None, None),
        P("section", None, None, "tensor"),
    )
    out_specs = (
        P("section", "dp", "tensor", None),
        P("section", "dp", "tensor", None),
        P("section", None, None, None),
        P("section", None, None, "tensor"),
    )
    pairs = mesh.shape["section"] == 2 and mesh.shape["tensor"] == 4 and mesh.shape["dp"] % 2 == 0
    return jax.shard_map(
        per_pair if pairs else per_device, mesh=mesh, in_specs=in_specs, out_specs=out_specs, check_vma=False
    )
```

```python
from functools import partial

import jax
import jax.numpy as jnp
from jax import lax
from jax.experimental import pallas as pl
from jax.experimental.pallas import tpu as pltpu
from jax.sharding import PartitionSpec as P

HEAD_DIM = 64


adapter_scale = 8.0
norm_eps = 1e-05
masked_score = -1000000000.0
highest_precision = lax.Precision.HIGHEST


def from_behind(block, axis, distance):
    devices = range(lax.axis_size(axis))
    route = [(i - distance, i) for i in devices if i - distance in devices]
    return lax.ppermute(block, axis, route)


def layer_norm(values, gain_rows, shifts):
    center = jnp.mean(values, axis=-1, keepdims=True)
    centered = values - center
    spread = jnp.mean(centered * centered, axis=-1, keepdims=True)
    return centered * lax.rsqrt(spread + norm_eps) * gain_rows + shifts


def row_layout(bucket, lengths_row, row_count):
    item_span = jnp.right_shift(jnp.int32(row_count), 3 - bucket)
    positions = jnp.arange(row_count, dtype=jnp.int32)
    item_index = positions // item_span
    within = positions - item_index * item_span
    chosen = (
        item_index[:, None] == jnp.arange(lengths_row.shape[0], dtype=jnp.int32)[None, :]
    ).astype(jnp.int32)
    length = jnp.sum(chosen * lengths_row[None, :], axis=1)
    return (item_index, within < length)


def allowed_keys(item_index, is_valid):
    positions = jnp.arange(item_index.shape[0], dtype=jnp.int32)
    same_item = item_index[:, None] == item_index[None, :]
    causal = positions[None, :] <= positions[:, None]
    key_seen = is_valid[None, :] | (positions[None, :] == positions[:, None])
    return same_item & causal & key_seen


def take_slot(buffer, slot_index):
    return lax.dynamic_index_in_dim(buffer, slot_index, 0, keepdims=False)


def put_slot(buffer, slot_index, is_live, update):
    previous = take_slot(buffer, slot_index)
    return lax.dynamic_update_index_in_dim(
        buffer, jnp.where(is_live, update, previous), slot_index, 0
    )


def per_device(
    tokens,
    cotangent,
    buckets,
    lengths,
    norm_gain_pairs,
    norm_bias_pairs,
    query_key_value_weight,
    query_value_bias,
    output_weight,
    upward_weight,
    upward_bias,
    down_weight,
    output_bias,
    adapter_down,
    adapter_upper,
):
    section_index = lax.axis_index("section")
    tensor_count = lax.axis_size("tensor")
    micro_count, own_rows, model_width = tokens.shape
    row_count = own_rows * tensor_count
    own_start = lax.axis_index("tensor") * own_rows
    gain_sets = norm_gain_pairs[0].astype(jnp.float32)
    shift_sets = norm_bias_pairs[0].astype(jnp.float32)
    weight_qkv = query_key_value_weight[0]
    bias_query_value = query_value_bias[0].astype(jnp.float32)
    weight_out = output_weight[0]
    weight_up = upward_weight[0]
    bias_up = upward_bias[0].astype(jnp.float32)
    weight_down = down_weight[0]
    biases = output_bias[0].astype(jnp.float32)
    down_factor = adapter_down[0]
    upper_factor = adapter_upper[0]
    factor_wide = down_factor.astype(jnp.float32)
    local_width = weight_qkv.shape[2]
    local_heads = local_width // HEAD_DIM
    score_scale = HEAD_DIM ** (-0.5)

    def widen(values):
        return lax.all_gather(values, "tensor", axis=0, tiled=True)

    def widen_back(values):
        return lax.all_gather(values, "tensor", axis=0, tiled=True)

    def settle(source, weight):

        def row_term(first_row, row_span):
            return jnp.dot(source, weight, preferred_element_type=jnp.float32)

        return lax.psum_scatter(
            row_term(jnp.int32(0), lax.axis_size("tensor") * own_rows).astype(jnp.bfloat16),
            "tensor",
            scatter_dimension=0,
            tiled=True,
        ).astype(jnp.float32)

    def settle_back(row_term):
        return lax.psum_scatter(
            row_term(jnp.int32(0), lax.axis_size("tensor") * own_rows).astype(jnp.bfloat16),
            "tensor",
            scatter_dimension=0,
            tiled=True,
        ).astype(jnp.float32)

    def layout_of(slot_index):
        item_index, is_valid = row_layout(
            take_slot(buckets, slot_index), take_slot(lengths, slot_index), row_count
        )
        own_valid = lax.dynamic_slice_in_dim(is_valid, own_start, own_rows, 0)
        return (allowed_keys(item_index, is_valid), own_valid)

    def attend(normed, allowed):
        reduced_query = jnp.dot(
            normed, down_factor[0].T, preferred_element_type=jnp.float32
        ).astype(jnp.bfloat16)
        reduced_value = jnp.dot(
            normed, down_factor[1].T, preferred_element_type=jnp.float32
        ).astype(jnp.bfloat16)
        blended_rows = jnp.einsum(
            "rd,dcn->rcn", normed, weight_qkv, preferred_element_type=jnp.float32
        )
        query_matrix_rows = (
            blended_rows[:, 0]
            + bias_query_value[0]
            + adapter_scale
            * jnp.dot(reduced_query, upper_factor[0], preferred_element_type=jnp.float32)
        )
        value_matrix_rows = (
            blended_rows[:, 2]
            + bias_query_value[1]
            + adapter_scale
            * jnp.dot(reduced_value, upper_factor[1], preferred_element_type=jnp.float32)
        )
        packed = jnp.stack(
            [query_matrix_rows, blended_rows[:, 1], value_matrix_rows], axis=1
        ).astype(jnp.bfloat16)
        head_split = packed.reshape(row_count, 3, local_heads, HEAD_DIM)
        scores = (
            jnp.einsum(
                "qhe,khe->hqk",
                head_split[:, 0],
                head_split[:, 1],
                preferred_element_type=jnp.float32,
            )
            * score_scale
        )
        scores = jnp.where(allowed[None], scores, masked_score)
        top_score = jnp.max(scores, axis=-1, keepdims=True)
        exponent = jnp.exp(scores - top_score)
        attn_probs = exponent / jnp.sum(exponent, axis=-1, keepdims=True)
        return (reduced_query, reduced_value, head_split, attn_probs)

    def forward(hidden, allowed):
        normed = widen(layer_norm(hidden, gain_sets[0], shift_sets[0]).astype(jnp.bfloat16))
        reduced_query, reduced_value, head_split, attn_probs = attend(normed, allowed)
        probs_low = attn_probs.astype(jnp.bfloat16)
        mixed_heads = jnp.einsum(
            "hqk,khe->qhe", probs_low, head_split[:, 2], preferred_element_type=jnp.float32
        )
        attended = mixed_heads.reshape(row_count, local_width).astype(jnp.bfloat16)
        middle = hidden + (settle(attended, weight_out) + biases[0])
        normed_two = widen(layer_norm(middle, gain_sets[1], shift_sets[1]).astype(jnp.bfloat16))
        hidden_pre = jnp.dot(normed_two, weight_up, preferred_element_type=jnp.float32) + bias_up
        activated = jax.nn.gelu(hidden_pre, approximate=True).astype(jnp.bfloat16)
        output = middle + (settle(activated, weight_down) + biases[1])
        return (output, normed, middle, normed_two)

    def backward(hidden, grad_out, allowed, normed, middle, normed_two):
        reduced_query, reduced_value, head_split, attn_probs = attend(normed, allowed)
        probs_low = attn_probs.astype(jnp.bfloat16)
        hidden_pre = jnp.dot(normed_two, weight_up, preferred_element_type=jnp.float32) + bias_up
        grad_branch = widen_back(grad_out.astype(jnp.bfloat16))
        grad_act = jnp.einsum(
            "rd,fd->rf", grad_branch, weight_down, preferred_element_type=jnp.float32
        )
        gelu_pull = jax.vjp(partial(jax.nn.gelu, approximate=True), hidden_pre)[1]
        grad_pre = gelu_pull(grad_act)[0].astype(jnp.bfloat16)

        def mlp_term(first_row, row_span):
            return jnp.einsum("rf,df->rd", grad_pre, weight_up, preferred_element_type=jnp.float32)

        grad_norm_two = settle_back(mlp_term)
        second_pull = jax.vjp(
            partial(layer_norm, gain_rows=gain_sets[1], shifts=shift_sets[1]), middle
        )[1]
        grad_middle = grad_out + second_pull(grad_norm_two)[0]
        grad_attn = widen_back(grad_middle.astype(jnp.bfloat16))
        grad_heads = jnp.einsum(
            "rd,nd->rn", grad_attn, weight_out, preferred_element_type=jnp.float32
        )
        grad_heads = grad_heads.astype(jnp.bfloat16).reshape(row_count, local_heads, HEAD_DIM)
        grad_probs = jnp.einsum(
            "qhe,khe->hqk", grad_heads, head_split[:, 2], preferred_element_type=jnp.float32
        )
        grad_scores = attn_probs * (
            grad_probs - jnp.sum(attn_probs * grad_probs, axis=-1, keepdims=True)
        )
        grad_scores = grad_scores.astype(jnp.bfloat16)
        grad_query = (
            jnp.einsum(
                "hqk,khe->qhe", grad_scores, head_split[:, 1], preferred_element_type=jnp.float32
            )
            * score_scale
        )
        grad_key = (
            jnp.einsum(
                "hqk,qhe->khe", grad_scores, head_split[:, 0], preferred_element_type=jnp.float32
            )
            * score_scale
        )
        grad_value = jnp.einsum(
            "hqk,qhe->khe", probs_low, grad_heads, preferred_element_type=jnp.float32
        )
        grad_packed = (
            jnp.stack([grad_query, grad_key, grad_value], axis=1)
            .reshape(row_count, 3, local_width)
            .astype(jnp.bfloat16)
        )
        grad_pair = jnp.stack([grad_packed[:, 0], grad_packed[:, 2]])
        gradient_reduced = adapter_scale * jnp.einsum(
            "jrn,jkn->jrk", grad_pair, upper_factor, preferred_element_type=jnp.float32
        )

        def attn_term(first_row, row_span):
            dense_part = jnp.einsum(
                "rcn,dcn->rd", grad_packed, weight_qkv, preferred_element_type=jnp.float32
            )
            return dense_part + jnp.einsum(
                "jrk,jkd->rd", gradient_reduced, factor_wide, precision=highest_precision
            )

        grad_normed = settle_back(attn_term)
        first_pull = jax.vjp(
            partial(layer_norm, gain_rows=gain_sets[0], shifts=shift_sets[0]), hidden
        )[1]
        grad_hidden = grad_middle + first_pull(grad_normed)[0]
        grad_factor_a = jnp.einsum(
            "jrk,rd->jkd", gradient_reduced, normed.astype(jnp.float32), precision=highest_precision
        )
        gradient_upper_factor = adapter_scale * jnp.stack(
            [
                jnp.einsum(
                    "rk,rn->kn",
                    reduced_query,
                    grad_packed[:, 0],
                    preferred_element_type=jnp.float32,
                ),
                jnp.einsum(
                    "rk,rn->kn",
                    reduced_value,
                    grad_packed[:, 2],
                    preferred_element_type=jnp.float32,
                ),
            ]
        )
        return (grad_hidden, grad_factor_a, gradient_upper_factor)

    zero_rows = jnp.zeros((micro_count, own_rows, model_width), jnp.bfloat16)
    saved_start = ()

    def record(buffers, slot_index, is_live, layer_input, results):
        kept_in, outputs, saved = buffers
        output, normed, middle, normed_two = results
        low_output = output.astype(jnp.bfloat16)
        kept_in = put_slot(kept_in, slot_index, is_live, layer_input)
        outputs = put_slot(outputs, slot_index, is_live, low_output)
        return ((kept_in, outputs, saved), low_output)

    buffers = (zero_rows, zero_rows, saved_start)

    def run_phase(buffers, sources, phase_section):

        def phase_turn(slot_index, buffers):
            allowed, own_valid = layout_of(slot_index)
            layer_input = take_slot(sources, slot_index)
            results = forward(layer_input.astype(jnp.float32), allowed)
            return record(
                buffers, slot_index, section_index == phase_section, layer_input, results
            )[0]

        return lax.fori_loop(0, micro_count, phase_turn, buffers)

    buffers = run_phase(buffers, tokens, 0)
    received = from_behind(buffers[1], "section", 1)
    buffers = run_phase(buffers, received, 1)
    kept_in, outputs, saved = buffers

    def back_step(slot_index, grad_out, allowed):
        hidden = take_slot(kept_in, slot_index).astype(jnp.float32)
        output, normed, middle, normed_two = forward(hidden, allowed)
        return backward(hidden, grad_out, allowed, normed, middle, normed_two)

    def top_grad(slot_index, own_valid):
        return take_slot(cotangent, slot_index).astype(jnp.float32) * own_valid[:, None].astype(
            jnp.float32
        )

    zero_a = jnp.zeros(down_factor.shape, jnp.float32)
    zero_b = jnp.zeros(upper_factor.shape, jnp.float32)

    def run_back(loop_state, sources, phase_section):

        def phase_turn(slot_index, loop_state):
            grads_in, sum_a, sum_b = loop_state
            allowed, own_valid = layout_of(slot_index)
            if phase_section == 1:
                grad_out = top_grad(slot_index, own_valid)
            else:
                grad_out = take_slot(sources, slot_index).astype(jnp.float32)
            is_live = section_index == phase_section
            grad_hidden, grad_a, grad_b = back_step(slot_index, grad_out, allowed)
            grads_in = put_slot(grads_in, slot_index, is_live, grad_hidden.astype(jnp.bfloat16))
            sum_a = sum_a + jnp.where(is_live, grad_a, 0.0)
            sum_b = sum_b + jnp.where(is_live, grad_b, 0.0)
            return (grads_in, sum_a, sum_b)

        return lax.fori_loop(0, micro_count, phase_turn, loop_state)

    loop_state = run_back((zero_rows, zero_a, zero_b), zero_rows, 1)
    received_grads = from_behind(loop_state[0], "section", -1)
    grads_in, sum_a, sum_b = run_back(loop_state, received_grads, 0)
    total_a = lax.psum(sum_a, ("dp", "tensor"))
    total_b = lax.psum(sum_b, "dp")
    return (outputs[None], grads_in[None], total_a[None], total_b[None])


R = 256
D = 1024
NEG = -1e30
F32 = jnp.float32
BF16 = jnp.bfloat16
MESH = pl.DeviceIdType.MESH
CHUNK = 128


def nn(a, b):
    return lax.dot_general(a, b, (((1,), (0,)), ((), ())), preferred_element_type=F32)


def nt(a, b):
    return lax.dot_general(a, b, (((1,), (1,)), ((), ())), preferred_element_type=F32)


def tn(a, b):
    return lax.dot_general(a, b, (((0,), (0,)), ((), ())), preferred_element_type=F32)


def normalize(v):
    centered = v - jnp.mean(v, axis=-1, keepdims=True)
    rs = lax.rsqrt(jnp.mean(centered * centered, axis=-1, keepdims=True) + norm_eps)
    return centered * rs, rs


def norm_pull(v, g):
    xhat, rs = normalize(v)
    return rs * (
        g
        - jnp.mean(g, axis=-1, keepdims=True)
        - xhat * jnp.mean(g * xhat, axis=-1, keepdims=True)
    )


def gelu_pair(z):
    c = 0.7978845608028654
    z2 = z * z
    t = jnp.tanh(c * (z + 0.044715 * (z2 * z)))
    half = 0.5 * (1.0 + t)
    slope = half + (0.5 * c) * z * (1.0 - t * t) * (1.0 + (3.0 * 0.044715) * z2)
    return z * half, slope


def fused_kernel(
    dp_count,
    tok, cot, buckets, lengths, gain_in, shift_in, wq_in, bqv_in, wo_in, wu_in, bu_in, wd_in, bo_in, ad_in, au_in,
    act, ig, out_a, out_b,
    SP, WQ, WO, WU, WD, H, DY, MID, GP, Q, KV, OT, LSE, SND, RCV, BIG, MSK, DR, DQ, AB, U, OACC, PB,
    GA, GB, GCA, GCB, GXA, GXB, GZA, GZB,
    tok_sem, tok_ys, tok_xs, wl, ws_r, ws_s, wy_r, wy_s, wz_r, wz_s, wa_r, wa_s, wb_r, wb_s,
    kv_rcv, kv_snd, x_rcv, x_snd, last_rcv, last_snd, dr_rcv, dr_snd, out_rcv, out_snd, gc_r, gc_s, gx_r, gx_s, gz_r, gz_s,
):
    s = lax.axis_index("section")
    d = lax.axis_index("dp")
    t = lax.axis_index("tensor")
    x = lax.rem(t, 2)
    y = lax.div(t, 2)
    sib = (1 - s, d, t)
    xp = (s, d, y * 2 + 1 - x)
    yp = (s, d, (1 - y) * 2 + x)
    z_half = lax.rem(d, 2)
    zp = (s, d + 1 - 2 * z_half, t)
    flip = s + x - 2 * s * x
    own_i = flip

    def blk_of(i):
        return 2 * i + (s + i - 2 * s * i)

    bar = pltpu.get_barrier_semaphore()
    for ds_ in range(2):
        for dx in range(2):
            for dy in range(2):
                if ds_ or dx or dy:
                    s2 = 1 - s if ds_ else s
                    x2 = 1 - x if dx else x
                    y2 = 1 - y if dy else y
                    pl.semaphore_signal(bar, 1, device_id=(s2, d, y2 * 2 + x2), device_id_type=MESH)
    for k in range(1, dp_count):
        pl.semaphore_signal(bar, 1, device_id=(s, lax.rem(d + k, dp_count), t), device_id_type=MESH)
    pl.semaphore_wait(bar, 7 + dp_count - 1)

    def row_copies(src, dst, w):
        def local():
            return pltpu.make_async_copy(src.at[y], dst.at[y], tok_sem.at[w, y])

        def to_y():
            return pltpu.make_async_remote_copy(
                src.at[1 - y], dst.at[y], tok_ys.at[w], tok_sem.at[w, y], device_id=yp, device_id_type=MESH)

        def first_x():
            return pltpu.make_async_remote_copy(
                src.at[y], dst.at[y], tok_xs.at[w], tok_sem.at[w, y], device_id=xp, device_id_type=MESH)

        def then_x():
            return pltpu.make_async_remote_copy(
                dst.at[own_i], dst.at[own_i], tok_xs.at[w], tok_sem.at[w, own_i],
                device_id=xp, device_id_type=MESH)

        return local, to_y, first_x, then_x

    def rows_first(src, dst, w):
        local, _, first_x, _ = row_copies(src, dst, w)

        @pl.when(y == own_i)
        def _():
            first_x().start()
            local().start()

    def rows_swap(src, dst, w):
        @pl.when(y == own_i)
        def _():
            row_copies(src, dst, w)[1]().start()

    def rows_relay(src, dst, w):
        pltpu.make_async_copy(src.at[0], dst.at[own_i], tok_sem.at[w, own_i]).wait()

        @pl.when(y != own_i)
        def _():
            row_copies(src, dst, w)[3]().start()

    def rows_rest(src, dst, w):
        pltpu.make_async_copy(src.at[0], dst.at[1 - own_i], tok_sem.at[w, 1 - own_i]).wait()

    def rows_done(src, dst, w):
        _, to_y, first_x, _ = row_copies(src, dst, w)
        if w == 0:
            first_x().wait_send()

        @pl.when(y == own_i)
        def _():
            to_y().wait_send()

    pieces = (None, (wq_in, WQ, 2), (wo_in, WO, 1), (wu_in, WU, 2), (wd_in, WD, 2))
    base = (7, 0, 2, 3, 5)

    def sources(p, rows):
        src, dst, _ = pieces[p]
        if p == 1:
            return [
                (src.at[c, rows, :], dst.at[s, y, rows, c * 256 : c * 256 + 256]) for c in range(3)
            ]
        return [(src.at[0, rows, :], dst.at[s, y, rows, :])]

    def chunk(p, c, half):
        dst, parts = pieces[p][1], pieces[p][2]
        size = dst.shape[2] // (2 * parts)
        return pl.ds(pl.multiple_of((half * parts + c) * size, size), size)

    def block(p, l, j, rows):
        return pieces[p][1].at[l, j, rows, :]

    def own_start(p):
        everything = pl.ds(0, pieces[p][1].shape[2])
        for src, dst in sources(p, everything):
            pltpu.make_async_copy(src, dst, wl.at[p]).start()
            pltpu.make_async_remote_copy(
                src, dst, ws_s.at[p], ws_r.at[p], device_id=sib, device_id_type=MESH).start()

    def y_start(p):
        if p == 0:
            small_copy(yp, wy_s.at[7], wy_r.at[7]).start()
            return
        for c in range(pieces[p][2]):
            for src, dst in sources(p, chunk(p, c, z_half)):
                k = base[p] + c
                pltpu.make_async_remote_copy(
                    src, dst, wy_s.at[k], wy_r.at[k], device_id=yp, device_id_type=MESH).start()

    def small_copy(to, snd, rcv):
        return pltpu.make_async_remote_copy(
            SP.at[s, y], SP.at[s, y], snd, rcv, device_id=to, device_id_type=MESH)

    def passed(p, c, half, to, snd, rcv):
        ref = SP.at[s, 1 - y] if p == 0 else block(p, s, 1 - y, chunk(p, c, half))
        return pltpu.make_async_remote_copy(ref, ref, snd, rcv, device_id=to, device_id_type=MESH)

    def relay_y(l, p, c=0):
        k = base[p] + c

        @pl.when(l == s)
        def _():
            passed(p, c, z_half, sib, wa_s.at[k], wy_r.at[k]).wait_recv()
            if p:
                passed(p, c, z_half, zp, wz_s.at[k], wz_r.at[k]).start()
            passed(p, c, z_half, sib, wa_s.at[k], wa_r.at[k]).start()

    def relay_z(l, p, c=0):
        k = base[p] + c

        @pl.when(l == s)
        def _():
            passed(p, c, 1 - z_half, zp, wz_s.at[k], wz_r.at[k]).wait_recv()
            passed(p, c, 1 - z_half, sib, wb_s.at[k], wb_r.at[k]).start()

    def own_wait(l, p):
        @pl.when(l == s)
        def _():
            if p:
                ref = pieces[p][1].at[s, y]
                pltpu.make_async_copy(ref, ref, wl.at[p]).wait()

        @pl.when(l != s)
        def _():
            ref = pieces[p][1].at[1 - s, y] if p else SP.at[1 - s, y]
            pltpu.make_async_copy(ref, ref, ws_r.at[p]).wait()

    def other_wait(l, p):
        @pl.when(l != s)
        def _():
            if p == 0:
                ref = SP.at[1 - s, 1 - y]
                pltpu.make_async_copy(ref, ref, wa_r.at[7]).wait()
            else:
                for c in range(pieces[p][2]):
                    k = base[p] + c
                    ref = block(p, 1 - s, 1 - y, chunk(p, c, 0))
                    pltpu.make_async_copy(ref, ref, wa_r.at[k]).wait()
                    pltpu.make_async_copy(ref, ref, wb_r.at[k]).wait()

    @pl.when(s == 0)
    def _():
        y_start(1)

    rows_swap(tok, H.at[0], 0)
    rows_first(tok, H.at[0], 0)
    SP[s, y] = jnp.zeros(SP.shape[2:], F32)
    for k, (ref, row) in enumerate(
        ((gain_in, 0), (shift_in, 0), (gain_in, 1), (shift_in, 1), (bo_in, 0), (bo_in, 1))
    ):
        SP[s, y, k : k + 1, :] = ref[0, row : row + 1, :].astype(F32)
    SP[s, y, 8:12, :] = ad_in[0, 0].astype(F32)
    SP[s, y, 12:16, :] = ad_in[0, 1].astype(F32)
    SP[s, y, 16:17, :] = bu_in[...].astype(F32)
    SP[s, y, 17:18, 0:256] = bqv_in[0, 0:1, :].astype(F32)
    SP[s, y, 17:18, 512:768] = bqv_in[0, 1:2, :].astype(F32)
    SP[s, y, 24:28, 0:256] = au_in[0, 0].astype(F32)
    SP[s, y, 28:32, 512:768] = au_in[0, 1].astype(F32)
    small_copy(sib, ws_s.at[0], ws_r.at[0]).start()
    for p in range(1, 5):
        own_start(p)

    @pl.when(s == 0)
    def _():
        y_start(0)
        for p in range(2, 5):
            y_start(p)

    shift = 7 + buckets[y]
    span_mask = lax.shift_left(jnp.int32(1), shift) - 1

    def length_of(pos):
        item = lax.shift_right_logical(pos, jnp.broadcast_to(shift, pos.shape))
        got = jnp.zeros(pos.shape, jnp.int32)
        for k in range(lengths.shape[1]):
            got = jnp.where(item == k, lengths[y, k], got)
        return item, jnp.bitwise_and(pos, span_mask) < got

    def build_mask(i):
        b = blk_of(i)
        q_row = b * R + lax.broadcasted_iota(jnp.int32, (1, R), 1)
        q_item = lax.shift_right_logical(q_row, jnp.broadcast_to(shift, q_row.shape))

        def rows(r, carry):
            r0 = pl.multiple_of(r * CHUNK, CHUNK)
            k_row = r0 + lax.broadcasted_iota(jnp.int32, (CHUNK, 1), 0)
            k_item, k_ok = length_of(k_row)
            k_tag = jnp.where(k_ok, k_item, -1)
            same = (k_tag == q_item) & (k_row <= q_row)
            allowed = same | (k_row == q_row)
            MSK[pl.ds(pl.multiple_of(i * 2 * R + r0, CHUNK), CHUNK), :] = jnp.where(allowed, 0.0, NEG).astype(BF16)
            return carry

        lax.fori_loop(0, (b + 1) * (R // CHUNK), rows, 0)

    build_mask(0)
    build_mask(1)
    GA[...] = jnp.zeros(GA.shape, F32)
    GB[...] = jnp.zeros(GB.shape, F32)

    def x_copy(slot, i):
        return pltpu.make_async_remote_copy(
            SND.at[slot, i], RCV.at[slot * 2 + (i if slot < 2 else 0)], x_snd.at[slot, i], x_rcv.at[slot, i],
            device_id=xp, device_id_type=MESH)

    def last_copy(c, i):
        rows = slice(c * 64, c * 64 + 64)
        return pltpu.make_async_remote_copy(
            SND.at[0, i, rows, :], RCV.at[i, rows, :], last_snd.at[c], last_rcv.at[c],
            device_id=xp, device_id_type=MESH)

    def by_rows(body):
        body(slice(0, R))

    total_rows = slice(3 * R, 4 * R)

    def gather(n, term):
        for c in range(4):
            part = term[:, c * R : c * R + R]
            BIG[c, total_rows, :] = part if n == 0 else BIG[c, total_rows, :] + part

    def gathered():
        return jnp.concatenate([BIG[c, total_rows, :] for c in range(4)], axis=1).astype(BF16)

    def swapped(slot, i, rows):
        return SND[slot, i, rows, :].astype(F32) + RCV[slot * 2 + (i if slot < 2 else 0), rows, :].astype(F32)

    def send_result(which, layer, src, rows=slice(0, R)):
        src = src.at[rows, :]
        dst = act if which < 2 else ig
        o = 0 if which < 2 else 1
        here = (s == layer) & (y == own_i)

        @pl.when(here)
        def _():
            pltpu.make_async_copy(src, dst.at[y, rows, :], out_rcv.at[o, y]).start()

        @pl.when(jnp.logical_not(here))
        def _():
            pltpu.make_async_remote_copy(
                src, dst.at[y, rows, :], out_snd.at[which], out_rcv.at[o, y],
                device_id=(layer, d, own_i * 2 + x), device_id_type=MESH).start()

    def send_result_done(which, layer, src):
        dst = act if which < 2 else ig
        o = 0 if which < 2 else 1
        here = (s == layer) & (y == own_i)

        @pl.when(jnp.logical_not(here))
        def _():
            pltpu.make_async_remote_copy(
                src, dst.at[y], out_snd.at[which], out_rcv.at[o, y],
                device_id=(layer, d, own_i * 2 + x), device_id_type=MESH).wait_send()

    def vec(l, k):
        return SP[l, 0, k : k + 1, :]

    def head_lanes(pair):
        return pl.ds(pl.multiple_of(pair * 128, 128), 128)

    def split_pair(v, axis):
        which = lax.broadcasted_iota(jnp.int32, v.shape, axis) < HEAD_DIM
        zero = jnp.zeros_like(v)
        return jnp.where(which, v, zero), jnp.where(which, zero, v)

    def kv_copy(l, i):
        rows = pl.ds(pl.multiple_of(blk_of(i) * R, R), R)
        return pltpu.make_async_remote_copy(
            KV.at[l, :, rows, :], KV.at[l, :, rows, :], kv_snd.at[l, i], kv_rcv.at[l, i],
            device_id=sib, device_id_type=MESH)

    def kv_wait(l, i):
        b = 2 * i + (1 - s + i - 2 * (1 - s) * i)
        rows = pl.ds(pl.multiple_of(b * R, R), R)
        pltpu.make_async_remote_copy(
            KV.at[l, :, rows, :], KV.at[l, :, rows, :], kv_snd.at[l, i], kv_rcv.at[l, i],
            device_id=sib, device_id_type=MESH).wait_recv()

    GROUP = 4

    def attend(l, i):
        b = blk_of(i)

        def group_turn(g, carry):
            def lanes_of(k):
                return pl.ds(pl.multiple_of(g * (GROUP * HEAD_DIM) + k * 128, 128), 128)

            def first(j, tops):
                rows = pl.ds(pl.multiple_of(j * R, R), R)
                mask = MSK[pl.ds(pl.multiple_of((i * 2 + j) * R, R), R), :].astype(F32)
                new = []
                for k in range(GROUP // 2):
                    qs = split_pair(Q[l, i, :, lanes_of(k)], 1)
                    keys = KV[l, 0, rows, lanes_of(k)]
                    for e in range(2):
                        st = nt(keys, qs[e]) + mask
                        BIG[2 * k + e, rows, :] = st
                        new.append(jnp.maximum(tops[2 * k + e], jnp.max(st, axis=0, keepdims=True)))
                return tuple(new)

            tops = lax.fori_loop(0, b + 1, first, (jnp.full((1, R), NEG, F32),) * GROUP)
            for k in range(GROUP):
                OACC[k] = jnp.zeros(OACC.shape[1:], F32)

            def second(j, sums):
                rows = pl.ds(pl.multiple_of(j * R, R), R)
                new = []
                for k in range(GROUP):
                    p = jnp.exp(BIG[k, rows, :] - tops[k])
                    new.append(sums[k] + jnp.sum(p, axis=0, keepdims=True))
                    PB[k] = p.astype(BF16)
                for k in range(GROUP // 2):
                    values = jnp.transpose(KV[l, 1, rows, lanes_of(k)])
                    for e in range(2):
                        OACC[2 * k + e] += nn(values[e * 64 : e * 64 + 64], PB[2 * k + e])
                return tuple(new)

            sums = lax.fori_loop(0, b + 1, second, (jnp.zeros((1, R), F32),) * GROUP)
            for k in range(GROUP):
                OT[l, i, pl.ds(pl.multiple_of((g * GROUP + k) * 64, 64), 64), :] = (
                    OACC[k] * (1.0 / sums[k])
                ).astype(BF16)
                LSE[l, i, g * GROUP + k] = tops[k] + jnp.log(sums[k])
            return carry

        lax.fori_loop(0, Q.shape[3] // (GROUP * HEAD_DIM), group_turn, 0)

    def forward_attention(l, i):
        b = blk_of(i)

        @pl.when(i == 0)
        def _():
            @pl.when(l == 0)
            def _():
                relay_y(l, 1, 0)
                rows_relay(tok, H.at[0], 0)
                relay_y(l, 0)
                relay_y(l, 1, 1)
                relay_z(l, 1, 0)

                @pl.when(own_i == 1)
                def _():
                    rows_rest(tok, H.at[0], 0)

                rows_first(cot, DY, 1)

            own_wait(l, 0)
            other_wait(l, 0)
            own_wait(l, 1)

            @pl.when(l == 1)
            def _():
                rows_relay(cot, DY, 1)
                relay_z(l, 1, 0)

            relay_y(l, 2)
            relay_z(l, 1, 1)
            other_wait(l, 1)

        @pl.when(i == 1)
        def _():
            @pl.when((l == 0) & (own_i == 0))
            def _():
                rows_rest(tok, H.at[0], 0)

            relay_y(l, 3, 0)
            relay_y(l, 3, 1)

        @pl.when(l == 1)
        def _():
            x_copy(1, i).wait_recv()

            def rows_in(rows):
                h = MID[0, i, rows, :] + (swapped(1, i, rows) + vec(0, 5))
                H[1, i, rows, :] = h.astype(BF16)

            by_rows(rows_in)

            @pl.when(i == own_i)
            def _():
                send_result(0, 0, H.at[1, i])

        def rows_norm(rows):
            xhat, _ = normalize(H[l, i, rows, :].astype(F32))
            AB[rows, :] = (xhat * vec(l, 0) + vec(l, 1)).astype(BF16)

        by_rows(rows_norm)
        u = nt(AB[...], SP[l, 0, 8:16, :].astype(BF16)).astype(BF16)
        U[l, i] = nt(SP[l, 0, 8:16, :].astype(BF16), AB[...]).astype(BF16)
        own_rows = pl.ds(pl.multiple_of(b * R, R), R)
        for j in range(2):
            up = SP[l, j, 24:32, 0:768].astype(BF16)
            qkv = nn(AB[...], WQ[l, j]) + (adapter_scale * nn(u, up) + SP[l, j, 17:18, 0:768])
            cols = slice(j * 256, j * 256 + 256)
            Q[l, i, :, cols] = (qkv[:, 0:256] * HEAD_DIM ** -0.5).astype(BF16)
            KV[l, 0, own_rows, cols] = qkv[:, 256:512].astype(BF16)
            KV[l, 1, own_rows, cols] = qkv[:, 512:768].astype(BF16)

        @pl.when(b != 3)
        def _():
            kv_copy(l, i).start()

        @pl.when((s == 1) & (i == 0))
        def _():
            kv_wait(l, 0)

        @pl.when((s == 0) & (i == 1))
        def _():
            kv_wait(l, 0)
            kv_wait(l, 1)

        attend(l, i)

        @pl.when(i == 0)
        def _():
            own_wait(l, 2)
            relay_z(l, 2)
            other_wait(l, 2)

        @pl.when(l == 1)
        def _():
            x_copy(0, i).wait_send()

        SND[0, i] = (tn(OT[l, i, 0:256, :], WO[l, 0]) + tn(OT[l, i, 256:512, :], WO[l, 1])).astype(BF16)
        x_copy(0, i).start()

    def forward_ff(l, i):
        @pl.when(i == 0)
        def _():
            @pl.when((s == 1) & (l == 0))
            def _():
                for p in range(5):
                    y_start(p)

            own_wait(l, 3)
            own_wait(l, 4)
            relay_z(l, 3, 0)
            relay_y(l, 4, 0)
            relay_z(l, 3, 1)
            relay_y(l, 4, 1)

        @pl.when((i == 1) & (l == 0))
        def _():
            rows_swap(cot, DY, 1)
            relay_y(1, 0)
            relay_y(1, 1, 0)
            relay_y(1, 1, 1)

        x_copy(0, i).wait_recv()

        def rows_mid(rows):
            mid = H[l, i, rows, :].astype(F32) + (swapped(0, i, rows) + vec(l, 4))
            MID[l, i, rows, :] = mid
            xhat, _ = normalize(mid)
            AB[rows, :] = (xhat * vec(l, 2) + vec(l, 3)).astype(BF16)

        by_rows(rows_mid)
        for n in range(4):
            j, half = (y if n < 2 else 1 - y), n % 2
            cols = slice(half * 512, half * 512 + 512)
            if n == 2:

                @pl.when(i == 0)
                def _():
                    relay_z(l, 4, 0)
                    relay_z(l, 4, 1)
                    other_wait(l, 3)
                    other_wait(l, 4)

            z = nn(AB[...], WU[l, j, :, cols]) + SP[l, j, 16:17, cols]
            g, slope = gelu_pair(z)
            GP[l, i, :, n * 512 : n * 512 + 512] = slope.astype(BF16)
            term = nn(g.astype(BF16), WD[l, j, cols, :])
            gather(n, term)
        SND[1 + l, i] = gathered()

        @pl.when(l == 0)
        def _():
            x_copy(1, i).start()

        @pl.when((l == 1) & (i != own_i))
        def _():
            x_copy(2, i).start()

    def fwd_layer(l, carry):
        def a_turn(i, c):
            forward_attention(l, i)
            return c

        def f_turn(i, c):
            forward_ff(l, i)
            return c

        lax.fori_loop(0, 2, a_turn, 0)
        lax.fori_loop(0, 2, f_turn, 0)
        return carry

    lax.fori_loop(0, 2, fwd_layer, 0)

    def finish_forward():
        x_copy(2, own_i).wait_recv()

        def rows_out(rows):
            out = MID[1, own_i, rows, :] + (swapped(2, own_i, rows) + vec(1, 5))
            SND[2, own_i, rows, :] = out.astype(BF16)

        by_rows(rows_out)
        send_result(1, 1, SND.at[2, own_i])

    def backward_ff(l, i):
        @pl.when(l == 1)
        def _():
            @pl.when(i == own_i)
            def _():
                row_copies(cot, DY, 1)[3]().wait_send()

            @pl.when(i != own_i)
            def _():
                rows_rest(cot, DY, 1)

            def rows_valid(rows):
                pos = blk_of(i) * R + lax.broadcasted_iota(jnp.int32, (R, 1), 0)
                _, ok = length_of(pos)
                DY[i, rows, :] = (DY[i, rows, :].astype(F32) * jnp.where(ok, 1.0, 0.0)).astype(BF16)

            by_rows(rows_valid)

        @pl.when(l == 0)
        def _():
            x_copy(0, i).wait_recv()

            def rows_in(rows):
                g = swapped(0, i, rows) * vec(1, 0)
                DY[i, rows, :] = (MID[1, i, rows, :] + norm_pull(H[1, i, rows, :].astype(F32), g)).astype(BF16)

            by_rows(rows_in)

            @pl.when(i == own_i)
            def _():
                send_result(2, 1, DY.at[i])

        for n in range(4):
            j, half = (y if n < 2 else 1 - y), n % 2
            cols = slice(half * 512, half * 512 + 512)
            dg = nt(DY[i], WD[l, j, cols, :])
            dz = (GP[l, i, :, n * 512 : n * 512 + 512].astype(F32) * dg).astype(BF16)
            term = nt(dz, WU[l, j, :, cols])
            gather(n, term)

        x_copy(1, i).wait_send()
        SND[1, i] = gathered()
        x_copy(1, i).start()

    def dr_copy(k, b):
        rows = pl.ds(pl.multiple_of(b * R, R), R)
        return pltpu.make_async_remote_copy(
            BIG.at[:, rows, :], DR.at[k], dr_snd.at[k], dr_rcv.at[k], device_id=sib, device_id_type=MESH)

    def attend_back(l, i):
        b = blk_of(i)
        pairs = Q.shape[3] // 128
        place = RCV.at[2 + i]

        def back_rows(k):
            return place[(k % 2) * 128 : (k % 2) * 128 + 128, 512 + (k // 2) * 256 : 768 + (k // 2) * 256]

        deltas = []
        for k in range(pairs):
            rows = slice(k * 128, k * 128 + 128)
            prod = back_rows(k).astype(F32) * OT[l, i, rows, :].astype(F32)
            deltas.append(jnp.sum(prod[0:64], axis=0, keepdims=True))
            deltas.append(jnp.sum(prod[64:128], axis=0, keepdims=True))
            OACC[2 * k] = jnp.zeros(OACC.shape[1:], F32)
            OACC[2 * k + 1] = jnp.zeros(OACC.shape[1:], F32)

        def turn(j, c):
            rows = pl.ds(pl.multiple_of(j * R, R), R)
            mask = MSK[pl.ds(pl.multiple_of((i * 2 + j) * R, R), R), :].astype(F32)
            for k in range(pairs):
                lanes = slice(k * 128, k * 128 + 128)
                qs = split_pair(Q[l, i, :, lanes], 1)
                dots = split_pair(back_rows(k), 0)
                keys = KV[l, 0, rows, lanes]
                values = KV[l, 1, rows, lanes]
                for e in range(2):
                    h = 2 * k + e
                    p = jnp.exp(nt(keys, qs[e]) + mask - LSE[l, i, h])
                    dp = nn(values, dots[e])
                    PB[h] = (p * (dp - deltas[h])).astype(BF16)
                    PB[2 * pairs + h] = p.astype(BF16)
            for k in range(pairs):
                lanes = slice(k * 128, k * 128 + 128)
                half = slice((k % 2) * 128, (k % 2) * 128 + 128)
                qs = split_pair(Q[l, i, :, lanes], 1)
                dos = split_pair(place[:, lanes], 1)
                h = 2 * k
                BIG[k // 2, rows, half] += nn(PB[h], qs[0]) + nn(PB[h + 1], qs[1])
                BIG[2 + k // 2, rows, half] += nn(PB[2 * pairs + h], dos[0]) + nn(PB[2 * pairs + h + 1], dos[1])
            for k in range(pairs):
                keys = jnp.transpose(KV[l, 0, rows, k * 128 : k * 128 + 128])
                for e in range(2):
                    OACC[2 * k + e] += nn(keys[e * 64 : e * 64 + 64], PB[2 * k + e])
            return c

        lax.fori_loop(0, b + 1, turn, 0)
        for k in range(pairs):
            dq = jnp.concatenate([OACC[2 * k], OACC[2 * k + 1]], axis=0) * HEAD_DIM ** -0.5
            DQ[k // 2, :, (k % 2) * 128 : (k % 2) * 128 + 128] = jnp.transpose(dq).astype(BF16)

    def backward_attention(l, i):
        b = blk_of(i)
        x_copy(1, i).wait_recv()

        def rows_mid(rows):
            g = swapped(1, i, rows) * vec(l, 2)
            dmid = DY[i, rows, :].astype(F32) + norm_pull(MID[l, i, rows, :], g)
            MID[l, i, rows, :] = dmid
            AB[rows, :] = dmid.astype(BF16)

        by_rows(rows_mid)
        for j in range(2):
            RCV[2 + i, :, 512 + j * 256 : 768 + j * 256] = nt(WO[l, j], AB[...]).astype(BF16)
            RCV[2 + i, :, j * 256 : j * 256 + 256] = nt(AB[...], WO[l, j]).astype(BF16)

        @pl.when(i == 1)
        def _():
            @pl.when(l == 0)
            def _():
                @pl.when(s == 0)
                def _():
                    dr_copy(0, 1).wait_send()
                    dr_copy(1, 2).wait_send()

                @pl.when(s == 1)
                def _():
                    dr_copy(0, 0).wait_send()

            def clear(r, c):
                rows = pl.ds(pl.multiple_of(r * R, R), R)
                BIG[:, rows, :] = jnp.zeros((4, R, 256), F32)
                return c

            lax.fori_loop(0, 4, clear, 0)

        attend_back(l, i)
        own = pl.ds(pl.multiple_of(b * R, R), R)

        @pl.when((s == 0) & (i == 1))
        def _():
            dr_copy(0, 1).start()
            dr_copy(1, 2).start()

        @pl.when(b != 3)
        def _():
            def add(k):
                dr_copy(k, b).wait_recv()
                for c in range(4):
                    BIG[c, own, :] += DR[k, c]

            @pl.when(s == 1)
            def _():
                add(i)

            @pl.when((s == 1) & (i == 0))
            def _():
                dr_copy(0, 0).start()

            @pl.when(s == 0)
            def _():
                add(0)

        for j in range(2):
            DQ[j, :, 256:512] = BIG[j, own, :].astype(BF16)
            DQ[j, :, 512:768] = BIG[2 + j, own, :].astype(BF16)

        def rows_norm(rows):
            xhat, _ = normalize(H[l, i, rows, :].astype(F32))
            AB[rows, :] = (xhat * vec(l, 0) + vec(l, 1)).astype(BF16)

        by_rows(rows_norm)
        ups = [SP[l, j, 24:32, 0:768].astype(BF16) for j in range(2)]
        du = (adapter_scale * (nt(ups[0], DQ[0]) + nt(ups[1], DQ[1]))).astype(BF16)
        GA[l] += nn(du, AB[...])
        top = lax.broadcasted_iota(jnp.int32, (8, 256), 0) < 4
        for j in range(2):
            gq = nn(U[l, i], DQ[j, :, 0:256])
            gv = nn(U[l, i], DQ[j, :, 512:768])
            GB[l, j] += adapter_scale * jnp.where(top, gq, gv)

        x_copy(0, i).wait_send()
        SND[0, i] = (
            nt(DQ[0], WQ[l, 0]) + nt(DQ[1], WQ[l, 1]) + tn(du, SP[l, 0, 8:16, :].astype(BF16))
        ).astype(BF16)

        @pl.when(l == 1)
        def _():
            x_copy(0, i).start()

        @pl.when((l == 0) & (i != own_i))
        def _():
            for c in range(4):
                last_copy(c, i).start()

    def core_copies(l):
        return (
            pltpu.make_async_remote_copy(
                GA.at[l], GCA, gc_s.at[0], gc_r.at[0], device_id=sib, device_id_type=MESH),
            pltpu.make_async_remote_copy(
                GB.at[l], GCB, gc_s.at[1], gc_r.at[1], device_id=sib, device_id_type=MESH),
        )

    def plane_copies(l):
        out = []
        for k, (dx, dy) in enumerate(((1, 0), (0, 1), (1, 1))):
            x2 = 1 - x if dx else x
            y2 = 1 - y if dy else y
            to = (s, d, y2 * 2 + x2)
            out.append(pltpu.make_async_remote_copy(
                GA.at[l], GXA.at[k], gx_s.at[k], gx_r.at[k], device_id=to, device_id_type=MESH))
        out.append(pltpu.make_async_remote_copy(
            GB.at[l, 1 - y], GXB, gx_s.at[3], gx_r.at[3], device_id=yp, device_id_type=MESH))
        return out

    def line_copies():
        out = []
        for k in range(1, dp_count):
            to = (s, lax.rem(d + k, dp_count), t)
            out.append(pltpu.make_async_remote_copy(
                GZA.at[d], GZA.at[d], gz_s.at[0, k - 1], gz_r.at[0, k - 1], device_id=to, device_id_type=MESH))
            out.append(pltpu.make_async_remote_copy(
                GZB.at[d], GZB.at[d], gz_s.at[1, k - 1], gz_r.at[1, k - 1], device_id=to, device_id_type=MESH))
        return out

    def sum_core(l):
        @pl.when(s != l)
        def _():
            for c in core_copies(l):
                c.start()

    def sum_plane(l):
        @pl.when(s == l)
        def _():
            for c in core_copies(l):
                c.wait_recv()
            GA[l] += GCA[...]
            GB[l] += GCB[...]
            for c in plane_copies(l):
                c.start()

    def sum_line(l):
        @pl.when(s == l)
        def _():
            for c in plane_copies(l):
                c.wait_recv()
            GZA[d] = (GA[l] + GXA[0]) + (GXA[1] + GXA[2])
            GZB[d] = GB[l, y] + GXB[...]
            for c in line_copies():
                c.start()

    def sum_end(l):
        @pl.when(s == l)
        def _():
            for c in line_copies():
                c.wait_recv()
            total_a, total_b = GZA[0], GZB[0]
            for k in range(1, dp_count):
                total_a, total_b = total_a + GZA[k], total_b + GZB[k]
            out_a[0, 0] = total_a[0:4]
            out_a[0, 1] = total_a[4:8]
            out_b[0, 0] = total_b[0:4]
            out_b[0, 1] = total_b[4:8]

    def bwd_layer(back, carry):
        l = 1 - back

        def f_turn(k, c):
            @pl.when((l == 0) & (k == 1))
            def _():
                sum_plane(1)

            backward_ff(l, 1 - k)
            return c

        def a_turn(k, c):
            @pl.when((l == 0) & (k == 0))
            def _():
                sum_line(1)

            @pl.when((l == 0) & (k == 1))
            def _():
                sum_end(1)

            backward_attention(l, 1 - k)
            return c

        lax.fori_loop(0, 2, f_turn, 0)

        @pl.when(l == 1)
        def _():
            finish_forward()

        lax.fori_loop(0, 2, a_turn, 0)
        sum_core(l)
        return carry

    lax.fori_loop(0, 2, bwd_layer, 0)
    sum_plane(0)

    for c in range(4):
        last_copy(c, own_i).wait_recv()
        rows = slice(c * 64, c * 64 + 64)
        g = swapped(0, own_i, rows) * vec(0, 0)
        AB[rows, :] = (MID[0, own_i, rows, :] + norm_pull(H[0, own_i, rows, :].astype(F32), g)).astype(BF16)
        send_result(3, 0, AB, rows)
    sum_line(0)

    for c in range(4):
        last_copy(c, 1 - own_i).wait_send()
    for i in range(2):
        x_copy(1, i).wait_send()
    x_copy(2, 1 - own_i).wait_send()
    def sent(ref, sem):
        pltpu.make_async_remote_copy(ref, ref, sem, sem, device_id=sib, device_id_type=MESH).wait_send()

    for p in range(5):
        sent(pieces[p][1].at[s, y] if p else SP.at[s, y], ws_s.at[p])
        for c in range(pieces[p][2] if p else 1):
            k = base[p] + c
            ref = block(p, s, y, chunk(p, c, 0)) if p else SP.at[s, y]
            sent(ref, wy_s.at[k])
            sent(ref, wa_s.at[k])
            if p:
                sent(ref, wz_s.at[k])
                sent(ref, wb_s.at[k])
    rows_done(tok, H.at[0], 0)
    rows_done(cot, DY, 1)
    for l in range(2):
        kv_copy(l, 0).wait_send()

        @pl.when(s == 1)
        def _():
            kv_copy(l, 1).wait_send()

    @pl.when(s == 0)
    def _():
        dr_copy(0, 1).wait_send()
        dr_copy(1, 2).wait_send()

    @pl.when(s == 1)
    def _():
        dr_copy(0, 0).wait_send()

    @pl.when(s == 0)
    def _():
        for c in core_copies(1) + tuple(plane_copies(0)) + tuple(line_copies()):
            c.wait_send()

    @pl.when(s == 1)
    def _():
        for c in core_copies(0) + tuple(plane_copies(1)) + tuple(line_copies()):
            c.wait_send()

    send_result_done(0, 0, H.at[1, 0])
    send_result_done(1, 1, H.at[1, 0])
    send_result_done(2, 1, H.at[1, 0])
    send_result_done(3, 0, H.at[1, 0])
    for o, ref in ((0, act), (1, ig)):
        for m in range(2):
            pltpu.make_async_copy(tok.at[0], ref.at[m], out_rcv.at[o, m]).wait()
    sum_end(0)


def per_pair(
    tokens, cotangent, buckets, lengths, norm_gain_pairs, norm_bias_pairs, query_key_value_weight,
    query_value_bias, output_weight, upward_weight, upward_bias, down_weight, output_bias,
    adapter_down, adapter_upper,
):
    weight_qkv = query_key_value_weight[0].transpose(1, 0, 2)
    dp_count = lax.axis_size("dp")
    anywhere = pl.BlockSpec(memory_space=pl.ANY)
    scalars = pl.BlockSpec(memory_space=pltpu.SMEM)
    vmem = pl.BlockSpec(memory_space=pltpu.VMEM)
    dma = pltpu.SemaphoreType.DMA
    act, ig, total_a, total_b = pl.pallas_call(
        partial(fused_kernel, dp_count),
        out_shape=(
            jax.ShapeDtypeStruct((2, R, D), BF16),
            jax.ShapeDtypeStruct((2, R, D), BF16),
            jax.ShapeDtypeStruct((1, 2, 4, D), F32),
            jax.ShapeDtypeStruct((1, 2, 4, 256), F32),
        ),
        in_specs=[anywhere, anywhere, scalars, scalars, vmem, vmem, anywhere, vmem, anywhere, anywhere, vmem,
                  anywhere, vmem, vmem, vmem],
        out_specs=(anywhere, anywhere, vmem, vmem),
        scratch_shapes=[
            pltpu.VMEM((2, 2, 32, D), F32),
            pltpu.VMEM((2, 2, D, 768), BF16),
            pltpu.VMEM((2, 2, 256, D), BF16),
            pltpu.VMEM((2, 2, D, 1024), BF16),
            pltpu.VMEM((2, 2, 1024, D), BF16),
            pltpu.VMEM((2, 2, R, D), BF16),
            pltpu.VMEM((2, R, D), BF16),
            pltpu.VMEM((2, 2, R, D), F32),
            pltpu.VMEM((2, 2, R, 2048), BF16),
            pltpu.VMEM((2, 2, R, 512), BF16),
            pltpu.VMEM((2, 2, 4 * R, 512), BF16),
            pltpu.VMEM((2, 2, 512, R), BF16),
            pltpu.VMEM((2, 2, 8, 1, R), F32),
            pltpu.VMEM((3, 2, R, D), BF16),
            pltpu.VMEM((5, R, D), BF16),
            pltpu.VMEM((4, 4 * R, R), F32),
            pltpu.VMEM((6 * R, R), BF16),
            pltpu.VMEM((2, 4, R, R), F32),
            pltpu.VMEM((2, R, 768), BF16),
            pltpu.VMEM((R, D), BF16),
            pltpu.VMEM((2, 2, 8, R), BF16),
            pltpu.VMEM((8, 64, R), F32),
            pltpu.VMEM((16, R, R), BF16),
            pltpu.VMEM((2, 8, D), F32),
            pltpu.VMEM((2, 2, 8, 256), F32),
            pltpu.VMEM((8, D), F32),
            pltpu.VMEM((2, 8, 256), F32),
            pltpu.VMEM((3, 8, D), F32),
            pltpu.VMEM((8, 256), F32),
            pltpu.VMEM((dp_count, 8, D), F32),
            pltpu.VMEM((dp_count, 8, 256), F32),
            dma((2, 2)),
            dma((2,)),
            dma((2,)),
            dma((5,)),
            dma((5,)),
            dma((5,)),
            dma((8,)),
            dma((8,)),
            dma((7,)),
            dma((7,)),
            dma((8,)),
            dma((8,)),
            dma((7,)),
            dma((7,)),
            dma((2, 2)),
            dma((2, 2)),
            dma((3, 2)),
            dma((3, 2)),
            dma((4,)),
            dma((4,)),
            dma((2,)),
            dma((2,)),
            dma((2, 2)),
            dma((4,)),
            dma((2,)),
            dma((2,)),
            dma((4,)),
            dma((4,)),
            dma((2, dp_count - 1)),
            dma((2, dp_count - 1)),
        ],
        compiler_params=pltpu.CompilerParams(
            collective_id=0, has_side_effects=True, vmem_limit_bytes=127 * 2**19
        ),
        name="two_layers",
    )(
        tokens, cotangent, buckets, lengths, norm_gain_pairs, norm_bias_pairs, weight_qkv, query_value_bias,
        output_weight, upward_weight, upward_bias, down_weight, output_bias, adapter_down, adapter_upper,
    )
    return act[None], ig[None], total_a, total_b


def solution(mesh):
    in_specs = (
        P("dp", "tensor", None),
        P("dp", "tensor", None),
        P("dp"),
        P("dp", None),
        P("section", None, None),
        P("section", None, None),
        P("section", None, None, "tensor"),
        P("section", None, "tensor"),
        P("section", "tensor", None),
        P("section", None, "tensor"),
        P("section", "tensor"),
        P("section", "tensor", None),
        P("section", None, None),
        P("section", None, None, None),
        P("section", None, None, "tensor"),
    )
    out_specs = (
        P("section", "dp", "tensor", None),
        P("section", "dp", "tensor", None),
        P("section", None, None, None),
        P("section", None, None, "tensor"),
    )
    pairs = mesh.shape["section"] == 2 and mesh.shape["tensor"] == 4 and mesh.shape["dp"] % 2 == 0
    return jax.shard_map(
        per_pair if pairs else per_device, mesh=mesh, in_specs=in_specs, out_specs=out_specs, check_vma=False
    )
```

```python
from functools import partial

import jax
import jax.numpy as jnp
from jax import lax
from jax.experimental import pallas as pl
from jax.experimental.pallas import tpu as pltpu
from jax.sharding import PartitionSpec as P

HEAD_DIM = 64


adapter_scale = 8.0
norm_eps = 1e-05
masked_score = -1000000000.0
highest_precision = lax.Precision.HIGHEST


def from_behind(block, axis, distance):
    devices = range(lax.axis_size(axis))
    route = [(i - distance, i) for i in devices if i - distance in devices]
    return lax.ppermute(block, axis, route)


def layer_norm(values, gain_rows, shifts):
    center = jnp.mean(values, axis=-1, keepdims=True)
    centered = values - center
    spread = jnp.mean(centered * centered, axis=-1, keepdims=True)
    return centered * lax.rsqrt(spread + norm_eps) * gain_rows + shifts


def row_layout(bucket, lengths_row, row_count):
    item_span = jnp.right_shift(jnp.int32(row_count), 3 - bucket)
    positions = jnp.arange(row_count, dtype=jnp.int32)
    item_index = positions // item_span
    within = positions - item_index * item_span
    chosen = (
        item_index[:, None] == jnp.arange(lengths_row.shape[0], dtype=jnp.int32)[None, :]
    ).astype(jnp.int32)
    length = jnp.sum(chosen * lengths_row[None, :], axis=1)
    return (item_index, within < length)


def allowed_keys(item_index, is_valid):
    positions = jnp.arange(item_index.shape[0], dtype=jnp.int32)
    same_item = item_index[:, None] == item_index[None, :]
    causal = positions[None, :] <= positions[:, None]
    key_seen = is_valid[None, :] | (positions[None, :] == positions[:, None])
    return same_item & causal & key_seen


def take_slot(buffer, slot_index):
    return lax.dynamic_index_in_dim(buffer, slot_index, 0, keepdims=False)


def put_slot(buffer, slot_index, is_live, update):
    previous = take_slot(buffer, slot_index)
    return lax.dynamic_update_index_in_dim(
        buffer, jnp.where(is_live, update, previous), slot_index, 0
    )


def per_device(
    tokens,
    cotangent,
    buckets,
    lengths,
    norm_gain_pairs,
    norm_bias_pairs,
    query_key_value_weight,
    query_value_bias,
    output_weight,
    upward_weight,
    upward_bias,
    down_weight,
    output_bias,
    adapter_down,
    adapter_upper,
):
    section_index = lax.axis_index("section")
    tensor_count = lax.axis_size("tensor")
    micro_count, own_rows, model_width = tokens.shape
    row_count = own_rows * tensor_count
    own_start = lax.axis_index("tensor") * own_rows
    gain_sets = norm_gain_pairs[0].astype(jnp.float32)
    shift_sets = norm_bias_pairs[0].astype(jnp.float32)
    weight_qkv = query_key_value_weight[0]
    bias_query_value = query_value_bias[0].astype(jnp.float32)
    weight_out = output_weight[0]
    weight_up = upward_weight[0]
    bias_up = upward_bias[0].astype(jnp.float32)
    weight_down = down_weight[0]
    biases = output_bias[0].astype(jnp.float32)
    down_factor = adapter_down[0]
    upper_factor = adapter_upper[0]
    factor_wide = down_factor.astype(jnp.float32)
    local_width = weight_qkv.shape[2]
    local_heads = local_width // HEAD_DIM
    score_scale = HEAD_DIM ** (-0.5)

    def widen(values):
        return lax.all_gather(values, "tensor", axis=0, tiled=True)

    def widen_back(values):
        return lax.all_gather(values, "tensor", axis=0, tiled=True)

    def settle(source, weight):

        def row_term(first_row, row_span):
            return jnp.dot(source, weight, preferred_element_type=jnp.float32)

        return lax.psum_scatter(
            row_term(jnp.int32(0), lax.axis_size("tensor") * own_rows).astype(jnp.bfloat16),
            "tensor",
            scatter_dimension=0,
            tiled=True,
        ).astype(jnp.float32)

    def settle_back(row_term):
        return lax.psum_scatter(
            row_term(jnp.int32(0), lax.axis_size("tensor") * own_rows).astype(jnp.bfloat16),
            "tensor",
            scatter_dimension=0,
            tiled=True,
        ).astype(jnp.float32)

    def layout_of(slot_index):
        item_index, is_valid = row_layout(
            take_slot(buckets, slot_index), take_slot(lengths, slot_index), row_count
        )
        own_valid = lax.dynamic_slice_in_dim(is_valid, own_start, own_rows, 0)
        return (allowed_keys(item_index, is_valid), own_valid)

    def attend(normed, allowed):
        reduced_query = jnp.dot(
            normed, down_factor[0].T, preferred_element_type=jnp.float32
        ).astype(jnp.bfloat16)
        reduced_value = jnp.dot(
            normed, down_factor[1].T, preferred_element_type=jnp.float32
        ).astype(jnp.bfloat16)
        blended_rows = jnp.einsum(
            "rd,dcn->rcn", normed, weight_qkv, preferred_element_type=jnp.float32
        )
        query_matrix_rows = (
            blended_rows[:, 0]
            + bias_query_value[0]
            + adapter_scale
            * jnp.dot(reduced_query, upper_factor[0], preferred_element_type=jnp.float32)
        )
        value_matrix_rows = (
            blended_rows[:, 2]
            + bias_query_value[1]
            + adapter_scale
            * jnp.dot(reduced_value, upper_factor[1], preferred_element_type=jnp.float32)
        )
        packed = jnp.stack(
            [query_matrix_rows, blended_rows[:, 1], value_matrix_rows], axis=1
        ).astype(jnp.bfloat16)
        head_split = packed.reshape(row_count, 3, local_heads, HEAD_DIM)
        scores = (
            jnp.einsum(
                "qhe,khe->hqk",
                head_split[:, 0],
                head_split[:, 1],
                preferred_element_type=jnp.float32,
            )
            * score_scale
        )
        scores = jnp.where(allowed[None], scores, masked_score)
        top_score = jnp.max(scores, axis=-1, keepdims=True)
        exponent = jnp.exp(scores - top_score)
        attn_probs = exponent / jnp.sum(exponent, axis=-1, keepdims=True)
        return (reduced_query, reduced_value, head_split, attn_probs)

    def forward(hidden, allowed):
        normed = widen(layer_norm(hidden, gain_sets[0], shift_sets[0]).astype(jnp.bfloat16))
        reduced_query, reduced_value, head_split, attn_probs = attend(normed, allowed)
        probs_low = attn_probs.astype(jnp.bfloat16)
        mixed_heads = jnp.einsum(
            "hqk,khe->qhe", probs_low, head_split[:, 2], preferred_element_type=jnp.float32
        )
        attended = mixed_heads.reshape(row_count, local_width).astype(jnp.bfloat16)
        middle = hidden + (settle(attended, weight_out) + biases[0])
        normed_two = widen(layer_norm(middle, gain_sets[1], shift_sets[1]).astype(jnp.bfloat16))
        hidden_pre = jnp.dot(normed_two, weight_up, preferred_element_type=jnp.float32) + bias_up
        activated = jax.nn.gelu(hidden_pre, approximate=True).astype(jnp.bfloat16)
        output = middle + (settle(activated, weight_down) + biases[1])
        return (output, normed, middle, normed_two)

    def backward(hidden, grad_out, allowed, normed, middle, normed_two):
        reduced_query, reduced_value, head_split, attn_probs = attend(normed, allowed)
        probs_low = attn_probs.astype(jnp.bfloat16)
        hidden_pre = jnp.dot(normed_two, weight_up, preferred_element_type=jnp.float32) + bias_up
        grad_branch = widen_back(grad_out.astype(jnp.bfloat16))
        grad_act = jnp.einsum(
            "rd,fd->rf", grad_branch, weight_down, preferred_element_type=jnp.float32
        )
        gelu_pull = jax.vjp(partial(jax.nn.gelu, approximate=True), hidden_pre)[1]
        grad_pre = gelu_pull(grad_act)[0].astype(jnp.bfloat16)

        def mlp_term(first_row, row_span):
            return jnp.einsum("rf,df->rd", grad_pre, weight_up, preferred_element_type=jnp.float32)

        grad_norm_two = settle_back(mlp_term)
        second_pull = jax.vjp(
            partial(layer_norm, gain_rows=gain_sets[1], shifts=shift_sets[1]), middle
        )[1]
        grad_middle = grad_out + second_pull(grad_norm_two)[0]
        grad_attn = widen_back(grad_middle.astype(jnp.bfloat16))
        grad_heads = jnp.einsum(
            "rd,nd->rn", grad_attn, weight_out, preferred_element_type=jnp.float32
        )
        grad_heads = grad_heads.astype(jnp.bfloat16).reshape(row_count, local_heads, HEAD_DIM)
        grad_probs = jnp.einsum(
            "qhe,khe->hqk", grad_heads, head_split[:, 2], preferred_element_type=jnp.float32
        )
        grad_scores = attn_probs * (
            grad_probs - jnp.sum(attn_probs * grad_probs, axis=-1, keepdims=True)
        )
        grad_scores = grad_scores.astype(jnp.bfloat16)
        grad_query = (
            jnp.einsum(
                "hqk,khe->qhe", grad_scores, head_split[:, 1], preferred_element_type=jnp.float32
            )
            * score_scale
        )
        grad_key = (
            jnp.einsum(
                "hqk,qhe->khe", grad_scores, head_split[:, 0], preferred_element_type=jnp.float32
            )
            * score_scale
        )
        grad_value = jnp.einsum(
            "hqk,qhe->khe", probs_low, grad_heads, preferred_element_type=jnp.float32
        )
        grad_packed = (
            jnp.stack([grad_query, grad_key, grad_value], axis=1)
            .reshape(row_count, 3, local_width)
            .astype(jnp.bfloat16)
        )
        grad_pair = jnp.stack([grad_packed[:, 0], grad_packed[:, 2]])
        gradient_reduced = adapter_scale * jnp.einsum(
            "jrn,jkn->jrk", grad_pair, upper_factor, preferred_element_type=jnp.float32
        )

        def attn_term(first_row, row_span):
            dense_part = jnp.einsum(
                "rcn,dcn->rd", grad_packed, weight_qkv, preferred_element_type=jnp.float32
            )
            return dense_part + jnp.einsum(
                "jrk,jkd->rd", gradient_reduced, factor_wide, precision=highest_precision
            )

        grad_normed = settle_back(attn_term)
        first_pull = jax.vjp(
            partial(layer_norm, gain_rows=gain_sets[0], shifts=shift_sets[0]), hidden
        )[1]
        grad_hidden = grad_middle + first_pull(grad_normed)[0]
        grad_factor_a = jnp.einsum(
            "jrk,rd->jkd", gradient_reduced, normed.astype(jnp.float32), precision=highest_precision
        )
        gradient_upper_factor = adapter_scale * jnp.stack(
            [
                jnp.einsum(
                    "rk,rn->kn",
                    reduced_query,
                    grad_packed[:, 0],
                    preferred_element_type=jnp.float32,
                ),
                jnp.einsum(
                    "rk,rn->kn",
                    reduced_value,
                    grad_packed[:, 2],
                    preferred_element_type=jnp.float32,
                ),
            ]
        )
        return (grad_hidden, grad_factor_a, gradient_upper_factor)

    zero_rows = jnp.zeros((micro_count, own_rows, model_width), jnp.bfloat16)
    saved_start = ()

    def record(buffers, slot_index, is_live, layer_input, results):
        kept_in, outputs, saved = buffers
        output, normed, middle, normed_two = results
        low_output = output.astype(jnp.bfloat16)
        kept_in = put_slot(kept_in, slot_index, is_live, layer_input)
        outputs = put_slot(outputs, slot_index, is_live, low_output)
        return ((kept_in, outputs, saved), low_output)

    buffers = (zero_rows, zero_rows, saved_start)

    def run_phase(buffers, sources, phase_section):

        def phase_turn(slot_index, buffers):
            allowed, own_valid = layout_of(slot_index)
            layer_input = take_slot(sources, slot_index)
            results = forward(layer_input.astype(jnp.float32), allowed)
            return record(
                buffers, slot_index, section_index == phase_section, layer_input, results
            )[0]

        return lax.fori_loop(0, micro_count, phase_turn, buffers)

    buffers = run_phase(buffers, tokens, 0)
    received = from_behind(buffers[1], "section", 1)
    buffers = run_phase(buffers, received, 1)
    kept_in, outputs, saved = buffers

    def back_step(slot_index, grad_out, allowed):
        hidden = take_slot(kept_in, slot_index).astype(jnp.float32)
        output, normed, middle, normed_two = forward(hidden, allowed)
        return backward(hidden, grad_out, allowed, normed, middle, normed_two)

    def top_grad(slot_index, own_valid):
        return take_slot(cotangent, slot_index).astype(jnp.float32) * own_valid[:, None].astype(
            jnp.float32
        )

    zero_a = jnp.zeros(down_factor.shape, jnp.float32)
    zero_b = jnp.zeros(upper_factor.shape, jnp.float32)

    def run_back(loop_state, sources, phase_section):

        def phase_turn(slot_index, loop_state):
            grads_in, sum_a, sum_b = loop_state
            allowed, own_valid = layout_of(slot_index)
            if phase_section == 1:
                grad_out = top_grad(slot_index, own_valid)
            else:
                grad_out = take_slot(sources, slot_index).astype(jnp.float32)
            is_live = section_index == phase_section
            grad_hidden, grad_a, grad_b = back_step(slot_index, grad_out, allowed)
            grads_in = put_slot(grads_in, slot_index, is_live, grad_hidden.astype(jnp.bfloat16))
            sum_a = sum_a + jnp.where(is_live, grad_a, 0.0)
            sum_b = sum_b + jnp.where(is_live, grad_b, 0.0)
            return (grads_in, sum_a, sum_b)

        return lax.fori_loop(0, micro_count, phase_turn, loop_state)

    loop_state = run_back((zero_rows, zero_a, zero_b), zero_rows, 1)
    received_grads = from_behind(loop_state[0], "section", -1)
    grads_in, sum_a, sum_b = run_back(loop_state, received_grads, 0)
    total_a = lax.psum(sum_a, ("dp", "tensor"))
    total_b = lax.psum(sum_b, "dp")
    return (outputs[None], grads_in[None], total_a[None], total_b[None])


R = 256
D = 1024
NEG = -1e30
F32 = jnp.float32
BF16 = jnp.bfloat16
MESH = pl.DeviceIdType.MESH
CHUNK = 128


def nn(a, b):
    return lax.dot_general(a, b, (((1,), (0,)), ((), ())), preferred_element_type=F32)


def nt(a, b):
    return lax.dot_general(a, b, (((1,), (1,)), ((), ())), preferred_element_type=F32)


def tn(a, b):
    return lax.dot_general(a, b, (((0,), (0,)), ((), ())), preferred_element_type=F32)


def normalize(v):
    centered = v - jnp.mean(v, axis=-1, keepdims=True)
    rs = lax.rsqrt(jnp.mean(centered * centered, axis=-1, keepdims=True) + norm_eps)
    return centered * rs, rs


def norm_pull(v, g):
    xhat, rs = normalize(v)
    return rs * (
        g
        - jnp.mean(g, axis=-1, keepdims=True)
        - xhat * jnp.mean(g * xhat, axis=-1, keepdims=True)
    )


def gelu_pair(z):
    c = 0.7978845608028654
    z2 = z * z
    t = jnp.tanh(c * (z + 0.044715 * (z2 * z)))
    half = 0.5 * (1.0 + t)
    slope = half + (0.5 * c) * z * (1.0 - t * t) * (1.0 + (3.0 * 0.044715) * z2)
    return z * half, slope


def fused_kernel(
    dp_count,
    tok, cot, buckets, lengths, gain_in, shift_in, wq_in, bqv_in, wo_in, wu_in, bu_in, wd_in, bo_in, ad_in, au_in,
    act, ig, out_a, out_b,
    SP, WQ, WO, WU, WD, H, DY, MID, GP, Q, KV, OT, LSE, SND, RCV, BIG, MSK, DR, DQ, AB, U, OACC, PB,
    GA, GB, GCA, GCB, GXA, GXB, GZA, GZB,
    tok_sem, tok_ys, tok_xs, wl, ws_r, ws_s, wy_r, wy_s, wz_r, wz_s, wa_r, wa_s, wb_r, wb_s,
    kv_rcv, kv_snd, x_rcv, x_snd, last_rcv, last_snd, dr_rcv, dr_snd, out_rcv, out_snd, gc_r, gc_s, gx_r, gx_s, gz_r, gz_s,
):
    s = lax.axis_index("section")
    d = lax.axis_index("dp")
    t = lax.axis_index("tensor")
    x = lax.rem(t, 2)
    y = lax.div(t, 2)
    sib = (1 - s, d, t)
    xp = (s, d, y * 2 + 1 - x)
    yp = (s, d, (1 - y) * 2 + x)
    z_half = lax.rem(d, 2)
    zp = (s, d + 1 - 2 * z_half, t)
    flip = s + x - 2 * s * x
    own_i = flip

    def blk_of(i):
        return 2 * i + (s + i - 2 * s * i)

    bar = pltpu.get_barrier_semaphore()
    for ds_ in range(2):
        for dx in range(2):
            for dy in range(2):
                if ds_ or dx or dy:
                    s2 = 1 - s if ds_ else s
                    x2 = 1 - x if dx else x
                    y2 = 1 - y if dy else y
                    pl.semaphore_signal(bar, 1, device_id=(s2, d, y2 * 2 + x2), device_id_type=MESH)
    for k in range(1, dp_count):
        pl.semaphore_signal(bar, 1, device_id=(s, lax.rem(d + k, dp_count), t), device_id_type=MESH)
    pl.semaphore_wait(bar, 7 + dp_count - 1)

    def row_copies(src, dst, w):
        def local():
            return pltpu.make_async_copy(src.at[y], dst.at[y], tok_sem.at[w, y])

        def to_y():
            return pltpu.make_async_remote_copy(
                src.at[1 - y], dst.at[y], tok_ys.at[w], tok_sem.at[w, y], device_id=yp, device_id_type=MESH)

        def first_x():
            return pltpu.make_async_remote_copy(
                src.at[y], dst.at[y], tok_xs.at[w], tok_sem.at[w, y], device_id=xp, device_id_type=MESH)

        def then_x():
            return pltpu.make_async_remote_copy(
                dst.at[own_i], dst.at[own_i], tok_xs.at[w], tok_sem.at[w, own_i],
                device_id=xp, device_id_type=MESH)

        return local, to_y, first_x, then_x

    def rows_first(src, dst, w):
        local, _, first_x, _ = row_copies(src, dst, w)

        @pl.when(y == own_i)
        def _():
            first_x().start()
            local().start()

    def rows_swap(src, dst, w):
        @pl.when(y == own_i)
        def _():
            row_copies(src, dst, w)[1]().start()

    def rows_relay(src, dst, w):
        pltpu.make_async_copy(src.at[0], dst.at[own_i], tok_sem.at[w, own_i]).wait()

        @pl.when(y != own_i)
        def _():
            row_copies(src, dst, w)[3]().start()

    def rows_rest(src, dst, w):
        pltpu.make_async_copy(src.at[0], dst.at[1 - own_i], tok_sem.at[w, 1 - own_i]).wait()

    def rows_done(src, dst, w):
        _, to_y, first_x, _ = row_copies(src, dst, w)
        if w == 0:
            first_x().wait_send()

        @pl.when(y == own_i)
        def _():
            to_y().wait_send()

    pieces = (None, (wq_in, WQ, 4), (wo_in, WO, 1), (wu_in, WU, 4), (wd_in, WD, 4))
    base = (13, 0, 4, 5, 9)

    def relayer(l, c):
        return 1 - l if c % 2 else l

    def sources(p, rows):
        src, dst, _ = pieces[p]
        if p == 1:
            return [
                (src.at[c, rows, :], dst.at[s, y, rows, c * 256 : c * 256 + 256]) for c in range(3)
            ]
        return [(src.at[0, rows, :], dst.at[s, y, rows, :])]

    def chunk(p, c, half):
        dst, parts = pieces[p][1], pieces[p][2]
        size = dst.shape[2] // (2 * parts)
        return pl.ds(pl.multiple_of((half * parts + c) * size, size), size)

    def block(p, l, j, rows):
        return pieces[p][1].at[l, j, rows, :]

    def own_start(p):
        everything = pl.ds(0, pieces[p][1].shape[2])
        for src, dst in sources(p, everything):
            pltpu.make_async_copy(src, dst, wl.at[p]).start()
            pltpu.make_async_remote_copy(
                src, dst, ws_s.at[p], ws_r.at[p], device_id=sib, device_id_type=MESH).start()

    def whole_by_y(l, p, c):
        return l == 0 and p == 4 and c >= 2

    def y_start(l, p):
        for c in range(pieces[p][2] if p else 1):
            k = base[p] + c

            @pl.when(s == relayer(l, c))
            def _():
                if p == 0:
                    ref = SP.at[l, y, 16:32, :]
                    pltpu.make_async_remote_copy(
                        ref, ref, wy_s.at[k], wy_r.at[k], device_id=yp, device_id_type=MESH).start()
                    return
                rows = chunk(p, c, z_half)
                mine = block(p, l, y, rows)
                for src, dst in [(mine, mine)] if c % 2 else sources(p, rows):
                    pltpu.make_async_remote_copy(
                        src, dst, wy_s.at[k], wy_r.at[k], device_id=yp, device_id_type=MESH).start()
                if whole_by_y(l, p, c):
                    rows = chunk(p, c, 1 - z_half)
                    mine = block(p, l, y, rows)
                    for src, dst in [(mine, mine)] if c % 2 else sources(p, rows):
                        pltpu.make_async_remote_copy(
                            src, dst, wz_s.at[k], wz_r.at[k], device_id=yp, device_id_type=MESH).start()

    def small_copy(to, snd, rcv):
        return pltpu.make_async_remote_copy(
            SP.at[s, y], SP.at[s, y], snd, rcv, device_id=to, device_id_type=MESH)

    def passed(l, p, c, half, to, snd, rcv):
        ref = SP.at[l, 1 - y, 16:32, :] if p == 0 else block(p, l, 1 - y, chunk(p, c, half))
        return pltpu.make_async_remote_copy(ref, ref, snd, rcv, device_id=to, device_id_type=MESH)

    def relay_y(l, p):
        for c in range(pieces[p][2] if p else 1):
            k = base[p] + c

            @pl.when(s == relayer(l, c))
            def _():
                passed(l, p, c, z_half, sib, wa_s.at[k], wy_r.at[k]).wait_recv()
                if p and not (p == 4 and c >= 2):
                    passed(l, p, c, z_half, zp, wz_s.at[k], wz_r.at[k]).start()

                if p == 4 and c >= 2:

                    @pl.when(l == 1)
                    def _():
                        passed(l, p, c, z_half, zp, wz_s.at[k], wz_r.at[k]).start()

                passed(l, p, c, z_half, sib, wa_s.at[k], wa_r.at[k]).start()

    def relay_z(l, p):
        for c in range(pieces[p][2]):
            k = base[p] + c

            @pl.when(s == relayer(l, c))
            def _():
                passed(l, p, c, 1 - z_half, zp, wz_s.at[k], wz_r.at[k]).wait_recv()
                passed(l, p, c, 1 - z_half, sib, wb_s.at[k], wb_r.at[k]).start()

    def own_wait(l, p):
        @pl.when(l == s)
        def _():
            if p:
                ref = pieces[p][1].at[s, y]
                pltpu.make_async_copy(ref, ref, wl.at[p]).wait()

        @pl.when(l != s)
        def _():
            ref = pieces[p][1].at[1 - s, y] if p else SP.at[1 - s, y]
            pltpu.make_async_copy(ref, ref, ws_r.at[p]).wait()

    def other_wait(l, p):
        for c in range(pieces[p][2] if p else 1):
            k = base[p] + c

            @pl.when(s != relayer(l, c))
            def _():
                if p == 0:
                    ref = SP.at[l, 1 - y, 16:32, :]
                    pltpu.make_async_copy(ref, ref, wa_r.at[13]).wait()
                else:
                    ref = block(p, l, 1 - y, chunk(p, c, 0))
                    pltpu.make_async_copy(ref, ref, wa_r.at[k]).wait()
                    pltpu.make_async_copy(ref, ref, wb_r.at[k]).wait()

    rows_swap(tok, H.at[0], 0)
    rows_first(tok, H.at[0], 0)
    own_start(1)
    SP[s, y] = jnp.zeros(SP.shape[2:], F32)
    for k, (ref, row) in enumerate(
        ((gain_in, 0), (shift_in, 0), (gain_in, 1), (shift_in, 1), (bo_in, 0), (bo_in, 1))
    ):
        SP[s, y, k : k + 1, :] = ref[0, row : row + 1, :].astype(F32)
    SP[s, y, 8:12, :] = ad_in[0, 0].astype(F32)
    SP[s, y, 12:16, :] = ad_in[0, 1].astype(F32)
    SP[s, y, 16:17, :] = bu_in[...].astype(F32)
    SP[s, y, 17:18, 0:256] = bqv_in[0, 0:1, :].astype(F32)
    SP[s, y, 17:18, 512:768] = bqv_in[0, 1:2, :].astype(F32)
    SP[s, y, 24:28, 0:256] = au_in[0, 0].astype(F32)
    SP[s, y, 28:32, 512:768] = au_in[0, 1].astype(F32)
    small_copy(sib, ws_s.at[0], ws_r.at[0]).start()
    y_start(0, 0)
    for p in range(2, 5):
        own_start(p)
    for l in range(2):
        for p in range(5):
            own_wait(l, p)
            if l or p:
                y_start(l, p)

    shift = 7 + buckets[y]
    span_mask = lax.shift_left(jnp.int32(1), shift) - 1

    def length_of(pos):
        item = lax.shift_right_logical(pos, jnp.broadcast_to(shift, pos.shape))
        got = jnp.zeros(pos.shape, jnp.int32)
        for k in range(lengths.shape[1]):
            got = jnp.where(item == k, lengths[y, k], got)
        return item, jnp.bitwise_and(pos, span_mask) < got

    def build_mask(i):
        b = blk_of(i)
        q_row = b * R + lax.broadcasted_iota(jnp.int32, (1, R), 1)
        q_item = lax.shift_right_logical(q_row, jnp.broadcast_to(shift, q_row.shape))

        def rows(r, carry):
            r0 = pl.multiple_of(r * CHUNK, CHUNK)
            k_row = r0 + lax.broadcasted_iota(jnp.int32, (CHUNK, 1), 0)
            k_item, k_ok = length_of(k_row)
            k_tag = jnp.where(k_ok, k_item, -1)
            same = (k_tag == q_item) & (k_row <= q_row)
            allowed = same | (k_row == q_row)
            MSK[pl.ds(pl.multiple_of(i * 2 * R + r0, CHUNK), CHUNK), :] = jnp.where(allowed, 0.0, NEG).astype(BF16)
            return carry

        lax.fori_loop(0, (b + 1) * (R // CHUNK), rows, 0)

    build_mask(0)
    build_mask(1)
    GA[...] = jnp.zeros(GA.shape, F32)
    GB[...] = jnp.zeros(GB.shape, F32)

    def x_copy(slot, i):
        return pltpu.make_async_remote_copy(
            SND.at[slot, i], RCV.at[slot * 2 + (i if slot < 2 else 0)], x_snd.at[slot, i], x_rcv.at[slot, i],
            device_id=xp, device_id_type=MESH)

    def last_copy(c, i):
        rows = slice(c * 64, c * 64 + 64)
        return pltpu.make_async_remote_copy(
            SND.at[0, i, rows, :], RCV.at[i, rows, :], last_snd.at[c], last_rcv.at[c],
            device_id=xp, device_id_type=MESH)

    def by_rows(body):
        body(slice(0, R))

    total_rows = slice(3 * R, 4 * R)

    def gather(n, term):
        for c in range(4):
            part = term[:, c * R : c * R + R]
            BIG[c, total_rows, :] = part if n == 0 else BIG[c, total_rows, :] + part

    def gathered():
        return jnp.concatenate([BIG[c, total_rows, :] for c in range(4)], axis=1).astype(BF16)

    def swapped(slot, i, rows):
        return SND[slot, i, rows, :].astype(F32) + RCV[slot * 2 + (i if slot < 2 else 0), rows, :].astype(F32)

    def send_result(which, layer, src, rows=slice(0, R)):
        src = src.at[rows, :]
        dst = act if which < 2 else ig
        o = 0 if which < 2 else 1
        here = (s == layer) & (y == own_i)

        @pl.when(here)
        def _():
            pltpu.make_async_copy(src, dst.at[y, rows, :], out_rcv.at[o, y]).start()

        @pl.when(jnp.logical_not(here))
        def _():
            pltpu.make_async_remote_copy(
                src, dst.at[y, rows, :], out_snd.at[which], out_rcv.at[o, y],
                device_id=(layer, d, own_i * 2 + x), device_id_type=MESH).start()

    def send_result_done(which, layer, src):
        dst = act if which < 2 else ig
        o = 0 if which < 2 else 1
        here = (s == layer) & (y == own_i)

        @pl.when(jnp.logical_not(here))
        def _():
            pltpu.make_async_remote_copy(
                src, dst.at[y], out_snd.at[which], out_rcv.at[o, y],
                device_id=(layer, d, own_i * 2 + x), device_id_type=MESH).wait_send()

    def vec(l, k):
        return SP[l, y, k : k + 1, :]

    def head_lanes(pair):
        return pl.ds(pl.multiple_of(pair * 128, 128), 128)

    def split_pair(v, axis):
        which = lax.broadcasted_iota(jnp.int32, v.shape, axis) < HEAD_DIM
        zero = jnp.zeros_like(v)
        return jnp.where(which, v, zero), jnp.where(which, zero, v)

    def kv_copy(l, i):
        rows = pl.ds(pl.multiple_of(blk_of(i) * R, R), R)
        return pltpu.make_async_remote_copy(
            KV.at[l, :, rows, :], KV.at[l, :, rows, :], kv_snd.at[l, i], kv_rcv.at[l, i],
            device_id=sib, device_id_type=MESH)

    def kv_wait(l, i):
        b = 2 * i + (1 - s + i - 2 * (1 - s) * i)
        rows = pl.ds(pl.multiple_of(b * R, R), R)
        pltpu.make_async_remote_copy(
            KV.at[l, :, rows, :], KV.at[l, :, rows, :], kv_snd.at[l, i], kv_rcv.at[l, i],
            device_id=sib, device_id_type=MESH).wait_recv()

    GROUP = 4

    def attend(l, i):
        b = blk_of(i)

        def group_turn(g, carry):
            def lanes_of(k):
                return pl.ds(pl.multiple_of(g * (GROUP * HEAD_DIM) + k * 128, 128), 128)

            def first(j, tops):
                rows = pl.ds(pl.multiple_of(j * R, R), R)
                mask = MSK[pl.ds(pl.multiple_of((i * 2 + j) * R, R), R), :].astype(F32)
                new = []
                for k in range(GROUP // 2):
                    qs = split_pair(Q[l, i, :, lanes_of(k)], 1)
                    keys = KV[l, 0, rows, lanes_of(k)]
                    for e in range(2):
                        st = nt(keys, qs[e]) + mask
                        BIG[2 * k + e, rows, :] = st
                        new.append(jnp.maximum(tops[2 * k + e], jnp.max(st, axis=0, keepdims=True)))
                return tuple(new)

            tops = lax.fori_loop(0, b + 1, first, (jnp.full((1, R), NEG, F32),) * GROUP)
            for k in range(GROUP):
                OACC[k] = jnp.zeros(OACC.shape[1:], F32)

            def second(j, sums):
                rows = pl.ds(pl.multiple_of(j * R, R), R)
                new = []
                for k in range(GROUP):
                    p = jnp.exp(BIG[k, rows, :] - tops[k])
                    new.append(sums[k] + jnp.sum(p, axis=0, keepdims=True))
                    PB[k] = p.astype(BF16)
                for k in range(GROUP // 2):
                    values = jnp.transpose(KV[l, 1, rows, lanes_of(k)])
                    for e in range(2):
                        OACC[2 * k + e] += nn(values[e * 64 : e * 64 + 64], PB[2 * k + e])
                return tuple(new)

            sums = lax.fori_loop(0, b + 1, second, (jnp.zeros((1, R), F32),) * GROUP)
            for k in range(GROUP):
                OT[l, i, pl.ds(pl.multiple_of((g * GROUP + k) * 64, 64), 64), :] = (
                    OACC[k] * (1.0 / sums[k])
                ).astype(BF16)
                LSE[l, i, g * GROUP + k] = tops[k] + jnp.log(sums[k])
            return carry

        lax.fori_loop(0, Q.shape[3] // (GROUP * HEAD_DIM), group_turn, 0)

    def forward_attention(l, i):
        b = blk_of(i)

        @pl.when(i == 0)
        def _():
            @pl.when(l == 0)
            def _():
                rows_relay(tok, H.at[0], 0)
                relay_y(l, 0)
                relay_y(l, 1)
                rows_first(cot, DY, 1)

                @pl.when(own_i == 1)
                def _():
                    rows_rest(tok, H.at[0], 0)

            other_wait(l, 0)
            relay_z(l, 1)

            @pl.when(l == 1)
            def _():
                relay_y(l, 2)
                relay_y(l, 3)

            other_wait(l, 1)

        @pl.when(i == 1)
        def _():
            @pl.when((l == 0) & (own_i == 0))
            def _():
                rows_rest(tok, H.at[0], 0)


        @pl.when(l == 1)
        def _():
            x_copy(1, i).wait_recv()

            def rows_in(rows):
                h = MID[0, i, rows, :] + (swapped(1, i, rows) + vec(0, 5))
                H[1, i, rows, :] = h.astype(BF16)

            by_rows(rows_in)

            @pl.when(i == own_i)
            def _():
                send_result(0, 0, H.at[1, i])

        def rows_norm(rows):
            xhat, _ = normalize(H[l, i, rows, :].astype(F32))
            AB[rows, :] = (xhat * vec(l, 0) + vec(l, 1)).astype(BF16)

        by_rows(rows_norm)
        u = nt(AB[...], SP[l, y, 8:16, :].astype(BF16)).astype(BF16)
        U[l, i] = nt(SP[l, y, 8:16, :].astype(BF16), AB[...]).astype(BF16)
        own_rows = pl.ds(pl.multiple_of(b * R, R), R)
        for j in range(2):
            up = SP[l, j, 24:32, 0:768].astype(BF16)
            qkv = nn(AB[...], WQ[l, j]) + (adapter_scale * nn(u, up) + SP[l, j, 17:18, 0:768])
            cols = slice(j * 256, j * 256 + 256)
            Q[l, i, :, cols] = (qkv[:, 0:256] * HEAD_DIM ** -0.5).astype(BF16)
            KV[l, 0, own_rows, cols] = qkv[:, 256:512].astype(BF16)
            KV[l, 1, own_rows, cols] = qkv[:, 512:768].astype(BF16)

        @pl.when(b != 3)
        def _():
            kv_copy(l, i).start()

        @pl.when((s == 1) & (i == 0))
        def _():
            kv_wait(l, 0)

        @pl.when((s == 0) & (i == 1))
        def _():
            kv_wait(l, 0)
            kv_wait(l, 1)

        @pl.when((i == 0) & (l == 0))
        def _():
            relay_y(l, 2)

        @pl.when(i == 1)
        def _():
            @pl.when(l == 0)
            def _():
                relay_y(l, 3)

            @pl.when(l == 1)
            def _():
                relay_y(l, 4)

        attend(l, i)

        @pl.when(i == 0)
        def _():
            relay_z(l, 2)
            other_wait(l, 2)

        @pl.when(l == 1)
        def _():
            x_copy(0, i).wait_send()

        SND[0, i] = (tn(OT[l, i, 0:256, :], WO[l, 0]) + tn(OT[l, i, 256:512, :], WO[l, 1])).astype(BF16)
        x_copy(0, i).start()

    def forward_ff(l, i):
        @pl.when((i == 0) & (l == 0))
        def _():
            relay_y(l, 4)

        @pl.when((i == 1) & (l == 0))
        def _():
            rows_swap(cot, DY, 1)

        @pl.when((i == 1) & (l == 1))
        def _():
            rows_relay(cot, DY, 1)

        x_copy(0, i).wait_recv()

        def rows_mid(rows):
            mid = H[l, i, rows, :].astype(F32) + (swapped(0, i, rows) + vec(l, 4))
            MID[l, i, rows, :] = mid
            xhat, _ = normalize(mid)
            AB[rows, :] = (xhat * vec(l, 2) + vec(l, 3)).astype(BF16)

        by_rows(rows_mid)
        for n in range(4):
            j, half = (y if n < 2 else 1 - y), n % 2
            cols = slice(half * 512, half * 512 + 512)
            if n == 2:

                @pl.when(i == 0)
                def _():
                    relay_z(l, 3)
                    relay_z(l, 4)
                    other_wait(l, 3)
                    other_wait(l, 4)

            z = nn(AB[...], WU[l, j, :, cols]) + SP[l, j, 16:17, cols]
            g, slope = gelu_pair(z)
            GP[l, i, :, n * 512 : n * 512 + 512] = slope.astype(BF16)
            term = nn(g.astype(BF16), WD[l, j, cols, :])
            gather(n, term)
        SND[1 + l, i] = gathered()

        @pl.when(l == 0)
        def _():
            x_copy(1, i).start()

            @pl.when(i == 1)
            def _():
                relay_y(1, 0)
                relay_y(1, 1)

        @pl.when((l == 1) & (i != own_i))
        def _():
            x_copy(2, i).start()

    def fwd_layer(l, carry):
        def a_turn(i, c):
            forward_attention(l, i)
            return c

        def f_turn(i, c):
            forward_ff(l, i)
            return c

        lax.fori_loop(0, 2, a_turn, 0)
        lax.fori_loop(0, 2, f_turn, 0)
        return carry

    lax.fori_loop(0, 2, fwd_layer, 0)

    def finish_forward():
        x_copy(2, own_i).wait_recv()

        def rows_out(rows):
            out = MID[1, own_i, rows, :] + (swapped(2, own_i, rows) + vec(1, 5))
            SND[2, own_i, rows, :] = out.astype(BF16)

        by_rows(rows_out)
        send_result(1, 1, SND.at[2, own_i])

    def backward_ff(l, i):
        @pl.when(l == 1)
        def _():
            @pl.when(i == own_i)
            def _():
                row_copies(cot, DY, 1)[3]().wait_send()

            @pl.when(i != own_i)
            def _():
                rows_rest(cot, DY, 1)

            def rows_valid(rows):
                pos = blk_of(i) * R + lax.broadcasted_iota(jnp.int32, (R, 1), 0)
                _, ok = length_of(pos)
                DY[i, rows, :] = (DY[i, rows, :].astype(F32) * jnp.where(ok, 1.0, 0.0)).astype(BF16)

            by_rows(rows_valid)

        @pl.when(l == 0)
        def _():
            x_copy(0, i).wait_recv()

            def rows_in(rows):
                g = swapped(0, i, rows) * vec(1, 0)
                DY[i, rows, :] = (MID[1, i, rows, :] + norm_pull(H[1, i, rows, :].astype(F32), g)).astype(BF16)

            by_rows(rows_in)

            @pl.when(i == own_i)
            def _():
                send_result(2, 1, DY.at[i])

        for n in range(4):
            j, half = (y if n < 2 else 1 - y), n % 2
            cols = slice(half * 512, half * 512 + 512)
            dg = nt(DY[i], WD[l, j, cols, :])
            dz = (GP[l, i, :, n * 512 : n * 512 + 512].astype(F32) * dg).astype(BF16)
            term = nt(dz, WU[l, j, :, cols])
            gather(n, term)

        x_copy(1, i).wait_send()
        SND[1, i] = gathered()
        x_copy(1, i).start()

    def dr_copy(k, b):
        rows = pl.ds(pl.multiple_of(b * R, R), R)
        return pltpu.make_async_remote_copy(
            BIG.at[:, rows, :], DR.at[k], dr_snd.at[k], dr_rcv.at[k], device_id=sib, device_id_type=MESH)

    def attend_back(l, i):
        b = blk_of(i)
        pairs = Q.shape[3] // 128
        place = RCV.at[2 + i]

        def back_rows(k):
            return place[(k % 2) * 128 : (k % 2) * 128 + 128, 512 + (k // 2) * 256 : 768 + (k // 2) * 256]

        deltas = []
        for k in range(pairs):
            rows = slice(k * 128, k * 128 + 128)
            prod = back_rows(k).astype(F32) * OT[l, i, rows, :].astype(F32)
            deltas.append(jnp.sum(prod[0:64], axis=0, keepdims=True))
            deltas.append(jnp.sum(prod[64:128], axis=0, keepdims=True))
            OACC[2 * k] = jnp.zeros(OACC.shape[1:], F32)
            OACC[2 * k + 1] = jnp.zeros(OACC.shape[1:], F32)

        def turn(j, c):
            rows = pl.ds(pl.multiple_of(j * R, R), R)
            mask = MSK[pl.ds(pl.multiple_of((i * 2 + j) * R, R), R), :].astype(F32)
            for k in range(pairs):
                lanes = slice(k * 128, k * 128 + 128)
                qs = split_pair(Q[l, i, :, lanes], 1)
                dots = split_pair(back_rows(k), 0)
                keys = KV[l, 0, rows, lanes]
                values = KV[l, 1, rows, lanes]
                for e in range(2):
                    h = 2 * k + e
                    p = jnp.exp(nt(keys, qs[e]) + mask - LSE[l, i, h])
                    dp = nn(values, dots[e])
                    PB[h] = (p * (dp - deltas[h])).astype(BF16)
                    PB[2 * pairs + h] = p.astype(BF16)
            for k in range(pairs):
                lanes = slice(k * 128, k * 128 + 128)
                half = slice((k % 2) * 128, (k % 2) * 128 + 128)
                qs = split_pair(Q[l, i, :, lanes], 1)
                dos = split_pair(place[:, lanes], 1)
                h = 2 * k
                BIG[k // 2, rows, half] += nn(PB[h], qs[0]) + nn(PB[h + 1], qs[1])
                BIG[2 + k // 2, rows, half] += nn(PB[2 * pairs + h], dos[0]) + nn(PB[2 * pairs + h + 1], dos[1])
            for k in range(pairs):
                keys = jnp.transpose(KV[l, 0, rows, k * 128 : k * 128 + 128])
                for e in range(2):
                    OACC[2 * k + e] += nn(keys[e * 64 : e * 64 + 64], PB[2 * k + e])
            return c

        lax.fori_loop(0, b + 1, turn, 0)
        for k in range(pairs):
            dq = jnp.concatenate([OACC[2 * k], OACC[2 * k + 1]], axis=0) * HEAD_DIM ** -0.5
            DQ[k // 2, :, (k % 2) * 128 : (k % 2) * 128 + 128] = jnp.transpose(dq).astype(BF16)

    def backward_attention(l, i):
        b = blk_of(i)
        x_copy(1, i).wait_recv()

        def rows_mid(rows):
            g = swapped(1, i, rows) * vec(l, 2)
            dmid = DY[i, rows, :].astype(F32) + norm_pull(MID[l, i, rows, :], g)
            MID[l, i, rows, :] = dmid
            AB[rows, :] = dmid.astype(BF16)

        by_rows(rows_mid)
        for j in range(2):
            RCV[2 + i, :, 512 + j * 256 : 768 + j * 256] = nt(WO[l, j], AB[...]).astype(BF16)
            RCV[2 + i, :, j * 256 : j * 256 + 256] = nt(AB[...], WO[l, j]).astype(BF16)

        @pl.when(i == 1)
        def _():
            @pl.when(l == 0)
            def _():
                @pl.when(s == 0)
                def _():
                    dr_copy(0, 1).wait_send()
                    dr_copy(1, 2).wait_send()

                @pl.when(s == 1)
                def _():
                    dr_copy(0, 0).wait_send()

            def clear(r, c):
                rows = pl.ds(pl.multiple_of(r * R, R), R)
                BIG[:, rows, :] = jnp.zeros((4, R, 256), F32)
                return c

            lax.fori_loop(0, 4, clear, 0)

        attend_back(l, i)
        own = pl.ds(pl.multiple_of(b * R, R), R)

        @pl.when((s == 0) & (i == 1))
        def _():
            dr_copy(0, 1).start()
            dr_copy(1, 2).start()

        @pl.when(b != 3)
        def _():
            def add(k):
                dr_copy(k, b).wait_recv()
                for c in range(4):
                    BIG[c, own, :] += DR[k, c]

            @pl.when(s == 1)
            def _():
                add(i)

            @pl.when((s == 1) & (i == 0))
            def _():
                dr_copy(0, 0).start()

            @pl.when(s == 0)
            def _():
                add(0)

        for j in range(2):
            DQ[j, :, 256:512] = BIG[j, own, :].astype(BF16)
            DQ[j, :, 512:768] = BIG[2 + j, own, :].astype(BF16)

        def rows_norm(rows):
            xhat, _ = normalize(H[l, i, rows, :].astype(F32))
            AB[rows, :] = (xhat * vec(l, 0) + vec(l, 1)).astype(BF16)

        by_rows(rows_norm)
        ups = [SP[l, j, 24:32, 0:768].astype(BF16) for j in range(2)]
        du = (adapter_scale * (nt(ups[0], DQ[0]) + nt(ups[1], DQ[1]))).astype(BF16)
        GA[l] += nn(du, AB[...])
        top = lax.broadcasted_iota(jnp.int32, (8, 256), 0) < 4
        for j in range(2):
            gq = nn(U[l, i], DQ[j, :, 0:256])
            gv = nn(U[l, i], DQ[j, :, 512:768])
            GB[l, j] += adapter_scale * jnp.where(top, gq, gv)

        x_copy(0, i).wait_send()
        SND[0, i] = (
            nt(DQ[0], WQ[l, 0]) + nt(DQ[1], WQ[l, 1]) + tn(du, SP[l, y, 8:16, :].astype(BF16))
        ).astype(BF16)

        @pl.when(l == 1)
        def _():
            x_copy(0, i).start()

        @pl.when((l == 0) & (i != own_i))
        def _():
            for c in range(4):
                last_copy(c, i).start()

    def core_copies(l):
        return (
            pltpu.make_async_remote_copy(
                GA.at[l], GCA, gc_s.at[0], gc_r.at[0], device_id=sib, device_id_type=MESH),
            pltpu.make_async_remote_copy(
                GB.at[l], GCB, gc_s.at[1], gc_r.at[1], device_id=sib, device_id_type=MESH),
        )

    def plane_copies(l):
        out = []
        for k, (dx, dy) in enumerate(((1, 0), (0, 1), (1, 1))):
            x2 = 1 - x if dx else x
            y2 = 1 - y if dy else y
            to = (s, d, y2 * 2 + x2)
            out.append(pltpu.make_async_remote_copy(
                GA.at[l], GXA.at[k], gx_s.at[k], gx_r.at[k], device_id=to, device_id_type=MESH))
        out.append(pltpu.make_async_remote_copy(
            GB.at[l, 1 - y], GXB, gx_s.at[3], gx_r.at[3], device_id=yp, device_id_type=MESH))
        return out

    def line_copies():
        out = []
        for k in range(1, dp_count):
            to = (s, lax.rem(d + k, dp_count), t)
            out.append(pltpu.make_async_remote_copy(
                GZA.at[d], GZA.at[d], gz_s.at[0, k - 1], gz_r.at[0, k - 1], device_id=to, device_id_type=MESH))
            out.append(pltpu.make_async_remote_copy(
                GZB.at[d], GZB.at[d], gz_s.at[1, k - 1], gz_r.at[1, k - 1], device_id=to, device_id_type=MESH))
        return out

    def sum_core(l):
        @pl.when(s != l)
        def _():
            for c in core_copies(l):
                c.start()

    def sum_plane(l):
        @pl.when(s == l)
        def _():
            for c in core_copies(l):
                c.wait_recv()
            GA[l] += GCA[...]
            GB[l] += GCB[...]
            for c in plane_copies(l):
                c.start()

    def sum_line(l):
        @pl.when(s == l)
        def _():
            for c in plane_copies(l):
                c.wait_recv()
            GZA[d] = (GA[l] + GXA[0]) + (GXA[1] + GXA[2])
            GZB[d] = GB[l, y] + GXB[...]
            for c in line_copies():
                c.start()

    def sum_end(l):
        @pl.when(s == l)
        def _():
            for c in line_copies():
                c.wait_recv()
            total_a, total_b = GZA[0], GZB[0]
            for k in range(1, dp_count):
                total_a, total_b = total_a + GZA[k], total_b + GZB[k]
            out_a[0, 0] = total_a[0:4]
            out_a[0, 1] = total_a[4:8]
            out_b[0, 0] = total_b[0:4]
            out_b[0, 1] = total_b[4:8]

    def bwd_layer(back, carry):
        l = 1 - back

        def f_turn(k, c):
            @pl.when((l == 0) & (k == 1))
            def _():
                sum_plane(1)

            backward_ff(l, 1 - k)
            return c

        def a_turn(k, c):
            @pl.when((l == 0) & (k == 0))
            def _():
                sum_line(1)

            @pl.when((l == 0) & (k == 1))
            def _():
                sum_end(1)

            backward_attention(l, 1 - k)
            return c

        lax.fori_loop(0, 2, f_turn, 0)

        @pl.when(l == 1)
        def _():
            finish_forward()

        lax.fori_loop(0, 2, a_turn, 0)
        sum_core(l)
        return carry

    lax.fori_loop(0, 2, bwd_layer, 0)
    sum_plane(0)

    for c in range(4):
        last_copy(c, own_i).wait_recv()
        rows = slice(c * 64, c * 64 + 64)
        g = swapped(0, own_i, rows) * vec(0, 0)
        AB[rows, :] = (MID[0, own_i, rows, :] + norm_pull(H[0, own_i, rows, :].astype(F32), g)).astype(BF16)
        send_result(3, 0, AB, rows)
    sum_line(0)

    for c in range(4):
        last_copy(c, 1 - own_i).wait_send()
    for i in range(2):
        x_copy(1, i).wait_send()
    x_copy(2, 1 - own_i).wait_send()
    def sent(ref, sem):
        pltpu.make_async_remote_copy(ref, ref, sem, sem, device_id=sib, device_id_type=MESH).wait_send()

    for p in range(5):
        sent(pieces[p][1].at[s, y] if p else SP.at[s, y], ws_s.at[p])
        for c in range(pieces[p][2] if p else 1):
            k = base[p] + c
            ref = block(p, s, y, chunk(p, c, 0)) if p else SP.at[s, y, 16:32, :]
            sent(ref, wy_s.at[k])
            sent(ref, wa_s.at[k])
            if p:
                sent(ref, wz_s.at[k])
                sent(ref, wb_s.at[k])
    rows_done(tok, H.at[0], 0)
    rows_done(cot, DY, 1)
    for l in range(2):
        kv_copy(l, 0).wait_send()

        @pl.when(s == 1)
        def _():
            kv_copy(l, 1).wait_send()

    @pl.when(s == 0)
    def _():
        dr_copy(0, 1).wait_send()
        dr_copy(1, 2).wait_send()

    @pl.when(s == 1)
    def _():
        dr_copy(0, 0).wait_send()

    @pl.when(s == 0)
    def _():
        for c in core_copies(1) + tuple(plane_copies(0)) + tuple(line_copies()):
            c.wait_send()

    @pl.when(s == 1)
    def _():
        for c in core_copies(0) + tuple(plane_copies(1)) + tuple(line_copies()):
            c.wait_send()

    send_result_done(0, 0, H.at[1, 0])
    send_result_done(1, 1, H.at[1, 0])
    send_result_done(2, 1, H.at[1, 0])
    send_result_done(3, 0, H.at[1, 0])
    for o, ref in ((0, act), (1, ig)):
        for m in range(2):
            pltpu.make_async_copy(tok.at[0], ref.at[m], out_rcv.at[o, m]).wait()
    sum_end(0)


def copy_kernel(a_in, g_in, ta_in, tb_in, a_out, g_out, ta_out, tb_out, held_a, held_g, held_ta, held_tb, load, store):
    moves = []
    for k, (src, held, dst) in enumerate(((a_in, held_a, a_out), (g_in, held_g, g_out))):
        for m in range(src.shape[0]):
            moves.append((src.at[m], held.at[m], dst.at[0, m], 2 * k + m))
    moves.append((ta_in, held_ta, ta_out, 4))
    moves.append((tb_in, held_tb, tb_out, 5))
    for src, held, dst, k in moves:
        pltpu.make_async_copy(src, held, load.at[k]).start()
    for src, held, dst, k in moves:
        pltpu.make_async_copy(src, held, load.at[k]).wait()
        pltpu.make_async_copy(held, dst, store.at[k]).start()
    for src, held, dst, k in moves:
        pltpu.make_async_copy(held, dst, store.at[k]).wait()


def settle(act, ig, total_a, total_b):
    anywhere = pl.BlockSpec(memory_space=pl.ANY)
    shapes = [(1,) + act.shape, (1,) + ig.shape, total_a.shape, total_b.shape]
    kinds = [act.dtype, ig.dtype, total_a.dtype, total_b.dtype]
    return pl.pallas_call(
        copy_kernel,
        out_shape=tuple(jax.ShapeDtypeStruct(a, b) for a, b in zip(shapes, kinds)),
        in_specs=[anywhere] * 4,
        out_specs=(anywhere,) * 4,
        scratch_shapes=[
            pltpu.VMEM(v.shape, v.dtype) for v in (act, ig, total_a, total_b)
        ] + [pltpu.SemaphoreType.DMA((6,))] * 2,
        name="settle",
    )(act, ig, total_a, total_b)


def per_pair(
    tokens, cotangent, buckets, lengths, norm_gain_pairs, norm_bias_pairs, query_key_value_weight,
    query_value_bias, output_weight, upward_weight, upward_bias, down_weight, output_bias,
    adapter_down, adapter_upper,
):
    weight_qkv = query_key_value_weight[0].transpose(1, 0, 2)
    dp_count = lax.axis_size("dp")
    anywhere = pl.BlockSpec(memory_space=pl.ANY)
    scalars = pl.BlockSpec(memory_space=pltpu.SMEM)
    vmem = pl.BlockSpec(memory_space=pltpu.VMEM)
    dma = pltpu.SemaphoreType.DMA
    act, ig, total_a, total_b = pl.pallas_call(
        partial(fused_kernel, dp_count),
        out_shape=(
            jax.ShapeDtypeStruct((2, R, D), BF16),
            jax.ShapeDtypeStruct((2, R, D), BF16),
            jax.ShapeDtypeStruct((1, 2, 4, D), F32),
            jax.ShapeDtypeStruct((1, 2, 4, 256), F32),
        ),
        in_specs=[anywhere, anywhere, scalars, scalars, vmem, vmem, anywhere, vmem, anywhere, anywhere, vmem,
                  anywhere, vmem, vmem, vmem],
        out_specs=(anywhere, anywhere, vmem, vmem),
        scratch_shapes=[
            pltpu.VMEM((2, 2, 32, D), F32),
            pltpu.VMEM((2, 2, D, 768), BF16),
            pltpu.VMEM((2, 2, 256, D), BF16),
            pltpu.VMEM((2, 2, D, 1024), BF16),
            pltpu.VMEM((2, 2, 1024, D), BF16),
            pltpu.VMEM((2, 2, R, D), BF16),
            pltpu.VMEM((2, R, D), BF16),
            pltpu.VMEM((2, 2, R, D), F32),
            pltpu.VMEM((2, 2, R, 2048), BF16),
            pltpu.VMEM((2, 2, R, 512), BF16),
            pltpu.VMEM((2, 2, 4 * R, 512), BF16),
            pltpu.VMEM((2, 2, 512, R), BF16),
            pltpu.VMEM((2, 2, 8, 1, R), F32),
            pltpu.VMEM((3, 2, R, D), BF16),
            pltpu.VMEM((5, R, D), BF16),
            pltpu.VMEM((4, 4 * R, R), F32),
            pltpu.VMEM((6 * R, R), BF16),
            pltpu.VMEM((2, 4, R, R), F32),
            pltpu.VMEM((2, R, 768), BF16),
            pltpu.VMEM((R, D), BF16),
            pltpu.VMEM((2, 2, 8, R), BF16),
            pltpu.VMEM((8, 64, R), F32),
            pltpu.VMEM((16, R, R), BF16),
            pltpu.VMEM((2, 8, D), F32),
            pltpu.VMEM((2, 2, 8, 256), F32),
            pltpu.VMEM((8, D), F32),
            pltpu.VMEM((2, 8, 256), F32),
            pltpu.VMEM((3, 8, D), F32),
            pltpu.VMEM((8, 256), F32),
            pltpu.VMEM((dp_count, 8, D), F32),
            pltpu.VMEM((dp_count, 8, 256), F32),
            dma((2, 2)),
            dma((2,)),
            dma((2,)),
            dma((5,)),
            dma((5,)),
            dma((5,)),
            dma((14,)),
            dma((14,)),
            dma((13,)),
            dma((13,)),
            dma((14,)),
            dma((14,)),
            dma((13,)),
            dma((13,)),
            dma((2, 2)),
            dma((2, 2)),
            dma((3, 2)),
            dma((3, 2)),
            dma((4,)),
            dma((4,)),
            dma((2,)),
            dma((2,)),
            dma((2, 2)),
            dma((4,)),
            dma((2,)),
            dma((2,)),
            dma((4,)),
            dma((4,)),
            dma((2, dp_count - 1)),
            dma((2, dp_count - 1)),
        ],
        compiler_params=pltpu.CompilerParams(
            collective_id=0, has_side_effects=True, vmem_limit_bytes=127 * 2**19
        ),
        name="two_layers",
    )(
        tokens, cotangent, buckets, lengths, norm_gain_pairs, norm_bias_pairs, weight_qkv, query_value_bias,
        output_weight, upward_weight, upward_bias, down_weight, output_bias, adapter_down, adapter_upper,
    )
    return settle(act, ig, total_a, total_b)


def solution(mesh):
    in_specs = (
        P("dp", "tensor", None),
        P("dp", "tensor", None),
        P("dp"),
        P("dp", None),
        P("section", None, None),
        P("section", None, None),
        P("section", None, None, "tensor"),
        P("section", None, "tensor"),
        P("section", "tensor", None),
        P("section", None, "tensor"),
        P("section", "tensor"),
        P("section", "tensor", None),
        P("section", None, None),
        P("section", None, None, None),
        P("section", None, None, "tensor"),
    )
    out_specs = (
        P("section", "dp", "tensor", None),
        P("section", "dp", "tensor", None),
        P("section", None, None, None),
        P("section", None, None, "tensor"),
    )
    pairs = mesh.shape["section"] == 2 and mesh.shape["tensor"] == 4 and mesh.shape["dp"] % 2 == 0
    return jax.shard_map(
        per_pair if pairs else per_device, mesh=mesh, in_specs=in_specs, out_specs=out_specs, check_vma=False
    )
```

```python
from functools import partial

import jax
import jax.numpy as jnp
from jax import lax
from jax.experimental import pallas as pl
from jax.experimental.pallas import tpu as pltpu
from jax.sharding import PartitionSpec as P

HEAD_DIM = 64


adapter_scale = 8.0
norm_eps = 1e-05
masked_score = -1000000000.0
highest_precision = lax.Precision.HIGHEST


def from_behind(block, axis, distance):
    devices = range(lax.axis_size(axis))
    route = [(i - distance, i) for i in devices if i - distance in devices]
    return lax.ppermute(block, axis, route)


def layer_norm(values, gain_rows, shifts):
    center = jnp.mean(values, axis=-1, keepdims=True)
    centered = values - center
    spread = jnp.mean(centered * centered, axis=-1, keepdims=True)
    return centered * lax.rsqrt(spread + norm_eps) * gain_rows + shifts


def row_layout(bucket, lengths_row, row_count):
    item_span = jnp.right_shift(jnp.int32(row_count), 3 - bucket)
    positions = jnp.arange(row_count, dtype=jnp.int32)
    item_index = positions // item_span
    within = positions - item_index * item_span
    chosen = (
        item_index[:, None] == jnp.arange(lengths_row.shape[0], dtype=jnp.int32)[None, :]
    ).astype(jnp.int32)
    length = jnp.sum(chosen * lengths_row[None, :], axis=1)
    return (item_index, within < length)


def allowed_keys(item_index, is_valid):
    positions = jnp.arange(item_index.shape[0], dtype=jnp.int32)
    same_item = item_index[:, None] == item_index[None, :]
    causal = positions[None, :] <= positions[:, None]
    key_seen = is_valid[None, :] | (positions[None, :] == positions[:, None])
    return same_item & causal & key_seen


def take_slot(buffer, slot_index):
    return lax.dynamic_index_in_dim(buffer, slot_index, 0, keepdims=False)


def put_slot(buffer, slot_index, is_live, update):
    previous = take_slot(buffer, slot_index)
    return lax.dynamic_update_index_in_dim(
        buffer, jnp.where(is_live, update, previous), slot_index, 0
    )


def per_device(
    tokens,
    cotangent,
    buckets,
    lengths,
    norm_gain_pairs,
    norm_bias_pairs,
    query_key_value_weight,
    query_value_bias,
    output_weight,
    upward_weight,
    upward_bias,
    down_weight,
    output_bias,
    adapter_down,
    adapter_upper,
):
    section_index = lax.axis_index("section")
    tensor_count = lax.axis_size("tensor")
    micro_count, own_rows, model_width = tokens.shape
    row_count = own_rows * tensor_count
    own_start = lax.axis_index("tensor") * own_rows
    gain_sets = norm_gain_pairs[0].astype(jnp.float32)
    shift_sets = norm_bias_pairs[0].astype(jnp.float32)
    weight_qkv = query_key_value_weight[0]
    bias_query_value = query_value_bias[0].astype(jnp.float32)
    weight_out = output_weight[0]
    weight_up = upward_weight[0]
    bias_up = upward_bias[0].astype(jnp.float32)
    weight_down = down_weight[0]
    biases = output_bias[0].astype(jnp.float32)
    down_factor = adapter_down[0]
    upper_factor = adapter_upper[0]
    factor_wide = down_factor.astype(jnp.float32)
    local_width = weight_qkv.shape[2]
    local_heads = local_width // HEAD_DIM
    score_scale = HEAD_DIM ** (-0.5)

    def widen(values):
        return lax.all_gather(values, "tensor", axis=0, tiled=True)

    def widen_back(values):
        return lax.all_gather(values, "tensor", axis=0, tiled=True)

    def settle(source, weight):

        def row_term(first_row, row_span):
            return jnp.dot(source, weight, preferred_element_type=jnp.float32)

        return lax.psum_scatter(
            row_term(jnp.int32(0), lax.axis_size("tensor") * own_rows).astype(jnp.bfloat16),
            "tensor",
            scatter_dimension=0,
            tiled=True,
        ).astype(jnp.float32)

    def settle_back(row_term):
        return lax.psum_scatter(
            row_term(jnp.int32(0), lax.axis_size("tensor") * own_rows).astype(jnp.bfloat16),
            "tensor",
            scatter_dimension=0,
            tiled=True,
        ).astype(jnp.float32)

    def layout_of(slot_index):
        item_index, is_valid = row_layout(
            take_slot(buckets, slot_index), take_slot(lengths, slot_index), row_count
        )
        own_valid = lax.dynamic_slice_in_dim(is_valid, own_start, own_rows, 0)
        return (allowed_keys(item_index, is_valid), own_valid)

    def attend(normed, allowed):
        reduced_query = jnp.dot(
            normed, down_factor[0].T, preferred_element_type=jnp.float32
        ).astype(jnp.bfloat16)
        reduced_value = jnp.dot(
            normed, down_factor[1].T, preferred_element_type=jnp.float32
        ).astype(jnp.bfloat16)
        blended_rows = jnp.einsum(
            "rd,dcn->rcn", normed, weight_qkv, preferred_element_type=jnp.float32
        )
        query_matrix_rows = (
            blended_rows[:, 0]
            + bias_query_value[0]
            + adapter_scale
            * jnp.dot(reduced_query, upper_factor[0], preferred_element_type=jnp.float32)
        )
        value_matrix_rows = (
            blended_rows[:, 2]
            + bias_query_value[1]
            + adapter_scale
            * jnp.dot(reduced_value, upper_factor[1], preferred_element_type=jnp.float32)
        )
        packed = jnp.stack(
            [query_matrix_rows, blended_rows[:, 1], value_matrix_rows], axis=1
        ).astype(jnp.bfloat16)
        head_split = packed.reshape(row_count, 3, local_heads, HEAD_DIM)
        scores = (
            jnp.einsum(
                "qhe,khe->hqk",
                head_split[:, 0],
                head_split[:, 1],
                preferred_element_type=jnp.float32,
            )
            * score_scale
        )
        scores = jnp.where(allowed[None], scores, masked_score)
        top_score = jnp.max(scores, axis=-1, keepdims=True)
        exponent = jnp.exp(scores - top_score)
        attn_probs = exponent / jnp.sum(exponent, axis=-1, keepdims=True)
        return (reduced_query, reduced_value, head_split, attn_probs)

    def forward(hidden, allowed):
        normed = widen(layer_norm(hidden, gain_sets[0], shift_sets[0]).astype(jnp.bfloat16))
        reduced_query, reduced_value, head_split, attn_probs = attend(normed, allowed)
        probs_low = attn_probs.astype(jnp.bfloat16)
        mixed_heads = jnp.einsum(
            "hqk,khe->qhe", probs_low, head_split[:, 2], preferred_element_type=jnp.float32
        )
        attended = mixed_heads.reshape(row_count, local_width).astype(jnp.bfloat16)
        middle = hidden + (settle(attended, weight_out) + biases[0])
        normed_two = widen(layer_norm(middle, gain_sets[1], shift_sets[1]).astype(jnp.bfloat16))
        hidden_pre = jnp.dot(normed_two, weight_up, preferred_element_type=jnp.float32) + bias_up
        activated = jax.nn.gelu(hidden_pre, approximate=True).astype(jnp.bfloat16)
        output = middle + (settle(activated, weight_down) + biases[1])
        return (output, normed, middle, normed_two)

    def backward(hidden, grad_out, allowed, normed, middle, normed_two):
        reduced_query, reduced_value, head_split, attn_probs = attend(normed, allowed)
        probs_low = attn_probs.astype(jnp.bfloat16)
        hidden_pre = jnp.dot(normed_two, weight_up, preferred_element_type=jnp.float32) + bias_up
        grad_branch = widen_back(grad_out.astype(jnp.bfloat16))
        grad_act = jnp.einsum(
            "rd,fd->rf", grad_branch, weight_down, preferred_element_type=jnp.float32
        )
        gelu_pull = jax.vjp(partial(jax.nn.gelu, approximate=True), hidden_pre)[1]
        grad_pre = gelu_pull(grad_act)[0].astype(jnp.bfloat16)

        def mlp_term(first_row, row_span):
            return jnp.einsum("rf,df->rd", grad_pre, weight_up, preferred_element_type=jnp.float32)

        grad_norm_two = settle_back(mlp_term)
        second_pull = jax.vjp(
            partial(layer_norm, gain_rows=gain_sets[1], shifts=shift_sets[1]), middle
        )[1]
        grad_middle = grad_out + second_pull(grad_norm_two)[0]
        grad_attn = widen_back(grad_middle.astype(jnp.bfloat16))
        grad_heads = jnp.einsum(
            "rd,nd->rn", grad_attn, weight_out, preferred_element_type=jnp.float32
        )
        grad_heads = grad_heads.astype(jnp.bfloat16).reshape(row_count, local_heads, HEAD_DIM)
        grad_probs = jnp.einsum(
            "qhe,khe->hqk", grad_heads, head_split[:, 2], preferred_element_type=jnp.float32
        )
        grad_scores = attn_probs * (
            grad_probs - jnp.sum(attn_probs * grad_probs, axis=-1, keepdims=True)
        )
        grad_scores = grad_scores.astype(jnp.bfloat16)
        grad_query = (
            jnp.einsum(
                "hqk,khe->qhe", grad_scores, head_split[:, 1], preferred_element_type=jnp.float32
            )
            * score_scale
        )
        grad_key = (
            jnp.einsum(
                "hqk,qhe->khe", grad_scores, head_split[:, 0], preferred_element_type=jnp.float32
            )
            * score_scale
        )
        grad_value = jnp.einsum(
            "hqk,qhe->khe", probs_low, grad_heads, preferred_element_type=jnp.float32
        )
        grad_packed = (
            jnp.stack([grad_query, grad_key, grad_value], axis=1)
            .reshape(row_count, 3, local_width)
            .astype(jnp.bfloat16)
        )
        grad_pair = jnp.stack([grad_packed[:, 0], grad_packed[:, 2]])
        gradient_reduced = adapter_scale * jnp.einsum(
            "jrn,jkn->jrk", grad_pair, upper_factor, preferred_element_type=jnp.float32
        )

        def attn_term(first_row, row_span):
            dense_part = jnp.einsum(
                "rcn,dcn->rd", grad_packed, weight_qkv, preferred_element_type=jnp.float32
            )
            return dense_part + jnp.einsum(
                "jrk,jkd->rd", gradient_reduced, factor_wide, precision=highest_precision
            )

        grad_normed = settle_back(attn_term)
        first_pull = jax.vjp(
            partial(layer_norm, gain_rows=gain_sets[0], shifts=shift_sets[0]), hidden
        )[1]
        grad_hidden = grad_middle + first_pull(grad_normed)[0]
        grad_factor_a = jnp.einsum(
            "jrk,rd->jkd", gradient_reduced, normed.astype(jnp.float32), precision=highest_precision
        )
        gradient_upper_factor = adapter_scale * jnp.stack(
            [
                jnp.einsum(
                    "rk,rn->kn",
                    reduced_query,
                    grad_packed[:, 0],
                    preferred_element_type=jnp.float32,
                ),
                jnp.einsum(
                    "rk,rn->kn",
                    reduced_value,
                    grad_packed[:, 2],
                    preferred_element_type=jnp.float32,
                ),
            ]
        )
        return (grad_hidden, grad_factor_a, gradient_upper_factor)

    zero_rows = jnp.zeros((micro_count, own_rows, model_width), jnp.bfloat16)
    saved_start = ()

    def record(buffers, slot_index, is_live, layer_input, results):
        kept_in, outputs, saved = buffers
        output, normed, middle, normed_two = results
        low_output = output.astype(jnp.bfloat16)
        kept_in = put_slot(kept_in, slot_index, is_live, layer_input)
        outputs = put_slot(outputs, slot_index, is_live, low_output)
        return ((kept_in, outputs, saved), low_output)

    buffers = (zero_rows, zero_rows, saved_start)

    def run_phase(buffers, sources, phase_section):

        def phase_turn(slot_index, buffers):
            allowed, own_valid = layout_of(slot_index)
            layer_input = take_slot(sources, slot_index)
            results = forward(layer_input.astype(jnp.float32), allowed)
            return record(
                buffers, slot_index, section_index == phase_section, layer_input, results
            )[0]

        return lax.fori_loop(0, micro_count, phase_turn, buffers)

    buffers = run_phase(buffers, tokens, 0)
    received = from_behind(buffers[1], "section", 1)
    buffers = run_phase(buffers, received, 1)
    kept_in, outputs, saved = buffers

    def back_step(slot_index, grad_out, allowed):
        hidden = take_slot(kept_in, slot_index).astype(jnp.float32)
        output, normed, middle, normed_two = forward(hidden, allowed)
        return backward(hidden, grad_out, allowed, normed, middle, normed_two)

    def top_grad(slot_index, own_valid):
        return take_slot(cotangent, slot_index).astype(jnp.float32) * own_valid[:, None].astype(
            jnp.float32
        )

    zero_a = jnp.zeros(down_factor.shape, jnp.float32)
    zero_b = jnp.zeros(upper_factor.shape, jnp.float32)

    def run_back(loop_state, sources, phase_section):

        def phase_turn(slot_index, loop_state):
            grads_in, sum_a, sum_b = loop_state
            allowed, own_valid = layout_of(slot_index)
            if phase_section == 1:
                grad_out = top_grad(slot_index, own_valid)
            else:
                grad_out = take_slot(sources, slot_index).astype(jnp.float32)
            is_live = section_index == phase_section
            grad_hidden, grad_a, grad_b = back_step(slot_index, grad_out, allowed)
            grads_in = put_slot(grads_in, slot_index, is_live, grad_hidden.astype(jnp.bfloat16))
            sum_a = sum_a + jnp.where(is_live, grad_a, 0.0)
            sum_b = sum_b + jnp.where(is_live, grad_b, 0.0)
            return (grads_in, sum_a, sum_b)

        return lax.fori_loop(0, micro_count, phase_turn, loop_state)

    loop_state = run_back((zero_rows, zero_a, zero_b), zero_rows, 1)
    received_grads = from_behind(loop_state[0], "section", -1)
    grads_in, sum_a, sum_b = run_back(loop_state, received_grads, 0)
    total_a = lax.psum(sum_a, ("dp", "tensor"))
    total_b = lax.psum(sum_b, "dp")
    return (outputs[None], grads_in[None], total_a[None], total_b[None])


R = 256
D = 1024
NEG = -1e30
F32 = jnp.float32
BF16 = jnp.bfloat16
MESH = pl.DeviceIdType.MESH
CHUNK = 128


def nn(a, b):
    return lax.dot_general(a, b, (((1,), (0,)), ((), ())), preferred_element_type=F32)


def nt(a, b):
    return lax.dot_general(a, b, (((1,), (1,)), ((), ())), preferred_element_type=F32)


def tn(a, b):
    return lax.dot_general(a, b, (((0,), (0,)), ((), ())), preferred_element_type=F32)


def normalize(v):
    centered = v - jnp.mean(v, axis=-1, keepdims=True)
    rs = lax.rsqrt(jnp.mean(centered * centered, axis=-1, keepdims=True) + norm_eps)
    return centered * rs, rs


def norm_pull(v, g):
    xhat, rs = normalize(v)
    return rs * (
        g
        - jnp.mean(g, axis=-1, keepdims=True)
        - xhat * jnp.mean(g * xhat, axis=-1, keepdims=True)
    )


def gelu_pair(z):
    c = 0.7978845608028654
    z2 = z * z
    t = jnp.tanh(c * (z + 0.044715 * (z2 * z)))
    half = 0.5 * (1.0 + t)
    slope = half + (0.5 * c) * z * (1.0 - t * t) * (1.0 + (3.0 * 0.044715) * z2)
    return z * half, slope


def fused_kernel(
    dp_count,
    tok, cot, buckets, lengths, gain_in, shift_in, wq_in, bqv_in, wo_in, wu_in, bu_in, wd_in, bo_in, ad_in, au_in,
    act, ig, out_a, out_b,
    SP, WQ, WO, WU, WD, H, DY, MID, GP, Q, KV, OT, LSE, SND, RCV, BIG, MSK, DR, DQ, AB, U, OACC, PB,
    GA, GB, GCA, GCB, GXA, GXB, GZA, GZB,
    tok_sem, tok_ys, tok_xs, wl, ws_r, ws_s, wy_r, wy_s, wz_r, wz_s, wa_r, wa_s, wb_r, wb_s,
    kv_rcv, kv_snd, x_rcv, x_snd, last_rcv, last_snd, dr_rcv, dr_snd, out_rcv, out_snd, gc_r, gc_s, gx_r, gx_s, gz_r, gz_s,
):
    s = lax.axis_index("section")
    d = lax.axis_index("dp")
    t = lax.axis_index("tensor")
    x = lax.rem(t, 2)
    y = lax.div(t, 2)
    sib = (1 - s, d, t)
    xp = (s, d, y * 2 + 1 - x)
    yp = (s, d, (1 - y) * 2 + x)
    z_half = lax.rem(d, 2)
    zp = (s, d + 1 - 2 * z_half, t)
    flip = s + x - 2 * s * x
    own_i = flip

    def blk_of(i):
        return 2 * i + (s + i - 2 * s * i)

    bar = pltpu.get_barrier_semaphore()
    for ds_ in range(2):
        for dx in range(2):
            for dy in range(2):
                if ds_ or dx or dy:
                    s2 = 1 - s if ds_ else s
                    x2 = 1 - x if dx else x
                    y2 = 1 - y if dy else y
                    pl.semaphore_signal(bar, 1, device_id=(s2, d, y2 * 2 + x2), device_id_type=MESH)
    for k in range(1, dp_count):
        pl.semaphore_signal(bar, 1, device_id=(s, lax.rem(d + k, dp_count), t), device_id_type=MESH)
    pl.semaphore_wait(bar, 7 + dp_count - 1)

    def row_copies(src, dst, w):
        def local():
            return pltpu.make_async_copy(src.at[y], dst.at[y], tok_sem.at[w, y])

        def to_y():
            return pltpu.make_async_remote_copy(
                src.at[1 - y], dst.at[y], tok_ys.at[w], tok_sem.at[w, y], device_id=yp, device_id_type=MESH)

        def first_x():
            return pltpu.make_async_remote_copy(
                src.at[y], dst.at[y], tok_xs.at[w], tok_sem.at[w, y], device_id=xp, device_id_type=MESH)

        def then_x():
            return pltpu.make_async_remote_copy(
                dst.at[own_i], dst.at[own_i], tok_xs.at[w], tok_sem.at[w, own_i],
                device_id=xp, device_id_type=MESH)

        return local, to_y, first_x, then_x

    def rows_first(src, dst, w):
        local, _, first_x, _ = row_copies(src, dst, w)

        @pl.when(y == own_i)
        def _():
            first_x().start()
            local().start()

    def rows_swap(src, dst, w):
        @pl.when(y == own_i)
        def _():
            row_copies(src, dst, w)[1]().start()

    def rows_relay(src, dst, w):
        pltpu.make_async_copy(src.at[0], dst.at[own_i], tok_sem.at[w, own_i]).wait()

        @pl.when(y != own_i)
        def _():
            row_copies(src, dst, w)[3]().start()

    def rows_rest(src, dst, w):
        pltpu.make_async_copy(src.at[0], dst.at[1 - own_i], tok_sem.at[w, 1 - own_i]).wait()

    def rows_done(src, dst, w):
        _, to_y, first_x, _ = row_copies(src, dst, w)
        if w == 0:
            first_x().wait_send()

        @pl.when(y == own_i)
        def _():
            to_y().wait_send()

    pieces = (None, (wq_in, WQ, 4), (wo_in, WO, 1), (wu_in, WU, 4), (wd_in, WD, 4))
    base = (13, 0, 4, 5, 9)

    def relayer(l, c):
        return 1 - l if c % 2 else l

    def sources(p, rows):
        src, dst, _ = pieces[p]
        if p == 1:
            return [
                (src.at[c, rows, :], dst.at[s, y, rows, c * 256 : c * 256 + 256]) for c in range(3)
            ]
        return [(src.at[0, rows, :], dst.at[s, y, rows, :])]

    def chunk(p, c, half):
        dst, parts = pieces[p][1], pieces[p][2]
        size = dst.shape[2] // (2 * parts)
        return pl.ds(pl.multiple_of((half * parts + c) * size, size), size)

    def block(p, l, j, rows):
        return pieces[p][1].at[l, j, rows, :]

    def own_start(p):
        everything = pl.ds(0, pieces[p][1].shape[2])
        for src, dst in sources(p, everything):
            pltpu.make_async_copy(src, dst, wl.at[p]).start()
            pltpu.make_async_remote_copy(
                src, dst, ws_s.at[p], ws_r.at[p], device_id=sib, device_id_type=MESH).start()

    def whole_by_y(l, p, c):
        return l == 0 and p == 4 and c >= 2

    def y_start(l, p):
        for c in range(pieces[p][2] if p else 1):
            k = base[p] + c

            @pl.when(s == relayer(l, c))
            def _():
                if p == 0:
                    ref = SP.at[l, y, 16:32, :]
                    pltpu.make_async_remote_copy(
                        ref, ref, wy_s.at[k], wy_r.at[k], device_id=yp, device_id_type=MESH).start()
                    return
                rows = chunk(p, c, z_half)
                mine = block(p, l, y, rows)
                for src, dst in [(mine, mine)] if c % 2 else sources(p, rows):
                    pltpu.make_async_remote_copy(
                        src, dst, wy_s.at[k], wy_r.at[k], device_id=yp, device_id_type=MESH).start()
                if whole_by_y(l, p, c):
                    rows = chunk(p, c, 1 - z_half)
                    mine = block(p, l, y, rows)
                    for src, dst in [(mine, mine)] if c % 2 else sources(p, rows):
                        pltpu.make_async_remote_copy(
                            src, dst, wz_s.at[k], wz_r.at[k], device_id=yp, device_id_type=MESH).start()

    def small_copy(to, snd, rcv):
        return pltpu.make_async_remote_copy(
            SP.at[s, y], SP.at[s, y], snd, rcv, device_id=to, device_id_type=MESH)

    def passed(l, p, c, half, to, snd, rcv):
        ref = SP.at[l, 1 - y, 16:32, :] if p == 0 else block(p, l, 1 - y, chunk(p, c, half))
        return pltpu.make_async_remote_copy(ref, ref, snd, rcv, device_id=to, device_id_type=MESH)

    def relay_y(l, p):
        for c in range(pieces[p][2] if p else 1):
            k = base[p] + c

            @pl.when(s == relayer(l, c))
            def _():
                passed(l, p, c, z_half, sib, wa_s.at[k], wy_r.at[k]).wait_recv()
                if p and not (p == 4 and c >= 2):
                    passed(l, p, c, z_half, zp, wz_s.at[k], wz_r.at[k]).start()

                if p == 4 and c >= 2:

                    @pl.when(l == 1)
                    def _():
                        passed(l, p, c, z_half, zp, wz_s.at[k], wz_r.at[k]).start()

                passed(l, p, c, z_half, sib, wa_s.at[k], wa_r.at[k]).start()

    def relay_z(l, p):
        for c in range(pieces[p][2]):
            k = base[p] + c

            @pl.when(s == relayer(l, c))
            def _():
                passed(l, p, c, 1 - z_half, zp, wz_s.at[k], wz_r.at[k]).wait_recv()
                passed(l, p, c, 1 - z_half, sib, wb_s.at[k], wb_r.at[k]).start()

    def own_wait(l, p):
        @pl.when(l == s)
        def _():
            if p:
                ref = pieces[p][1].at[s, y]
                pltpu.make_async_copy(ref, ref, wl.at[p]).wait()

        @pl.when(l != s)
        def _():
            ref = pieces[p][1].at[1 - s, y] if p else SP.at[1 - s, y]
            pltpu.make_async_copy(ref, ref, ws_r.at[p]).wait()

    def other_wait(l, p):
        for c in range(pieces[p][2] if p else 1):
            k = base[p] + c

            @pl.when(s != relayer(l, c))
            def _():
                if p == 0:
                    ref = SP.at[l, 1 - y, 16:32, :]
                    pltpu.make_async_copy(ref, ref, wa_r.at[13]).wait()
                else:
                    ref = block(p, l, 1 - y, chunk(p, c, 0))
                    pltpu.make_async_copy(ref, ref, wa_r.at[k]).wait()
                    pltpu.make_async_copy(ref, ref, wb_r.at[k]).wait()

    rows_swap(tok, H.at[0], 0)
    rows_first(tok, H.at[0], 0)
    own_start(1)
    SP[s, y] = jnp.zeros(SP.shape[2:], F32)
    for k, (ref, row) in enumerate(
        ((gain_in, 0), (shift_in, 0), (gain_in, 1), (shift_in, 1), (bo_in, 0), (bo_in, 1))
    ):
        SP[s, y, k : k + 1, :] = ref[0, row : row + 1, :].astype(F32)
    SP[s, y, 8:12, :] = ad_in[0, 0].astype(F32)
    SP[s, y, 12:16, :] = ad_in[0, 1].astype(F32)
    SP[s, y, 16:17, :] = bu_in[...].astype(F32)
    SP[s, y, 17:18, 0:256] = bqv_in[0, 0:1, :].astype(F32)
    SP[s, y, 17:18, 512:768] = bqv_in[0, 1:2, :].astype(F32)
    SP[s, y, 24:28, 0:256] = au_in[0, 0].astype(F32)
    SP[s, y, 28:32, 512:768] = au_in[0, 1].astype(F32)
    small_copy(sib, ws_s.at[0], ws_r.at[0]).start()
    y_start(0, 0)
    for p in range(2, 5):
        own_start(p)
    for l in range(2):
        for p in range(5):
            own_wait(l, p)
            if l or p:
                y_start(l, p)

    shift = 7 + buckets[y]
    span_mask = lax.shift_left(jnp.int32(1), shift) - 1

    def length_of(pos):
        item = lax.shift_right_logical(pos, jnp.broadcast_to(shift, pos.shape))
        got = jnp.zeros(pos.shape, jnp.int32)
        for k in range(lengths.shape[1]):
            got = jnp.where(item == k, lengths[y, k], got)
        return item, jnp.bitwise_and(pos, span_mask) < got

    def build_mask(i):
        b = blk_of(i)
        q_row = b * R + lax.broadcasted_iota(jnp.int32, (1, R), 1)
        q_item = lax.shift_right_logical(q_row, jnp.broadcast_to(shift, q_row.shape))

        def rows(r, carry):
            r0 = pl.multiple_of(r * CHUNK, CHUNK)
            k_row = r0 + lax.broadcasted_iota(jnp.int32, (CHUNK, 1), 0)
            k_item, k_ok = length_of(k_row)
            k_tag = jnp.where(k_ok, k_item, -1)
            same = (k_tag == q_item) & (k_row <= q_row)
            allowed = same | (k_row == q_row)
            MSK[pl.ds(pl.multiple_of(i * 2 * R + r0, CHUNK), CHUNK), :] = jnp.where(allowed, 0.0, NEG).astype(BF16)
            return carry

        lax.fori_loop(0, (b + 1) * (R // CHUNK), rows, 0)

    build_mask(0)
    build_mask(1)
    GA[...] = jnp.zeros(GA.shape, F32)
    GB[...] = jnp.zeros(GB.shape, F32)

    def x_copy(slot, i):
        return pltpu.make_async_remote_copy(
            SND.at[slot, i], RCV.at[slot * 2 + (i if slot < 2 else 0)], x_snd.at[slot, i], x_rcv.at[slot, i],
            device_id=xp, device_id_type=MESH)

    def last_copy(c, i):
        rows = slice(c * 64, c * 64 + 64)
        return pltpu.make_async_remote_copy(
            SND.at[0, i, rows, :], RCV.at[i, rows, :], last_snd.at[c], last_rcv.at[c],
            device_id=xp, device_id_type=MESH)

    def by_rows(body):
        body(slice(0, R))

    total_rows = slice(3 * R, 4 * R)

    def gather(n, term):
        for c in range(4):
            part = term[:, c * R : c * R + R]
            BIG[c, total_rows, :] = part if n == 0 else BIG[c, total_rows, :] + part

    def gathered():
        return jnp.concatenate([BIG[c, total_rows, :] for c in range(4)], axis=1).astype(BF16)

    def swapped(slot, i, rows):
        return SND[slot, i, rows, :].astype(F32) + RCV[slot * 2 + (i if slot < 2 else 0), rows, :].astype(F32)

    def send_result(which, layer, src, rows=slice(0, R)):
        src = src.at[rows, :]
        dst = act if which < 2 else ig
        o = 0 if which < 2 else 1
        here = (s == layer) & (y == own_i)

        @pl.when(here)
        def _():
            pltpu.make_async_copy(src, dst.at[y, rows, :], out_rcv.at[o, y]).start()

        @pl.when(jnp.logical_not(here))
        def _():
            pltpu.make_async_remote_copy(
                src, dst.at[y, rows, :], out_snd.at[which], out_rcv.at[o, y],
                device_id=(layer, d, own_i * 2 + x), device_id_type=MESH).start()

    def send_result_done(which, layer, src):
        dst = act if which < 2 else ig
        o = 0 if which < 2 else 1
        here = (s == layer) & (y == own_i)

        @pl.when(jnp.logical_not(here))
        def _():
            pltpu.make_async_remote_copy(
                src, dst.at[y], out_snd.at[which], out_rcv.at[o, y],
                device_id=(layer, d, own_i * 2 + x), device_id_type=MESH).wait_send()

    def vec(l, k):
        return SP[l, y, k : k + 1, :]

    def head_lanes(pair):
        return pl.ds(pl.multiple_of(pair * 128, 128), 128)

    def split_pair(v, axis):
        which = lax.broadcasted_iota(jnp.int32, v.shape, axis) < HEAD_DIM
        zero = jnp.zeros_like(v)
        return jnp.where(which, v, zero), jnp.where(which, zero, v)

    def kv_copy(l, i):
        rows = pl.ds(pl.multiple_of(blk_of(i) * R, R), R)
        return pltpu.make_async_remote_copy(
            KV.at[l, :, rows, :], KV.at[l, :, rows, :], kv_snd.at[l, i], kv_rcv.at[l, i],
            device_id=sib, device_id_type=MESH)

    def kv_wait(l, i):
        b = 2 * i + (1 - s + i - 2 * (1 - s) * i)
        rows = pl.ds(pl.multiple_of(b * R, R), R)
        pltpu.make_async_remote_copy(
            KV.at[l, :, rows, :], KV.at[l, :, rows, :], kv_snd.at[l, i], kv_rcv.at[l, i],
            device_id=sib, device_id_type=MESH).wait_recv()

    GROUP = 4

    def attend(l, i):
        b = blk_of(i)

        def group_turn(g, carry):
            def lanes_of(k):
                return pl.ds(pl.multiple_of(g * (GROUP * HEAD_DIM) + k * 128, 128), 128)

            def first(j, tops):
                rows = pl.ds(pl.multiple_of(j * R, R), R)
                mask = MSK[pl.ds(pl.multiple_of((i * 2 + j) * R, R), R), :].astype(F32)
                new = []
                for k in range(GROUP // 2):
                    qs = split_pair(Q[l, i, :, lanes_of(k)], 1)
                    keys = KV[l, 0, rows, lanes_of(k)]
                    for e in range(2):
                        st = nt(keys, qs[e]) + mask
                        BIG[2 * k + e, rows, :] = st
                        new.append(jnp.maximum(tops[2 * k + e], jnp.max(st, axis=0, keepdims=True)))
                return tuple(new)

            tops = lax.fori_loop(0, b + 1, first, (jnp.full((1, R), NEG, F32),) * GROUP)
            for k in range(GROUP):
                OACC[k] = jnp.zeros(OACC.shape[1:], F32)

            def second(j, sums):
                rows = pl.ds(pl.multiple_of(j * R, R), R)
                new = []
                for k in range(GROUP):
                    p = jnp.exp(BIG[k, rows, :] - tops[k])
                    new.append(sums[k] + jnp.sum(p, axis=0, keepdims=True))
                    PB[k] = p.astype(BF16)
                for k in range(GROUP // 2):
                    values = jnp.transpose(KV[l, 1, rows, lanes_of(k)])
                    for e in range(2):
                        OACC[2 * k + e] += nn(values[e * 64 : e * 64 + 64], PB[2 * k + e])
                return tuple(new)

            sums = lax.fori_loop(0, b + 1, second, (jnp.zeros((1, R), F32),) * GROUP)
            for k in range(GROUP):
                OT[l, i, pl.ds(pl.multiple_of((g * GROUP + k) * 64, 64), 64), :] = (
                    OACC[k] * (1.0 / sums[k])
                ).astype(BF16)
                LSE[l, i, g * GROUP + k] = tops[k] + jnp.log(sums[k])
            return carry

        lax.fori_loop(0, Q.shape[3] // (GROUP * HEAD_DIM), group_turn, 0)

    def forward_attention(l, i):
        b = blk_of(i)

        @pl.when(i == 0)
        def _():
            @pl.when(l == 0)
            def _():
                rows_relay(tok, H.at[0], 0)
                relay_y(l, 0)
                relay_y(l, 1)
                rows_first(cot, DY, 1)

                @pl.when(own_i == 1)
                def _():
                    rows_rest(tok, H.at[0], 0)

            other_wait(l, 0)
            relay_z(l, 1)

            @pl.when(l == 1)
            def _():
                relay_y(l, 2)
                relay_y(l, 3)

            other_wait(l, 1)

        @pl.when(i == 1)
        def _():
            @pl.when((l == 0) & (own_i == 0))
            def _():
                rows_rest(tok, H.at[0], 0)


        @pl.when(l == 1)
        def _():
            x_copy(1, i).wait_recv()

            def rows_in(rows):
                h = MID[0, i, rows, :] + (swapped(1, i, rows) + vec(0, 5))
                H[1, i, rows, :] = h.astype(BF16)

            by_rows(rows_in)

            @pl.when(i == own_i)
            def _():
                send_result(0, 0, H.at[1, i])

        def rows_norm(rows):
            xhat, _ = normalize(H[l, i, rows, :].astype(F32))
            AB[rows, :] = (xhat * vec(l, 0) + vec(l, 1)).astype(BF16)

        by_rows(rows_norm)
        u = nt(AB[...], SP[l, y, 8:16, :].astype(BF16)).astype(BF16)
        own_rows = pl.ds(pl.multiple_of(b * R, R), R)
        for j in range(2):
            up = SP[l, j, 24:32, 256:768].astype(BF16)
            cols = slice(j * 256, j * 256 + 256)
            pair = nn(AB[...], WQ[l, j, :, 256:768]) + (adapter_scale * nn(u, up) + SP[l, j, 17:18, 256:768])
            KV[l, 0, own_rows, cols] = pair[:, 0:256].astype(BF16)
            KV[l, 1, own_rows, cols] = pair[:, 256:512].astype(BF16)

        @pl.when(b != 3)
        def _():
            kv_copy(l, i).start()

        for j in range(2):
            up = SP[l, j, 24:32, 0:256].astype(BF16)
            q = nn(AB[...], WQ[l, j, :, 0:256]) + (adapter_scale * nn(u, up) + SP[l, j, 17:18, 0:256])
            Q[l, i, :, j * 256 : j * 256 + 256] = (q * HEAD_DIM ** -0.5).astype(BF16)
        U[l, i] = nt(SP[l, y, 8:16, :].astype(BF16), AB[...]).astype(BF16)

        @pl.when((s == 1) & (i == 0))
        def _():
            kv_wait(l, 0)

        @pl.when((s == 0) & (i == 1))
        def _():
            kv_wait(l, 0)
            kv_wait(l, 1)

        @pl.when((i == 0) & (l == 0))
        def _():
            relay_y(l, 2)

        @pl.when(i == 1)
        def _():
            @pl.when(l == 0)
            def _():
                relay_y(l, 3)

            @pl.when(l == 1)
            def _():
                relay_y(l, 4)

        attend(l, i)

        @pl.when(i == 0)
        def _():
            relay_z(l, 2)
            other_wait(l, 2)

        @pl.when(l == 1)
        def _():
            x_copy(0, i).wait_send()

        SND[0, i] = (tn(OT[l, i, 0:256, :], WO[l, 0]) + tn(OT[l, i, 256:512, :], WO[l, 1])).astype(BF16)
        x_copy(0, i).start()

    def forward_ff(l, i):
        @pl.when((i == 0) & (l == 0))
        def _():
            relay_y(l, 4)

        @pl.when((i == 1) & (l == 0))
        def _():
            rows_swap(cot, DY, 1)

        @pl.when((i == 1) & (l == 1))
        def _():
            rows_relay(cot, DY, 1)

        x_copy(0, i).wait_recv()

        def rows_mid(rows):
            mid = H[l, i, rows, :].astype(F32) + (swapped(0, i, rows) + vec(l, 4))
            MID[l, i, rows, :] = mid
            xhat, _ = normalize(mid)
            AB[rows, :] = (xhat * vec(l, 2) + vec(l, 3)).astype(BF16)

        by_rows(rows_mid)
        for n in range(4):
            j, half = (y if n < 2 else 1 - y), n % 2
            cols = slice(half * 512, half * 512 + 512)
            if n == 2:

                @pl.when(i == 0)
                def _():
                    relay_z(l, 3)
                    relay_z(l, 4)
                    other_wait(l, 3)
                    other_wait(l, 4)

            z = nn(AB[...], WU[l, j, :, cols]) + SP[l, j, 16:17, cols]
            g, slope = gelu_pair(z)
            GP[l, i, :, n * 512 : n * 512 + 512] = slope.astype(BF16)
            term = nn(g.astype(BF16), WD[l, j, cols, :])
            gather(n, term)
        SND[1 + l, i] = gathered()

        @pl.when(l == 0)
        def _():
            x_copy(1, i).start()

            @pl.when(i == 1)
            def _():
                relay_y(1, 0)
                relay_y(1, 1)

        @pl.when((l == 1) & (i != own_i))
        def _():
            x_copy(2, i).start()

    def fwd_layer(l, carry):
        def a_turn(i, c):
            forward_attention(l, i)
            return c

        def f_turn(i, c):
            forward_ff(l, i)
            return c

        lax.fori_loop(0, 2, a_turn, 0)
        lax.fori_loop(0, 2, f_turn, 0)
        return carry

    lax.fori_loop(0, 2, fwd_layer, 0)

    def finish_forward():
        x_copy(2, own_i).wait_recv()

        def rows_out(rows):
            out = MID[1, own_i, rows, :] + (swapped(2, own_i, rows) + vec(1, 5))
            SND[2, own_i, rows, :] = out.astype(BF16)

        by_rows(rows_out)
        send_result(1, 1, SND.at[2, own_i])

    def backward_ff(l, i):
        @pl.when(l == 1)
        def _():
            @pl.when(i == own_i)
            def _():
                row_copies(cot, DY, 1)[3]().wait_send()

            @pl.when(i != own_i)
            def _():
                rows_rest(cot, DY, 1)

            def rows_valid(rows):
                pos = blk_of(i) * R + lax.broadcasted_iota(jnp.int32, (R, 1), 0)
                _, ok = length_of(pos)
                DY[i, rows, :] = (DY[i, rows, :].astype(F32) * jnp.where(ok, 1.0, 0.0)).astype(BF16)

            by_rows(rows_valid)

        @pl.when(l == 0)
        def _():
            x_copy(0, i).wait_recv()

            def rows_in(rows):
                g = swapped(0, i, rows) * vec(1, 0)
                DY[i, rows, :] = (MID[1, i, rows, :] + norm_pull(H[1, i, rows, :].astype(F32), g)).astype(BF16)

            by_rows(rows_in)

            @pl.when(i == own_i)
            def _():
                send_result(2, 1, DY.at[i])

        for n in range(4):
            j, half = (y if n < 2 else 1 - y), n % 2
            cols = slice(half * 512, half * 512 + 512)
            dg = nt(DY[i], WD[l, j, cols, :])
            dz = (GP[l, i, :, n * 512 : n * 512 + 512].astype(F32) * dg).astype(BF16)
            term = nt(dz, WU[l, j, :, cols])
            gather(n, term)

        x_copy(1, i).wait_send()
        SND[1, i] = gathered()
        x_copy(1, i).start()

    def dr_copy(k, b):
        rows = pl.ds(pl.multiple_of(b * R, R), R)
        return pltpu.make_async_remote_copy(
            BIG.at[:, rows, :], DR.at[k], dr_snd.at[k], dr_rcv.at[k], device_id=sib, device_id_type=MESH)

    def attend_back(l, i):
        b = blk_of(i)
        pairs = Q.shape[3] // 128
        place = RCV.at[2 + i]

        def back_rows(k):
            return place[(k % 2) * 128 : (k % 2) * 128 + 128, 512 + (k // 2) * 256 : 768 + (k // 2) * 256]

        deltas = []
        for k in range(pairs):
            rows = slice(k * 128, k * 128 + 128)
            prod = back_rows(k).astype(F32) * OT[l, i, rows, :].astype(F32)
            deltas.append(jnp.sum(prod[0:64], axis=0, keepdims=True))
            deltas.append(jnp.sum(prod[64:128], axis=0, keepdims=True))
            OACC[2 * k] = jnp.zeros(OACC.shape[1:], F32)
            OACC[2 * k + 1] = jnp.zeros(OACC.shape[1:], F32)

        def turn(j, c):
            rows = pl.ds(pl.multiple_of(j * R, R), R)
            mask = MSK[pl.ds(pl.multiple_of((i * 2 + j) * R, R), R), :].astype(F32)
            for k in range(pairs):
                lanes = slice(k * 128, k * 128 + 128)
                qs = split_pair(Q[l, i, :, lanes], 1)
                dots = split_pair(back_rows(k), 0)
                keys = KV[l, 0, rows, lanes]
                values = KV[l, 1, rows, lanes]
                for e in range(2):
                    h = 2 * k + e
                    p = jnp.exp(nt(keys, qs[e]) + mask - LSE[l, i, h])
                    dp = nn(values, dots[e])
                    PB[h] = (p * (dp - deltas[h])).astype(BF16)
                    PB[2 * pairs + h] = p.astype(BF16)
            for k in range(pairs):
                lanes = slice(k * 128, k * 128 + 128)
                half = slice((k % 2) * 128, (k % 2) * 128 + 128)
                qs = split_pair(Q[l, i, :, lanes], 1)
                dos = split_pair(place[:, lanes], 1)
                h = 2 * k
                BIG[k // 2, rows, half] += nn(PB[h], qs[0]) + nn(PB[h + 1], qs[1])
                BIG[2 + k // 2, rows, half] += nn(PB[2 * pairs + h], dos[0]) + nn(PB[2 * pairs + h + 1], dos[1])
            for k in range(pairs):
                keys = jnp.transpose(KV[l, 0, rows, k * 128 : k * 128 + 128])
                for e in range(2):
                    OACC[2 * k + e] += nn(keys[e * 64 : e * 64 + 64], PB[2 * k + e])
            for k in range(2):

                @pl.when((s == 0) & (i == 1) & (j == k + 1))
                def _():
                    dr_copy(k, k + 1).start()

            return c

        lax.fori_loop(0, b + 1, turn, 0)
        for k in range(pairs):
            dq = jnp.concatenate([OACC[2 * k], OACC[2 * k + 1]], axis=0) * HEAD_DIM ** -0.5
            DQ[k // 2, :, (k % 2) * 128 : (k % 2) * 128 + 128] = jnp.transpose(dq).astype(BF16)

    def backward_attention(l, i):
        b = blk_of(i)
        x_copy(1, i).wait_recv()

        def rows_mid(rows):
            g = swapped(1, i, rows) * vec(l, 2)
            dmid = DY[i, rows, :].astype(F32) + norm_pull(MID[l, i, rows, :], g)
            MID[l, i, rows, :] = dmid
            AB[rows, :] = dmid.astype(BF16)

        by_rows(rows_mid)
        for j in range(2):
            RCV[2 + i, :, 512 + j * 256 : 768 + j * 256] = nt(WO[l, j], AB[...]).astype(BF16)
            RCV[2 + i, :, j * 256 : j * 256 + 256] = nt(AB[...], WO[l, j]).astype(BF16)

        @pl.when(i == 1)
        def _():
            @pl.when(l == 0)
            def _():
                @pl.when(s == 0)
                def _():
                    dr_copy(0, 1).wait_send()
                    dr_copy(1, 2).wait_send()

                @pl.when(s == 1)
                def _():
                    dr_copy(0, 0).wait_send()

            def clear(r, c):
                rows = pl.ds(pl.multiple_of(r * R, R), R)
                BIG[:, rows, :] = jnp.zeros((4, R, 256), F32)
                return c

            lax.fori_loop(0, 4, clear, 0)

        attend_back(l, i)
        own = pl.ds(pl.multiple_of(b * R, R), R)

        def rows_norm(rows):
            xhat, _ = normalize(H[l, i, rows, :].astype(F32))
            AB[rows, :] = (xhat * vec(l, 0) + vec(l, 1)).astype(BF16)

        by_rows(rows_norm)

        @pl.when(b != 3)
        def _():
            def add(k):
                dr_copy(k, b).wait_recv()
                for c in range(4):
                    BIG[c, own, :] += DR[k, c]

            @pl.when(s == 1)
            def _():
                add(i)

            @pl.when((s == 1) & (i == 0))
            def _():
                dr_copy(0, 0).start()

            @pl.when(s == 0)
            def _():
                add(0)

        for j in range(2):
            DQ[j, :, 256:512] = BIG[j, own, :].astype(BF16)
            DQ[j, :, 512:768] = BIG[2 + j, own, :].astype(BF16)

        ups = [SP[l, j, 24:32, 0:768].astype(BF16) for j in range(2)]
        du = (adapter_scale * (nt(ups[0], DQ[0]) + nt(ups[1], DQ[1]))).astype(BF16)
        GA[l] += nn(du, AB[...])
        top = lax.broadcasted_iota(jnp.int32, (8, 256), 0) < 4
        for j in range(2):
            gq = nn(U[l, i], DQ[j, :, 0:256])
            gv = nn(U[l, i], DQ[j, :, 512:768])
            GB[l, j] += adapter_scale * jnp.where(top, gq, gv)

        x_copy(0, i).wait_send()
        SND[0, i] = (
            nt(DQ[0], WQ[l, 0]) + nt(DQ[1], WQ[l, 1]) + tn(du, SP[l, y, 8:16, :].astype(BF16))
        ).astype(BF16)

        @pl.when(l == 1)
        def _():
            x_copy(0, i).start()

        @pl.when((l == 0) & (i != own_i))
        def _():
            for c in range(4):
                last_copy(c, i).start()

    def core_copies(l):
        return (
            pltpu.make_async_remote_copy(
                GA.at[l], GCA, gc_s.at[0], gc_r.at[0], device_id=sib, device_id_type=MESH),
            pltpu.make_async_remote_copy(
                GB.at[l], GCB, gc_s.at[1], gc_r.at[1], device_id=sib, device_id_type=MESH),
        )

    def plane_copies(l):
        out = []
        for k, (dx, dy) in enumerate(((1, 0), (0, 1), (1, 1))):
            x2 = 1 - x if dx else x
            y2 = 1 - y if dy else y
            to = (s, d, y2 * 2 + x2)
            out.append(pltpu.make_async_remote_copy(
                GA.at[l], GXA.at[k], gx_s.at[k], gx_r.at[k], device_id=to, device_id_type=MESH))
        out.append(pltpu.make_async_remote_copy(
            GB.at[l, 1 - y], GXB, gx_s.at[3], gx_r.at[3], device_id=yp, device_id_type=MESH))
        return out

    def line_copies():
        out = []
        for k in range(1, dp_count):
            to = (s, lax.rem(d + k, dp_count), t)
            out.append(pltpu.make_async_remote_copy(
                GZA.at[d], GZA.at[d], gz_s.at[0, k - 1], gz_r.at[0, k - 1], device_id=to, device_id_type=MESH))
            out.append(pltpu.make_async_remote_copy(
                GZB.at[d], GZB.at[d], gz_s.at[1, k - 1], gz_r.at[1, k - 1], device_id=to, device_id_type=MESH))
        return out

    def sum_core(l):
        @pl.when(s != l)
        def _():
            for c in core_copies(l):
                c.start()

    def sum_plane(l):
        @pl.when(s == l)
        def _():
            for c in core_copies(l):
                c.wait_recv()
            GA[l] += GCA[...]
            GB[l] += GCB[...]
            for c in plane_copies(l):
                c.start()

    def sum_line(l):
        @pl.when(s == l)
        def _():
            for c in plane_copies(l):
                c.wait_recv()
            GZA[d] = (GA[l] + GXA[0]) + (GXA[1] + GXA[2])
            GZB[d] = GB[l, y] + GXB[...]
            for c in line_copies():
                c.start()

    def sum_end(l):
        @pl.when(s == l)
        def _():
            for c in line_copies():
                c.wait_recv()
            total_a, total_b = GZA[0], GZB[0]
            for k in range(1, dp_count):
                total_a, total_b = total_a + GZA[k], total_b + GZB[k]
            out_a[0, 0] = total_a[0:4]
            out_a[0, 1] = total_a[4:8]
            out_b[0, 0] = total_b[0:4]
            out_b[0, 1] = total_b[4:8]

    def bwd_layer(back, carry):
        l = 1 - back

        def f_turn(k, c):
            @pl.when((l == 0) & (k == 1))
            def _():
                sum_plane(1)

            backward_ff(l, 1 - k)
            return c

        def a_turn(k, c):
            @pl.when((l == 0) & (k == 0))
            def _():
                sum_line(1)

            @pl.when((l == 0) & (k == 1))
            def _():
                sum_end(1)

            backward_attention(l, 1 - k)
            return c

        lax.fori_loop(0, 2, f_turn, 0)

        @pl.when(l == 1)
        def _():
            finish_forward()

        lax.fori_loop(0, 2, a_turn, 0)
        sum_core(l)
        return carry

    lax.fori_loop(0, 2, bwd_layer, 0)
    sum_plane(0)

    for c in range(4):
        last_copy(c, own_i).wait_recv()
        rows = slice(c * 64, c * 64 + 64)
        g = swapped(0, own_i, rows) * vec(0, 0)
        AB[rows, :] = (MID[0, own_i, rows, :] + norm_pull(H[0, own_i, rows, :].astype(F32), g)).astype(BF16)
        send_result(3, 0, AB, rows)
    sum_line(0)

    for c in range(4):
        last_copy(c, 1 - own_i).wait_send()
    for i in range(2):
        x_copy(1, i).wait_send()
    x_copy(2, 1 - own_i).wait_send()
    def sent(ref, sem):
        pltpu.make_async_remote_copy(ref, ref, sem, sem, device_id=sib, device_id_type=MESH).wait_send()

    for p in range(5):
        sent(pieces[p][1].at[s, y] if p else SP.at[s, y], ws_s.at[p])
        for c in range(pieces[p][2] if p else 1):
            k = base[p] + c
            ref = block(p, s, y, chunk(p, c, 0)) if p else SP.at[s, y, 16:32, :]
            sent(ref, wy_s.at[k])
            sent(ref, wa_s.at[k])
            if p:
                sent(ref, wz_s.at[k])
                sent(ref, wb_s.at[k])
    rows_done(tok, H.at[0], 0)
    rows_done(cot, DY, 1)
    for l in range(2):
        kv_copy(l, 0).wait_send()

        @pl.when(s == 1)
        def _():
            kv_copy(l, 1).wait_send()

    @pl.when(s == 0)
    def _():
        dr_copy(0, 1).wait_send()
        dr_copy(1, 2).wait_send()

    @pl.when(s == 1)
    def _():
        dr_copy(0, 0).wait_send()

    @pl.when(s == 0)
    def _():
        for c in core_copies(1) + tuple(plane_copies(0)) + tuple(line_copies()):
            c.wait_send()

    @pl.when(s == 1)
    def _():
        for c in core_copies(0) + tuple(plane_copies(1)) + tuple(line_copies()):
            c.wait_send()

    send_result_done(0, 0, H.at[1, 0])
    send_result_done(1, 1, H.at[1, 0])
    send_result_done(2, 1, H.at[1, 0])
    send_result_done(3, 0, H.at[1, 0])
    for o, ref in ((0, act), (1, ig)):
        for m in range(2):
            pltpu.make_async_copy(tok.at[0], ref.at[m], out_rcv.at[o, m]).wait()
    sum_end(0)


def copy_kernel(a_in, g_in, ta_in, tb_in, a_out, g_out, ta_out, tb_out, held_a, held_g, held_ta, held_tb, load, store):
    moves = []
    for k, (src, held, dst) in enumerate(((a_in, held_a, a_out), (g_in, held_g, g_out))):
        for m in range(src.shape[0]):
            moves.append((src.at[m], held.at[m], dst.at[0, m], 2 * k + m))
    moves.append((ta_in, held_ta, ta_out, 4))
    moves.append((tb_in, held_tb, tb_out, 5))
    for src, held, dst, k in moves:
        pltpu.make_async_copy(src, held, load.at[k]).start()
    for src, held, dst, k in moves:
        pltpu.make_async_copy(src, held, load.at[k]).wait()
        pltpu.make_async_copy(held, dst, store.at[k]).start()
    for src, held, dst, k in moves:
        pltpu.make_async_copy(held, dst, store.at[k]).wait()


def settle(act, ig, total_a, total_b):
    anywhere = pl.BlockSpec(memory_space=pl.ANY)
    shapes = [(1,) + act.shape, (1,) + ig.shape, total_a.shape, total_b.shape]
    kinds = [act.dtype, ig.dtype, total_a.dtype, total_b.dtype]
    return pl.pallas_call(
        copy_kernel,
        out_shape=tuple(jax.ShapeDtypeStruct(a, b) for a, b in zip(shapes, kinds)),
        in_specs=[anywhere] * 4,
        out_specs=(anywhere,) * 4,
        scratch_shapes=[
            pltpu.VMEM(v.shape, v.dtype) for v in (act, ig, total_a, total_b)
        ] + [pltpu.SemaphoreType.DMA((6,))] * 2,
        name="settle",
    )(act, ig, total_a, total_b)


def per_pair(
    tokens, cotangent, buckets, lengths, norm_gain_pairs, norm_bias_pairs, query_key_value_weight,
    query_value_bias, output_weight, upward_weight, upward_bias, down_weight, output_bias,
    adapter_down, adapter_upper,
):
    weight_qkv = query_key_value_weight[0].transpose(1, 0, 2)
    dp_count = lax.axis_size("dp")
    anywhere = pl.BlockSpec(memory_space=pl.ANY)
    scalars = pl.BlockSpec(memory_space=pltpu.SMEM)
    vmem = pl.BlockSpec(memory_space=pltpu.VMEM)
    dma = pltpu.SemaphoreType.DMA
    act, ig, total_a, total_b = pl.pallas_call(
        partial(fused_kernel, dp_count),
        out_shape=(
            jax.ShapeDtypeStruct((2, R, D), BF16),
            jax.ShapeDtypeStruct((2, R, D), BF16),
            jax.ShapeDtypeStruct((1, 2, 4, D), F32),
            jax.ShapeDtypeStruct((1, 2, 4, 256), F32),
        ),
        in_specs=[anywhere, anywhere, scalars, scalars, vmem, vmem, anywhere, vmem, anywhere, anywhere, vmem,
                  anywhere, vmem, vmem, vmem],
        out_specs=(anywhere, anywhere, vmem, vmem),
        scratch_shapes=[
            pltpu.VMEM((2, 2, 32, D), F32),
            pltpu.VMEM((2, 2, D, 768), BF16),
            pltpu.VMEM((2, 2, 256, D), BF16),
            pltpu.VMEM((2, 2, D, 1024), BF16),
            pltpu.VMEM((2, 2, 1024, D), BF16),
            pltpu.VMEM((2, 2, R, D), BF16),
            pltpu.VMEM((2, R, D), BF16),
            pltpu.VMEM((2, 2, R, D), F32),
            pltpu.VMEM((2, 2, R, 2048), BF16),
            pltpu.VMEM((2, 2, R, 512), BF16),
            pltpu.VMEM((2, 2, 4 * R, 512), BF16),
            pltpu.VMEM((2, 2, 512, R), BF16),
            pltpu.VMEM((2, 2, 8, 1, R), F32),
            pltpu.VMEM((3, 2, R, D), BF16),
            pltpu.VMEM((5, R, D), BF16),
            pltpu.VMEM((4, 4 * R, R), F32),
            pltpu.VMEM((6 * R, R), BF16),
            pltpu.VMEM((2, 4, R, R), F32),
            pltpu.VMEM((2, R, 768), BF16),
            pltpu.VMEM((R, D), BF16),
            pltpu.VMEM((2, 2, 8, R), BF16),
            pltpu.VMEM((8, 64, R), F32),
            pltpu.VMEM((16, R, R), BF16),
            pltpu.VMEM((2, 8, D), F32),
            pltpu.VMEM((2, 2, 8, 256), F32),
            pltpu.VMEM((8, D), F32),
            pltpu.VMEM((2, 8, 256), F32),
            pltpu.VMEM((3, 8, D), F32),
            pltpu.VMEM((8, 256), F32),
            pltpu.VMEM((dp_count, 8, D), F32),
            pltpu.VMEM((dp_count, 8, 256), F32),
            dma((2, 2)),
            dma((2,)),
            dma((2,)),
            dma((5,)),
            dma((5,)),
            dma((5,)),
            dma((14,)),
            dma((14,)),
            dma((13,)),
            dma((13,)),
            dma((14,)),
            dma((14,)),
            dma((13,)),
            dma((13,)),
            dma((2, 2)),
            dma((2, 2)),
            dma((3, 2)),
            dma((3, 2)),
            dma((4,)),
            dma((4,)),
            dma((2,)),
            dma((2,)),
            dma((2, 2)),
            dma((4,)),
            dma((2,)),
            dma((2,)),
            dma((4,)),
            dma((4,)),
            dma((2, dp_count - 1)),
            dma((2, dp_count - 1)),
        ],
        compiler_params=pltpu.CompilerParams(
            collective_id=0, has_side_effects=True, vmem_limit_bytes=127 * 2**19
        ),
        name="two_layers",
    )(
        tokens, cotangent, buckets, lengths, norm_gain_pairs, norm_bias_pairs, weight_qkv, query_value_bias,
        output_weight, upward_weight, upward_bias, down_weight, output_bias, adapter_down, adapter_upper,
    )
    return settle(act, ig, total_a, total_b)


def solution(mesh):
    in_specs = (
        P("dp", "tensor", None),
        P("dp", "tensor", None),
        P("dp"),
        P("dp", None),
        P("section", None, None),
        P("section", None, None),
        P("section", None, None, "tensor"),
        P("section", None, "tensor"),
        P("section", "tensor", None),
        P("section", None, "tensor"),
        P("section", "tensor"),
        P("section", "tensor", None),
        P("section", None, None),
        P("section", None, None, None),
        P("section", None, None, "tensor"),
    )
    out_specs = (
        P("section", "dp", "tensor", None),
        P("section", "dp", "tensor", None),
        P("section", None, None, None),
        P("section", None, None, "tensor"),
    )
    pairs = mesh.shape["section"] == 2 and mesh.shape["tensor"] == 4 and mesh.shape["dp"] % 2 == 0
    return jax.shard_map(
        per_pair if pairs else per_device, mesh=mesh, in_specs=in_specs, out_specs=out_specs, check_vma=False
    )
```

```python
from functools import partial

import jax
import jax.numpy as jnp
from jax import lax
from jax.experimental import pallas as pl
from jax.experimental.pallas import tpu as pltpu
from jax.sharding import PartitionSpec as P

HEAD_DIM = 64


adapter_scale = 8.0
norm_eps = 1e-05
masked_score = -1000000000.0
highest_precision = lax.Precision.HIGHEST


def from_behind(block, axis, distance):
    devices = range(lax.axis_size(axis))
    route = [(i - distance, i) for i in devices if i - distance in devices]
    return lax.ppermute(block, axis, route)


def layer_norm(values, gain_rows, shifts):
    center = jnp.mean(values, axis=-1, keepdims=True)
    centered = values - center
    spread = jnp.mean(centered * centered, axis=-1, keepdims=True)
    return centered * lax.rsqrt(spread + norm_eps) * gain_rows + shifts


def row_layout(bucket, lengths_row, row_count):
    item_span = jnp.right_shift(jnp.int32(row_count), 3 - bucket)
    positions = jnp.arange(row_count, dtype=jnp.int32)
    item_index = positions // item_span
    within = positions - item_index * item_span
    chosen = (
        item_index[:, None] == jnp.arange(lengths_row.shape[0], dtype=jnp.int32)[None, :]
    ).astype(jnp.int32)
    length = jnp.sum(chosen * lengths_row[None, :], axis=1)
    return (item_index, within < length)


def allowed_keys(item_index, is_valid):
    positions = jnp.arange(item_index.shape[0], dtype=jnp.int32)
    same_item = item_index[:, None] == item_index[None, :]
    causal = positions[None, :] <= positions[:, None]
    key_seen = is_valid[None, :] | (positions[None, :] == positions[:, None])
    return same_item & causal & key_seen


def take_slot(buffer, slot_index):
    return lax.dynamic_index_in_dim(buffer, slot_index, 0, keepdims=False)


def put_slot(buffer, slot_index, is_live, update):
    previous = take_slot(buffer, slot_index)
    return lax.dynamic_update_index_in_dim(
        buffer, jnp.where(is_live, update, previous), slot_index, 0
    )


def per_device(
    tokens,
    cotangent,
    buckets,
    lengths,
    norm_gain_pairs,
    norm_bias_pairs,
    query_key_value_weight,
    query_value_bias,
    output_weight,
    upward_weight,
    upward_bias,
    down_weight,
    output_bias,
    adapter_down,
    adapter_upper,
):
    section_index = lax.axis_index("section")
    tensor_count = lax.axis_size("tensor")
    micro_count, own_rows, model_width = tokens.shape
    row_count = own_rows * tensor_count
    own_start = lax.axis_index("tensor") * own_rows
    gain_sets = norm_gain_pairs[0].astype(jnp.float32)
    shift_sets = norm_bias_pairs[0].astype(jnp.float32)
    weight_qkv = query_key_value_weight[0]
    bias_query_value = query_value_bias[0].astype(jnp.float32)
    weight_out = output_weight[0]
    weight_up = upward_weight[0]
    bias_up = upward_bias[0].astype(jnp.float32)
    weight_down = down_weight[0]
    biases = output_bias[0].astype(jnp.float32)
    down_factor = adapter_down[0]
    upper_factor = adapter_upper[0]
    factor_wide = down_factor.astype(jnp.float32)
    local_width = weight_qkv.shape[2]
    local_heads = local_width // HEAD_DIM
    score_scale = HEAD_DIM ** (-0.5)

    def widen(values):
        return lax.all_gather(values, "tensor", axis=0, tiled=True)

    def widen_back(values):
        return lax.all_gather(values, "tensor", axis=0, tiled=True)

    def settle(source, weight):

        def row_term(first_row, row_span):
            return jnp.dot(source, weight, preferred_element_type=jnp.float32)

        return lax.psum_scatter(
            row_term(jnp.int32(0), lax.axis_size("tensor") * own_rows).astype(jnp.bfloat16),
            "tensor",
            scatter_dimension=0,
            tiled=True,
        ).astype(jnp.float32)

    def settle_back(row_term):
        return lax.psum_scatter(
            row_term(jnp.int32(0), lax.axis_size("tensor") * own_rows).astype(jnp.bfloat16),
            "tensor",
            scatter_dimension=0,
            tiled=True,
        ).astype(jnp.float32)

    def layout_of(slot_index):
        item_index, is_valid = row_layout(
            take_slot(buckets, slot_index), take_slot(lengths, slot_index), row_count
        )
        own_valid = lax.dynamic_slice_in_dim(is_valid, own_start, own_rows, 0)
        return (allowed_keys(item_index, is_valid), own_valid)

    def attend(normed, allowed):
        reduced_query = jnp.dot(
            normed, down_factor[0].T, preferred_element_type=jnp.float32
        ).astype(jnp.bfloat16)
        reduced_value = jnp.dot(
            normed, down_factor[1].T, preferred_element_type=jnp.float32
        ).astype(jnp.bfloat16)
        blended_rows = jnp.einsum(
            "rd,dcn->rcn", normed, weight_qkv, preferred_element_type=jnp.float32
        )
        query_matrix_rows = (
            blended_rows[:, 0]
            + bias_query_value[0]
            + adapter_scale
            * jnp.dot(reduced_query, upper_factor[0], preferred_element_type=jnp.float32)
        )
        value_matrix_rows = (
            blended_rows[:, 2]
            + bias_query_value[1]
            + adapter_scale
            * jnp.dot(reduced_value, upper_factor[1], preferred_element_type=jnp.float32)
        )
        packed = jnp.stack(
            [query_matrix_rows, blended_rows[:, 1], value_matrix_rows], axis=1
        ).astype(jnp.bfloat16)
        head_split = packed.reshape(row_count, 3, local_heads, HEAD_DIM)
        scores = (
            jnp.einsum(
                "qhe,khe->hqk",
                head_split[:, 0],
                head_split[:, 1],
                preferred_element_type=jnp.float32,
            )
            * score_scale
        )
        scores = jnp.where(allowed[None], scores, masked_score)
        top_score = jnp.max(scores, axis=-1, keepdims=True)
        exponent = jnp.exp(scores - top_score)
        attn_probs = exponent / jnp.sum(exponent, axis=-1, keepdims=True)
        return (reduced_query, reduced_value, head_split, attn_probs)

    def forward(hidden, allowed):
        normed = widen(layer_norm(hidden, gain_sets[0], shift_sets[0]).astype(jnp.bfloat16))
        reduced_query, reduced_value, head_split, attn_probs = attend(normed, allowed)
        probs_low = attn_probs.astype(jnp.bfloat16)
        mixed_heads = jnp.einsum(
            "hqk,khe->qhe", probs_low, head_split[:, 2], preferred_element_type=jnp.float32
        )
        attended = mixed_heads.reshape(row_count, local_width).astype(jnp.bfloat16)
        middle = hidden + (settle(attended, weight_out) + biases[0])
        normed_two = widen(layer_norm(middle, gain_sets[1], shift_sets[1]).astype(jnp.bfloat16))
        hidden_pre = jnp.dot(normed_two, weight_up, preferred_element_type=jnp.float32) + bias_up
        activated = jax.nn.gelu(hidden_pre, approximate=True).astype(jnp.bfloat16)
        output = middle + (settle(activated, weight_down) + biases[1])
        return (output, normed, middle, normed_two)

    def backward(hidden, grad_out, allowed, normed, middle, normed_two):
        reduced_query, reduced_value, head_split, attn_probs = attend(normed, allowed)
        probs_low = attn_probs.astype(jnp.bfloat16)
        hidden_pre = jnp.dot(normed_two, weight_up, preferred_element_type=jnp.float32) + bias_up
        grad_branch = widen_back(grad_out.astype(jnp.bfloat16))
        grad_act = jnp.einsum(
            "rd,fd->rf", grad_branch, weight_down, preferred_element_type=jnp.float32
        )
        gelu_pull = jax.vjp(partial(jax.nn.gelu, approximate=True), hidden_pre)[1]
        grad_pre = gelu_pull(grad_act)[0].astype(jnp.bfloat16)

        def mlp_term(first_row, row_span):
            return jnp.einsum("rf,df->rd", grad_pre, weight_up, preferred_element_type=jnp.float32)

        grad_norm_two = settle_back(mlp_term)
        second_pull = jax.vjp(
            partial(layer_norm, gain_rows=gain_sets[1], shifts=shift_sets[1]), middle
        )[1]
        grad_middle = grad_out + second_pull(grad_norm_two)[0]
        grad_attn = widen_back(grad_middle.astype(jnp.bfloat16))
        grad_heads = jnp.einsum(
            "rd,nd->rn", grad_attn, weight_out, preferred_element_type=jnp.float32
        )
        grad_heads = grad_heads.astype(jnp.bfloat16).reshape(row_count, local_heads, HEAD_DIM)
        grad_probs = jnp.einsum(
            "qhe,khe->hqk", grad_heads, head_split[:, 2], preferred_element_type=jnp.float32
        )
        grad_scores = attn_probs * (
            grad_probs - jnp.sum(attn_probs * grad_probs, axis=-1, keepdims=True)
        )
        grad_scores = grad_scores.astype(jnp.bfloat16)
        grad_query = (
            jnp.einsum(
                "hqk,khe->qhe", grad_scores, head_split[:, 1], preferred_element_type=jnp.float32
            )
            * score_scale
        )
        grad_key = (
            jnp.einsum(
                "hqk,qhe->khe", grad_scores, head_split[:, 0], preferred_element_type=jnp.float32
            )
            * score_scale
        )
        grad_value = jnp.einsum(
            "hqk,qhe->khe", probs_low, grad_heads, preferred_element_type=jnp.float32
        )
        grad_packed = (
            jnp.stack([grad_query, grad_key, grad_value], axis=1)
            .reshape(row_count, 3, local_width)
            .astype(jnp.bfloat16)
        )
        grad_pair = jnp.stack([grad_packed[:, 0], grad_packed[:, 2]])
        gradient_reduced = adapter_scale * jnp.einsum(
            "jrn,jkn->jrk", grad_pair, upper_factor, preferred_element_type=jnp.float32
        )

        def attn_term(first_row, row_span):
            dense_part = jnp.einsum(
                "rcn,dcn->rd", grad_packed, weight_qkv, preferred_element_type=jnp.float32
            )
            return dense_part + jnp.einsum(
                "jrk,jkd->rd", gradient_reduced, factor_wide, precision=highest_precision
            )

        grad_normed = settle_back(attn_term)
        first_pull = jax.vjp(
            partial(layer_norm, gain_rows=gain_sets[0], shifts=shift_sets[0]), hidden
        )[1]
        grad_hidden = grad_middle + first_pull(grad_normed)[0]
        grad_factor_a = jnp.einsum(
            "jrk,rd->jkd", gradient_reduced, normed.astype(jnp.float32), precision=highest_precision
        )
        gradient_upper_factor = adapter_scale * jnp.stack(
            [
                jnp.einsum(
                    "rk,rn->kn",
                    reduced_query,
                    grad_packed[:, 0],
                    preferred_element_type=jnp.float32,
                ),
                jnp.einsum(
                    "rk,rn->kn",
                    reduced_value,
                    grad_packed[:, 2],
                    preferred_element_type=jnp.float32,
                ),
            ]
        )
        return (grad_hidden, grad_factor_a, gradient_upper_factor)

    zero_rows = jnp.zeros((micro_count, own_rows, model_width), jnp.bfloat16)
    saved_start = ()

    def record(buffers, slot_index, is_live, layer_input, results):
        kept_in, outputs, saved = buffers
        output, normed, middle, normed_two = results
        low_output = output.astype(jnp.bfloat16)
        kept_in = put_slot(kept_in, slot_index, is_live, layer_input)
        outputs = put_slot(outputs, slot_index, is_live, low_output)
        return ((kept_in, outputs, saved), low_output)

    buffers = (zero_rows, zero_rows, saved_start)

    def run_phase(buffers, sources, phase_section):

        def phase_turn(slot_index, buffers):
            allowed, own_valid = layout_of(slot_index)
            layer_input = take_slot(sources, slot_index)
            results = forward(layer_input.astype(jnp.float32), allowed)
            return record(
                buffers, slot_index, section_index == phase_section, layer_input, results
            )[0]

        return lax.fori_loop(0, micro_count, phase_turn, buffers)

    buffers = run_phase(buffers, tokens, 0)
    received = from_behind(buffers[1], "section", 1)
    buffers = run_phase(buffers, received, 1)
    kept_in, outputs, saved = buffers

    def back_step(slot_index, grad_out, allowed):
        hidden = take_slot(kept_in, slot_index).astype(jnp.float32)
        output, normed, middle, normed_two = forward(hidden, allowed)
        return backward(hidden, grad_out, allowed, normed, middle, normed_two)

    def top_grad(slot_index, own_valid):
        return take_slot(cotangent, slot_index).astype(jnp.float32) * own_valid[:, None].astype(
            jnp.float32
        )

    zero_a = jnp.zeros(down_factor.shape, jnp.float32)
    zero_b = jnp.zeros(upper_factor.shape, jnp.float32)

    def run_back(loop_state, sources, phase_section):

        def phase_turn(slot_index, loop_state):
            grads_in, sum_a, sum_b = loop_state
            allowed, own_valid = layout_of(slot_index)
            if phase_section == 1:
                grad_out = top_grad(slot_index, own_valid)
            else:
                grad_out = take_slot(sources, slot_index).astype(jnp.float32)
            is_live = section_index == phase_section
            grad_hidden, grad_a, grad_b = back_step(slot_index, grad_out, allowed)
            grads_in = put_slot(grads_in, slot_index, is_live, grad_hidden.astype(jnp.bfloat16))
            sum_a = sum_a + jnp.where(is_live, grad_a, 0.0)
            sum_b = sum_b + jnp.where(is_live, grad_b, 0.0)
            return (grads_in, sum_a, sum_b)

        return lax.fori_loop(0, micro_count, phase_turn, loop_state)

    loop_state = run_back((zero_rows, zero_a, zero_b), zero_rows, 1)
    received_grads = from_behind(loop_state[0], "section", -1)
    grads_in, sum_a, sum_b = run_back(loop_state, received_grads, 0)
    total_a = lax.psum(sum_a, ("dp", "tensor"))
    total_b = lax.psum(sum_b, "dp")
    return (outputs[None], grads_in[None], total_a[None], total_b[None])


R = 256
D = 1024
NEG = -1e30
F32 = jnp.float32
BF16 = jnp.bfloat16
MESH = pl.DeviceIdType.MESH
CHUNK = 128


def nn(a, b):
    return lax.dot_general(a, b, (((1,), (0,)), ((), ())), preferred_element_type=F32)


def nt(a, b):
    return lax.dot_general(a, b, (((1,), (1,)), ((), ())), preferred_element_type=F32)


def tn(a, b):
    return lax.dot_general(a, b, (((0,), (0,)), ((), ())), preferred_element_type=F32)


def normalize(v):
    centered = v - jnp.mean(v, axis=-1, keepdims=True)
    rs = lax.rsqrt(jnp.mean(centered * centered, axis=-1, keepdims=True) + norm_eps)
    return centered * rs, rs


def norm_pull(v, g):
    xhat, rs = normalize(v)
    return rs * (
        g
        - jnp.mean(g, axis=-1, keepdims=True)
        - xhat * jnp.mean(g * xhat, axis=-1, keepdims=True)
    )


def gelu_pair(z):
    c = 0.7978845608028654
    z2 = z * z
    t = jnp.tanh(c * (z + 0.044715 * (z2 * z)))
    half = 0.5 * (1.0 + t)
    slope = half + (0.5 * c) * z * (1.0 - t * t) * (1.0 + (3.0 * 0.044715) * z2)
    return z * half, slope


def fused_kernel(
    dp_count,
    tok, cot, buckets, lengths, gain_in, shift_in, wq_in, bqv_in, wo_in, wu_in, bu_in, wd_in, bo_in, ad_in, au_in,
    act, ig, out_a, out_b,
    SP, WQ, WO, WU, WD, H, DY, MID, GP, Q, KV, OT, LSE, SND, RCV, BIG, MSK, DR, DQ, AB, U, OACC, PB,
    GA, GB, GCA, GCB, GXA, GXB, GZA, GZB,
    tok_sem, tok_ys, tok_xs, wl, ws_r, ws_s, wy_r, wy_s, wz_r, wz_s, wa_r, wa_s, wb_r, wb_s,
    kv_rcv, kv_snd, x_rcv, x_snd, last_rcv, last_snd, dr_rcv, dr_snd, out_rcv, out_snd, gc_r, gc_s, gx_r, gx_s, gz_r, gz_s,
):
    s = lax.axis_index("section")
    d = lax.axis_index("dp")
    t = lax.axis_index("tensor")
    x = lax.rem(t, 2)
    y = lax.div(t, 2)
    sib = (1 - s, d, t)
    xp = (s, d, y * 2 + 1 - x)
    yp = (s, d, (1 - y) * 2 + x)
    z_half = lax.rem(d, 2)
    zp = (s, d + 1 - 2 * z_half, t)
    flip = s + x - 2 * s * x
    own_i = flip

    def blk_of(i):
        return 2 * i + (s + i - 2 * s * i)

    bar = pltpu.get_barrier_semaphore()
    for ds_ in range(2):
        for dx in range(2):
            for dy in range(2):
                if ds_ or dx or dy:
                    s2 = 1 - s if ds_ else s
                    x2 = 1 - x if dx else x
                    y2 = 1 - y if dy else y
                    pl.semaphore_signal(bar, 1, device_id=(s2, d, y2 * 2 + x2), device_id_type=MESH)
    for k in range(1, dp_count):
        pl.semaphore_signal(bar, 1, device_id=(s, lax.rem(d + k, dp_count), t), device_id_type=MESH)
    pl.semaphore_wait(bar, 7 + dp_count - 1)

    def row_copies(src, dst, w):
        def local():
            return pltpu.make_async_copy(src.at[y], dst.at[y], tok_sem.at[w, y])

        def to_y():
            return pltpu.make_async_remote_copy(
                src.at[1 - y], dst.at[y], tok_ys.at[w], tok_sem.at[w, y], device_id=yp, device_id_type=MESH)

        def first_x():
            return pltpu.make_async_remote_copy(
                src.at[y], dst.at[y], tok_xs.at[w], tok_sem.at[w, y], device_id=xp, device_id_type=MESH)

        def then_x():
            return pltpu.make_async_remote_copy(
                dst.at[own_i], dst.at[own_i], tok_xs.at[w], tok_sem.at[w, own_i],
                device_id=xp, device_id_type=MESH)

        return local, to_y, first_x, then_x

    def rows_first(src, dst, w):
        local, _, first_x, _ = row_copies(src, dst, w)

        @pl.when(y == own_i)
        def _():
            first_x().start()
            local().start()

    def rows_swap(src, dst, w):
        @pl.when(y == own_i)
        def _():
            row_copies(src, dst, w)[1]().start()

    def rows_relay(src, dst, w):
        pltpu.make_async_copy(src.at[0], dst.at[own_i], tok_sem.at[w, own_i]).wait()

        @pl.when(y != own_i)
        def _():
            row_copies(src, dst, w)[3]().start()

    def rows_rest(src, dst, w):
        pltpu.make_async_copy(src.at[0], dst.at[1 - own_i], tok_sem.at[w, 1 - own_i]).wait()

    def rows_done(src, dst, w):
        _, to_y, first_x, _ = row_copies(src, dst, w)
        if w == 0:
            first_x().wait_send()

        @pl.when(y == own_i)
        def _():
            to_y().wait_send()

    pieces = (None, (wq_in, WQ, 4), (wo_in, WO, 1), (wu_in, WU, 4), (wd_in, WD, 4))
    base = (13, 0, 4, 5, 9)

    def relayer(l, c):
        return 1 - l if c % 2 else l

    def sources(p, rows):
        src, dst, _ = pieces[p]
        if p == 1:
            return [
                (src.at[c, rows, :], dst.at[s, y, rows, c * 256 : c * 256 + 256]) for c in range(3)
            ]
        return [(src.at[0, rows, :], dst.at[s, y, rows, :])]

    def chunk(p, c, half):
        dst, parts = pieces[p][1], pieces[p][2]
        size = dst.shape[2] // (2 * parts)
        return pl.ds(pl.multiple_of((half * parts + c) * size, size), size)

    def block(p, l, j, rows):
        return pieces[p][1].at[l, j, rows, :]

    def own_start(p):
        everything = pl.ds(0, pieces[p][1].shape[2])
        for src, dst in sources(p, everything):
            pltpu.make_async_copy(src, dst, wl.at[p]).start()
            pltpu.make_async_remote_copy(
                src, dst, ws_s.at[p], ws_r.at[p], device_id=sib, device_id_type=MESH).start()

    def whole_by_y(l, p, c):
        return p == 4 and c >= 2

    def y_start(l, p):
        for c in range(pieces[p][2] if p else 1):
            k = base[p] + c

            @pl.when(s == relayer(l, c))
            def _():
                if p == 0:
                    ref = SP.at[l, y, 16:32, :]
                    pltpu.make_async_remote_copy(
                        ref, ref, wy_s.at[k], wy_r.at[k], device_id=yp, device_id_type=MESH).start()
                    return
                rows = chunk(p, c, z_half)
                mine = block(p, l, y, rows)
                for src, dst in [(mine, mine)] if c % 2 else sources(p, rows):
                    pltpu.make_async_remote_copy(
                        src, dst, wy_s.at[k], wy_r.at[k], device_id=yp, device_id_type=MESH).start()
                if whole_by_y(l, p, c):
                    rows = chunk(p, c, 1 - z_half)
                    mine = block(p, l, y, rows)
                    for src, dst in [(mine, mine)] if c % 2 else sources(p, rows):
                        pltpu.make_async_remote_copy(
                            src, dst, wz_s.at[k], wz_r.at[k], device_id=yp, device_id_type=MESH).start()

    def small_copy(to, snd, rcv):
        return pltpu.make_async_remote_copy(
            SP.at[s, y], SP.at[s, y], snd, rcv, device_id=to, device_id_type=MESH)

    def passed(l, p, c, half, to, snd, rcv):
        ref = SP.at[l, 1 - y, 16:32, :] if p == 0 else block(p, l, 1 - y, chunk(p, c, half))
        return pltpu.make_async_remote_copy(ref, ref, snd, rcv, device_id=to, device_id_type=MESH)

    def relay_y(l, p):
        for c in range(pieces[p][2] if p else 1):
            k = base[p] + c

            @pl.when(s == relayer(l, c))
            def _():
                passed(l, p, c, z_half, sib, wa_s.at[k], wy_r.at[k]).wait_recv()
                if p and not (p == 4 and c >= 2):
                    passed(l, p, c, z_half, zp, wz_s.at[k], wz_r.at[k]).start()

                passed(l, p, c, z_half, sib, wa_s.at[k], wa_r.at[k]).start()

    def relay_z(l, p):
        for c in range(pieces[p][2]):
            k = base[p] + c

            @pl.when(s == relayer(l, c))
            def _():
                passed(l, p, c, 1 - z_half, zp, wz_s.at[k], wz_r.at[k]).wait_recv()
                passed(l, p, c, 1 - z_half, sib, wb_s.at[k], wb_r.at[k]).start()

    def own_wait(l, p):
        @pl.when(l == s)
        def _():
            if p:
                ref = pieces[p][1].at[s, y]
                pltpu.make_async_copy(ref, ref, wl.at[p]).wait()

        @pl.when(l != s)
        def _():
            ref = pieces[p][1].at[1 - s, y] if p else SP.at[1 - s, y]
            pltpu.make_async_copy(ref, ref, ws_r.at[p]).wait()

    def other_wait(l, p):
        for c in range(pieces[p][2] if p else 1):
            k = base[p] + c

            @pl.when(s != relayer(l, c))
            def _():
                if p == 0:
                    ref = SP.at[l, 1 - y, 16:32, :]
                    pltpu.make_async_copy(ref, ref, wa_r.at[13]).wait()
                else:
                    ref = block(p, l, 1 - y, chunk(p, c, 0))
                    pltpu.make_async_copy(ref, ref, wa_r.at[k]).wait()
                    pltpu.make_async_copy(ref, ref, wb_r.at[k]).wait()

    rows_swap(tok, H.at[0], 0)
    rows_first(tok, H.at[0], 0)
    own_start(1)
    SP[s, y] = jnp.zeros(SP.shape[2:], F32)
    for k, (ref, row) in enumerate(
        ((gain_in, 0), (shift_in, 0), (gain_in, 1), (shift_in, 1), (bo_in, 0), (bo_in, 1))
    ):
        SP[s, y, k : k + 1, :] = ref[0, row : row + 1, :].astype(F32)
    SP[s, y, 8:12, :] = ad_in[0, 0].astype(F32)
    SP[s, y, 12:16, :] = ad_in[0, 1].astype(F32)
    SP[s, y, 16:17, :] = bu_in[...].astype(F32)
    SP[s, y, 17:18, 0:256] = bqv_in[0, 0:1, :].astype(F32)
    SP[s, y, 17:18, 512:768] = bqv_in[0, 1:2, :].astype(F32)
    SP[s, y, 24:28, 0:256] = au_in[0, 0].astype(F32)
    SP[s, y, 28:32, 512:768] = au_in[0, 1].astype(F32)
    small_copy(sib, ws_s.at[0], ws_r.at[0]).start()
    y_start(0, 0)
    for p in range(2, 5):
        own_start(p)
    for l in range(2):
        for p in range(5):
            own_wait(l, p)
            if l or p:
                y_start(l, p)

    shift = 7 + buckets[y]
    span_mask = lax.shift_left(jnp.int32(1), shift) - 1

    def length_of(pos):
        item = lax.shift_right_logical(pos, jnp.broadcast_to(shift, pos.shape))
        got = jnp.zeros(pos.shape, jnp.int32)
        for k in range(lengths.shape[1]):
            got = jnp.where(item == k, lengths[y, k], got)
        return item, jnp.bitwise_and(pos, span_mask) < got

    def build_mask(i):
        b = blk_of(i)
        q_row = b * R + lax.broadcasted_iota(jnp.int32, (1, R), 1)
        q_item = lax.shift_right_logical(q_row, jnp.broadcast_to(shift, q_row.shape))

        def rows(r, carry):
            r0 = pl.multiple_of(r * CHUNK, CHUNK)
            k_row = r0 + lax.broadcasted_iota(jnp.int32, (CHUNK, 1), 0)
            k_item, k_ok = length_of(k_row)
            k_tag = jnp.where(k_ok, k_item, -1)
            same = (k_tag == q_item) & (k_row <= q_row)
            allowed = same | (k_row == q_row)
            MSK[pl.ds(pl.multiple_of(i * 2 * R + r0, CHUNK), CHUNK), :] = jnp.where(allowed, 0.0, NEG).astype(BF16)
            return carry

        lax.fori_loop(0, (b + 1) * (R // CHUNK), rows, 0)

    build_mask(0)
    build_mask(1)
    GA[...] = jnp.zeros(GA.shape, F32)
    GB[...] = jnp.zeros(GB.shape, F32)

    def x_copy(slot, i):
        return pltpu.make_async_remote_copy(
            SND.at[slot, i], RCV.at[slot * 2 + (i if slot < 2 else 0)], x_snd.at[slot, i], x_rcv.at[slot, i],
            device_id=xp, device_id_type=MESH)

    def last_copy(c, i):
        rows = slice(c * 64, c * 64 + 64)
        return pltpu.make_async_remote_copy(
            SND.at[0, i, rows, :], RCV.at[i, rows, :], last_snd.at[c], last_rcv.at[c],
            device_id=xp, device_id_type=MESH)

    def by_rows(body):
        body(slice(0, R))

    total_rows = slice(3 * R, 4 * R)

    def gather(n, term):
        for c in range(4):
            part = term[:, c * R : c * R + R]
            BIG[c, total_rows, :] = part if n == 0 else BIG[c, total_rows, :] + part

    def gathered():
        return jnp.concatenate([BIG[c, total_rows, :] for c in range(4)], axis=1).astype(BF16)

    def swapped(slot, i, rows):
        return SND[slot, i, rows, :].astype(F32) + RCV[slot * 2 + (i if slot < 2 else 0), rows, :].astype(F32)

    def send_result(which, layer, src, rows=slice(0, R)):
        src = src.at[rows, :]
        dst = act if which < 2 else ig
        o = 0 if which < 2 else 1
        here = (s == layer) & (y == own_i)

        @pl.when(here)
        def _():
            pltpu.make_async_copy(src, dst.at[y, rows, :], out_rcv.at[o, y]).start()

        @pl.when(jnp.logical_not(here))
        def _():
            pltpu.make_async_remote_copy(
                src, dst.at[y, rows, :], out_snd.at[which], out_rcv.at[o, y],
                device_id=(layer, d, own_i * 2 + x), device_id_type=MESH).start()

    def send_result_done(which, layer, src):
        dst = act if which < 2 else ig
        o = 0 if which < 2 else 1
        here = (s == layer) & (y == own_i)

        @pl.when(jnp.logical_not(here))
        def _():
            pltpu.make_async_remote_copy(
                src, dst.at[y], out_snd.at[which], out_rcv.at[o, y],
                device_id=(layer, d, own_i * 2 + x), device_id_type=MESH).wait_send()

    def vec(l, k):
        return SP[l, y, k : k + 1, :]

    def head_lanes(pair):
        return pl.ds(pl.multiple_of(pair * 128, 128), 128)

    def split_pair(v, axis):
        which = lax.broadcasted_iota(jnp.int32, v.shape, axis) < HEAD_DIM
        zero = jnp.zeros_like(v)
        return jnp.where(which, v, zero), jnp.where(which, zero, v)

    def kv_copy(l, i):
        rows = pl.ds(pl.multiple_of(blk_of(i) * R, R), R)
        return pltpu.make_async_remote_copy(
            KV.at[l, :, rows, :], KV.at[l, :, rows, :], kv_snd.at[l, i], kv_rcv.at[l, i],
            device_id=sib, device_id_type=MESH)

    def kv_wait(l, i):
        b = 2 * i + (1 - s + i - 2 * (1 - s) * i)
        rows = pl.ds(pl.multiple_of(b * R, R), R)
        pltpu.make_async_remote_copy(
            KV.at[l, :, rows, :], KV.at[l, :, rows, :], kv_snd.at[l, i], kv_rcv.at[l, i],
            device_id=sib, device_id_type=MESH).wait_recv()

    GROUP = 4

    def attend(l, i):
        b = blk_of(i)

        def group_turn(g, carry):
            def lanes_of(k):
                return pl.ds(pl.multiple_of(g * (GROUP * HEAD_DIM) + k * 128, 128), 128)

            def first(j, tops):
                rows = pl.ds(pl.multiple_of(j * R, R), R)
                mask = MSK[pl.ds(pl.multiple_of((i * 2 + j) * R, R), R), :].astype(F32)
                new = []
                for k in range(GROUP // 2):
                    qs = split_pair(Q[l, i, :, lanes_of(k)], 1)
                    keys = KV[l, 0, rows, lanes_of(k)]
                    for e in range(2):
                        st = nt(keys, qs[e]) + mask
                        BIG[2 * k + e, rows, :] = st
                        new.append(jnp.maximum(tops[2 * k + e], jnp.max(st, axis=0, keepdims=True)))
                return tuple(new)

            tops = lax.fori_loop(0, b + 1, first, (jnp.full((1, R), NEG, F32),) * GROUP)
            for k in range(GROUP):
                OACC[k] = jnp.zeros(OACC.shape[1:], F32)

            def second(j, sums):
                rows = pl.ds(pl.multiple_of(j * R, R), R)
                new = []
                for k in range(GROUP):
                    p = jnp.exp(BIG[k, rows, :] - tops[k])
                    new.append(sums[k] + jnp.sum(p, axis=0, keepdims=True))
                    PB[k] = p.astype(BF16)
                for k in range(GROUP // 2):
                    values = jnp.transpose(KV[l, 1, rows, lanes_of(k)])
                    for e in range(2):
                        OACC[2 * k + e] += nn(values[e * 64 : e * 64 + 64], PB[2 * k + e])
                return tuple(new)

            sums = lax.fori_loop(0, b + 1, second, (jnp.zeros((1, R), F32),) * GROUP)
            for k in range(GROUP):
                OT[l, i, pl.ds(pl.multiple_of((g * GROUP + k) * 64, 64), 64), :] = (
                    OACC[k] * (1.0 / sums[k])
                ).astype(BF16)
                LSE[l, i, g * GROUP + k] = tops[k] + jnp.log(sums[k])
            return carry

        lax.fori_loop(0, Q.shape[3] // (GROUP * HEAD_DIM), group_turn, 0)

    def forward_attention(l, i):
        b = blk_of(i)

        @pl.when(i == 0)
        def _():
            @pl.when(l == 0)
            def _():
                rows_relay(tok, H.at[0], 0)
                relay_y(l, 0)
                relay_y(l, 1)
                rows_first(cot, DY, 1)

                @pl.when(own_i == 1)
                def _():
                    rows_rest(tok, H.at[0], 0)

            other_wait(l, 0)
            relay_z(l, 1)

            @pl.when(l == 1)
            def _():
                relay_y(l, 2)
                relay_y(l, 3)

            other_wait(l, 1)

        @pl.when(i == 1)
        def _():
            @pl.when((l == 0) & (own_i == 0))
            def _():
                rows_rest(tok, H.at[0], 0)


        @pl.when(l == 1)
        def _():
            x_copy(1, i).wait_recv()

            def rows_in(rows):
                h = MID[0, i, rows, :] + (swapped(1, i, rows) + vec(0, 5))
                H[1, i, rows, :] = h.astype(BF16)

            by_rows(rows_in)

            @pl.when(i == own_i)
            def _():
                send_result(0, 0, H.at[1, i])

        def rows_norm(rows):
            xhat, _ = normalize(H[l, i, rows, :].astype(F32))
            AB[rows, :] = (xhat * vec(l, 0) + vec(l, 1)).astype(BF16)

        by_rows(rows_norm)
        u = nt(AB[...], SP[l, y, 8:16, :].astype(BF16)).astype(BF16)
        own_rows = pl.ds(pl.multiple_of(b * R, R), R)
        for j in range(2):
            up = SP[l, j, 24:32, 256:768].astype(BF16)
            cols = slice(j * 256, j * 256 + 256)
            pair = nn(AB[...], WQ[l, j, :, 256:768]) + (adapter_scale * nn(u, up) + SP[l, j, 17:18, 256:768])
            KV[l, 0, own_rows, cols] = pair[:, 0:256].astype(BF16)
            KV[l, 1, own_rows, cols] = pair[:, 256:512].astype(BF16)

        @pl.when(b != 3)
        def _():
            kv_copy(l, i).start()

        for j in range(2):
            up = SP[l, j, 24:32, 0:256].astype(BF16)
            q = nn(AB[...], WQ[l, j, :, 0:256]) + (adapter_scale * nn(u, up) + SP[l, j, 17:18, 0:256])
            Q[l, i, :, j * 256 : j * 256 + 256] = (q * HEAD_DIM ** -0.5).astype(BF16)
        U[l, i] = nt(SP[l, y, 8:16, :].astype(BF16), AB[...]).astype(BF16)

        @pl.when((s == 1) & (i == 0))
        def _():
            kv_wait(l, 0)

        @pl.when((s == 0) & (i == 1))
        def _():
            kv_wait(l, 0)
            kv_wait(l, 1)

        @pl.when((i == 0) & (l == 0))
        def _():
            relay_y(l, 2)

        @pl.when(i == 1)
        def _():
            @pl.when(l == 0)
            def _():
                relay_y(l, 3)

            @pl.when(l == 1)
            def _():
                relay_y(l, 4)

        attend(l, i)

        @pl.when(i == 0)
        def _():
            relay_z(l, 2)
            other_wait(l, 2)

        @pl.when(l == 1)
        def _():
            x_copy(0, i).wait_send()

        SND[0, i] = (tn(OT[l, i, 0:256, :], WO[l, 0]) + tn(OT[l, i, 256:512, :], WO[l, 1])).astype(BF16)
        x_copy(0, i).start()

    def forward_ff(l, i):
        @pl.when((i == 0) & (l == 0))
        def _():
            relay_y(l, 4)

        @pl.when((i == 1) & (l == 0))
        def _():
            rows_swap(cot, DY, 1)

        @pl.when((i == 1) & (l == 1))
        def _():
            rows_relay(cot, DY, 1)

        x_copy(0, i).wait_recv()

        def rows_mid(rows):
            mid = H[l, i, rows, :].astype(F32) + (swapped(0, i, rows) + vec(l, 4))
            MID[l, i, rows, :] = mid
            xhat, _ = normalize(mid)
            AB[rows, :] = (xhat * vec(l, 2) + vec(l, 3)).astype(BF16)

        by_rows(rows_mid)
        for n in range(4):
            j, half = (y if n < 2 else 1 - y), n % 2
            cols = slice(half * 512, half * 512 + 512)
            if n == 2:

                @pl.when(i == 0)
                def _():
                    relay_z(l, 3)
                    relay_z(l, 4)
                    other_wait(l, 3)
                    other_wait(l, 4)

            z = nn(AB[...], WU[l, j, :, cols]) + SP[l, j, 16:17, cols]
            g, slope = gelu_pair(z)
            GP[l, i, :, n * 512 : n * 512 + 512] = slope.astype(BF16)
            term = nn(g.astype(BF16), WD[l, j, cols, :])
            gather(n, term)
        SND[1 + l, i] = gathered()

        @pl.when(l == 0)
        def _():
            x_copy(1, i).start()

            @pl.when(i == 1)
            def _():
                relay_y(1, 0)
                relay_y(1, 1)

        @pl.when((l == 1) & (i != own_i))
        def _():
            x_copy(2, i).start()

    def fwd_layer(l, carry):
        def a_turn(i, c):
            forward_attention(l, i)
            return c

        def f_turn(i, c):
            forward_ff(l, i)
            return c

        lax.fori_loop(0, 2, a_turn, 0)
        lax.fori_loop(0, 2, f_turn, 0)
        return carry

    lax.fori_loop(0, 2, fwd_layer, 0)

    def finish_forward():
        x_copy(2, own_i).wait_recv()

        def rows_out(rows):
            out = MID[1, own_i, rows, :] + (swapped(2, own_i, rows) + vec(1, 5))
            SND[2, own_i, rows, :] = out.astype(BF16)

        by_rows(rows_out)
        send_result(1, 1, SND.at[2, own_i])

    def backward_ff(l, i):
        @pl.when(l == 1)
        def _():
            @pl.when(i == own_i)
            def _():
                row_copies(cot, DY, 1)[3]().wait_send()

            @pl.when(i != own_i)
            def _():
                rows_rest(cot, DY, 1)

            def rows_valid(rows):
                pos = blk_of(i) * R + lax.broadcasted_iota(jnp.int32, (R, 1), 0)
                _, ok = length_of(pos)
                DY[i, rows, :] = (DY[i, rows, :].astype(F32) * jnp.where(ok, 1.0, 0.0)).astype(BF16)

            by_rows(rows_valid)

        @pl.when(l == 0)
        def _():
            x_copy(0, i).wait_recv()

            def rows_in(rows):
                g = swapped(0, i, rows) * vec(1, 0)
                DY[i, rows, :] = (MID[1, i, rows, :] + norm_pull(H[1, i, rows, :].astype(F32), g)).astype(BF16)

            by_rows(rows_in)

            @pl.when(i == own_i)
            def _():
                send_result(2, 1, DY.at[i])

        for n in range(4):
            j, half = (y if n < 2 else 1 - y), n % 2
            cols = slice(half * 512, half * 512 + 512)
            dg = nt(DY[i], WD[l, j, cols, :])
            dz = (GP[l, i, :, n * 512 : n * 512 + 512].astype(F32) * dg).astype(BF16)
            term = nt(dz, WU[l, j, :, cols])
            gather(n, term)

        x_copy(1, i).wait_send()
        SND[1, i] = gathered()
        x_copy(1, i).start()

    def dr_copy(k, b):
        rows = pl.ds(pl.multiple_of(b * R, R), R)
        return pltpu.make_async_remote_copy(
            BIG.at[:, rows, :], DR.at[k], dr_snd.at[k], dr_rcv.at[k], device_id=sib, device_id_type=MESH)

    def attend_back(l, i):
        b = blk_of(i)
        pairs = Q.shape[3] // 128
        place = RCV.at[2 + i]

        def back_rows(k):
            return place[(k % 2) * 128 : (k % 2) * 128 + 128, 512 + (k // 2) * 256 : 768 + (k // 2) * 256]

        deltas = []
        for k in range(pairs):
            rows = slice(k * 128, k * 128 + 128)
            prod = back_rows(k).astype(F32) * OT[l, i, rows, :].astype(F32)
            deltas.append(jnp.sum(prod[0:64], axis=0, keepdims=True))
            deltas.append(jnp.sum(prod[64:128], axis=0, keepdims=True))
            OACC[2 * k] = jnp.zeros(OACC.shape[1:], F32)
            OACC[2 * k + 1] = jnp.zeros(OACC.shape[1:], F32)

        def turn(step, c):
            j = lax.rem(2 * b - step, b + 1)
            rows = pl.ds(pl.multiple_of(j * R, R), R)
            mask = MSK[pl.ds(pl.multiple_of((i * 2 + j) * R, R), R), :].astype(F32)
            for k in range(pairs):
                lanes = slice(k * 128, k * 128 + 128)
                qs = split_pair(Q[l, i, :, lanes], 1)
                dots = split_pair(back_rows(k), 0)
                keys = KV[l, 0, rows, lanes]
                values = KV[l, 1, rows, lanes]
                for e in range(2):
                    h = 2 * k + e
                    p = jnp.exp(nt(keys, qs[e]) + mask - LSE[l, i, h])
                    dp = nn(values, dots[e])
                    PB[h] = (p * (dp - deltas[h])).astype(BF16)
                    PB[2 * pairs + h] = p.astype(BF16)
            for k in range(pairs):
                lanes = slice(k * 128, k * 128 + 128)
                half = slice((k % 2) * 128, (k % 2) * 128 + 128)
                qs = split_pair(Q[l, i, :, lanes], 1)
                dos = split_pair(place[:, lanes], 1)
                h = 2 * k
                BIG[k // 2, rows, half] += nn(PB[h], qs[0]) + nn(PB[h + 1], qs[1])
                BIG[2 + k // 2, rows, half] += nn(PB[2 * pairs + h], dos[0]) + nn(PB[2 * pairs + h + 1], dos[1])
            for k in range(pairs):
                keys = jnp.transpose(KV[l, 0, rows, k * 128 : k * 128 + 128])
                for e in range(2):
                    OACC[2 * k + e] += nn(keys[e * 64 : e * 64 + 64], PB[2 * k + e])
            for k in range(2):

                @pl.when((s == 0) & (i == 1) & (j == k + 1))
                def _():
                    dr_copy(k, k + 1).start()

            return c

        lax.fori_loop(0, b + 1, turn, 0)
        for k in range(pairs):
            dq = jnp.concatenate([OACC[2 * k], OACC[2 * k + 1]], axis=0) * HEAD_DIM ** -0.5
            DQ[k // 2, :, (k % 2) * 128 : (k % 2) * 128 + 128] = jnp.transpose(dq).astype(BF16)

    def backward_attention(l, i):
        b = blk_of(i)
        x_copy(1, i).wait_recv()

        def rows_mid(rows):
            g = swapped(1, i, rows) * vec(l, 2)
            dmid = DY[i, rows, :].astype(F32) + norm_pull(MID[l, i, rows, :], g)
            MID[l, i, rows, :] = dmid
            AB[rows, :] = dmid.astype(BF16)

        by_rows(rows_mid)
        for j in range(2):
            RCV[2 + i, :, 512 + j * 256 : 768 + j * 256] = nt(WO[l, j], AB[...]).astype(BF16)
            RCV[2 + i, :, j * 256 : j * 256 + 256] = nt(AB[...], WO[l, j]).astype(BF16)

        @pl.when(i == 1)
        def _():
            @pl.when(l == 0)
            def _():
                @pl.when(s == 0)
                def _():
                    dr_copy(0, 1).wait_send()
                    dr_copy(1, 2).wait_send()

                @pl.when(s == 1)
                def _():
                    dr_copy(0, 0).wait_send()

            def clear(r, c):
                rows = pl.ds(pl.multiple_of(r * R, R), R)
                BIG[:, rows, :] = jnp.zeros((4, R, 256), F32)
                return c

            lax.fori_loop(0, 4, clear, 0)

        attend_back(l, i)
        own = pl.ds(pl.multiple_of(b * R, R), R)

        def rows_norm(rows):
            xhat, _ = normalize(H[l, i, rows, :].astype(F32))
            AB[rows, :] = (xhat * vec(l, 0) + vec(l, 1)).astype(BF16)

        by_rows(rows_norm)

        @pl.when(b != 3)
        def _():
            def add(k):
                dr_copy(k, b).wait_recv()
                for c in range(4):
                    BIG[c, own, :] += DR[k, c]

            @pl.when(s == 1)
            def _():
                add(i)

            @pl.when((s == 1) & (i == 0))
            def _():
                dr_copy(0, 0).start()

            @pl.when(s == 0)
            def _():
                add(0)

        for j in range(2):
            DQ[j, :, 256:512] = BIG[j, own, :].astype(BF16)
            DQ[j, :, 512:768] = BIG[2 + j, own, :].astype(BF16)

        ups = [SP[l, j, 24:32, 0:768].astype(BF16) for j in range(2)]
        du = (adapter_scale * (nt(ups[0], DQ[0]) + nt(ups[1], DQ[1]))).astype(BF16)
        GA[l] += nn(du, AB[...])
        top = lax.broadcasted_iota(jnp.int32, (8, 256), 0) < 4
        for j in range(2):
            gq = nn(U[l, i], DQ[j, :, 0:256])
            gv = nn(U[l, i], DQ[j, :, 512:768])
            GB[l, j] += adapter_scale * jnp.where(top, gq, gv)

        x_copy(0, i).wait_send()
        SND[0, i] = (
            nt(DQ[0], WQ[l, 0]) + nt(DQ[1], WQ[l, 1]) + tn(du, SP[l, y, 8:16, :].astype(BF16))
        ).astype(BF16)

        @pl.when(l == 1)
        def _():
            x_copy(0, i).start()

        @pl.when((l == 0) & (i != own_i))
        def _():
            for c in range(4):
                last_copy(c, i).start()

    def core_copies(l):
        return (
            pltpu.make_async_remote_copy(
                GA.at[l], GCA, gc_s.at[0], gc_r.at[0], device_id=sib, device_id_type=MESH),
            pltpu.make_async_remote_copy(
                GB.at[l], GCB, gc_s.at[1], gc_r.at[1], device_id=sib, device_id_type=MESH),
        )

    def plane_copies(l):
        out = []
        for k, (dx, dy) in enumerate(((1, 0), (0, 1), (1, 1))):
            x2 = 1 - x if dx else x
            y2 = 1 - y if dy else y
            to = (s, d, y2 * 2 + x2)
            out.append(pltpu.make_async_remote_copy(
                GA.at[l], GXA.at[k], gx_s.at[k], gx_r.at[k], device_id=to, device_id_type=MESH))
        out.append(pltpu.make_async_remote_copy(
            GB.at[l, 1 - y], GXB, gx_s.at[3], gx_r.at[3], device_id=yp, device_id_type=MESH))
        return out

    def line_copies():
        out = []
        for k in range(1, dp_count):
            to = (s, lax.rem(d + k, dp_count), t)
            out.append(pltpu.make_async_remote_copy(
                GZA.at[d], GZA.at[d], gz_s.at[0, k - 1], gz_r.at[0, k - 1], device_id=to, device_id_type=MESH))
            out.append(pltpu.make_async_remote_copy(
                GZB.at[d], GZB.at[d], gz_s.at[1, k - 1], gz_r.at[1, k - 1], device_id=to, device_id_type=MESH))
        return out

    def sum_core(l):
        @pl.when(s != l)
        def _():
            for c in core_copies(l):
                c.start()

    def sum_plane(l):
        @pl.when(s == l)
        def _():
            for c in core_copies(l):
                c.wait_recv()
            GA[l] += GCA[...]
            GB[l] += GCB[...]
            for c in plane_copies(l):
                c.start()

    def sum_line(l):
        @pl.when(s == l)
        def _():
            for c in plane_copies(l):
                c.wait_recv()
            GZA[d] = (GA[l] + GXA[0]) + (GXA[1] + GXA[2])
            GZB[d] = GB[l, y] + GXB[...]
            for c in line_copies():
                c.start()

    def sum_end(l):
        @pl.when(s == l)
        def _():
            for c in line_copies():
                c.wait_recv()
            total_a, total_b = GZA[0], GZB[0]
            for k in range(1, dp_count):
                total_a, total_b = total_a + GZA[k], total_b + GZB[k]
            out_a[0, 0] = total_a[0:4]
            out_a[0, 1] = total_a[4:8]
            out_b[0, 0] = total_b[0:4]
            out_b[0, 1] = total_b[4:8]

    def bwd_layer(back, carry):
        l = 1 - back

        def f_turn(k, c):
            @pl.when((l == 0) & (k == 1))
            def _():
                sum_plane(1)

            backward_ff(l, 1 - k)
            return c

        def a_turn(k, c):
            @pl.when((l == 0) & (k == 0))
            def _():
                sum_line(1)

            @pl.when((l == 0) & (k == 1))
            def _():
                sum_end(1)

            backward_attention(l, 1 - k)
            return c

        lax.fori_loop(0, 2, f_turn, 0)

        @pl.when(l == 1)
        def _():
            finish_forward()

        lax.fori_loop(0, 2, a_turn, 0)
        sum_core(l)
        return carry

    lax.fori_loop(0, 2, bwd_layer, 0)
    sum_plane(0)

    for c in range(4):
        last_copy(c, own_i).wait_recv()
        rows = slice(c * 64, c * 64 + 64)
        g = swapped(0, own_i, rows) * vec(0, 0)
        AB[rows, :] = (MID[0, own_i, rows, :] + norm_pull(H[0, own_i, rows, :].astype(F32), g)).astype(BF16)
        send_result(3, 0, AB, rows)
    sum_line(0)

    for c in range(4):
        last_copy(c, 1 - own_i).wait_send()
    for i in range(2):
        x_copy(1, i).wait_send()
    x_copy(2, 1 - own_i).wait_send()
    def sent(ref, sem):
        pltpu.make_async_remote_copy(ref, ref, sem, sem, device_id=sib, device_id_type=MESH).wait_send()

    for p in range(5):
        sent(pieces[p][1].at[s, y] if p else SP.at[s, y], ws_s.at[p])
        for c in range(pieces[p][2] if p else 1):
            k = base[p] + c
            ref = block(p, s, y, chunk(p, c, 0)) if p else SP.at[s, y, 16:32, :]
            sent(ref, wy_s.at[k])
            sent(ref, wa_s.at[k])
            if p:
                sent(ref, wz_s.at[k])
                sent(ref, wb_s.at[k])
    rows_done(tok, H.at[0], 0)
    rows_done(cot, DY, 1)
    for l in range(2):
        kv_copy(l, 0).wait_send()

        @pl.when(s == 1)
        def _():
            kv_copy(l, 1).wait_send()

    @pl.when(s == 0)
    def _():
        dr_copy(0, 1).wait_send()
        dr_copy(1, 2).wait_send()

    @pl.when(s == 1)
    def _():
        dr_copy(0, 0).wait_send()

    @pl.when(s == 0)
    def _():
        for c in core_copies(1) + tuple(plane_copies(0)) + tuple(line_copies()):
            c.wait_send()

    @pl.when(s == 1)
    def _():
        for c in core_copies(0) + tuple(plane_copies(1)) + tuple(line_copies()):
            c.wait_send()

    send_result_done(0, 0, H.at[1, 0])
    send_result_done(1, 1, H.at[1, 0])
    send_result_done(2, 1, H.at[1, 0])
    send_result_done(3, 0, H.at[1, 0])
    for o, ref in ((0, act), (1, ig)):
        for m in range(2):
            pltpu.make_async_copy(tok.at[0], ref.at[m], out_rcv.at[o, m]).wait()
    sum_end(0)


def copy_kernel(a_in, g_in, ta_in, tb_in, a_out, g_out, ta_out, tb_out, held_a, held_g, held_ta, held_tb, load, store):
    moves = []
    for k, (src, held, dst) in enumerate(((a_in, held_a, a_out), (g_in, held_g, g_out))):
        for m in range(src.shape[0]):
            moves.append((src.at[m], held.at[m], dst.at[0, m], 2 * k + m))
    moves.append((ta_in, held_ta, ta_out, 4))
    moves.append((tb_in, held_tb, tb_out, 5))
    for src, held, dst, k in moves:
        pltpu.make_async_copy(src, held, load.at[k]).start()
    for src, held, dst, k in moves:
        pltpu.make_async_copy(src, held, load.at[k]).wait()
        pltpu.make_async_copy(held, dst, store.at[k]).start()
    for src, held, dst, k in moves:
        pltpu.make_async_copy(held, dst, store.at[k]).wait()


def settle(act, ig, total_a, total_b):
    anywhere = pl.BlockSpec(memory_space=pl.ANY)
    shapes = [(1,) + act.shape, (1,) + ig.shape, total_a.shape, total_b.shape]
    kinds = [act.dtype, ig.dtype, total_a.dtype, total_b.dtype]
    return pl.pallas_call(
        copy_kernel,
        out_shape=tuple(jax.ShapeDtypeStruct(a, b) for a, b in zip(shapes, kinds)),
        in_specs=[anywhere] * 4,
        out_specs=(anywhere,) * 4,
        scratch_shapes=[
            pltpu.VMEM(v.shape, v.dtype) for v in (act, ig, total_a, total_b)
        ] + [pltpu.SemaphoreType.DMA((6,))] * 2,
        name="settle",
    )(act, ig, total_a, total_b)


def per_pair(
    tokens, cotangent, buckets, lengths, norm_gain_pairs, norm_bias_pairs, query_key_value_weight,
    query_value_bias, output_weight, upward_weight, upward_bias, down_weight, output_bias,
    adapter_down, adapter_upper,
):
    weight_qkv = query_key_value_weight[0].transpose(1, 0, 2)
    dp_count = lax.axis_size("dp")
    anywhere = pl.BlockSpec(memory_space=pl.ANY)
    scalars = pl.BlockSpec(memory_space=pltpu.SMEM)
    vmem = pl.BlockSpec(memory_space=pltpu.VMEM)
    dma = pltpu.SemaphoreType.DMA
    act, ig, total_a, total_b = pl.pallas_call(
        partial(fused_kernel, dp_count),
        out_shape=(
            jax.ShapeDtypeStruct((2, R, D), BF16),
            jax.ShapeDtypeStruct((2, R, D), BF16),
            jax.ShapeDtypeStruct((1, 2, 4, D), F32),
            jax.ShapeDtypeStruct((1, 2, 4, 256), F32),
        ),
        in_specs=[anywhere, anywhere, scalars, scalars, vmem, vmem, anywhere, vmem, anywhere, anywhere, vmem,
                  anywhere, vmem, vmem, vmem],
        out_specs=(anywhere, anywhere, vmem, vmem),
        scratch_shapes=[
            pltpu.VMEM((2, 2, 32, D), F32),
            pltpu.VMEM((2, 2, D, 768), BF16),
            pltpu.VMEM((2, 2, 256, D), BF16),
            pltpu.VMEM((2, 2, D, 1024), BF16),
            pltpu.VMEM((2, 2, 1024, D), BF16),
            pltpu.VMEM((2, 2, R, D), BF16),
            pltpu.VMEM((2, R, D), BF16),
            pltpu.VMEM((2, 2, R, D), F32),
            pltpu.VMEM((2, 2, R, 2048), BF16),
            pltpu.VMEM((2, 2, R, 512), BF16),
            pltpu.VMEM((2, 2, 4 * R, 512), BF16),
            pltpu.VMEM((2, 2, 512, R), BF16),
            pltpu.VMEM((2, 2, 8, 1, R), F32),
            pltpu.VMEM((3, 2, R, D), BF16),
            pltpu.VMEM((5, R, D), BF16),
            pltpu.VMEM((4, 4 * R, R), F32),
            pltpu.VMEM((6 * R, R), BF16),
            pltpu.VMEM((2, 4, R, R), F32),
            pltpu.VMEM((2, R, 768), BF16),
            pltpu.VMEM((R, D), BF16),
            pltpu.VMEM((2, 2, 8, R), BF16),
            pltpu.VMEM((8, 64, R), F32),
            pltpu.VMEM((16, R, R), BF16),
            pltpu.VMEM((2, 8, D), F32),
            pltpu.VMEM((2, 2, 8, 256), F32),
            pltpu.VMEM((8, D), F32),
            pltpu.VMEM((2, 8, 256), F32),
            pltpu.VMEM((3, 8, D), F32),
            pltpu.VMEM((8, 256), F32),
            pltpu.VMEM((dp_count, 8, D), F32),
            pltpu.VMEM((dp_count, 8, 256), F32),
            dma((2, 2)),
            dma((2,)),
            dma((2,)),
            dma((5,)),
            dma((5,)),
            dma((5,)),
            dma((14,)),
            dma((14,)),
            dma((13,)),
            dma((13,)),
            dma((14,)),
            dma((14,)),
            dma((13,)),
            dma((13,)),
            dma((2, 2)),
            dma((2, 2)),
            dma((3, 2)),
            dma((3, 2)),
            dma((4,)),
            dma((4,)),
            dma((2,)),
            dma((2,)),
            dma((2, 2)),
            dma((4,)),
            dma((2,)),
            dma((2,)),
            dma((4,)),
            dma((4,)),
            dma((2, dp_count - 1)),
            dma((2, dp_count - 1)),
        ],
        compiler_params=pltpu.CompilerParams(
            collective_id=0, has_side_effects=True, vmem_limit_bytes=127 * 2**19
        ),
        name="two_layers",
    )(
        tokens, cotangent, buckets, lengths, norm_gain_pairs, norm_bias_pairs, weight_qkv, query_value_bias,
        output_weight, upward_weight, upward_bias, down_weight, output_bias, adapter_down, adapter_upper,
    )
    return settle(act, ig, total_a, total_b)


def solution(mesh):
    in_specs = (
        P("dp", "tensor", None),
        P("dp", "tensor", None),
        P("dp"),
        P("dp", None),
        P("section", None, None),
        P("section", None, None),
        P("section", None, None, "tensor"),
        P("section", None, "tensor"),
        P("section", "tensor", None),
        P("section", None, "tensor"),
        P("section", "tensor"),
        P("section", "tensor", None),
        P("section", None, None),
        P("section", None, None, None),
        P("section", None, None, "tensor"),
    )
    out_specs = (
        P("section", "dp", "tensor", None),
        P("section", "dp", "tensor", None),
        P("section", None, None, None),
        P("section", None, None, "tensor"),
    )
    pairs = mesh.shape["section"] == 2 and mesh.shape["tensor"] == 4 and mesh.shape["dp"] % 2 == 0
    return jax.shard_map(
        per_pair if pairs else per_device, mesh=mesh, in_specs=in_specs, out_specs=out_specs, check_vma=False
    )
```

```python
from functools import partial

import jax
import jax.numpy as jnp
from jax import lax
from jax.experimental import pallas as pl
from jax.experimental.pallas import tpu as pltpu
from jax.sharding import PartitionSpec as P

HEAD_DIM = 64


adapter_scale = 8.0
norm_eps = 1e-05
masked_score = -1000000000.0
highest_precision = lax.Precision.HIGHEST


def from_behind(block, axis, distance):
    devices = range(lax.axis_size(axis))
    route = [(i - distance, i) for i in devices if i - distance in devices]
    return lax.ppermute(block, axis, route)


def layer_norm(values, gain_rows, shifts):
    center = jnp.mean(values, axis=-1, keepdims=True)
    centered = values - center
    spread = jnp.mean(centered * centered, axis=-1, keepdims=True)
    return centered * lax.rsqrt(spread + norm_eps) * gain_rows + shifts


def row_layout(bucket, lengths_row, row_count):
    item_span = jnp.right_shift(jnp.int32(row_count), 3 - bucket)
    positions = jnp.arange(row_count, dtype=jnp.int32)
    item_index = positions // item_span
    within = positions - item_index * item_span
    chosen = (
        item_index[:, None] == jnp.arange(lengths_row.shape[0], dtype=jnp.int32)[None, :]
    ).astype(jnp.int32)
    length = jnp.sum(chosen * lengths_row[None, :], axis=1)
    return (item_index, within < length)


def allowed_keys(item_index, is_valid):
    positions = jnp.arange(item_index.shape[0], dtype=jnp.int32)
    same_item = item_index[:, None] == item_index[None, :]
    causal = positions[None, :] <= positions[:, None]
    key_seen = is_valid[None, :] | (positions[None, :] == positions[:, None])
    return same_item & causal & key_seen


def take_slot(buffer, slot_index):
    return lax.dynamic_index_in_dim(buffer, slot_index, 0, keepdims=False)


def put_slot(buffer, slot_index, is_live, update):
    previous = take_slot(buffer, slot_index)
    return lax.dynamic_update_index_in_dim(
        buffer, jnp.where(is_live, update, previous), slot_index, 0
    )


def per_device(
    tokens,
    cotangent,
    buckets,
    lengths,
    norm_gain_pairs,
    norm_bias_pairs,
    query_key_value_weight,
    query_value_bias,
    output_weight,
    upward_weight,
    upward_bias,
    down_weight,
    output_bias,
    adapter_down,
    adapter_upper,
):
    section_index = lax.axis_index("section")
    tensor_count = lax.axis_size("tensor")
    micro_count, own_rows, model_width = tokens.shape
    row_count = own_rows * tensor_count
    own_start = lax.axis_index("tensor") * own_rows
    gain_sets = norm_gain_pairs[0].astype(jnp.float32)
    shift_sets = norm_bias_pairs[0].astype(jnp.float32)
    weight_qkv = query_key_value_weight[0]
    bias_query_value = query_value_bias[0].astype(jnp.float32)
    weight_out = output_weight[0]
    weight_up = upward_weight[0]
    bias_up = upward_bias[0].astype(jnp.float32)
    weight_down = down_weight[0]
    biases = output_bias[0].astype(jnp.float32)
    down_factor = adapter_down[0]
    upper_factor = adapter_upper[0]
    factor_wide = down_factor.astype(jnp.float32)
    local_width = weight_qkv.shape[2]
    local_heads = local_width // HEAD_DIM
    score_scale = HEAD_DIM ** (-0.5)

    def widen(values):
        return lax.all_gather(values, "tensor", axis=0, tiled=True)

    def widen_back(values):
        return lax.all_gather(values, "tensor", axis=0, tiled=True)

    def settle(source, weight):

        def row_term(first_row, row_span):
            return jnp.dot(source, weight, preferred_element_type=jnp.float32)

        return lax.psum_scatter(
            row_term(jnp.int32(0), lax.axis_size("tensor") * own_rows).astype(jnp.bfloat16),
            "tensor",
            scatter_dimension=0,
            tiled=True,
        ).astype(jnp.float32)

    def settle_back(row_term):
        return lax.psum_scatter(
            row_term(jnp.int32(0), lax.axis_size("tensor") * own_rows).astype(jnp.bfloat16),
            "tensor",
            scatter_dimension=0,
            tiled=True,
        ).astype(jnp.float32)

    def layout_of(slot_index):
        item_index, is_valid = row_layout(
            take_slot(buckets, slot_index), take_slot(lengths, slot_index), row_count
        )
        own_valid = lax.dynamic_slice_in_dim(is_valid, own_start, own_rows, 0)
        return (allowed_keys(item_index, is_valid), own_valid)

    def attend(normed, allowed):
        reduced_query = jnp.dot(
            normed, down_factor[0].T, preferred_element_type=jnp.float32
        ).astype(jnp.bfloat16)
        reduced_value = jnp.dot(
            normed, down_factor[1].T, preferred_element_type=jnp.float32
        ).astype(jnp.bfloat16)
        blended_rows = jnp.einsum(
            "rd,dcn->rcn", normed, weight_qkv, preferred_element_type=jnp.float32
        )
        query_matrix_rows = (
            blended_rows[:, 0]
            + bias_query_value[0]
            + adapter_scale
            * jnp.dot(reduced_query, upper_factor[0], preferred_element_type=jnp.float32)
        )
        value_matrix_rows = (
            blended_rows[:, 2]
            + bias_query_value[1]
            + adapter_scale
            * jnp.dot(reduced_value, upper_factor[1], preferred_element_type=jnp.float32)
        )
        packed = jnp.stack(
            [query_matrix_rows, blended_rows[:, 1], value_matrix_rows], axis=1
        ).astype(jnp.bfloat16)
        head_split = packed.reshape(row_count, 3, local_heads, HEAD_DIM)
        scores = (
            jnp.einsum(
                "qhe,khe->hqk",
                head_split[:, 0],
                head_split[:, 1],
                preferred_element_type=jnp.float32,
            )
            * score_scale
        )
        scores = jnp.where(allowed[None], scores, masked_score)
        top_score = jnp.max(scores, axis=-1, keepdims=True)
        exponent = jnp.exp(scores - top_score)
        attn_probs = exponent / jnp.sum(exponent, axis=-1, keepdims=True)
        return (reduced_query, reduced_value, head_split, attn_probs)

    def forward(hidden, allowed):
        normed = widen(layer_norm(hidden, gain_sets[0], shift_sets[0]).astype(jnp.bfloat16))
        reduced_query, reduced_value, head_split, attn_probs = attend(normed, allowed)
        probs_low = attn_probs.astype(jnp.bfloat16)
        mixed_heads = jnp.einsum(
            "hqk,khe->qhe", probs_low, head_split[:, 2], preferred_element_type=jnp.float32
        )
        attended = mixed_heads.reshape(row_count, local_width).astype(jnp.bfloat16)
        middle = hidden + (settle(attended, weight_out) + biases[0])
        normed_two = widen(layer_norm(middle, gain_sets[1], shift_sets[1]).astype(jnp.bfloat16))
        hidden_pre = jnp.dot(normed_two, weight_up, preferred_element_type=jnp.float32) + bias_up
        activated = jax.nn.gelu(hidden_pre, approximate=True).astype(jnp.bfloat16)
        output = middle + (settle(activated, weight_down) + biases[1])
        return (output, normed, middle, normed_two)

    def backward(hidden, grad_out, allowed, normed, middle, normed_two):
        reduced_query, reduced_value, head_split, attn_probs = attend(normed, allowed)
        probs_low = attn_probs.astype(jnp.bfloat16)
        hidden_pre = jnp.dot(normed_two, weight_up, preferred_element_type=jnp.float32) + bias_up
        grad_branch = widen_back(grad_out.astype(jnp.bfloat16))
        grad_act = jnp.einsum(
            "rd,fd->rf", grad_branch, weight_down, preferred_element_type=jnp.float32
        )
        gelu_pull = jax.vjp(partial(jax.nn.gelu, approximate=True), hidden_pre)[1]
        grad_pre = gelu_pull(grad_act)[0].astype(jnp.bfloat16)

        def mlp_term(first_row, row_span):
            return jnp.einsum("rf,df->rd", grad_pre, weight_up, preferred_element_type=jnp.float32)

        grad_norm_two = settle_back(mlp_term)
        second_pull = jax.vjp(
            partial(layer_norm, gain_rows=gain_sets[1], shifts=shift_sets[1]), middle
        )[1]
        grad_middle = grad_out + second_pull(grad_norm_two)[0]
        grad_attn = widen_back(grad_middle.astype(jnp.bfloat16))
        grad_heads = jnp.einsum(
            "rd,nd->rn", grad_attn, weight_out, preferred_element_type=jnp.float32
        )
        grad_heads = grad_heads.astype(jnp.bfloat16).reshape(row_count, local_heads, HEAD_DIM)
        grad_probs = jnp.einsum(
            "qhe,khe->hqk", grad_heads, head_split[:, 2], preferred_element_type=jnp.float32
        )
        grad_scores = attn_probs * (
            grad_probs - jnp.sum(attn_probs * grad_probs, axis=-1, keepdims=True)
        )
        grad_scores = grad_scores.astype(jnp.bfloat16)
        grad_query = (
            jnp.einsum(
                "hqk,khe->qhe", grad_scores, head_split[:, 1], preferred_element_type=jnp.float32
            )
            * score_scale
        )
        grad_key = (
            jnp.einsum(
                "hqk,qhe->khe", grad_scores, head_split[:, 0], preferred_element_type=jnp.float32
            )
            * score_scale
        )
        grad_value = jnp.einsum(
            "hqk,qhe->khe", probs_low, grad_heads, preferred_element_type=jnp.float32
        )
        grad_packed = (
            jnp.stack([grad_query, grad_key, grad_value], axis=1)
            .reshape(row_count, 3, local_width)
            .astype(jnp.bfloat16)
        )
        grad_pair = jnp.stack([grad_packed[:, 0], grad_packed[:, 2]])
        gradient_reduced = adapter_scale * jnp.einsum(
            "jrn,jkn->jrk", grad_pair, upper_factor, preferred_element_type=jnp.float32
        )

        def attn_term(first_row, row_span):
            dense_part = jnp.einsum(
                "rcn,dcn->rd", grad_packed, weight_qkv, preferred_element_type=jnp.float32
            )
            return dense_part + jnp.einsum(
                "jrk,jkd->rd", gradient_reduced, factor_wide, precision=highest_precision
            )

        grad_normed = settle_back(attn_term)
        first_pull = jax.vjp(
            partial(layer_norm, gain_rows=gain_sets[0], shifts=shift_sets[0]), hidden
        )[1]
        grad_hidden = grad_middle + first_pull(grad_normed)[0]
        grad_factor_a = jnp.einsum(
            "jrk,rd->jkd", gradient_reduced, normed.astype(jnp.float32), precision=highest_precision
        )
        gradient_upper_factor = adapter_scale * jnp.stack(
            [
                jnp.einsum(
                    "rk,rn->kn",
                    reduced_query,
                    grad_packed[:, 0],
                    preferred_element_type=jnp.float32,
                ),
                jnp.einsum(
                    "rk,rn->kn",
                    reduced_value,
                    grad_packed[:, 2],
                    preferred_element_type=jnp.float32,
                ),
            ]
        )
        return (grad_hidden, grad_factor_a, gradient_upper_factor)

    zero_rows = jnp.zeros((micro_count, own_rows, model_width), jnp.bfloat16)
    saved_start = ()

    def record(buffers, slot_index, is_live, layer_input, results):
        kept_in, outputs, saved = buffers
        output, normed, middle, normed_two = results
        low_output = output.astype(jnp.bfloat16)
        kept_in = put_slot(kept_in, slot_index, is_live, layer_input)
        outputs = put_slot(outputs, slot_index, is_live, low_output)
        return ((kept_in, outputs, saved), low_output)

    buffers = (zero_rows, zero_rows, saved_start)

    def run_phase(buffers, sources, phase_section):

        def phase_turn(slot_index, buffers):
            allowed, own_valid = layout_of(slot_index)
            layer_input = take_slot(sources, slot_index)
            results = forward(layer_input.astype(jnp.float32), allowed)
            return record(
                buffers, slot_index, section_index == phase_section, layer_input, results
            )[0]

        return lax.fori_loop(0, micro_count, phase_turn, buffers)

    buffers = run_phase(buffers, tokens, 0)
    received = from_behind(buffers[1], "section", 1)
    buffers = run_phase(buffers, received, 1)
    kept_in, outputs, saved = buffers

    def back_step(slot_index, grad_out, allowed):
        hidden = take_slot(kept_in, slot_index).astype(jnp.float32)
        output, normed, middle, normed_two = forward(hidden, allowed)
        return backward(hidden, grad_out, allowed, normed, middle, normed_two)

    def top_grad(slot_index, own_valid):
        return take_slot(cotangent, slot_index).astype(jnp.float32) * own_valid[:, None].astype(
            jnp.float32
        )

    zero_a = jnp.zeros(down_factor.shape, jnp.float32)
    zero_b = jnp.zeros(upper_factor.shape, jnp.float32)

    def run_back(loop_state, sources, phase_section):

        def phase_turn(slot_index, loop_state):
            grads_in, sum_a, sum_b = loop_state
            allowed, own_valid = layout_of(slot_index)
            if phase_section == 1:
                grad_out = top_grad(slot_index, own_valid)
            else:
                grad_out = take_slot(sources, slot_index).astype(jnp.float32)
            is_live = section_index == phase_section
            grad_hidden, grad_a, grad_b = back_step(slot_index, grad_out, allowed)
            grads_in = put_slot(grads_in, slot_index, is_live, grad_hidden.astype(jnp.bfloat16))
            sum_a = sum_a + jnp.where(is_live, grad_a, 0.0)
            sum_b = sum_b + jnp.where(is_live, grad_b, 0.0)
            return (grads_in, sum_a, sum_b)

        return lax.fori_loop(0, micro_count, phase_turn, loop_state)

    loop_state = run_back((zero_rows, zero_a, zero_b), zero_rows, 1)
    received_grads = from_behind(loop_state[0], "section", -1)
    grads_in, sum_a, sum_b = run_back(loop_state, received_grads, 0)
    total_a = lax.psum(sum_a, ("dp", "tensor"))
    total_b = lax.psum(sum_b, "dp")
    return (outputs[None], grads_in[None], total_a[None], total_b[None])


R = 256
D = 1024
NEG = -1e30
F32 = jnp.float32
BF16 = jnp.bfloat16
MESH = pl.DeviceIdType.MESH
CHUNK = 128


def nn(a, b):
    return lax.dot_general(a, b, (((1,), (0,)), ((), ())), preferred_element_type=F32)


def nt(a, b):
    return lax.dot_general(a, b, (((1,), (1,)), ((), ())), preferred_element_type=F32)


def tn(a, b):
    return lax.dot_general(a, b, (((0,), (0,)), ((), ())), preferred_element_type=F32)


def normalize(v):
    centered = v - jnp.mean(v, axis=-1, keepdims=True)
    rs = lax.rsqrt(jnp.mean(centered * centered, axis=-1, keepdims=True) + norm_eps)
    return centered * rs, rs


def norm_pull(v, g):
    xhat, rs = normalize(v)
    return rs * (
        g
        - jnp.mean(g, axis=-1, keepdims=True)
        - xhat * jnp.mean(g * xhat, axis=-1, keepdims=True)
    )


def gelu_pair(z):
    c = 0.7978845608028654
    z2 = z * z
    t = jnp.tanh(c * (z + 0.044715 * (z2 * z)))
    half = 0.5 * (1.0 + t)
    slope = half + (0.5 * c) * z * (1.0 - t * t) * (1.0 + (3.0 * 0.044715) * z2)
    return z * half, slope


def fused_kernel(
    dp_count,
    tok, cot, buckets, lengths, gain_in, shift_in, wq_in, bqv_in, wo_in, wu_in, bu_in, wd_in, bo_in, ad_in, au_in,
    act, ig, out_a, out_b,
    SP, WQ, WO, WU, WD, H, DY, MID, GP, Q, KV, OT, LSE, SND, RCV, BIG, MSK, DR, DQ, AB, U, OACC, PB,
    GA, GB, GCA, GCB, GXA, GXB, GZA, GZB,
    tok_sem, tok_ys, tok_xs, wl, ws_r, ws_s, wy_r, wy_s, wz_r, wz_s, wa_r, wa_s, wb_r, wb_s,
    kv_rcv, kv_snd, x_rcv, x_snd, last_rcv, last_snd, dr_rcv, dr_snd, out_rcv, out_snd, gc_r, gc_s, gx_r, gx_s, gz_r, gz_s,
):
    s = lax.axis_index("section")
    d = lax.axis_index("dp")
    t = lax.axis_index("tensor")
    x = lax.rem(t, 2)
    y = lax.div(t, 2)
    sib = (1 - s, d, t)
    xp = (s, d, y * 2 + 1 - x)
    yp = (s, d, (1 - y) * 2 + x)
    z_half = lax.rem(d, 2)
    zp = (s, d + 1 - 2 * z_half, t)
    flip = s + x - 2 * s * x
    own_i = flip

    def blk_of(i):
        return 2 * i + (s + i - 2 * s * i)

    bar = pltpu.get_barrier_semaphore()
    for ds_ in range(2):
        for dx in range(2):
            for dy in range(2):
                if ds_ or dx or dy:
                    s2 = 1 - s if ds_ else s
                    x2 = 1 - x if dx else x
                    y2 = 1 - y if dy else y
                    pl.semaphore_signal(bar, 1, device_id=(s2, d, y2 * 2 + x2), device_id_type=MESH)
    for k in range(1, dp_count):
        pl.semaphore_signal(bar, 1, device_id=(s, lax.rem(d + k, dp_count), t), device_id_type=MESH)
    pl.semaphore_wait(bar, 7 + dp_count - 1)

    def row_copies(src, dst, w):
        def local():
            return pltpu.make_async_copy(src.at[y], dst.at[y], tok_sem.at[w, y])

        def to_y():
            return pltpu.make_async_remote_copy(
                src.at[1 - y], dst.at[y], tok_ys.at[w], tok_sem.at[w, y], device_id=yp, device_id_type=MESH)

        def first_x():
            return pltpu.make_async_remote_copy(
                src.at[y], dst.at[y], tok_xs.at[w], tok_sem.at[w, y], device_id=xp, device_id_type=MESH)

        def then_x():
            return pltpu.make_async_remote_copy(
                dst.at[own_i], dst.at[own_i], tok_xs.at[w], tok_sem.at[w, own_i],
                device_id=xp, device_id_type=MESH)

        return local, to_y, first_x, then_x

    def rows_first(src, dst, w):
        local, _, first_x, _ = row_copies(src, dst, w)

        @pl.when(y == own_i)
        def _():
            first_x().start()
            local().start()

    def rows_swap(src, dst, w):
        @pl.when(y == own_i)
        def _():
            row_copies(src, dst, w)[1]().start()

    def rows_relay(src, dst, w):
        pltpu.make_async_copy(src.at[0], dst.at[own_i], tok_sem.at[w, own_i]).wait()

        @pl.when(y != own_i)
        def _():
            row_copies(src, dst, w)[3]().start()

    def rows_rest(src, dst, w):
        pltpu.make_async_copy(src.at[0], dst.at[1 - own_i], tok_sem.at[w, 1 - own_i]).wait()

    def rows_done(src, dst, w):
        _, to_y, first_x, _ = row_copies(src, dst, w)
        if w == 0:
            first_x().wait_send()

        @pl.when(y == own_i)
        def _():
            to_y().wait_send()

    pieces = (None, (wq_in, WQ, 4), (wo_in, WO, 1), (wu_in, WU, 4), (wd_in, WD, 4))
    base = (13, 0, 4, 5, 9)

    def relayer(l, c):
        return 1 - l if c % 2 else l

    def sources(p, rows):
        src, dst, _ = pieces[p]
        if p == 1:
            return [
                (src.at[c, rows, :], dst.at[s, y, rows, c * 256 : c * 256 + 256]) for c in range(3)
            ]
        return [(src.at[0, rows, :], dst.at[s, y, rows, :])]

    def chunk(p, c, half):
        dst, parts = pieces[p][1], pieces[p][2]
        size = dst.shape[2] // (2 * parts)
        return pl.ds(pl.multiple_of((half * parts + c) * size, size), size)

    def block(p, l, j, rows):
        return pieces[p][1].at[l, j, rows, :]

    def own_start(p):
        everything = pl.ds(0, pieces[p][1].shape[2])
        for src, dst in sources(p, everything):
            pltpu.make_async_copy(src, dst, wl.at[p]).start()
            pltpu.make_async_remote_copy(
                src, dst, ws_s.at[p], ws_r.at[p], device_id=sib, device_id_type=MESH).start()

    def whole_by_y(l, p, c):
        return p == 4 and c >= 2

    def y_start(l, p):
        for c in range(pieces[p][2] if p else 1):
            k = base[p] + c

            @pl.when(s == relayer(l, c))
            def _():
                if p == 0:
                    ref = SP.at[l, y, 16:32, :]
                    pltpu.make_async_remote_copy(
                        ref, ref, wy_s.at[k], wy_r.at[k], device_id=yp, device_id_type=MESH).start()
                    return
                rows = chunk(p, c, z_half)
                mine = block(p, l, y, rows)
                for src, dst in [(mine, mine)] if c % 2 else sources(p, rows):
                    pltpu.make_async_remote_copy(
                        src, dst, wy_s.at[k], wy_r.at[k], device_id=yp, device_id_type=MESH).start()
                if whole_by_y(l, p, c):
                    rows = chunk(p, c, 1 - z_half)
                    mine = block(p, l, y, rows)
                    for src, dst in [(mine, mine)] if c % 2 else sources(p, rows):
                        pltpu.make_async_remote_copy(
                            src, dst, wz_s.at[k], wz_r.at[k], device_id=yp, device_id_type=MESH).start()

    def small_copy(to, snd, rcv):
        return pltpu.make_async_remote_copy(
            SP.at[s, y], SP.at[s, y], snd, rcv, device_id=to, device_id_type=MESH)

    def passed(l, p, c, half, to, snd, rcv):
        ref = SP.at[l, 1 - y, 16:32, :] if p == 0 else block(p, l, 1 - y, chunk(p, c, half))
        return pltpu.make_async_remote_copy(ref, ref, snd, rcv, device_id=to, device_id_type=MESH)

    def relay_y(l, p):
        for c in range(pieces[p][2] if p else 1):
            k = base[p] + c

            @pl.when(s == relayer(l, c))
            def _():
                passed(l, p, c, z_half, sib, wa_s.at[k], wy_r.at[k]).wait_recv()
                if p and not (p == 4 and c >= 2):
                    passed(l, p, c, z_half, zp, wz_s.at[k], wz_r.at[k]).start()

                passed(l, p, c, z_half, sib, wa_s.at[k], wa_r.at[k]).start()

    def relay_z(l, p):
        for c in range(pieces[p][2]):
            k = base[p] + c

            @pl.when(s == relayer(l, c))
            def _():
                passed(l, p, c, 1 - z_half, zp, wz_s.at[k], wz_r.at[k]).wait_recv()
                passed(l, p, c, 1 - z_half, sib, wb_s.at[k], wb_r.at[k]).start()

    def own_wait(l, p):
        @pl.when(l == s)
        def _():
            if p:
                ref = pieces[p][1].at[s, y]
                pltpu.make_async_copy(ref, ref, wl.at[p]).wait()

        @pl.when(l != s)
        def _():
            ref = pieces[p][1].at[1 - s, y] if p else SP.at[1 - s, y]
            pltpu.make_async_copy(ref, ref, ws_r.at[p]).wait()

    def other_wait(l, p):
        for c in range(pieces[p][2] if p else 1):
            k = base[p] + c

            @pl.when(s != relayer(l, c))
            def _():
                if p == 0:
                    ref = SP.at[l, 1 - y, 16:32, :]
                    pltpu.make_async_copy(ref, ref, wa_r.at[13]).wait()
                else:
                    ref = block(p, l, 1 - y, chunk(p, c, 0))
                    pltpu.make_async_copy(ref, ref, wa_r.at[k]).wait()
                    pltpu.make_async_copy(ref, ref, wb_r.at[k]).wait()

    rows_swap(tok, H.at[0], 0)
    rows_first(tok, H.at[0], 0)
    own_start(1)
    SP[s, y] = jnp.zeros(SP.shape[2:], F32)
    for k, (ref, row) in enumerate(
        ((gain_in, 0), (shift_in, 0), (gain_in, 1), (shift_in, 1), (bo_in, 0), (bo_in, 1))
    ):
        SP[s, y, k : k + 1, :] = ref[0, row : row + 1, :].astype(F32)
    SP[s, y, 8:12, :] = ad_in[0, 0].astype(F32)
    SP[s, y, 12:16, :] = ad_in[0, 1].astype(F32)
    SP[s, y, 16:17, :] = bu_in[...].astype(F32)
    SP[s, y, 17:18, 0:256] = bqv_in[0, 0:1, :].astype(F32)
    SP[s, y, 17:18, 512:768] = bqv_in[0, 1:2, :].astype(F32)
    SP[s, y, 24:28, 0:256] = au_in[0, 0].astype(F32)
    SP[s, y, 28:32, 512:768] = au_in[0, 1].astype(F32)
    small_copy(sib, ws_s.at[0], ws_r.at[0]).start()
    y_start(0, 0)
    for p in range(2, 5):
        own_start(p)
    for l in range(2):
        for p in range(5):
            own_wait(l, p)
            if l or p:
                y_start(l, p)

    shift = 7 + buckets[y]
    span_mask = lax.shift_left(jnp.int32(1), shift) - 1

    def length_of(pos):
        item = lax.shift_right_logical(pos, jnp.broadcast_to(shift, pos.shape))
        got = jnp.zeros(pos.shape, jnp.int32)
        for k in range(lengths.shape[1]):
            got = jnp.where(item == k, lengths[y, k], got)
        return item, jnp.bitwise_and(pos, span_mask) < got

    def build_mask(i):
        b = blk_of(i)
        q_row = b * R + lax.broadcasted_iota(jnp.int32, (1, R), 1)
        q_item = lax.shift_right_logical(q_row, jnp.broadcast_to(shift, q_row.shape))

        def rows(r, carry):
            r0 = pl.multiple_of(r * CHUNK, CHUNK)
            k_row = r0 + lax.broadcasted_iota(jnp.int32, (CHUNK, 1), 0)
            k_item, k_ok = length_of(k_row)
            k_tag = jnp.where(k_ok, k_item, -1)
            same = (k_tag == q_item) & (k_row <= q_row)
            allowed = same | (k_row == q_row)
            MSK[pl.ds(pl.multiple_of(i * 2 * R + r0, CHUNK), CHUNK), :] = jnp.where(allowed, 0.0, NEG).astype(BF16)
            return carry

        lax.fori_loop(0, (b + 1) * (R // CHUNK), rows, 0)

    build_mask(0)
    build_mask(1)
    GA[...] = jnp.zeros(GA.shape, F32)
    GB[...] = jnp.zeros(GB.shape, F32)

    def x_copy(slot, i):
        return pltpu.make_async_remote_copy(
            SND.at[slot, i], RCV.at[slot * 2 + (i if slot < 2 else 0)], x_snd.at[slot, i], x_rcv.at[slot, i],
            device_id=xp, device_id_type=MESH)

    def last_copy(c, i):
        rows = slice(c * 64, c * 64 + 64)
        return pltpu.make_async_remote_copy(
            SND.at[0, i, rows, :], RCV.at[i, rows, :], last_snd.at[c], last_rcv.at[c],
            device_id=xp, device_id_type=MESH)

    def by_rows(body):
        body(slice(0, R))

    total_rows = slice(3 * R, 4 * R)

    def gather(n, term):
        for c in range(4):
            part = term[:, c * R : c * R + R]
            BIG[c, total_rows, :] = part if n == 0 else BIG[c, total_rows, :] + part

    def gathered():
        return jnp.concatenate([BIG[c, total_rows, :] for c in range(4)], axis=1).astype(BF16)

    def swapped(slot, i, rows):
        return SND[slot, i, rows, :].astype(F32) + RCV[slot * 2 + (i if slot < 2 else 0), rows, :].astype(F32)

    def send_result(which, layer, src, rows=slice(0, R)):
        src = src.at[rows, :]
        dst = act if which < 2 else ig
        o = 0 if which < 2 else 1
        here = (s == layer) & (y == own_i)

        @pl.when(here)
        def _():
            pltpu.make_async_copy(src, dst.at[y, rows, :], out_rcv.at[o, y]).start()

        @pl.when(jnp.logical_not(here))
        def _():
            pltpu.make_async_remote_copy(
                src, dst.at[y, rows, :], out_snd.at[which], out_rcv.at[o, y],
                device_id=(layer, d, own_i * 2 + x), device_id_type=MESH).start()

    def send_result_done(which, layer, src):
        dst = act if which < 2 else ig
        o = 0 if which < 2 else 1
        here = (s == layer) & (y == own_i)

        @pl.when(jnp.logical_not(here))
        def _():
            pltpu.make_async_remote_copy(
                src, dst.at[y], out_snd.at[which], out_rcv.at[o, y],
                device_id=(layer, d, own_i * 2 + x), device_id_type=MESH).wait_send()

    def vec(l, k):
        return SP[l, y, k : k + 1, :]

    def head_lanes(pair):
        return pl.ds(pl.multiple_of(pair * 128, 128), 128)

    def split_pair(v, axis):
        which = lax.broadcasted_iota(jnp.int32, v.shape, axis) < HEAD_DIM
        zero = jnp.zeros_like(v)
        return jnp.where(which, v, zero), jnp.where(which, zero, v)

    def kv_copy(l, i):
        rows = pl.ds(pl.multiple_of(blk_of(i) * R, R), R)
        return pltpu.make_async_remote_copy(
            KV.at[l, :, rows, :], KV.at[l, :, rows, :], kv_snd.at[l, i], kv_rcv.at[l, i],
            device_id=sib, device_id_type=MESH)

    def kv_wait(l, i):
        b = 2 * i + (1 - s + i - 2 * (1 - s) * i)
        rows = pl.ds(pl.multiple_of(b * R, R), R)
        pltpu.make_async_remote_copy(
            KV.at[l, :, rows, :], KV.at[l, :, rows, :], kv_snd.at[l, i], kv_rcv.at[l, i],
            device_id=sib, device_id_type=MESH).wait_recv()

    GROUP = 4

    def attend(l, i):
        b = blk_of(i)

        def group_turn(g, carry):
            def lanes_of(k):
                return pl.ds(pl.multiple_of(g * (GROUP * HEAD_DIM) + k * 128, 128), 128)

            def first(j, tops):
                rows = pl.ds(pl.multiple_of(j * R, R), R)
                mask = MSK[pl.ds(pl.multiple_of((i * 2 + j) * R, R), R), :].astype(F32)
                new = []
                for k in range(GROUP // 2):
                    qs = split_pair(Q[l, i, :, lanes_of(k)], 1)
                    keys = KV[l, 0, rows, lanes_of(k)]
                    for e in range(2):
                        st = nt(keys, qs[e]) + mask
                        BIG[2 * k + e, rows, :] = st
                        new.append(jnp.maximum(tops[2 * k + e], jnp.max(st, axis=0, keepdims=True)))
                return tuple(new)

            tops = lax.fori_loop(0, b + 1, first, (jnp.full((1, R), NEG, F32),) * GROUP)
            for k in range(GROUP):
                OACC[k] = jnp.zeros(OACC.shape[1:], F32)

            def second(j, sums):
                rows = pl.ds(pl.multiple_of(j * R, R), R)
                new = []
                for k in range(GROUP):
                    p = jnp.exp(BIG[k, rows, :] - tops[k])
                    new.append(sums[k] + jnp.sum(p, axis=0, keepdims=True))
                    PB[k] = p.astype(BF16)
                for k in range(GROUP // 2):
                    values = jnp.transpose(KV[l, 1, rows, lanes_of(k)])
                    for e in range(2):
                        OACC[2 * k + e] += nn(values[e * 64 : e * 64 + 64], PB[2 * k + e])
                return tuple(new)

            sums = lax.fori_loop(0, b + 1, second, (jnp.zeros((1, R), F32),) * GROUP)
            for k in range(GROUP):
                OT[l, i, pl.ds(pl.multiple_of((g * GROUP + k) * 64, 64), 64), :] = (
                    OACC[k] * (1.0 / sums[k])
                ).astype(BF16)
                LSE[l, i, g * GROUP + k] = tops[k] + jnp.log(sums[k])
            return carry

        lax.fori_loop(0, Q.shape[3] // (GROUP * HEAD_DIM), group_turn, 0)

    def forward_attention(l, i):
        b = blk_of(i)

        @pl.when(i == 0)
        def _():
            @pl.when(l == 0)
            def _():
                rows_relay(tok, H.at[0], 0)
                relay_y(l, 0)
                relay_y(l, 1)
                rows_first(cot, DY, 1)

                @pl.when(own_i == 1)
                def _():
                    rows_rest(tok, H.at[0], 0)

            other_wait(l, 0)
            relay_z(l, 1)

            @pl.when(l == 1)
            def _():
                relay_y(l, 2)
                relay_y(l, 3)

            other_wait(l, 1)

        @pl.when(i == 1)
        def _():
            @pl.when((l == 0) & (own_i == 0))
            def _():
                rows_rest(tok, H.at[0], 0)


        @pl.when(l == 1)
        def _():
            x_copy(1, i).wait_recv()

            def rows_in(rows):
                h = MID[0, i, rows, :] + (swapped(1, i, rows) + vec(0, 5))
                H[1, i, rows, :] = h.astype(BF16)

            by_rows(rows_in)

            @pl.when(i == own_i)
            def _():
                send_result(0, 0, H.at[1, i])

        def rows_norm(rows):
            xhat, _ = normalize(H[l, i, rows, :].astype(F32))
            AB[rows, :] = (xhat * vec(l, 0) + vec(l, 1)).astype(BF16)

        by_rows(rows_norm)
        u = nt(AB[...], SP[l, y, 8:16, :].astype(BF16)).astype(BF16)
        own_rows = pl.ds(pl.multiple_of(b * R, R), R)
        for j in range(2):
            up = SP[l, j, 24:32, 256:768].astype(BF16)
            cols = slice(j * 256, j * 256 + 256)
            pair = nn(AB[...], WQ[l, j, :, 256:768]) + (adapter_scale * nn(u, up) + SP[l, j, 17:18, 256:768])
            KV[l, 0, own_rows, cols] = pair[:, 0:256].astype(BF16)
            KV[l, 1, own_rows, cols] = pair[:, 256:512].astype(BF16)

        @pl.when(b != 3)
        def _():
            kv_copy(l, i).start()

        for j in range(2):
            up = SP[l, j, 24:32, 0:256].astype(BF16)
            q = nn(AB[...], WQ[l, j, :, 0:256]) + (adapter_scale * nn(u, up) + SP[l, j, 17:18, 0:256])
            Q[l, i, :, j * 256 : j * 256 + 256] = (q * HEAD_DIM ** -0.5).astype(BF16)
        U[l, i] = nt(SP[l, y, 8:16, :].astype(BF16), AB[...]).astype(BF16)

        @pl.when((s == 1) & (i == 0))
        def _():
            kv_wait(l, 0)

        @pl.when((s == 0) & (i == 1))
        def _():
            kv_wait(l, 0)
            kv_wait(l, 1)

        @pl.when((i == 0) & (l == 0))
        def _():
            relay_y(l, 2)

        @pl.when(i == 1)
        def _():
            @pl.when(l == 0)
            def _():
                relay_y(l, 3)

            @pl.when(l == 1)
            def _():
                relay_y(l, 4)

        attend(l, i)

        @pl.when(i == 0)
        def _():
            relay_z(l, 2)
            other_wait(l, 2)

        @pl.when(l == 1)
        def _():
            x_copy(0, i).wait_send()

        SND[0, i] = (tn(OT[l, i, 0:256, :], WO[l, 0]) + tn(OT[l, i, 256:512, :], WO[l, 1])).astype(BF16)
        x_copy(0, i).start()

    def forward_ff(l, i):
        @pl.when((i == 0) & (l == 0))
        def _():
            relay_y(l, 4)

        @pl.when((i == 1) & (l == 0))
        def _():
            rows_swap(cot, DY, 1)

        @pl.when((i == 1) & (l == 1))
        def _():
            rows_relay(cot, DY, 1)

        x_copy(0, i).wait_recv()

        def rows_mid(rows):
            mid = H[l, i, rows, :].astype(F32) + (swapped(0, i, rows) + vec(l, 4))
            MID[l, i, rows, :] = mid
            xhat, _ = normalize(mid)
            AB[rows, :] = (xhat * vec(l, 2) + vec(l, 3)).astype(BF16)

        by_rows(rows_mid)
        for n in range(4):
            j, half = (y if n < 2 else 1 - y), n % 2
            cols = slice(half * 512, half * 512 + 512)
            if n == 2:

                @pl.when(i == 0)
                def _():
                    relay_z(l, 3)
                    relay_z(l, 4)
                    other_wait(l, 3)
                    other_wait(l, 4)

            z = nn(AB[...], WU[l, j, :, cols]) + SP[l, j, 16:17, cols]
            g, slope = gelu_pair(z)
            GP[l, i, :, n * 512 : n * 512 + 512] = slope.astype(BF16)
            term = nn(g.astype(BF16), WD[l, j, cols, :])
            gather(n, term)
        SND[1 + l, i] = gathered()

        @pl.when(l == 0)
        def _():
            x_copy(1, i).start()

            @pl.when(i == 1)
            def _():
                relay_y(1, 0)
                relay_y(1, 1)

        @pl.when((l == 1) & (i != own_i))
        def _():
            x_copy(2, i).start()

    def fwd_layer(l, carry):
        def a_turn(i, c):
            forward_attention(l, i)
            return c

        def f_turn(i, c):
            forward_ff(l, i)
            return c

        lax.fori_loop(0, 2, a_turn, 0)
        lax.fori_loop(0, 2, f_turn, 0)
        return carry

    lax.fori_loop(0, 2, fwd_layer, 0)

    def finish_forward():
        x_copy(2, own_i).wait_recv()

        def rows_out(rows):
            out = MID[1, own_i, rows, :] + (swapped(2, own_i, rows) + vec(1, 5))
            SND[2, own_i, rows, :] = out.astype(BF16)

        by_rows(rows_out)
        send_result(1, 1, SND.at[2, own_i])

    def backward_ff(l, i):
        @pl.when(l == 1)
        def _():
            @pl.when(i == own_i)
            def _():
                row_copies(cot, DY, 1)[3]().wait_send()

            @pl.when(i != own_i)
            def _():
                rows_rest(cot, DY, 1)

            def rows_valid(rows):
                pos = blk_of(i) * R + lax.broadcasted_iota(jnp.int32, (R, 1), 0)
                _, ok = length_of(pos)
                DY[i, rows, :] = (DY[i, rows, :].astype(F32) * jnp.where(ok, 1.0, 0.0)).astype(BF16)

            by_rows(rows_valid)

        @pl.when(l == 0)
        def _():
            x_copy(0, i).wait_recv()

            def rows_in(rows):
                g = swapped(0, i, rows) * vec(1, 0)
                DY[i, rows, :] = (MID[1, i, rows, :] + norm_pull(H[1, i, rows, :].astype(F32), g)).astype(BF16)

            by_rows(rows_in)

            @pl.when(i == own_i)
            def _():
                send_result(2, 1, DY.at[i])

        for n in range(4):
            j, half = (y if n < 2 else 1 - y), n % 2
            cols = slice(half * 512, half * 512 + 512)
            dg = nt(DY[i], WD[l, j, cols, :])
            dz = (GP[l, i, :, n * 512 : n * 512 + 512].astype(F32) * dg).astype(BF16)
            term = nt(dz, WU[l, j, :, cols])
            gather(n, term)

        x_copy(1, i).wait_send()
        SND[1, i] = gathered()
        x_copy(1, i).start()

    def dr_copy(k, b):
        rows = pl.ds(pl.multiple_of(b * R, R), R)
        return pltpu.make_async_remote_copy(
            BIG.at[:, rows, :], DR.at[k], dr_snd.at[k], dr_rcv.at[k], device_id=sib, device_id_type=MESH)

    def attend_back(l, i):
        b = blk_of(i)
        pairs = Q.shape[3] // 128
        place = RCV.at[2 + i]

        def back_rows(k):
            return place[(k % 2) * 128 : (k % 2) * 128 + 128, 512 + (k // 2) * 256 : 768 + (k // 2) * 256]

        deltas = []
        for k in range(pairs):
            rows = slice(k * 128, k * 128 + 128)
            prod = back_rows(k).astype(F32) * OT[l, i, rows, :].astype(F32)
            deltas.append(jnp.sum(prod[0:64], axis=0, keepdims=True))
            deltas.append(jnp.sum(prod[64:128], axis=0, keepdims=True))
            OACC[2 * k] = jnp.zeros(OACC.shape[1:], F32)
            OACC[2 * k + 1] = jnp.zeros(OACC.shape[1:], F32)

        def turn(step, c):
            j = lax.rem(2 * b - step, b + 1)
            rows = pl.ds(pl.multiple_of(j * R, R), R)
            mask = MSK[pl.ds(pl.multiple_of((i * 2 + j) * R, R), R), :].astype(F32)
            for k in range(pairs):
                lanes = slice(k * 128, k * 128 + 128)
                qs = split_pair(Q[l, i, :, lanes], 1)
                dots = split_pair(back_rows(k), 0)
                keys = KV[l, 0, rows, lanes]
                values = KV[l, 1, rows, lanes]
                for e in range(2):
                    h = 2 * k + e
                    p = jnp.exp(nt(keys, qs[e]) + mask - LSE[l, i, h])
                    dp = nn(values, dots[e])
                    PB[h] = (p * (dp - deltas[h])).astype(BF16)
                    PB[2 * pairs + h] = p.astype(BF16)
            for k in range(pairs):
                lanes = slice(k * 128, k * 128 + 128)
                half = slice((k % 2) * 128, (k % 2) * 128 + 128)
                qs = split_pair(Q[l, i, :, lanes], 1)
                dos = split_pair(place[:, lanes], 1)
                h = 2 * k
                BIG[k // 2, rows, half] += nn(PB[h], qs[0]) + nn(PB[h + 1], qs[1])
                BIG[2 + k // 2, rows, half] += nn(PB[2 * pairs + h], dos[0]) + nn(PB[2 * pairs + h + 1], dos[1])
            for k in range(pairs):
                keys = jnp.transpose(KV[l, 0, rows, k * 128 : k * 128 + 128])
                for e in range(2):
                    OACC[2 * k + e] += nn(keys[e * 64 : e * 64 + 64], PB[2 * k + e])
            for k in range(2):

                @pl.when((s == 0) & (i == 1) & (j == k + 1))
                def _():
                    dr_copy(k, k + 1).start()

            @pl.when((s == 1) & (i == 0) & (j == 0))
            def _():
                dr_copy(0, b).wait_recv()
                for q in range(4):
                    BIG[q, pl.ds(pl.multiple_of(b * R, R), R), :] += DR[0, q]
                dr_copy(0, 0).start()

            return c

        lax.fori_loop(0, b + 1, turn, 0)
        for k in range(pairs):
            dq = jnp.concatenate([OACC[2 * k], OACC[2 * k + 1]], axis=0) * HEAD_DIM ** -0.5
            DQ[k // 2, :, (k % 2) * 128 : (k % 2) * 128 + 128] = jnp.transpose(dq).astype(BF16)

    def backward_attention(l, i):
        b = blk_of(i)
        x_copy(1, i).wait_recv()

        def rows_mid(rows):
            g = swapped(1, i, rows) * vec(l, 2)
            dmid = DY[i, rows, :].astype(F32) + norm_pull(MID[l, i, rows, :], g)
            MID[l, i, rows, :] = dmid
            AB[rows, :] = dmid.astype(BF16)

        by_rows(rows_mid)
        for j in range(2):
            RCV[2 + i, :, 512 + j * 256 : 768 + j * 256] = nt(WO[l, j], AB[...]).astype(BF16)
            RCV[2 + i, :, j * 256 : j * 256 + 256] = nt(AB[...], WO[l, j]).astype(BF16)

        @pl.when(i == 1)
        def _():
            @pl.when(l == 0)
            def _():
                @pl.when(s == 0)
                def _():
                    dr_copy(0, 1).wait_send()
                    dr_copy(1, 2).wait_send()

                @pl.when(s == 1)
                def _():
                    dr_copy(0, 0).wait_send()

            def clear(r, c):
                rows = pl.ds(pl.multiple_of(r * R, R), R)
                BIG[:, rows, :] = jnp.zeros((4, R, 256), F32)
                return c

            lax.fori_loop(0, 4, clear, 0)

        attend_back(l, i)
        own = pl.ds(pl.multiple_of(b * R, R), R)

        def rows_norm(rows):
            xhat, _ = normalize(H[l, i, rows, :].astype(F32))
            AB[rows, :] = (xhat * vec(l, 0) + vec(l, 1)).astype(BF16)

        by_rows(rows_norm)

        @pl.when(b != 3)
        def _():
            def add(k):
                dr_copy(k, b).wait_recv()
                for c in range(4):
                    BIG[c, own, :] += DR[k, c]

            @pl.when((s == 1) & (i == 1))
            def _():
                add(1)

            @pl.when(s == 0)
            def _():
                add(0)

        for j in range(2):
            DQ[j, :, 256:512] = BIG[j, own, :].astype(BF16)
            DQ[j, :, 512:768] = BIG[2 + j, own, :].astype(BF16)

        ups = [SP[l, j, 24:32, 0:768].astype(BF16) for j in range(2)]
        du = (adapter_scale * (nt(ups[0], DQ[0]) + nt(ups[1], DQ[1]))).astype(BF16)
        GA[l] += nn(du, AB[...])
        top = lax.broadcasted_iota(jnp.int32, (8, 256), 0) < 4
        for j in range(2):
            gq = nn(U[l, i], DQ[j, :, 0:256])
            gv = nn(U[l, i], DQ[j, :, 512:768])
            GB[l, j] += adapter_scale * jnp.where(top, gq, gv)

        x_copy(0, i).wait_send()
        SND[0, i] = (
            nt(DQ[0], WQ[l, 0]) + nt(DQ[1], WQ[l, 1]) + tn(du, SP[l, y, 8:16, :].astype(BF16))
        ).astype(BF16)

        @pl.when(l == 1)
        def _():
            x_copy(0, i).start()

        @pl.when((l == 0) & (i != own_i))
        def _():
            for c in range(4):
                last_copy(c, i).start()

    def core_copies(l):
        return (
            pltpu.make_async_remote_copy(
                GA.at[l], GCA, gc_s.at[0], gc_r.at[0], device_id=sib, device_id_type=MESH),
            pltpu.make_async_remote_copy(
                GB.at[l], GCB, gc_s.at[1], gc_r.at[1], device_id=sib, device_id_type=MESH),
        )

    def plane_copies(l):
        out = []
        for k, (dx, dy) in enumerate(((1, 0), (0, 1), (1, 1))):
            x2 = 1 - x if dx else x
            y2 = 1 - y if dy else y
            to = (s, d, y2 * 2 + x2)
            out.append(pltpu.make_async_remote_copy(
                GA.at[l], GXA.at[k], gx_s.at[k], gx_r.at[k], device_id=to, device_id_type=MESH))
        out.append(pltpu.make_async_remote_copy(
            GB.at[l, 1 - y], GXB, gx_s.at[3], gx_r.at[3], device_id=yp, device_id_type=MESH))
        return out

    def line_copies():
        out = []
        for k in range(1, dp_count):
            to = (s, lax.rem(d + k, dp_count), t)
            out.append(pltpu.make_async_remote_copy(
                GZA.at[d], GZA.at[d], gz_s.at[0, k - 1], gz_r.at[0, k - 1], device_id=to, device_id_type=MESH))
            out.append(pltpu.make_async_remote_copy(
                GZB.at[d], GZB.at[d], gz_s.at[1, k - 1], gz_r.at[1, k - 1], device_id=to, device_id_type=MESH))
        return out

    def sum_core(l):
        @pl.when(s != l)
        def _():
            for c in core_copies(l):
                c.start()

    def sum_plane(l):
        @pl.when(s == l)
        def _():
            for c in core_copies(l):
                c.wait_recv()
            GA[l] += GCA[...]
            GB[l] += GCB[...]
            for c in plane_copies(l):
                c.start()

    def sum_line(l):
        @pl.when(s == l)
        def _():
            for c in plane_copies(l):
                c.wait_recv()
            GZA[d] = (GA[l] + GXA[0]) + (GXA[1] + GXA[2])
            GZB[d] = GB[l, y] + GXB[...]
            for c in line_copies():
                c.start()

    def sum_end(l):
        @pl.when(s == l)
        def _():
            for c in line_copies():
                c.wait_recv()
            total_a, total_b = GZA[0], GZB[0]
            for k in range(1, dp_count):
                total_a, total_b = total_a + GZA[k], total_b + GZB[k]
            out_a[0, 0] = total_a[0:4]
            out_a[0, 1] = total_a[4:8]
            out_b[0, 0] = total_b[0:4]
            out_b[0, 1] = total_b[4:8]

    def bwd_layer(back, carry):
        l = 1 - back

        def f_turn(k, c):
            @pl.when((l == 0) & (k == 1))
            def _():
                sum_plane(1)

            backward_ff(l, 1 - k)
            return c

        def a_turn(k, c):
            @pl.when((l == 0) & (k == 0))
            def _():
                sum_line(1)

            @pl.when((l == 0) & (k == 1))
            def _():
                sum_end(1)

            backward_attention(l, 1 - k)
            return c

        lax.fori_loop(0, 2, f_turn, 0)

        @pl.when(l == 1)
        def _():
            finish_forward()

        lax.fori_loop(0, 2, a_turn, 0)
        sum_core(l)
        return carry

    lax.fori_loop(0, 2, bwd_layer, 0)
    sum_plane(0)

    for c in range(4):
        last_copy(c, own_i).wait_recv()
        rows = slice(c * 64, c * 64 + 64)
        g = swapped(0, own_i, rows) * vec(0, 0)
        AB[rows, :] = (MID[0, own_i, rows, :] + norm_pull(H[0, own_i, rows, :].astype(F32), g)).astype(BF16)
        send_result(3, 0, AB, rows)
    sum_line(0)

    for c in range(4):
        last_copy(c, 1 - own_i).wait_send()
    for i in range(2):
        x_copy(1, i).wait_send()
    x_copy(2, 1 - own_i).wait_send()
    def sent(ref, sem):
        pltpu.make_async_remote_copy(ref, ref, sem, sem, device_id=sib, device_id_type=MESH).wait_send()

    for p in range(5):
        sent(pieces[p][1].at[s, y] if p else SP.at[s, y], ws_s.at[p])
        for c in range(pieces[p][2] if p else 1):
            k = base[p] + c
            ref = block(p, s, y, chunk(p, c, 0)) if p else SP.at[s, y, 16:32, :]
            sent(ref, wy_s.at[k])
            sent(ref, wa_s.at[k])
            if p:
                sent(ref, wz_s.at[k])
                sent(ref, wb_s.at[k])
    rows_done(tok, H.at[0], 0)
    rows_done(cot, DY, 1)
    for l in range(2):
        kv_copy(l, 0).wait_send()

        @pl.when(s == 1)
        def _():
            kv_copy(l, 1).wait_send()

    @pl.when(s == 0)
    def _():
        dr_copy(0, 1).wait_send()
        dr_copy(1, 2).wait_send()

    @pl.when(s == 1)
    def _():
        dr_copy(0, 0).wait_send()

    @pl.when(s == 0)
    def _():
        for c in core_copies(1) + tuple(plane_copies(0)) + tuple(line_copies()):
            c.wait_send()

    @pl.when(s == 1)
    def _():
        for c in core_copies(0) + tuple(plane_copies(1)) + tuple(line_copies()):
            c.wait_send()

    send_result_done(0, 0, H.at[1, 0])
    send_result_done(1, 1, H.at[1, 0])
    send_result_done(2, 1, H.at[1, 0])
    send_result_done(3, 0, H.at[1, 0])
    for o, ref in ((0, act), (1, ig)):
        for m in range(2):
            pltpu.make_async_copy(tok.at[0], ref.at[m], out_rcv.at[o, m]).wait()
    sum_end(0)


def copy_kernel(a_in, g_in, ta_in, tb_in, a_out, g_out, ta_out, tb_out, held_a, held_g, held_ta, held_tb, load, store):
    moves = []
    for k, (src, held, dst) in enumerate(((a_in, held_a, a_out), (g_in, held_g, g_out))):
        for m in range(src.shape[0]):
            moves.append((src.at[m], held.at[m], dst.at[0, m], 2 * k + m))
    moves.append((ta_in, held_ta, ta_out, 4))
    moves.append((tb_in, held_tb, tb_out, 5))
    for src, held, dst, k in moves:
        pltpu.make_async_copy(src, held, load.at[k]).start()
    for src, held, dst, k in moves:
        pltpu.make_async_copy(src, held, load.at[k]).wait()
        pltpu.make_async_copy(held, dst, store.at[k]).start()
    for src, held, dst, k in moves:
        pltpu.make_async_copy(held, dst, store.at[k]).wait()


def settle(act, ig, total_a, total_b):
    anywhere = pl.BlockSpec(memory_space=pl.ANY)
    shapes = [(1,) + act.shape, (1,) + ig.shape, total_a.shape, total_b.shape]
    kinds = [act.dtype, ig.dtype, total_a.dtype, total_b.dtype]
    return pl.pallas_call(
        copy_kernel,
        out_shape=tuple(jax.ShapeDtypeStruct(a, b) for a, b in zip(shapes, kinds)),
        in_specs=[anywhere] * 4,
        out_specs=(anywhere,) * 4,
        scratch_shapes=[
            pltpu.VMEM(v.shape, v.dtype) for v in (act, ig, total_a, total_b)
        ] + [pltpu.SemaphoreType.DMA((6,))] * 2,
        name="settle",
    )(act, ig, total_a, total_b)


def per_pair(
    tokens, cotangent, buckets, lengths, norm_gain_pairs, norm_bias_pairs, query_key_value_weight,
    query_value_bias, output_weight, upward_weight, upward_bias, down_weight, output_bias,
    adapter_down, adapter_upper,
):
    weight_qkv = query_key_value_weight[0].transpose(1, 0, 2)
    dp_count = lax.axis_size("dp")
    anywhere = pl.BlockSpec(memory_space=pl.ANY)
    scalars = pl.BlockSpec(memory_space=pltpu.SMEM)
    vmem = pl.BlockSpec(memory_space=pltpu.VMEM)
    dma = pltpu.SemaphoreType.DMA
    act, ig, total_a, total_b = pl.pallas_call(
        partial(fused_kernel, dp_count),
        out_shape=(
            jax.ShapeDtypeStruct((2, R, D), BF16),
            jax.ShapeDtypeStruct((2, R, D), BF16),
            jax.ShapeDtypeStruct((1, 2, 4, D), F32),
            jax.ShapeDtypeStruct((1, 2, 4, 256), F32),
        ),
        in_specs=[anywhere, anywhere, scalars, scalars, vmem, vmem, anywhere, vmem, anywhere, anywhere, vmem,
                  anywhere, vmem, vmem, vmem],
        out_specs=(anywhere, anywhere, vmem, vmem),
        scratch_shapes=[
            pltpu.VMEM((2, 2, 32, D), F32),
            pltpu.VMEM((2, 2, D, 768), BF16),
            pltpu.VMEM((2, 2, 256, D), BF16),
            pltpu.VMEM((2, 2, D, 1024), BF16),
            pltpu.VMEM((2, 2, 1024, D), BF16),
            pltpu.VMEM((2, 2, R, D), BF16),
            pltpu.VMEM((2, R, D), BF16),
            pltpu.VMEM((2, 2, R, D), F32),
            pltpu.VMEM((2, 2, R, 2048), BF16),
            pltpu.VMEM((2, 2, R, 512), BF16),
            pltpu.VMEM((2, 2, 4 * R, 512), BF16),
            pltpu.VMEM((2, 2, 512, R), BF16),
            pltpu.VMEM((2, 2, 8, 1, R), F32),
            pltpu.VMEM((3, 2, R, D), BF16),
            pltpu.VMEM((5, R, D), BF16),
            pltpu.VMEM((4, 4 * R, R), F32),
            pltpu.VMEM((6 * R, R), BF16),
            pltpu.VMEM((2, 4, R, R), F32),
            pltpu.VMEM((2, R, 768), BF16),
            pltpu.VMEM((R, D), BF16),
            pltpu.VMEM((2, 2, 8, R), BF16),
            pltpu.VMEM((8, 64, R), F32),
            pltpu.VMEM((16, R, R), BF16),
            pltpu.VMEM((2, 8, D), F32),
            pltpu.VMEM((2, 2, 8, 256), F32),
            pltpu.VMEM((8, D), F32),
            pltpu.VMEM((2, 8, 256), F32),
            pltpu.VMEM((3, 8, D), F32),
            pltpu.VMEM((8, 256), F32),
            pltpu.VMEM((dp_count, 8, D), F32),
            pltpu.VMEM((dp_count, 8, 256), F32),
            dma((2, 2)),
            dma((2,)),
            dma((2,)),
            dma((5,)),
            dma((5,)),
            dma((5,)),
            dma((14,)),
            dma((14,)),
            dma((13,)),
            dma((13,)),
            dma((14,)),
            dma((14,)),
            dma((13,)),
            dma((13,)),
            dma((2, 2)),
            dma((2, 2)),
            dma((3, 2)),
            dma((3, 2)),
            dma((4,)),
            dma((4,)),
            dma((2,)),
            dma((2,)),
            dma((2, 2)),
            dma((4,)),
            dma((2,)),
            dma((2,)),
            dma((4,)),
            dma((4,)),
            dma((2, dp_count - 1)),
            dma((2, dp_count - 1)),
        ],
        compiler_params=pltpu.CompilerParams(
            collective_id=0, has_side_effects=True, vmem_limit_bytes=127 * 2**19
        ),
        name="two_layers",
    )(
        tokens, cotangent, buckets, lengths, norm_gain_pairs, norm_bias_pairs, weight_qkv, query_value_bias,
        output_weight, upward_weight, upward_bias, down_weight, output_bias, adapter_down, adapter_upper,
    )
    return settle(act, ig, total_a, total_b)


def solution(mesh):
    in_specs = (
        P("dp", "tensor", None),
        P("dp", "tensor", None),
        P("dp"),
        P("dp", None),
        P("section", None, None),
        P("section", None, None),
        P("section", None, None, "tensor"),
        P("section", None, "tensor"),
        P("section", "tensor", None),
        P("section", None, "tensor"),
        P("section", "tensor"),
        P("section", "tensor", None),
        P("section", None, None),
        P("section", None, None, None),
        P("section", None, None, "tensor"),
    )
    out_specs = (
        P("section", "dp", "tensor", None),
        P("section", "dp", "tensor", None),
        P("section", None, None, None),
        P("section", None, None, "tensor"),
    )
    pairs = mesh.shape["section"] == 2 and mesh.shape["tensor"] == 4 and mesh.shape["dp"] % 2 == 0
    return jax.shard_map(
        per_pair if pairs else per_device, mesh=mesh, in_specs=in_specs, out_specs=out_specs, check_vma=False
    )
```
